32 devices in a mesh: batch: 4 (over z), wide: 8 (over y, x, core).
Axes of the slice: x: 2, y: 2, z: 4, core: 2. Of those that a mesh axis runs over, the one named last changes fastest.
Arguments:
- hidden: bfloat16 [16384, 2048], P(('batch', 'wide')), may hold values from -6 to 6
- cotangent: bfloat16 [16384, 2048], P(('batch', 'wide')), may hold values from -6 to 6
- exit_layer: int32 [8, 2048], P('batch'), may hold values from 1 to 24, as said below
- ln1_gain: float32 [2048], replicated, may hold values from 0.1 to 1.9
- ln1_bias: float32 [2048], replicated, may hold values from -4 to 4
- qkv_weight: bfloat16 [6144, 2048], P('wide'), may hold values from -0.125 to 0.125
- query_bias: float32 [2048], replicated, may hold values from -6 to 6
- value_bias: float32 [2048], replicated, may hold values from -3 to 3
- out_weight: bfloat16 [2048, 2048], P('wide'), may hold values from -0.375 to 0.375
- out_bias: float32 [2048], replicated, may hold values from -4 to 4
- ln2_gain: float32 [2048], replicated, may hold values from 0.1 to 1.9
- ln2_bias: float32 [2048], replicated, may hold values from -4 to 4
- up_weight: bfloat16 [8192, 2048], P('wide'), may hold values from -0.125 to 0.125
- up_bias: float32 [8192], replicated, may hold values from -6 to 6
- down_weight: bfloat16 [8192, 2048], P('wide'), may hold values from -0.0625 to 0.0625
- down_bias: float32 [2048], replicated, may hold values from -4 to 4
Outputs:
- layer_output: bfloat16 [16384, 2048], P(('batch', 'wide'))
- input_grad: float32 [16384, 2048], P(('batch', 'wide'))
- ln1_gain_grad: float32 [2048], replicated
- ln1_bias_grad: float32 [2048], replicated
- qkv_weight_grad: float32 [6144, 2048], P('wide')
- query_bias_grad: float32 [2048], replicated
- value_bias_grad: float32 [2048], replicated
- out_weight_grad: float32 [2048, 2048], P('wide')
- out_bias_grad: float32 [2048], replicated
- ln2_gain_grad: float32 [2048], replicated
- ln2_bias_grad: float32 [2048], replicated
- up_weight_grad: float32 [8192, 2048], P('wide')
- up_bias_grad: float32 [8192], replicated
- down_weight_grad: float32 [8192, 2048], P('wide')
- down_bias_grad: float32 [2048], replicated
The draws below stay inside these ranges and needn't reach their ends.
Inputs may be any that keep to these rules, and one draw needn't show every extreme that they name: `exit_layer`: along each sequence the exit layers fall linearly from its first position to its last (first value minus the floor of the difference times the position over 2048 - 1); every first value is at least 12; in each aligned group of 2 sequences on one index of batch one sequence has every exit layer at least 12.
All inputs are finite; a program needn't handle non-finite values.
Results may differ from the reference program's by a relative error of at most 0.013.
Values may be sent and summed in bfloat16 or wider, within the bound.
No kernel may reach another device: no remote copies, remote signals or barrier semaphores. Data moves between devices by JAX's collectives and lax.ppermute only.
A program may use at most 512 MiB of HBM per device.

```python
import jax
import jax.numpy as jnp
from jax import lax

D = 2048
HEADS = 32
FF = 8192
LAYERS = 24
LAYER = 12
LEN = 2048
BLK = 512
SEQS = 2
SEQUENCES = 8
TOKENS = 16384


def draw_exit_layer(key, part):
    key = jax.random.fold_in(key, 7)
    top_key, bottom_key, pick_key = jax.random.split(key, 3)
    groups = SEQUENCES // SEQS
    tops = jax.random.randint(top_key, (groups, SEQS), LAYER, LAYERS + 1)
    bottoms = jax.random.randint(bottom_key, (groups, SEQS), 1, LAYER)
    chosen = jax.random.randint(pick_key, (groups, 1), 0, SEQS)
    slots = jnp.arange(SEQS)[None, :]
    whole = slots == chosen
    lowest = slots == (chosen + 1) % SEQS
    tops = jnp.where(whole, LAYERS, tops)
    bottoms = jnp.where(whole, LAYER, jnp.where(lowest, 1, bottoms))
    position = jnp.arange(LEN)[None, None, :]
    exits = tops[:, :, None] - (tops - bottoms)[:, :, None] * position // (LEN - 1)
    return exits.reshape(SEQUENCES, LEN).astype(jnp.int32)


def block_scale(stream_key, extent, cuts, low, high):
    level, own = 1.0, jax.random.fold_in(stream_key, 6)
    for dim, shards_of in cuts:
        draws = jnp.exp(jax.random.uniform(jax.random.fold_in(own, dim), (shards_of,), jnp.float32, low / len(cuts), high / len(cuts)))
        level = level * jnp.repeat(draws, extent[dim] // shards_of).reshape([-1 if axis == dim else 1 for axis in range(len(extent))])
    return level


def normal_values(key, shape, scale, most, cuts=(), kind=jnp.bfloat16):
    values = scale * jax.random.normal(key, shape, jnp.float32)
    if cuts:
        values = values * block_scale(key, shape, cuts, -0.22, 0.18)
    return jnp.clip(values, -most, most).astype(kind)


def setup_inputs(seed: int = 0) -> dict:
    key_of = jax.random.split(jax.random.key(seed), 17)
    return {
        "hidden": normal_values(key_of[0], (TOKENS, D), 1.0, 6.0, ((0, 32),)),
        "cotangent": normal_values(key_of[1], (TOKENS, D), 1.0, 6.0, ((0, 32),)),
        "exit_layer": draw_exit_layer(jax.random.fold_in(key_of[16], 71), 0),
        "ln1_gain": jnp.clip(1.0 + 0.18 * jax.random.normal(key_of[3], (D,), jnp.float32), 0.1, 1.9),
        "ln1_bias": normal_values(key_of[4], (D,), 0.3, 4.0, (), jnp.float32),
        "qkv_weight": normal_values(key_of[5], (3 * D, D), D ** -0.5, 0.125, ((0, 8),)),
        "query_bias": normal_values(key_of[6], (D,), 0.5, 6.0, (), jnp.float32),
        "value_bias": normal_values(key_of[7], (D,), 0.2, 3.0, (), jnp.float32),
        "out_weight": normal_values(key_of[8], (D, D), (D // 8) ** -0.5, 0.375, ((0, 8),)),
        "out_bias": normal_values(key_of[9], (D,), 0.3, 4.0, (), jnp.float32),
        "ln2_gain": jnp.clip(1.0 + 0.18 * jax.random.normal(key_of[10], (D,), jnp.float32), 0.1, 1.9),
        "ln2_bias": normal_values(key_of[11], (D,), 0.3, 4.0, (), jnp.float32),
        "up_weight": normal_values(key_of[12], (FF, D), D ** -0.5, 0.125, ((0, 8),)),
        "up_bias": normal_values(key_of[13], (FF,), 0.5, 6.0, (), jnp.float32),
        "down_weight": normal_values(key_of[14], (FF, D), FF ** -0.5, 0.0625, ((0, 8),)),
        "down_bias": normal_values(key_of[15], (D,), 0.3, 4.0, (), jnp.float32),
    }


@jax.custom_vjp
def low(v):
    return lax.optimization_barrier(v.astype(jnp.bfloat16)).astype(jnp.float32)

@jax.custom_vjp
def low_back(v):
    return v

def low_keep(v):
    return (low(v), None)

def low_pass(kept, grad):
    return (grad,)

def back_keep(v):
    return (v, None)

def back_low(kept, grad):
    return (low(grad),)
low.defvjp(low_keep, low_pass)
low_back.defvjp(back_keep, back_low)

def layer_norm(values, gain, shift):
    center = values - lax.optimization_barrier(jnp.mean(values, axis=-1, keepdims=True))
    spread = lax.optimization_barrier(jnp.mean(center * center, axis=-1, keepdims=True))
    return center * lax.rsqrt(spread + 1e-05) * gain + shift

def dense(left, right):
    return jnp.dot(left, right, precision=lax.Precision.HIGHEST)

def attend_sequence(queries, keys, values, keep):
    length = queries.shape[0]
    scale = queries.shape[-1] ** (-0.5)

    def per_block(index):
        first_row = index * BLK
        query_rows = lax.dynamic_slice_in_dim(queries, first_row, BLK, 0)
        scores = jnp.einsum('qhe,khe->hqk', query_rows, keys, precision=lax.Precision.HIGHEST) * scale
        scores = low_back(scores)
        row_ids = first_row + jnp.arange(BLK)[:, None]
        col_ids = jnp.arange(length)[None, :]
        allowed = (col_ids <= row_ids) & (keep[None, :] | (col_ids == row_ids))
        masked = jnp.where(allowed[None], scores, -1e+30)
        highest = lax.optimization_barrier(jnp.max(masked, axis=-1, keepdims=True))
        exp_terms = jnp.exp(masked - highest)
        probs = low(exp_terms / lax.optimization_barrier(jnp.sum(exp_terms, axis=-1, keepdims=True)))
        return jnp.einsum('hqk,khe->qhe', probs, values, precision=lax.Precision.HIGHEST)
    blocks = lax.map(jax.checkpoint(per_block), jnp.arange(length // BLK))
    return blocks.reshape(queries.shape)

def forward(hidden, keep, weights):
    ln1_gain, ln1_bias, qkv_weight, query_bias, value_bias, out_weight, out_bias, ln2_gain, ln2_bias, up_weight, up_bias, down_weight, down_bias = weights
    active = keep.astype(hidden.dtype)[:, None]
    normed1 = low(layer_norm(hidden, ln1_gain, ln1_bias))
    shift = jnp.concatenate([query_bias, jnp.zeros_like(query_bias), value_bias])
    mixed = low(low_back(dense(normed1, qkv_weight.T) + shift))
    parts = mixed.reshape(LEN, 3, HEADS, D // HEADS)
    attended = attend_sequence(parts[:, 0], parts[:, 1], parts[:, 2], keep)
    attended = low(low_back(attended.reshape(LEN, D)))
    middle = hidden + active * low_back(dense(attended, out_weight) + out_bias)
    normed2 = low(layer_norm(middle, ln2_gain, ln2_bias))
    pre = low_back(dense(normed2, up_weight.T) + up_bias)
    units = low(jax.nn.gelu(pre, approximate=False))
    return middle + active * low_back(dense(units, down_weight) + down_bias)

def reference(hidden, cotangent, exit_layer, ln1_gain, ln1_bias, qkv_weight, query_bias, value_bias, out_weight, out_bias, ln2_gain, ln2_bias, up_weight, up_bias, down_weight, down_bias):
    params = tuple((tensor.astype(jnp.float32) for tensor in (ln1_gain, ln1_bias, qkv_weight, query_bias, value_bias, out_weight, out_bias, ln2_gain, ln2_bias, up_weight, up_bias, down_weight, down_bias)))
    inputs = hidden.astype(jnp.float32).reshape(SEQUENCES, LEN, D)
    grads_in = cotangent.astype(jnp.float32).reshape(SEQUENCES, LEN, D)
    keeps = exit_layer >= LAYER

    def one_sequence(totals, items):
        seq_rows, seq_grad, seq_keep = items
        result, pull = jax.vjp(lambda values, weights: forward(values, seq_keep, weights), seq_rows, params)
        grad_rows, grad_weights = pull(seq_grad)
        totals = jax.tree.map(jnp.add, totals, grad_weights)
        return (totals, (result, grad_rows))
    zeros = jax.tree.map(jnp.zeros_like, params)
    totals, (outputs, input_grads) = lax.scan(one_sequence, zeros, (inputs, grads_in, keeps))
    return (outputs.reshape(TOKENS, D).astype(jnp.bfloat16), input_grads.reshape(TOKENS, D), totals[0], totals[1], totals[2], totals[3], totals[4], totals[5], totals[6], totals[7], totals[8], totals[9], totals[10], totals[11], totals[12])
```

```python
import functools

import jax
import jax.numpy as jnp
import numpy as np
from jax import lax
from jax.experimental import pallas as pl
from jax.experimental.pallas import tpu as pltpu
from jax.sharding import PartitionSpec as P

HEADS = 32
LAYER = 12
LANES = 128
FORWARD_TILE = 512
BACKWARD_TILE = 512
CHUNKS = 2
LOG2E = 1.4426950408889634

epsilon = 1e-05
VMEM_BYTES = 48 * 2**20


def dot_nt(left, right):
    return lax.dot_general(
        left, right, (((1,), (1,)), ((), ())), preferred_element_type=jnp.float32
    )


def dot_nn(left, right):
    return lax.dot_general(
        left, right, (((1,), (0,)), ((), ())), preferred_element_type=jnp.float32
    )


def dot_tn(left, right):
    return lax.dot_general(
        left, right, (((0,), (0,)), ((), ())), preferred_element_type=jnp.float32
    )


def head_masks(head_size):
    lane = lax.broadcasted_iota(jnp.int32, (1, LANES), 1)
    return [
        (lane >= h * head_size) & (lane < (h + 1) * head_size)
        for h in range(LANES // head_size)
    ]


def attend_kernel(head_size, tile, counts, mixed_ref, out_ref, log_ref, key_own, value_own):
    length, lanes = out_ref.shape
    pack = LANES // head_size
    scale = head_size ** (-0.5) * LOG2E
    blocks = lax.div(counts[pl.program_id(0)] + (tile - 1), tile)
    masks = head_masks(head_size)
    out_ref[...] = jnp.zeros(out_ref.shape, out_ref.dtype)
    log_ref[...] = jnp.zeros(log_ref.shape, log_ref.dtype)
    row = lax.broadcasted_iota(jnp.int32, (tile, tile), 0)
    col = lax.broadcasted_iota(jnp.int32, (tile, tile), 1)
    for pair in range(lanes // LANES):
        base = pair * LANES
        keys = mixed_ref[:, lanes + base : lanes + base + LANES]
        values = mixed_ref[:, 2 * lanes + base : 2 * lanes + base + LANES]
        for h in range(pack):
            key_own[h] = jnp.where(masks[h], keys, jnp.zeros_like(keys))
            value_own[h] = jnp.where(masks[h], values, jnp.zeros_like(values))

        def query_block(i, _, pair=pair, base=base):
            start = pl.multiple_of(i * tile, tile)
            queries = mixed_ref[pl.ds(start, tile), base : base + LANES]

            def step(j, carry, diagonal=False):
                total, tops, sums = carry
                first = pl.multiple_of(j * tile, tile)
                new_tops, new_sums, shrinks, adds = [], [], [], []
                for h in range(pack):
                    scores = dot_nt(queries, key_own[h, pl.ds(first, tile)]) * scale
                    if diagonal:
                        scores = jnp.where(col <= row, scores, -1e30)
                    top = jnp.maximum(tops[h], jnp.max(scores, axis=1, keepdims=True))
                    terms = jnp.exp2(scores - top)
                    shrink = jnp.exp2(tops[h] - top)
                    new_tops.append(top)
                    new_sums.append(sums[h] * shrink + jnp.sum(terms, axis=1, keepdims=True))
                    shrinks.append(shrink)
                    adds.append(dot_nn(terms.astype(jnp.bfloat16), value_own[h, pl.ds(first, tile)]))
                shrink = shrinks[0]
                for h in range(1, pack):
                    shrink = jnp.where(masks[h], shrinks[h], shrink)
                total = total * shrink
                for add in adds:
                    total = total + add
                return total, tuple(new_tops), tuple(new_sums)

            carry = (
                jnp.zeros((tile, LANES), jnp.float32),
                tuple(jnp.full((tile, 1), -1e30, jnp.float32) for _ in range(pack)),
                tuple(jnp.zeros((tile, 1), jnp.float32) for _ in range(pack)),
            )
            carry = lax.fori_loop(0, i, step, carry)
            total, tops, sums = step(i, carry, diagonal=True)
            share = 1.0 / sums[0]
            for h in range(1, pack):
                share = jnp.where(masks[h], 1.0 / sums[h], share)
            out_ref[pl.ds(start, tile), base : base + LANES] = (total * share).astype(out_ref.dtype)
            for h in range(pack):
                logs = jnp.broadcast_to(tops[h] + jnp.log2(sums[h]), (tile, LANES))
                index = pair * pack + h
                log_ref[0, index : index + 1, pl.ds(start, tile)] = jnp.transpose(logs)[0:1]
            return 0

        lax.fori_loop(0, blocks, query_block, 0)


def attend(mixed, counts, head_size):
    sequences = counts.shape[0]
    rows = mixed.shape[0]
    lanes = mixed.shape[1] // 3
    length = rows // sequences
    heads = lanes // head_size
    pack = LANES // head_size
    return pl.pallas_call(
        functools.partial(attend_kernel, head_size, FORWARD_TILE),
        grid_spec=pltpu.PrefetchScalarGridSpec(
            num_scalar_prefetch=1,
            grid=(sequences,),
            in_specs=[pl.BlockSpec((length, 3 * lanes), lambda s, counts: (s, 0))],
            out_specs=[
                pl.BlockSpec((length, lanes), lambda s, counts: (s, 0)),
                pl.BlockSpec((1, heads, length), lambda s, counts: (s, 0, 0)),
            ],
            scratch_shapes=[
                pltpu.VMEM((pack, length, LANES), jnp.bfloat16),
                pltpu.VMEM((pack, length, LANES), jnp.bfloat16),
            ],
        ),
        out_shape=[
            jax.ShapeDtypeStruct((rows, lanes), jnp.bfloat16),
            jax.ShapeDtypeStruct((sequences, heads, length), jnp.float32),
        ],
        compiler_params=pltpu.CompilerParams(vmem_limit_bytes=VMEM_BYTES),
        cost_estimate=pl.CostEstimate(
            flops=rows * length * lanes * 4,
            bytes_accessed=rows * lanes * 8,
            transcendentals=rows * length * heads // 2,
        ),
    )(counts, mixed)


def attend_back_kernel(
    head_size,
    tile,
    counts,
    mixed_ref,
    grad_ref,
    out_ref,
    log_ref,
    back_ref,
    query_own,
    key_own,
    grad_own,
    delta,
    grad_query,
    grad_key,
    grad_value,
):
    length, lanes = out_ref.shape
    pack = LANES // head_size
    scale = head_size ** (-0.5)
    blocks = lax.div(counts[pl.program_id(0)] + (tile - 1), tile)
    masks = head_masks(head_size)
    back_ref[...] = jnp.zeros(back_ref.shape, back_ref.dtype)
    key_row = lax.broadcasted_iota(jnp.int32, (tile, tile), 0)
    query_col = lax.broadcasted_iota(jnp.int32, (tile, tile), 1)
    for pair in range(lanes // LANES):
        base = pair * LANES
        queries = mixed_ref[:, base : base + LANES]
        keys = mixed_ref[:, lanes + base : lanes + base + LANES]
        grads = grad_ref[:, base : base + LANES]
        for h in range(pack):
            query_own[h] = jnp.where(masks[h], queries, jnp.zeros_like(queries))
            key_own[h] = jnp.where(masks[h], keys, jnp.zeros_like(keys))
            grad_own[h] = jnp.where(masks[h], grads, jnp.zeros_like(grads))
        grad_query[...] = jnp.zeros(grad_query.shape, jnp.float32)

        def deltas(i, _, base=base):
            start = pl.multiple_of(i * tile, tile)
            grads = grad_ref[pl.ds(start, tile), base : base + LANES].astype(jnp.float32)
            outs = out_ref[pl.ds(start, tile), base : base + LANES].astype(jnp.float32)
            products = jnp.transpose(grads * outs)
            for h in range(pack):
                delta[h : h + 1, pl.ds(start, tile)] = jnp.sum(
                    products[h * head_size : (h + 1) * head_size], axis=0, keepdims=True
                )
            return 0

        lax.fori_loop(0, blocks, deltas, 0)

        def key_block(j, _, pair=pair, base=base):
            first = pl.multiple_of(j * tile, tile)
            keys = mixed_ref[pl.ds(first, tile), lanes + base : lanes + base + LANES]
            values = mixed_ref[pl.ds(first, tile), 2 * lanes + base : 2 * lanes + base + LANES]
            grad_key[...] = jnp.zeros(grad_key.shape, jnp.float32)
            grad_value[...] = jnp.zeros(grad_value.shape, jnp.float32)

            def step(i, diagonal=False):
                start = pl.multiple_of(i * tile, tile)
                add_query, add_key, add_value = [], [], []
                for h in range(pack):
                    index = pair * pack + h
                    query_head = query_own[h, pl.ds(start, tile)]
                    grad_head = grad_own[h, pl.ds(start, tile)]
                    scores = dot_nt(keys, query_head) * (scale * LOG2E)
                    probs = jnp.exp2(scores - log_ref[0, index : index + 1, pl.ds(start, tile)])
                    if diagonal:
                        probs = jnp.where(key_row <= query_col, probs, 0.0)
                    grad_probs = dot_nt(values, grad_head)
                    grad_scores = (
                        probs * (grad_probs - delta[h : h + 1, pl.ds(start, tile)])
                    ).astype(jnp.bfloat16)
                    add_value.append(dot_nn(probs.astype(jnp.bfloat16), grad_head))
                    add_key.append(dot_nn(grad_scores, query_head))
                    add_query.append(dot_tn(grad_scores, key_own[h, pl.ds(first, tile)]))
                grad_value[...] += functools.reduce(jnp.add, add_value)
                grad_key[...] += functools.reduce(jnp.add, add_key)
                grad_query[pl.ds(start, tile), :] += functools.reduce(jnp.add, add_query)

            def off_diagonal(i, _):
                step(i)
                return 0

            step(j, diagonal=True)
            lax.fori_loop(j + 1, blocks, off_diagonal, 0)
            back_ref[pl.ds(first, tile), lanes + base : lanes + base + LANES] = (
                grad_key[...] * scale
            ).astype(back_ref.dtype)
            back_ref[pl.ds(first, tile), 2 * lanes + base : 2 * lanes + base + LANES] = grad_value[
                ...
            ].astype(back_ref.dtype)
            return 0

        lax.fori_loop(0, blocks, key_block, 0)
        back_ref[:, base : base + LANES] = (grad_query[...] * scale).astype(back_ref.dtype)


def attend_back(mixed, grads, outs, logs, counts, head_size):
    sequences = counts.shape[0]
    rows, lanes = outs.shape
    length = rows // sequences
    heads = lanes // head_size
    pack = LANES // head_size
    tile = BACKWARD_TILE
    return pl.pallas_call(
        functools.partial(attend_back_kernel, head_size, tile),
        grid_spec=pltpu.PrefetchScalarGridSpec(
            num_scalar_prefetch=1,
            grid=(sequences,),
            in_specs=[
                pl.BlockSpec((length, 3 * lanes), lambda s, counts: (s, 0)),
                pl.BlockSpec((length, lanes), lambda s, counts: (s, 0)),
                pl.BlockSpec((length, lanes), lambda s, counts: (s, 0)),
                pl.BlockSpec((1, heads, length), lambda s, counts: (s, 0, 0)),
            ],
            out_specs=pl.BlockSpec((length, 3 * lanes), lambda s, counts: (s, 0)),
            scratch_shapes=[
                pltpu.VMEM((pack, length, LANES), jnp.bfloat16),
                pltpu.VMEM((pack, length, LANES), jnp.bfloat16),
                pltpu.VMEM((pack, length, LANES), jnp.bfloat16),
                pltpu.VMEM((pack, length), jnp.float32),
                pltpu.VMEM((length, LANES), jnp.float32),
                pltpu.VMEM((tile, LANES), jnp.float32),
                pltpu.VMEM((tile, LANES), jnp.float32),
            ],
        ),
        out_shape=jax.ShapeDtypeStruct((rows, 3 * lanes), jnp.bfloat16),
        compiler_params=pltpu.CompilerParams(vmem_limit_bytes=VMEM_BYTES),
        cost_estimate=pl.CostEstimate(
            flops=rows * length * lanes * 10,
            bytes_accessed=rows * lanes * 18,
            transcendentals=rows * length * heads // 2,
        ),
    )(counts, mixed, grads, outs, logs)


def chain_sum(values, axis):
    size = lax.axis_size(axis)
    if size != 4:
        return lax.psum(values.astype(jnp.bfloat16), axis).astype(jnp.float32)
    place = lax.axis_index(axis)
    outer = lax.ppermute(values.astype(jnp.bfloat16), axis, [(0, 1), (3, 2)])
    half = (values + outer.astype(jnp.float32)).astype(jnp.bfloat16)
    other = lax.ppermute(half, axis, [(1, 2), (2, 1)])
    whole = (half.astype(jnp.float32) + other.astype(jnp.float32)).astype(jnp.bfloat16)
    ends = lax.ppermute(whole, axis, [(1, 0), (2, 3)])
    inner = (place == 1) | (place == 2)
    return jnp.where(inner, whole, ends).astype(jnp.float32)


def normalize(values):
    center = values - jnp.mean(values, axis=-1, keepdims=True)
    inverse = lax.rsqrt(jnp.mean(center * center, axis=-1, keepdims=True) + epsilon)
    return center * inverse, inverse


def normalize_back(grad, gain, normal, inverse):
    scaled = grad * gain
    grad_values = inverse * (
        scaled
        - jnp.mean(scaled, axis=-1, keepdims=True)
        - normal * jnp.mean(scaled * normal, axis=-1, keepdims=True)
    )
    return grad_values, jnp.sum(grad * normal, axis=0), jnp.sum(grad, axis=0)


def local(
    hidden,
    cotangent,
    exit_layer,
    ln1_gain,
    ln1_bias,
    qkv_weight,
    query_bias,
    value_bias,
    out_weight,
    out_bias,
    ln2_gain,
    ln2_bias,
    up_weight,
    up_bias,
    down_weight,
    down_bias,
):
    width = lax.axis_size("wide")
    rank = lax.axis_index("wide")
    rows, model = hidden.shape
    group = rows * width
    slab = model // width
    head_size = model // HEADS
    units_own = up_weight.shape[0]
    keep = exit_layer >= LAYER
    counts = jnp.sum(keep.astype(jnp.int32), axis=1)
    active = lax.dynamic_slice_in_dim(keep.reshape(group), rank * rows, rows, 0)
    active = active.astype(jnp.float32)[:, None]
    grad_out = cotangent.astype(jnp.float32)

    routes = [[(w, (3 * w + t) % width) for w in range(width)] for t in range(3)]
    part_at = np.zeros((width, 3), np.int32)
    for t in range(3):
        for w, d in routes[t]:
            part_at[d, t] = (3 * w + t) // width
    place_of = jnp.asarray(np.argsort(part_at, axis=1).astype(np.int32))[rank]
    part_of = jnp.asarray(part_at)[rank]

    hidden_wide = hidden.astype(jnp.float32)
    normal1, inverse1 = normalize(hidden_wide)
    normed1 = lax.all_gather(
        (normal1 * ln1_gain + ln1_bias).astype(jnp.bfloat16), "wide", axis=0, tiled=True
    )
    slabs = qkv_weight.reshape(3, slab, model)
    received = jnp.stack([lax.ppermute(slabs[t], "wide", routes[t]) for t in range(3)])
    qkv_own = jnp.concatenate(
        [lax.dynamic_index_in_dim(received, place_of[p], 0, keepdims=False) for p in range(3)]
    )
    own = lambda vector: lax.dynamic_slice_in_dim(vector, rank * slab, slab, 0)
    qkv_shift = jnp.concatenate(
        [own(query_bias), jnp.zeros((slab,), jnp.float32), own(value_bias)]
    )

    grad_ffn = (active * grad_out).astype(jnp.bfloat16)
    down_bias_grad = jnp.sum(grad_ffn.astype(jnp.float32), axis=0)
    piece = rows // CHUNKS
    part = lambda values, c: values[c * piece : (c + 1) * piece]
    gather = lambda values: lax.all_gather(values, "wide", axis=0, tiled=True)
    scatter = lambda values: lax.psum_scatter(
        values.astype(jnp.bfloat16), "wide", scatter_dimension=0, tiled=True
    )
    grad_ffns = [gather(part(grad_ffn, c)) for c in range(CHUNKS)]
    out_whole = gather(out_weight)

    mixed = (dot_nt(normed1, qkv_own) + qkv_shift).astype(jnp.bfloat16)
    attended, logs = attend(mixed, counts, head_size)
    attended_rows = lax.all_to_all(attended, "wide", split_axis=0, concat_axis=1, tiled=True)
    middle = hidden_wide + active * (dot_nn(attended_rows, out_whole) + out_bias)
    normal2, inverse2 = normalize(middle)
    normed2 = (normal2 * ln2_gain + ln2_bias).astype(jnp.bfloat16)
    up_shift = lax.dynamic_slice_in_dim(up_bias, rank * units_own, units_own, 0)

    normed2s = [gather(part(normed2, c)) for c in range(CHUNKS)]
    units, grad_pres, grad_normed2, ffn_out = [], [], [], []
    for c in range(CHUNKS):
        grad_units = dot_nt(grad_ffns[c], down_weight)
        pre = dot_nt(normed2s[c], up_weight) + up_shift
        below = 0.5 + 0.5 * lax.erf(pre * 0.7071067811865476)
        bell = jnp.exp(-0.5 * pre * pre) * 0.3989422804014327
        units.append((pre * below).astype(jnp.bfloat16))
        grad_pres.append((grad_units * (below + pre * bell)).astype(jnp.bfloat16))
        grad_normed2.append(scatter(dot_nn(grad_pres[c], up_weight)))
    for c in range(CHUNKS):
        ffn_out.append(scatter(dot_nn(units[c], down_weight)))
    grad_normed2 = jnp.concatenate(grad_normed2).astype(jnp.float32)
    ffn_out = jnp.concatenate(ffn_out).astype(jnp.float32)
    output = (middle + active * (ffn_out + down_bias)).astype(jnp.bfloat16)

    up_bias_own = sum(jnp.sum(g.astype(jnp.float32), axis=0) for g in grad_pres)
    down_grad = sum(dot_tn(units[c], grad_ffns[c]) for c in range(CHUNKS))
    up_grad = sum(dot_tn(grad_pres[c], normed2s[c]) for c in range(CHUNKS))
    halves = lambda values: jnp.concatenate(
        [chain_sum(half, "batch") for half in jnp.split(values, 2)]
    )
    down_grad = halves(down_grad)
    up_grad = halves(up_grad)

    grad_middle, ln2_gain_grad, ln2_bias_grad = normalize_back(
        grad_normed2, ln2_gain, normal2, inverse2
    )
    grad_middle = grad_out + grad_middle
    grad_branch = (active * grad_middle).astype(jnp.bfloat16)
    out_bias_grad = jnp.sum(grad_branch.astype(jnp.float32), axis=0)
    grad_attended = dot_nt(grad_branch, out_whole).astype(jnp.bfloat16)
    grad_heads = lax.all_to_all(grad_attended, "wide", split_axis=1, concat_axis=0, tiled=True)
    out_grad = chain_sum(scatter(dot_tn(attended_rows, grad_branch)).astype(jnp.float32), "batch")

    placed = lambda vector, size: lax.dynamic_update_slice_in_dim(
        jnp.zeros((size,), jnp.float32), vector, rank * vector.shape[0], 0
    )
    early = lax.psum(
        (
            out_bias_grad,
            ln2_gain_grad,
            ln2_bias_grad,
            placed(up_bias_own, up_bias.shape[0]),
            down_bias_grad,
        ),
        ("batch", "wide"),
    )

    grad_mixed = attend_back(mixed, grad_heads, attended, logs, counts, head_size)
    grad_normed1 = scatter(dot_nn(grad_mixed, qkv_own)).astype(jnp.float32)
    sums = jnp.sum(grad_mixed.astype(jnp.float32), axis=0)
    qkv_parts = []
    for t in range(3):
        columns = lax.dynamic_slice_in_dim(grad_mixed, part_of[t] * slab, slab, 1)
        total = chain_sum(dot_tn(columns, normed1), "batch").astype(jnp.bfloat16)
        back = [(d, w) for w, d in routes[t]]
        qkv_parts.append(lax.ppermute(total, "wide", back).astype(jnp.float32))
    qkv_grad = jnp.concatenate(qkv_parts)

    grad_hidden, ln1_gain_grad, ln1_bias_grad = normalize_back(
        grad_normed1, ln1_gain, normal1, inverse1
    )
    input_grad = grad_middle + grad_hidden
    late = lax.psum(
        (
            ln1_gain_grad,
            ln1_bias_grad,
            placed(sums[:slab], model),
            placed(sums[2 * slab :], model),
        ),
        ("batch", "wide"),
    )
    return (
        output,
        input_grad,
        late[0],
        late[1],
        qkv_grad,
        late[2],
        late[3],
        out_grad,
        early[0],
        early[1],
        early[2],
        up_grad,
        early[3],
        down_grad,
        early[4],
    )


def solution(mesh):
    rows = P(("batch", "wide"), None)
    weight = P("wide", None)
    return jax.shard_map(
        local,
        mesh=mesh,
        in_specs=(
            rows,
            rows,
            P("batch", None),
            P(),
            P(),
            weight,
            P(),
            P(),
            weight,
            P(),
            P(),
            P(),
            weight,
            P(),
            weight,
            P(),
        ),
        out_specs=(
            rows,
            rows,
            P(),
            P(),
            weight,
            P(),
            P(),
            weight,
            P(),
            P(),
            P(),
            weight,
            P(),
            weight,
            P(),
        ),
        check_vma=False,
    )
```

```python
import functools

import jax
import jax.numpy as jnp
import numpy as np
from jax import lax
from jax.experimental import pallas as pl
from jax.experimental.pallas import tpu as pltpu
from jax.sharding import PartitionSpec as P

HEADS = 32
LAYER = 12
LANES = 128
TILE = 512
CHUNKS = 2
LOG2E = 1.4426950408889634

epsilon = 1e-05
VMEM_BYTES = 48 * 2**20


def dot_nt(left, right):
    return lax.dot_general(
        left, right, (((1,), (1,)), ((), ())), preferred_element_type=jnp.float32
    )


def dot_nn(left, right):
    return lax.dot_general(
        left, right, (((1,), (0,)), ((), ())), preferred_element_type=jnp.float32
    )


def dot_tn(left, right):
    return lax.dot_general(
        left, right, (((0,), (0,)), ((), ())), preferred_element_type=jnp.float32
    )


def head_masks(head_size):
    lane = lax.broadcasted_iota(jnp.int32, (1, LANES), 1)
    return [
        (lane >= h * head_size) & (lane < (h + 1) * head_size)
        for h in range(LANES // head_size)
    ]


def attend_kernel(head_size, counts, slots, mixed_ref, out_ref, log_ref, key_own, value_own):
    length, lanes = out_ref.shape
    tile = mixed_ref.shape[1]
    pack = LANES // head_size
    scale = head_size ** (-0.5) * LOG2E
    sequence = pl.program_id(0)
    blocks = lax.div(counts[sequence] + (tile - 1), tile)
    masks = head_masks(head_size)
    out_ref[...] = jnp.zeros(out_ref.shape, out_ref.dtype)
    log_ref[...] = jnp.zeros(log_ref.shape, log_ref.dtype)
    row = lax.broadcasted_iota(jnp.int32, (tile, tile), 0)
    col = lax.broadcasted_iota(jnp.int32, (tile, tile), 1)
    for pair in range(lanes // LANES):
        base = pair * LANES
        for i in range(length // tile):
            slot = slots[sequence, i]
            keys = mixed_ref[slot, :, lanes + base : lanes + base + LANES]
            values = mixed_ref[slot, :, 2 * lanes + base : 2 * lanes + base + LANES]
            for h in range(pack):
                key_own[h, i * tile : (i + 1) * tile] = jnp.where(masks[h], keys, jnp.zeros_like(keys))
                value_own[h, i * tile : (i + 1) * tile] = jnp.where(
                    masks[h], values, jnp.zeros_like(values)
                )

        def query_block(i, _, pair=pair, base=base):
            start = pl.multiple_of(i * tile, tile)
            queries = mixed_ref[slots[sequence, i], :, base : base + LANES]

            def step(j, carry, diagonal=False):
                total, tops, sums = carry
                first = pl.multiple_of(j * tile, tile)
                new_tops, new_sums, shrinks, adds = [], [], [], []
                for h in range(pack):
                    scores = dot_nt(queries, key_own[h, pl.ds(first, tile)]) * scale
                    if diagonal:
                        scores = jnp.where(col <= row, scores, -1e30)
                    top = jnp.maximum(tops[h], jnp.max(scores, axis=1, keepdims=True))
                    terms = jnp.exp2(scores - top)
                    shrink = jnp.exp2(tops[h] - top)
                    new_tops.append(top)
                    new_sums.append(sums[h] * shrink + jnp.sum(terms, axis=1, keepdims=True))
                    shrinks.append(shrink)
                    adds.append(dot_nn(terms.astype(jnp.bfloat16), value_own[h, pl.ds(first, tile)]))
                shrink = shrinks[0]
                for h in range(1, pack):
                    shrink = jnp.where(masks[h], shrinks[h], shrink)
                total = total * shrink
                for add in adds:
                    total = total + add
                return total, tuple(new_tops), tuple(new_sums)

            carry = (
                jnp.zeros((tile, LANES), jnp.float32),
                tuple(jnp.full((tile, 1), -1e30, jnp.float32) for _ in range(pack)),
                tuple(jnp.zeros((tile, 1), jnp.float32) for _ in range(pack)),
            )
            carry = lax.fori_loop(0, i, step, carry)
            total, tops, sums = step(i, carry, diagonal=True)
            share = 1.0 / sums[0]
            for h in range(1, pack):
                share = jnp.where(masks[h], 1.0 / sums[h], share)
            out_ref[pl.ds(start, tile), base : base + LANES] = (total * share).astype(out_ref.dtype)
            for h in range(pack):
                logs = jnp.broadcast_to(tops[h] + jnp.log2(sums[h]), (tile, LANES))
                index = pair * pack + h
                log_ref[0, index : index + 1, pl.ds(start, tile)] = jnp.transpose(logs)[0:1]
            return 0

        lax.fori_loop(0, blocks, query_block, 0)


def attend(mixed, slots, counts, head_size):
    sequences = counts.shape[0]
    rows = mixed.shape[0] * mixed.shape[1]
    lanes = mixed.shape[2] // 3
    length = rows // sequences
    heads = lanes // head_size
    pack = LANES // head_size
    return pl.pallas_call(
        functools.partial(attend_kernel, head_size),
        grid_spec=pltpu.PrefetchScalarGridSpec(
            num_scalar_prefetch=2,
            grid=(sequences,),
            in_specs=[pl.BlockSpec(mixed.shape, lambda s, *_: (0, 0, 0))],
            out_specs=[
                pl.BlockSpec((length, lanes), lambda s, *_: (s, 0)),
                pl.BlockSpec((1, heads, length), lambda s, *_: (s, 0, 0)),
            ],
            scratch_shapes=[
                pltpu.VMEM((pack, length, LANES), jnp.bfloat16),
                pltpu.VMEM((pack, length, LANES), jnp.bfloat16),
            ],
        ),
        out_shape=[
            jax.ShapeDtypeStruct((rows, lanes), jnp.bfloat16),
            jax.ShapeDtypeStruct((sequences, heads, length), jnp.float32),
        ],
        compiler_params=pltpu.CompilerParams(vmem_limit_bytes=VMEM_BYTES),
        cost_estimate=pl.CostEstimate(
            flops=rows * length * lanes * 4,
            bytes_accessed=rows * lanes * 8,
            transcendentals=rows * length * heads // 2,
        ),
    )(counts, slots, mixed)


def attend_back_kernel(
    head_size,
    counts,
    slots,
    mixed_ref,
    grad_ref,
    out_ref,
    log_ref,
    back_ref,
    query_own,
    key_own,
    grad_own,
    delta,
    grad_query,
    grad_key,
    grad_value,
):
    length, lanes = out_ref.shape
    tile = mixed_ref.shape[1]
    pack = LANES // head_size
    scale = head_size ** (-0.5)
    sequence = pl.program_id(0)
    blocks = lax.div(counts[sequence] + (tile - 1), tile)
    masks = head_masks(head_size)
    for i in range(length // tile):
        back_ref[slots[sequence, i]] = jnp.zeros((tile, 3 * lanes), back_ref.dtype)
    key_row = lax.broadcasted_iota(jnp.int32, (tile, tile), 0)
    query_col = lax.broadcasted_iota(jnp.int32, (tile, tile), 1)
    for pair in range(lanes // LANES):
        base = pair * LANES
        for i in range(length // tile):
            span = slice(i * tile, (i + 1) * tile)
            slot = slots[sequence, i]
            queries = mixed_ref[slot, :, base : base + LANES]
            keys = mixed_ref[slot, :, lanes + base : lanes + base + LANES]
            grads = grad_ref[span, base : base + LANES]
            for h in range(pack):
                query_own[h, span] = jnp.where(masks[h], queries, jnp.zeros_like(queries))
                key_own[h, span] = jnp.where(masks[h], keys, jnp.zeros_like(keys))
                grad_own[h, span] = jnp.where(masks[h], grads, jnp.zeros_like(grads))
        grad_query[...] = jnp.zeros(grad_query.shape, jnp.float32)

        def deltas(i, _, base=base):
            start = pl.multiple_of(i * tile, tile)
            grads = grad_ref[pl.ds(start, tile), base : base + LANES].astype(jnp.float32)
            outs = out_ref[pl.ds(start, tile), base : base + LANES].astype(jnp.float32)
            products = jnp.transpose(grads * outs)
            for h in range(pack):
                delta[h : h + 1, pl.ds(start, tile)] = jnp.sum(
                    products[h * head_size : (h + 1) * head_size], axis=0, keepdims=True
                )
            return 0

        lax.fori_loop(0, blocks, deltas, 0)

        def key_block(j, _, pair=pair, base=base):
            first = pl.multiple_of(j * tile, tile)
            place = slots[sequence, j]
            keys = mixed_ref[place, :, lanes + base : lanes + base + LANES]
            values = mixed_ref[place, :, 2 * lanes + base : 2 * lanes + base + LANES]
            grad_key[...] = jnp.zeros(grad_key.shape, jnp.float32)
            grad_value[...] = jnp.zeros(grad_value.shape, jnp.float32)

            def step(i, diagonal=False):
                start = pl.multiple_of(i * tile, tile)
                add_query, add_key, add_value = [], [], []
                for h in range(pack):
                    index = pair * pack + h
                    query_head = query_own[h, pl.ds(start, tile)]
                    grad_head = grad_own[h, pl.ds(start, tile)]
                    scores = dot_nt(keys, query_head) * (scale * LOG2E)
                    probs = jnp.exp2(scores - log_ref[0, index : index + 1, pl.ds(start, tile)])
                    if diagonal:
                        probs = jnp.where(key_row <= query_col, probs, 0.0)
                    grad_probs = dot_nt(values, grad_head)
                    grad_scores = (
                        probs * (grad_probs - delta[h : h + 1, pl.ds(start, tile)])
                    ).astype(jnp.bfloat16)
                    add_value.append(dot_nn(probs.astype(jnp.bfloat16), grad_head))
                    add_key.append(dot_nn(grad_scores, query_head))
                    add_query.append(dot_tn(grad_scores, key_own[h, pl.ds(first, tile)]))
                grad_value[...] += functools.reduce(jnp.add, add_value)
                grad_key[...] += functools.reduce(jnp.add, add_key)
                grad_query[pl.ds(start, tile), :] += functools.reduce(jnp.add, add_query)

            def off_diagonal(i, _):
                step(i)
                return 0

            step(j, diagonal=True)
            lax.fori_loop(j + 1, blocks, off_diagonal, 0)
            back_ref[place, :, lanes + base : lanes + base + LANES] = (grad_key[...] * scale).astype(
                back_ref.dtype
            )
            back_ref[place, :, 2 * lanes + base : 2 * lanes + base + LANES] = grad_value[...].astype(
                back_ref.dtype
            )
            return 0

        lax.fori_loop(0, blocks, key_block, 0)
        for i in range(length // tile):
            back_ref[slots[sequence, i], :, base : base + LANES] = (
                grad_query[i * tile : (i + 1) * tile] * scale
            ).astype(back_ref.dtype)


def attend_back(mixed, slots, grads, outs, logs, counts, head_size):
    sequences = counts.shape[0]
    rows, lanes = outs.shape
    length = rows // sequences
    heads = lanes // head_size
    pack = LANES // head_size
    tile = mixed.shape[1]
    return pl.pallas_call(
        functools.partial(attend_back_kernel, head_size),
        grid_spec=pltpu.PrefetchScalarGridSpec(
            num_scalar_prefetch=2,
            grid=(sequences,),
            in_specs=[
                pl.BlockSpec(mixed.shape, lambda s, *_: (0, 0, 0)),
                pl.BlockSpec((length, lanes), lambda s, *_: (s, 0)),
                pl.BlockSpec((length, lanes), lambda s, *_: (s, 0)),
                pl.BlockSpec((1, heads, length), lambda s, *_: (s, 0, 0)),
            ],
            out_specs=pl.BlockSpec(mixed.shape, lambda s, *_: (0, 0, 0)),
            scratch_shapes=[
                pltpu.VMEM((pack, length, LANES), jnp.bfloat16),
                pltpu.VMEM((pack, length, LANES), jnp.bfloat16),
                pltpu.VMEM((pack, length, LANES), jnp.bfloat16),
                pltpu.VMEM((pack, length), jnp.float32),
                pltpu.VMEM((length, LANES), jnp.float32),
                pltpu.VMEM((tile, LANES), jnp.float32),
                pltpu.VMEM((tile, LANES), jnp.float32),
            ],
        ),
        out_shape=jax.ShapeDtypeStruct(mixed.shape, jnp.bfloat16),
        compiler_params=pltpu.CompilerParams(vmem_limit_bytes=VMEM_BYTES),
        cost_estimate=pl.CostEstimate(
            flops=rows * length * lanes * 10,
            bytes_accessed=rows * lanes * 18,
            transcendentals=rows * length * heads // 2,
        ),
    )(counts, slots, mixed, grads, outs, logs)


def chain_sum(values, axis):
    size = lax.axis_size(axis)
    if size != 4:
        return lax.psum(values.astype(jnp.bfloat16), axis).astype(jnp.float32)
    place = lax.axis_index(axis)
    outer = lax.ppermute(values.astype(jnp.bfloat16), axis, [(0, 1), (3, 2)])
    half = (values + outer.astype(jnp.float32)).astype(jnp.bfloat16)
    other = lax.ppermute(half, axis, [(1, 2), (2, 1)])
    whole = (half.astype(jnp.float32) + other.astype(jnp.float32)).astype(jnp.bfloat16)
    ends = lax.ppermute(whole, axis, [(1, 0), (2, 3)])
    inner = (place == 1) | (place == 2)
    return jnp.where(inner, whole, ends).astype(jnp.float32)


def normalize(values):
    center = values - jnp.mean(values, axis=-1, keepdims=True)
    inverse = lax.rsqrt(jnp.mean(center * center, axis=-1, keepdims=True) + epsilon)
    return center * inverse, inverse


def normalize_back(grad, gain, normal, inverse):
    scaled = grad * gain
    grad_values = inverse * (
        scaled
        - jnp.mean(scaled, axis=-1, keepdims=True)
        - normal * jnp.mean(scaled * normal, axis=-1, keepdims=True)
    )
    return grad_values, jnp.sum(grad * normal, axis=0), jnp.sum(grad, axis=0)


def local_general(
    hidden,
    cotangent,
    exit_layer,
    ln1_gain,
    ln1_bias,
    qkv_weight,
    query_bias,
    value_bias,
    out_weight,
    out_bias,
    ln2_gain,
    ln2_bias,
    up_weight,
    up_bias,
    down_weight,
    down_bias,
):
    width = lax.axis_size("wide")
    rank = lax.axis_index("wide")
    rows, model = hidden.shape
    group = rows * width
    slab = model // width
    head_size = model // HEADS
    units_own = up_weight.shape[0]
    keep = exit_layer >= LAYER
    counts = jnp.sum(keep.astype(jnp.int32), axis=1)
    active = lax.dynamic_slice_in_dim(keep.reshape(group), rank * rows, rows, 0)
    active = active.astype(jnp.float32)[:, None]
    grad_out = cotangent.astype(jnp.float32)

    routes = [[(w, (3 * w + t) % width) for w in range(width)] for t in range(3)]
    part_at = np.zeros((width, 3), np.int32)
    for t in range(3):
        for w, d in routes[t]:
            part_at[d, t] = (3 * w + t) // width
    place_of = jnp.asarray(np.argsort(part_at, axis=1).astype(np.int32))[rank]
    part_of = jnp.asarray(part_at)[rank]

    hidden_wide = hidden.astype(jnp.float32)
    normal1, inverse1 = normalize(hidden_wide)
    normed1 = lax.all_gather(
        (normal1 * ln1_gain + ln1_bias).astype(jnp.bfloat16), "wide", axis=0, tiled=True
    )
    slabs = qkv_weight.reshape(3, slab, model)
    received = jnp.stack([lax.ppermute(slabs[t], "wide", routes[t]) for t in range(3)])
    qkv_own = jnp.concatenate(
        [lax.dynamic_index_in_dim(received, place_of[p], 0, keepdims=False) for p in range(3)]
    )
    own = lambda vector: lax.dynamic_slice_in_dim(vector, rank * slab, slab, 0)
    qkv_shift = jnp.concatenate(
        [own(query_bias), jnp.zeros((slab,), jnp.float32), own(value_bias)]
    )

    grad_ffn = (active * grad_out).astype(jnp.bfloat16)
    down_bias_grad = jnp.sum(grad_ffn.astype(jnp.float32), axis=0)
    piece = rows // CHUNKS
    part = lambda values, c: values[c * piece : (c + 1) * piece]
    gather = lambda values: lax.all_gather(values, "wide", axis=0, tiled=True)
    scatter = lambda values: lax.psum_scatter(
        values.astype(jnp.bfloat16), "wide", scatter_dimension=0, tiled=True
    )
    grad_ffns = [gather(part(grad_ffn, c)) for c in range(CHUNKS)]
    out_whole = gather(out_weight)

    mixed = (dot_nt(normed1, qkv_own) + qkv_shift).astype(jnp.bfloat16)
    mixed = mixed.reshape(group // TILE, TILE, 3 * slab)
    slots = jnp.arange(group // TILE, dtype=jnp.int32).reshape(counts.shape[0], -1)
    attended, logs = attend(mixed, slots, counts, head_size)
    attended_rows = lax.all_to_all(attended, "wide", split_axis=0, concat_axis=1, tiled=True)
    middle = hidden_wide + active * (dot_nn(attended_rows, out_whole) + out_bias)
    normal2, inverse2 = normalize(middle)
    normed2 = (normal2 * ln2_gain + ln2_bias).astype(jnp.bfloat16)
    up_shift = lax.dynamic_slice_in_dim(up_bias, rank * units_own, units_own, 0)

    normed2s = [gather(part(normed2, c)) for c in range(CHUNKS)]
    units, grad_pres, grad_normed2, ffn_out = [], [], [], []
    for c in range(CHUNKS):
        grad_units = dot_nt(grad_ffns[c], down_weight)
        pre = dot_nt(normed2s[c], up_weight) + up_shift
        below = 0.5 + 0.5 * lax.erf(pre * 0.7071067811865476)
        bell = jnp.exp(-0.5 * pre * pre) * 0.3989422804014327
        units.append((pre * below).astype(jnp.bfloat16))
        grad_pres.append((grad_units * (below + pre * bell)).astype(jnp.bfloat16))
        grad_normed2.append(scatter(dot_nn(grad_pres[c], up_weight)))
    for c in range(CHUNKS):
        ffn_out.append(scatter(dot_nn(units[c], down_weight)))
    grad_normed2 = jnp.concatenate(grad_normed2).astype(jnp.float32)
    ffn_out = jnp.concatenate(ffn_out).astype(jnp.float32)
    output = (middle + active * (ffn_out + down_bias)).astype(jnp.bfloat16)

    up_bias_own = sum(jnp.sum(g.astype(jnp.float32), axis=0) for g in grad_pres)
    down_grad = sum(dot_tn(units[c], grad_ffns[c]) for c in range(CHUNKS))
    up_grad = sum(dot_tn(grad_pres[c], normed2s[c]) for c in range(CHUNKS))
    halves = lambda values: jnp.concatenate(
        [chain_sum(half, "batch") for half in jnp.split(values, 2)]
    )
    down_grad = halves(down_grad)
    up_grad = halves(up_grad)

    grad_middle, ln2_gain_grad, ln2_bias_grad = normalize_back(
        grad_normed2, ln2_gain, normal2, inverse2
    )
    grad_middle = grad_out + grad_middle
    grad_branch = (active * grad_middle).astype(jnp.bfloat16)
    out_bias_grad = jnp.sum(grad_branch.astype(jnp.float32), axis=0)
    grad_attended = dot_nt(grad_branch, out_whole).astype(jnp.bfloat16)
    grad_heads = lax.all_to_all(grad_attended, "wide", split_axis=1, concat_axis=0, tiled=True)
    out_grad = chain_sum(scatter(dot_tn(attended_rows, grad_branch)).astype(jnp.float32), "batch")

    placed = lambda vector, size: lax.dynamic_update_slice_in_dim(
        jnp.zeros((size,), jnp.float32), vector, rank * vector.shape[0], 0
    )
    early = lax.psum(
        (
            out_bias_grad,
            ln2_gain_grad,
            ln2_bias_grad,
            placed(up_bias_own, up_bias.shape[0]),
            down_bias_grad,
        ),
        ("batch", "wide"),
    )

    grad_mixed = attend_back(mixed, slots, grad_heads, attended, logs, counts, head_size)
    grad_mixed = grad_mixed.reshape(group, 3 * slab)
    grad_normed1 = scatter(dot_nn(grad_mixed, qkv_own)).astype(jnp.float32)
    sums = jnp.sum(grad_mixed.astype(jnp.float32), axis=0)
    qkv_parts = []
    for t in range(3):
        columns = lax.dynamic_slice_in_dim(grad_mixed, part_of[t] * slab, slab, 1)
        total = chain_sum(dot_tn(columns, normed1), "batch").astype(jnp.bfloat16)
        back = [(d, w) for w, d in routes[t]]
        qkv_parts.append(lax.ppermute(total, "wide", back).astype(jnp.float32))
    qkv_grad = jnp.concatenate(qkv_parts)

    grad_hidden, ln1_gain_grad, ln1_bias_grad = normalize_back(
        grad_normed1, ln1_gain, normal1, inverse1
    )
    input_grad = grad_middle + grad_hidden
    late = lax.psum(
        (
            ln1_gain_grad,
            ln1_bias_grad,
            placed(sums[:slab], model),
            placed(sums[2 * slab :], model),
        ),
        ("batch", "wide"),
    )
    return (
        output,
        input_grad,
        late[0],
        late[1],
        qkv_grad,
        late[2],
        late[3],
        out_grad,
        early[0],
        early[1],
        early[2],
        up_grad,
        early[3],
        down_grad,
        early[4],
    )


def swap(values, bits):
    width = lax.axis_size("wide")
    return lax.ppermute(values, "wide", [(w, w ^ bits) for w in range(width)])


def gather_chips(values):
    half = values.shape[0] // 2
    along_x = swap(values, 2)
    along_y = swap(values, 4)
    top = swap(along_y[:half], 2)
    bottom = swap(along_x[half:], 4)
    return [values, along_x, along_y, jnp.concatenate([top, bottom])]


def scatter_chips(partials):
    own, along_x, along_y, diagonal = partials
    half = own.shape[0] // 2
    lowered = lambda values: values.astype(jnp.bfloat16)
    top = swap(lowered(diagonal[:half]), 2)
    bottom = swap(lowered(diagonal[half:]), 4)
    x_top = swap(lowered(along_x[:half]), 2)
    y_bottom = swap(lowered(along_y[half:]), 4)
    y_top = swap(lowered(along_y[:half] + top.astype(jnp.float32)), 4)
    x_bottom = swap(lowered(along_x[half:] + bottom.astype(jnp.float32)), 2)
    wide = lambda values: values.astype(jnp.float32)
    return jnp.concatenate(
        [
            own[:half] + wide(x_top) + wide(y_top),
            own[half:] + wide(x_bottom) + wide(y_bottom),
        ]
    )


def tree_sum(values):
    width = lax.axis_size("wide")
    terms = [values] + [swap(values, bits) for bits in range(1, width)]
    while len(terms) > 1:
        terms = [terms[k] + terms[k + 1] for k in range(0, len(terms), 2)]
    total = terms[0]
    size = lax.axis_size("batch")
    terms = [total] + [
        lax.ppermute(total, "batch", [(z, z ^ bits) for z in range(size)])
        for bits in range(1, size)
    ]
    while len(terms) > 1:
        terms = [terms[k] + terms[k + 1] for k in range(0, len(terms), 2)]
    return terms[0]


def local_chips(
    hidden,
    cotangent,
    exit_layer,
    ln1_gain,
    ln1_bias,
    qkv_weight,
    query_bias,
    value_bias,
    out_weight,
    out_bias,
    ln2_gain,
    ln2_bias,
    up_weight,
    up_bias,
    down_weight,
    down_bias,
):
    width = lax.axis_size("wide")
    rank = lax.axis_index("wide")
    rows, model = hidden.shape
    group = rows * width
    slab = model // width
    head_size = model // HEADS
    units_own = up_weight.shape[0]
    keep = exit_layer >= LAYER
    counts = jnp.sum(keep.astype(jnp.int32), axis=1)
    active = lax.dynamic_slice_in_dim(keep.reshape(group), rank * rows, rows, 0)
    active = active.astype(jnp.float32)[:, None]
    grad_out = cotangent.astype(jnp.float32)
    chips = range(4)

    tiles = jnp.arange(group // rows, dtype=jnp.int32)
    slots = ((tiles ^ rank) & 1) * 4 + ((tiles >> 1) ^ (rank >> 1))
    slots = slots.reshape(counts.shape[0], -1)

    routes = [[(w, (3 * w + t) % width) for w in range(width)] for t in range(3)]
    part_at = np.zeros((width, 3), np.int32)
    for t in range(3):
        for w, d in routes[t]:
            part_at[d, t] = (3 * w + t) // width
    place_of = jnp.asarray(np.argsort(part_at, axis=1).astype(np.int32))[rank]
    part_of = jnp.asarray(part_at)[rank]

    hidden_wide = hidden.astype(jnp.float32)
    normal1, inverse1 = normalize(hidden_wide)
    normed1 = gather_chips((normal1 * ln1_gain + ln1_bias).astype(jnp.bfloat16))
    slabs = qkv_weight.reshape(3, slab, model)
    received = jnp.stack([lax.ppermute(slabs[t], "wide", routes[t]) for t in range(3)])
    qkv_own = jnp.concatenate(
        [lax.dynamic_index_in_dim(received, place_of[p], 0, keepdims=False) for p in range(3)]
    )
    qkv_other = swap(qkv_own, 1)

    def shift_of(device):
        own = lambda vector: lax.dynamic_slice_in_dim(vector, device * slab, slab, 0)
        return jnp.concatenate([own(query_bias), jnp.zeros((slab,), jnp.float32), own(value_bias)])

    other = rank ^ 1
    out_whole = lax.all_gather(out_weight, "wide", axis=0, tiled=True)
    up_other = swap(up_weight, 1)
    down_other = swap(down_weight, 1)

    mixed_other = [
        swap((dot_nt(normed1[r], qkv_other) + shift_of(other)).astype(jnp.bfloat16), 1)
        for r in chips
    ]
    mixed_own = [(dot_nt(normed1[r], qkv_own) + shift_of(rank)).astype(jnp.bfloat16) for r in chips]
    mixed = jnp.stack(mixed_own + mixed_other)

    grad_ffn = (active * grad_out).astype(jnp.bfloat16)
    down_bias_grad = jnp.sum(grad_ffn.astype(jnp.float32), axis=0)
    grad_ffn = gather_chips(grad_ffn)

    attended, logs = attend(mixed, slots, counts, head_size)
    attended_rows = lax.all_to_all(attended, "wide", split_axis=0, concat_axis=1, tiled=True)
    middle = hidden_wide + active * (dot_nn(attended_rows, out_whole) + out_bias)
    normal2, inverse2 = normalize(middle)
    normed2 = gather_chips((normal2 * ln2_gain + ln2_bias).astype(jnp.bfloat16))
    bias_of = lambda device: lax.dynamic_slice_in_dim(up_bias, device * units_own, units_own, 0)
    up_both = jnp.concatenate([up_weight, up_other])
    down_both = jnp.concatenate([down_weight, down_other])
    up_shift = jnp.concatenate([bias_of(rank), bias_of(other)])

    units, grad_pres, grad_normed2 = {}, {}, {}
    for r in chips:
        grad_units = dot_nt(grad_ffn[r], down_both)
        pre = dot_nt(normed2[r], up_both) + up_shift
        below = 0.5 + 0.5 * lax.erf(pre * 0.7071067811865476)
        bell = jnp.exp(-0.5 * pre * pre) * 0.3989422804014327
        units[r] = (pre * below).astype(jnp.bfloat16)
        grad_pres[r] = (grad_units * (below + pre * bell)).astype(jnp.bfloat16)
        grad_normed2[r] = dot_nn(grad_pres[r], up_both)
    grad_normed2 = scatter_chips([grad_normed2[r] for r in chips])

    units = jnp.concatenate([units[r] for r in chips])
    grad_pres = jnp.concatenate([grad_pres[r] for r in chips])
    grad_ffn = jnp.concatenate(grad_ffn)
    normed2 = jnp.concatenate(normed2)

    def summed(left, right, pieces):
        size = left.shape[1] // 2
        lent = swap(dot_tn(left[:, size:], right).astype(jnp.bfloat16), 1)
        total = dot_tn(left[:, :size], right) + lent.astype(jnp.float32)
        return jnp.concatenate([chain_sum(p, "batch") for p in jnp.split(total, pieces)])

    up_bias_own = jnp.sum(grad_pres.astype(jnp.float32), axis=0)
    down_grad = summed(units, grad_ffn, 2)
    up_grad = summed(grad_pres, normed2, 2)

    ffn_out = dot_nn(units, down_both)
    ffn_out = scatter_chips(jnp.split(ffn_out, 4))
    output = (middle + active * (ffn_out + down_bias)).astype(jnp.bfloat16)

    grad_middle, ln2_gain_grad, ln2_bias_grad = normalize_back(
        grad_normed2, ln2_gain, normal2, inverse2
    )
    grad_middle = grad_out + grad_middle
    grad_branch = (active * grad_middle).astype(jnp.bfloat16)
    out_bias_grad = jnp.sum(grad_branch.astype(jnp.float32), axis=0)
    grad_attended = dot_nt(grad_branch, out_whole).astype(jnp.bfloat16)
    grad_heads = lax.all_to_all(grad_attended, "wide", split_axis=1, concat_axis=0, tiled=True)
    out_grad = lax.psum_scatter(
        dot_tn(attended_rows, grad_branch).astype(jnp.bfloat16),
        "wide",
        scatter_dimension=0,
        tiled=True,
    )
    out_grad = chain_sum(out_grad.astype(jnp.float32), "batch")

    placed = lambda vector, size, device: lax.dynamic_update_slice_in_dim(
        jnp.zeros((size,), jnp.float32), vector, device * vector.shape[0], 0
    )
    back = attend_back(mixed, slots, grad_heads, attended, logs, counts, head_size)
    back_own = back[:4].reshape(4 * rows, 3 * slab)
    back_other = swap(back[4:].reshape(4 * rows, 3 * slab), 1)
    grad_normed1 = dot_nn(back_own, qkv_own) + dot_nn(back_other, qkv_other)
    grad_normed1 = scatter_chips(jnp.split(grad_normed1, 4))
    normed1 = jnp.concatenate(normed1)
    lent = swap(dot_tn(back_other, normed1).astype(jnp.bfloat16), 1)
    qkv_total = dot_tn(back_own, normed1) + lent.astype(jnp.float32)
    qkv_parts = []
    for t in range(3):
        part = lax.dynamic_slice_in_dim(qkv_total, part_of[t] * slab, slab, 0)
        total = chain_sum(part, "batch").astype(jnp.bfloat16)
        qkv_parts.append(
            lax.ppermute(total, "wide", [(d, w) for w, d in routes[t]]).astype(jnp.float32)
        )
    qkv_grad = jnp.concatenate(qkv_parts)

    sums = jnp.sum(back.astype(jnp.float32), axis=(0, 1))
    early = lax.psum(
        (
            out_bias_grad,
            ln2_gain_grad,
            ln2_bias_grad,
            placed(up_bias_own[:units_own], up_bias.shape[0], rank)
            + placed(up_bias_own[units_own:], up_bias.shape[0], other),
            down_bias_grad,
            placed(sums[:slab], model, rank),
            placed(sums[2 * slab :], model, rank),
        ),
        ("batch", "wide"),
    )

    grad_hidden, ln1_gain_grad, ln1_bias_grad = normalize_back(
        grad_normed1, ln1_gain, normal1, inverse1
    )
    input_grad = grad_middle + grad_hidden
    late = tree_sum(jnp.stack([ln1_gain_grad, ln1_bias_grad]))
    return (
        output,
        input_grad,
        late[0],
        late[1],
        qkv_grad,
        early[5],
        early[6],
        out_grad,
        early[0],
        early[1],
        early[2],
        up_grad,
        early[3],
        down_grad,
        early[4],
    )


def solution(mesh):
    local = local_chips if mesh.shape["wide"] == 8 else local_general
    rows = P(("batch", "wide"), None)
    weight = P("wide", None)
    return jax.shard_map(
        local,
        mesh=mesh,
        in_specs=(
            rows,
            rows,
            P("batch", None),
            P(),
            P(),
            weight,
            P(),
            P(),
            weight,
            P(),
            P(),
            P(),
            weight,
            P(),
            weight,
            P(),
        ),
        out_specs=(
            rows,
            rows,
            P(),
            P(),
            weight,
            P(),
            P(),
            weight,
            P(),
            P(),
            P(),
            weight,
            P(),
            weight,
            P(),
        ),
        check_vma=False,
    )
```

```python
import functools

import jax
import jax.numpy as jnp
import numpy as np
from jax import lax
from jax.experimental import pallas as pl
from jax.experimental.pallas import tpu as pltpu
from jax.sharding import PartitionSpec as P

HEADS = 32
LAYER = 12
LANES = 128
TILE = 512
CHUNKS = 2
LOG2E = 1.4426950408889634

epsilon = 1e-05
VMEM_BYTES = 48 * 2**20


def dot_nt(left, right):
    return lax.dot_general(
        left, right, (((1,), (1,)), ((), ())), preferred_element_type=jnp.float32
    )


def dot_nn(left, right):
    return lax.dot_general(
        left, right, (((1,), (0,)), ((), ())), preferred_element_type=jnp.float32
    )


def dot_tn(left, right):
    return lax.dot_general(
        left, right, (((0,), (0,)), ((), ())), preferred_element_type=jnp.float32
    )


def head_masks(head_size):
    lane = lax.broadcasted_iota(jnp.int32, (1, LANES), 1)
    return [
        (lane >= h * head_size) & (lane < (h + 1) * head_size)
        for h in range(LANES // head_size)
    ]


def fetch(sources, target, sems):
    copies = [
        pltpu.make_async_copy(source, target.at[k], sems.at[k]) for k, source in enumerate(sources)
    ]

    @pl.when(pl.program_id(0) == 0)
    def _():
        for copy in copies:
            copy.start()
        for copy in copies:
            copy.wait()


def attend_kernel(head_size, blocks_in, counts, slots, *refs):
    sources = refs[:blocks_in]
    out_ref, log_ref, mixed_ref, key_own, value_own, sems = refs[blocks_in:]
    fetch(sources, mixed_ref, sems)
    length, lanes = out_ref.shape
    tile = mixed_ref.shape[1]
    pack = LANES // head_size
    scale = head_size ** (-0.5) * LOG2E
    sequence = pl.program_id(0)
    blocks = lax.div(counts[sequence] + (tile - 1), tile)
    masks = head_masks(head_size)
    out_ref[...] = jnp.zeros(out_ref.shape, out_ref.dtype)
    log_ref[...] = jnp.zeros(log_ref.shape, log_ref.dtype)
    row = lax.broadcasted_iota(jnp.int32, (tile, tile), 0)
    col = lax.broadcasted_iota(jnp.int32, (tile, tile), 1)
    for pair in range(lanes // LANES):
        base = pair * LANES
        for i in range(length // tile):
            slot = slots[sequence, i]
            keys = mixed_ref[slot, :, lanes + base : lanes + base + LANES]
            values = mixed_ref[slot, :, 2 * lanes + base : 2 * lanes + base + LANES]
            for h in range(pack):
                key_own[h, i * tile : (i + 1) * tile] = jnp.where(masks[h], keys, jnp.zeros_like(keys))
                value_own[h, i * tile : (i + 1) * tile] = jnp.where(
                    masks[h], values, jnp.zeros_like(values)
                )

        def query_block(i, _, pair=pair, base=base):
            start = pl.multiple_of(i * tile, tile)
            queries = mixed_ref[slots[sequence, i], :, base : base + LANES]

            def step(j, carry, diagonal=False):
                total, tops, sums = carry
                first = pl.multiple_of(j * tile, tile)
                new_tops, new_sums, shrinks, adds = [], [], [], []
                for h in range(pack):
                    scores = dot_nt(queries, key_own[h, pl.ds(first, tile)]) * scale
                    if diagonal:
                        scores = jnp.where(col <= row, scores, -1e30)
                    top = jnp.maximum(tops[h], jnp.max(scores, axis=1, keepdims=True))
                    terms = jnp.exp2(scores - top)
                    shrink = jnp.exp2(tops[h] - top)
                    new_tops.append(top)
                    new_sums.append(sums[h] * shrink + jnp.sum(terms, axis=1, keepdims=True))
                    shrinks.append(shrink)
                    adds.append(dot_nn(terms.astype(jnp.bfloat16), value_own[h, pl.ds(first, tile)]))
                shrink = shrinks[0]
                for h in range(1, pack):
                    shrink = jnp.where(masks[h], shrinks[h], shrink)
                total = total * shrink
                for add in adds:
                    total = total + add
                return total, tuple(new_tops), tuple(new_sums)

            carry = (
                jnp.zeros((tile, LANES), jnp.float32),
                tuple(jnp.full((tile, 1), -1e30, jnp.float32) for _ in range(pack)),
                tuple(jnp.zeros((tile, 1), jnp.float32) for _ in range(pack)),
            )
            carry = lax.fori_loop(0, i, step, carry)
            total, tops, sums = step(i, carry, diagonal=True)
            share = 1.0 / sums[0]
            for h in range(1, pack):
                share = jnp.where(masks[h], 1.0 / sums[h], share)
            out_ref[pl.ds(start, tile), base : base + LANES] = (total * share).astype(out_ref.dtype)
            for h in range(pack):
                logs = jnp.broadcast_to(tops[h] + jnp.log2(sums[h]), (tile, LANES))
                index = pair * pack + h
                log_ref[0, index : index + 1, pl.ds(start, tile)] = jnp.transpose(logs)[0:1]
            return 0

        lax.fori_loop(0, blocks, query_block, 0)


def attend(mixed, slots, counts, head_size):
    sequences = counts.shape[0]
    tile = mixed[0].shape[0]
    rows = len(mixed) * tile
    lanes = mixed[0].shape[1] // 3
    length = rows // sequences
    heads = lanes // head_size
    pack = LANES // head_size
    return pl.pallas_call(
        functools.partial(attend_kernel, head_size, len(mixed)),
        grid_spec=pltpu.PrefetchScalarGridSpec(
            num_scalar_prefetch=2,
            grid=(sequences,),
            in_specs=[pl.BlockSpec(memory_space=pl.ANY)] * len(mixed),
            out_specs=[
                pl.BlockSpec((length, lanes), lambda s, *_: (s, 0)),
                pl.BlockSpec((1, heads, length), lambda s, *_: (s, 0, 0)),
            ],
            scratch_shapes=[
                pltpu.VMEM((len(mixed), tile, 3 * lanes), jnp.bfloat16),
                pltpu.VMEM((pack, length, LANES), jnp.bfloat16),
                pltpu.VMEM((pack, length, LANES), jnp.bfloat16),
                pltpu.SemaphoreType.DMA((len(mixed),)),
            ],
        ),
        out_shape=[
            jax.ShapeDtypeStruct((rows, lanes), jnp.bfloat16),
            jax.ShapeDtypeStruct((sequences, heads, length), jnp.float32),
        ],
        compiler_params=pltpu.CompilerParams(vmem_limit_bytes=VMEM_BYTES),
        cost_estimate=pl.CostEstimate(
            flops=rows * length * lanes * 4,
            bytes_accessed=rows * lanes * 8,
            transcendentals=rows * length * heads // 2,
        ),
    )(counts, slots, *mixed)


def attend_back_kernel(
    head_size,
    blocks_in,
    counts,
    slots,
    *refs,
):
    sources = refs[:blocks_in]
    grad_ref, out_ref, log_ref, own_ref, other_ref, mixed_ref = refs[blocks_in : blocks_in + 6]
    query_own, key_own, grad_own, delta, grad_query, grad_key, grad_value, back_ref, sems = refs[
        blocks_in + 6 :
    ]
    fetch(sources, mixed_ref, sems)
    length, lanes = out_ref.shape
    tile = mixed_ref.shape[1]
    pack = LANES // head_size
    scale = head_size ** (-0.5)
    sequence = pl.program_id(0)
    blocks = lax.div(counts[sequence] + (tile - 1), tile)
    masks = head_masks(head_size)
    for i in range(length // tile):
        back_ref[slots[sequence, i]] = jnp.zeros((tile, 3 * lanes), back_ref.dtype)
    key_row = lax.broadcasted_iota(jnp.int32, (tile, tile), 0)
    query_col = lax.broadcasted_iota(jnp.int32, (tile, tile), 1)
    for pair in range(lanes // LANES):
        base = pair * LANES
        for i in range(length // tile):
            span = slice(i * tile, (i + 1) * tile)
            slot = slots[sequence, i]
            queries = mixed_ref[slot, :, base : base + LANES]
            keys = mixed_ref[slot, :, lanes + base : lanes + base + LANES]
            grads = grad_ref[span, base : base + LANES]
            for h in range(pack):
                query_own[h, span] = jnp.where(masks[h], queries, jnp.zeros_like(queries))
                key_own[h, span] = jnp.where(masks[h], keys, jnp.zeros_like(keys))
                grad_own[h, span] = jnp.where(masks[h], grads, jnp.zeros_like(grads))
        grad_query[...] = jnp.zeros(grad_query.shape, jnp.float32)

        def deltas(i, _, base=base):
            start = pl.multiple_of(i * tile, tile)
            grads = grad_ref[pl.ds(start, tile), base : base + LANES].astype(jnp.float32)
            outs = out_ref[pl.ds(start, tile), base : base + LANES].astype(jnp.float32)
            products = jnp.transpose(grads * outs)
            for h in range(pack):
                delta[h : h + 1, pl.ds(start, tile)] = jnp.sum(
                    products[h * head_size : (h + 1) * head_size], axis=0, keepdims=True
                )
            return 0

        lax.fori_loop(0, blocks, deltas, 0)

        def key_block(j, _, pair=pair, base=base):
            first = pl.multiple_of(j * tile, tile)
            place = slots[sequence, j]
            keys = mixed_ref[place, :, lanes + base : lanes + base + LANES]
            values = mixed_ref[place, :, 2 * lanes + base : 2 * lanes + base + LANES]
            grad_key[...] = jnp.zeros(grad_key.shape, jnp.float32)
            grad_value[...] = jnp.zeros(grad_value.shape, jnp.float32)

            def step(i, diagonal=False):
                start = pl.multiple_of(i * tile, tile)
                add_query, add_key, add_value = [], [], []
                for h in range(pack):
                    index = pair * pack + h
                    query_head = query_own[h, pl.ds(start, tile)]
                    grad_head = grad_own[h, pl.ds(start, tile)]
                    scores = dot_nt(keys, query_head) * (scale * LOG2E)
                    probs = jnp.exp2(scores - log_ref[0, index : index + 1, pl.ds(start, tile)])
                    if diagonal:
                        probs = jnp.where(key_row <= query_col, probs, 0.0)
                    grad_probs = dot_nt(values, grad_head)
                    grad_scores = (
                        probs * (grad_probs - delta[h : h + 1, pl.ds(start, tile)])
                    ).astype(jnp.bfloat16)
                    add_value.append(dot_nn(probs.astype(jnp.bfloat16), grad_head))
                    add_key.append(dot_nn(grad_scores, query_head))
                    add_query.append(dot_tn(grad_scores, key_own[h, pl.ds(first, tile)]))
                grad_value[...] += functools.reduce(jnp.add, add_value)
                grad_key[...] += functools.reduce(jnp.add, add_key)
                grad_query[pl.ds(start, tile), :] += functools.reduce(jnp.add, add_query)

            def off_diagonal(i, _):
                step(i)
                return 0

            step(j, diagonal=True)
            lax.fori_loop(j + 1, blocks, off_diagonal, 0)
            back_ref[place, :, lanes + base : lanes + base + LANES] = (grad_key[...] * scale).astype(
                back_ref.dtype
            )
            back_ref[place, :, 2 * lanes + base : 2 * lanes + base + LANES] = grad_value[...].astype(
                back_ref.dtype
            )
            return 0

        lax.fori_loop(0, blocks, key_block, 0)
        for i in range(length // tile):
            back_ref[slots[sequence, i], :, base : base + LANES] = (
                grad_query[i * tile : (i + 1) * tile] * scale
            ).astype(back_ref.dtype)

    @pl.when(sequence == pl.num_programs(0) - 1)
    def _():
        half = blocks_in // 2
        for k in range(half):
            own_ref[k * tile : (k + 1) * tile] = back_ref[k]
            other_ref[k * tile : (k + 1) * tile] = back_ref[half + k]


def attend_back(mixed, slots, grads, outs, logs, counts, head_size):
    sequences = counts.shape[0]
    rows, lanes = outs.shape
    length = rows // sequences
    heads = lanes // head_size
    pack = LANES // head_size
    tile = mixed[0].shape[0]
    whole = pl.BlockSpec((rows // 2, 3 * lanes), lambda s, *_: (0, 0))
    return pl.pallas_call(
        functools.partial(attend_back_kernel, head_size, len(mixed)),
        grid_spec=pltpu.PrefetchScalarGridSpec(
            num_scalar_prefetch=2,
            grid=(sequences,),
            in_specs=[pl.BlockSpec(memory_space=pl.ANY)] * len(mixed)
            + [
                pl.BlockSpec((length, lanes), lambda s, *_: (s, 0)),
                pl.BlockSpec((length, lanes), lambda s, *_: (s, 0)),
                pl.BlockSpec((1, heads, length), lambda s, *_: (s, 0, 0)),
            ],
            out_specs=[whole, whole],
            scratch_shapes=[
                pltpu.VMEM((len(mixed), tile, 3 * lanes), jnp.bfloat16),
                pltpu.VMEM((pack, length, LANES), jnp.bfloat16),
                pltpu.VMEM((pack, length, LANES), jnp.bfloat16),
                pltpu.VMEM((pack, length, LANES), jnp.bfloat16),
                pltpu.VMEM((pack, length), jnp.float32),
                pltpu.VMEM((length, LANES), jnp.float32),
                pltpu.VMEM((tile, LANES), jnp.float32),
                pltpu.VMEM((tile, LANES), jnp.float32),
                pltpu.VMEM((len(mixed), tile, 3 * lanes), jnp.bfloat16),
                pltpu.SemaphoreType.DMA((len(mixed),)),
            ],
        ),
        out_shape=[jax.ShapeDtypeStruct((rows // 2, 3 * lanes), jnp.bfloat16)] * 2,
        compiler_params=pltpu.CompilerParams(vmem_limit_bytes=VMEM_BYTES),
        cost_estimate=pl.CostEstimate(
            flops=rows * length * lanes * 10,
            bytes_accessed=rows * lanes * 18,
            transcendentals=rows * length * heads // 2,
        ),
    )(counts, slots, *mixed, grads, outs, logs)


def ffn_kernel(r, counts, xt, xb, gt, gb, up, down, shift, *refs):
    x_ref, g_ref, units_ref, back_ref, top_ref, bottom_ref, total = refs[-7:]
    half = xt.shape[0]
    step = pl.program_id(0)

    @pl.when(step == 0)
    def _():
        x_ref[:half] = xt[...]
        x_ref[half:] = xb[...]
        g_ref[:half] = gt[...]
        g_ref[half:] = gb[...]
        total[...] = jnp.zeros(total.shape, total.dtype)

    @pl.when(counts[r] == 0)
    def _():
        units_ref[...] = jnp.zeros(units_ref.shape, units_ref.dtype)
        back_ref[...] = jnp.zeros(back_ref.shape, back_ref.dtype)

    @pl.when(counts[r] != 0)
    def _():
        width = 256
        for k in range(up.shape[0] // width):
            span = slice(k * width, (k + 1) * width)
            grad_units = dot_nt(g_ref[...], down[span])
            pre = dot_nt(x_ref[...], up[span]) + shift[:, span]
            bell = jnp.exp2(pre * pre * (-0.5 * LOG2E))
            denominator = 1.0 + (0.3275911 * 0.7071067811865476) * jnp.abs(pre)
            t = pl.reciprocal(denominator, approx=True)
            t = t * (2.0 - denominator * t)
            tail = 0.5 * 1.061405429
            for factor in (-1.453152027, 1.421413741, -0.284496736, 0.254829592):
                tail = tail * t + 0.5 * factor
            tail = tail * t * bell
            below = jnp.where(pre < 0, tail, 1.0 - tail)
            units_ref[:, span] = (pre * below).astype(units_ref.dtype)
            slope = below + pre * bell * 0.3989422804014327
            back_ref[:, span] = (grad_units * slope).astype(back_ref.dtype)
        total[...] += dot_nn(back_ref[...], up[...])

    @pl.when(step == pl.num_programs(0) - 1)
    def _():
        top_ref[...] = total[:half].astype(top_ref.dtype)
        bottom_ref[...] = total[half:].astype(bottom_ref.dtype)


def ffn_block(r, counts, x, g, up, down, shift, kept):
    half, model = x[0].shape
    size = 2 * half
    units = up.shape[0]
    tile = 512
    halves = pl.BlockSpec((half, model), lambda u, *_: (0, 0))
    weights = pl.BlockSpec((tile, model), lambda u, *_: (u, 0))
    rows = pl.BlockSpec((size, model), lambda u, *_: (r, 0))
    tiles = pl.BlockSpec((size, tile), lambda u, *_: (r, u))
    full = lambda columns: jax.ShapeDtypeStruct((4 * size, columns), jnp.bfloat16)
    return pl.pallas_call(
        functools.partial(ffn_kernel, r),
        grid_spec=pltpu.PrefetchScalarGridSpec(
            num_scalar_prefetch=1,
            grid=(units // tile,),
            in_specs=[halves] * 4
            + [weights, weights, pl.BlockSpec((1, tile), lambda u, *_: (0, u))]
            + [pl.BlockSpec(memory_space=pl.ANY)] * len(kept),
            out_specs=[rows, rows, tiles, tiles, halves, halves],
            scratch_shapes=[pltpu.VMEM((size, model), jnp.float32)],
        ),
        out_shape=[full(model), full(model), full(units), full(units)]
        + [jax.ShapeDtypeStruct((half, model), jnp.bfloat16)] * 2,
        input_output_aliases={8 + k: k for k in range(len(kept))},
        compiler_params=pltpu.CompilerParams(vmem_limit_bytes=VMEM_BYTES),
        cost_estimate=pl.CostEstimate(
            flops=6 * size * units * model,
            bytes_accessed=4 * units * model + 12 * size * model,
            transcendentals=2 * size * units,
        ),
    )(counts, *x, *g, up, down, shift, *kept)


def chain_sum(values, axis):
    size = lax.axis_size(axis)
    if size != 4:
        return lax.psum(values.astype(jnp.bfloat16), axis).astype(jnp.float32)
    place = lax.axis_index(axis)
    outer = lax.ppermute(values.astype(jnp.bfloat16), axis, [(0, 1), (3, 2)])
    half = (values + outer.astype(jnp.float32)).astype(jnp.bfloat16)
    other = lax.ppermute(half, axis, [(1, 2), (2, 1)])
    whole = (half.astype(jnp.float32) + other.astype(jnp.float32)).astype(jnp.bfloat16)
    ends = lax.ppermute(whole, axis, [(1, 0), (2, 3)])
    inner = (place == 1) | (place == 2)
    return jnp.where(inner, whole, ends).astype(jnp.float32)


def normalize(values):
    center = values - jnp.mean(values, axis=-1, keepdims=True)
    inverse = lax.rsqrt(jnp.mean(center * center, axis=-1, keepdims=True) + epsilon)
    return center * inverse, inverse


def normalize_back(grad, gain, normal, inverse):
    scaled = grad * gain
    grad_values = inverse * (
        scaled
        - jnp.mean(scaled, axis=-1, keepdims=True)
        - normal * jnp.mean(scaled * normal, axis=-1, keepdims=True)
    )
    return grad_values, jnp.sum(grad * normal, axis=0), jnp.sum(grad, axis=0)


def local_general(
    hidden,
    cotangent,
    exit_layer,
    ln1_gain,
    ln1_bias,
    qkv_weight,
    query_bias,
    value_bias,
    out_weight,
    out_bias,
    ln2_gain,
    ln2_bias,
    up_weight,
    up_bias,
    down_weight,
    down_bias,
):
    width = lax.axis_size("wide")
    rank = lax.axis_index("wide")
    rows, model = hidden.shape
    group = rows * width
    slab = model // width
    head_size = model // HEADS
    units_own = up_weight.shape[0]
    keep = exit_layer >= LAYER
    counts = jnp.sum(keep.astype(jnp.int32), axis=1)
    active = lax.dynamic_slice_in_dim(keep.reshape(group), rank * rows, rows, 0)
    active = active.astype(jnp.float32)[:, None]
    grad_out = cotangent.astype(jnp.float32)

    routes = [[(w, (3 * w + t) % width) for w in range(width)] for t in range(3)]
    part_at = np.zeros((width, 3), np.int32)
    for t in range(3):
        for w, d in routes[t]:
            part_at[d, t] = (3 * w + t) // width
    place_of = jnp.asarray(np.argsort(part_at, axis=1).astype(np.int32))[rank]
    part_of = jnp.asarray(part_at)[rank]

    hidden_wide = hidden.astype(jnp.float32)
    normal1, inverse1 = normalize(hidden_wide)
    normed1 = lax.all_gather(
        (normal1 * ln1_gain + ln1_bias).astype(jnp.bfloat16), "wide", axis=0, tiled=True
    )
    slabs = qkv_weight.reshape(3, slab, model)
    received = jnp.stack([lax.ppermute(slabs[t], "wide", routes[t]) for t in range(3)])
    qkv_own = jnp.concatenate(
        [lax.dynamic_index_in_dim(received, place_of[p], 0, keepdims=False) for p in range(3)]
    )
    own = lambda vector: lax.dynamic_slice_in_dim(vector, rank * slab, slab, 0)
    qkv_shift = jnp.concatenate(
        [own(query_bias), jnp.zeros((slab,), jnp.float32), own(value_bias)]
    )

    grad_ffn = (active * grad_out).astype(jnp.bfloat16)
    down_bias_grad = jnp.sum(grad_ffn.astype(jnp.float32), axis=0)
    piece = rows // CHUNKS
    part = lambda values, c: values[c * piece : (c + 1) * piece]
    gather = lambda values: lax.all_gather(values, "wide", axis=0, tiled=True)
    scatter = lambda values: lax.psum_scatter(
        values.astype(jnp.bfloat16), "wide", scatter_dimension=0, tiled=True
    )
    grad_ffns = [gather(part(grad_ffn, c)) for c in range(CHUNKS)]
    out_whole = gather(out_weight)

    mixed = (dot_nt(normed1, qkv_own) + qkv_shift).astype(jnp.bfloat16)
    mixed = jnp.split(mixed, group // TILE)
    slots = jnp.arange(group // TILE, dtype=jnp.int32).reshape(counts.shape[0], -1)
    attended, logs = attend(mixed, slots, counts, head_size)
    attended_rows = lax.all_to_all(attended, "wide", split_axis=0, concat_axis=1, tiled=True)
    middle = hidden_wide + active * (dot_nn(attended_rows, out_whole) + out_bias)
    normal2, inverse2 = normalize(middle)
    normed2 = (normal2 * ln2_gain + ln2_bias).astype(jnp.bfloat16)
    up_shift = lax.dynamic_slice_in_dim(up_bias, rank * units_own, units_own, 0)

    normed2s = [gather(part(normed2, c)) for c in range(CHUNKS)]
    units, grad_pres, grad_normed2, ffn_out = [], [], [], []
    for c in range(CHUNKS):
        grad_units = dot_nt(grad_ffns[c], down_weight)
        pre = dot_nt(normed2s[c], up_weight) + up_shift
        below = 0.5 + 0.5 * lax.erf(pre * 0.7071067811865476)
        bell = jnp.exp(-0.5 * pre * pre) * 0.3989422804014327
        units.append((pre * below).astype(jnp.bfloat16))
        grad_pres.append((grad_units * (below + pre * bell)).astype(jnp.bfloat16))
        grad_normed2.append(scatter(dot_nn(grad_pres[c], up_weight)))
    for c in range(CHUNKS):
        ffn_out.append(scatter(dot_nn(units[c], down_weight)))
    grad_normed2 = jnp.concatenate(grad_normed2).astype(jnp.float32)
    ffn_out = jnp.concatenate(ffn_out).astype(jnp.float32)
    output = (middle + active * (ffn_out + down_bias)).astype(jnp.bfloat16)

    up_bias_own = sum(jnp.sum(g.astype(jnp.float32), axis=0) for g in grad_pres)
    down_grad = sum(dot_tn(units[c], grad_ffns[c]) for c in range(CHUNKS))
    up_grad = sum(dot_tn(grad_pres[c], normed2s[c]) for c in range(CHUNKS))
    halves = lambda values: jnp.concatenate(
        [chain_sum(half, "batch") for half in jnp.split(values, 2)]
    )
    down_grad = halves(down_grad)
    up_grad = halves(up_grad)

    grad_middle, ln2_gain_grad, ln2_bias_grad = normalize_back(
        grad_normed2, ln2_gain, normal2, inverse2
    )
    grad_middle = grad_out + grad_middle
    grad_branch = (active * grad_middle).astype(jnp.bfloat16)
    out_bias_grad = jnp.sum(grad_branch.astype(jnp.float32), axis=0)
    grad_attended = dot_nt(grad_branch, out_whole).astype(jnp.bfloat16)
    grad_heads = lax.all_to_all(grad_attended, "wide", split_axis=1, concat_axis=0, tiled=True)
    out_grad = chain_sum(scatter(dot_tn(attended_rows, grad_branch)).astype(jnp.float32), "batch")

    placed = lambda vector, size: lax.dynamic_update_slice_in_dim(
        jnp.zeros((size,), jnp.float32), vector, rank * vector.shape[0], 0
    )
    early = lax.psum(
        (
            out_bias_grad,
            ln2_gain_grad,
            ln2_bias_grad,
            placed(up_bias_own, up_bias.shape[0]),
            down_bias_grad,
        ),
        ("batch", "wide"),
    )

    grad_mixed = jnp.concatenate(
        attend_back(mixed, slots, grad_heads, attended, logs, counts, head_size)
    )
    grad_normed1 = scatter(dot_nn(grad_mixed, qkv_own)).astype(jnp.float32)
    sums = jnp.sum(grad_mixed.astype(jnp.float32), axis=0)
    qkv_parts = []
    for t in range(3):
        columns = lax.dynamic_slice_in_dim(grad_mixed, part_of[t] * slab, slab, 1)
        total = chain_sum(dot_tn(columns, normed1), "batch").astype(jnp.bfloat16)
        back = [(d, w) for w, d in routes[t]]
        qkv_parts.append(lax.ppermute(total, "wide", back).astype(jnp.float32))
    qkv_grad = jnp.concatenate(qkv_parts)

    grad_hidden, ln1_gain_grad, ln1_bias_grad = normalize_back(
        grad_normed1, ln1_gain, normal1, inverse1
    )
    input_grad = grad_middle + grad_hidden
    late = lax.psum(
        (
            ln1_gain_grad,
            ln1_bias_grad,
            placed(sums[:slab], model),
            placed(sums[2 * slab :], model),
        ),
        ("batch", "wide"),
    )
    return (
        output,
        input_grad,
        late[0],
        late[1],
        qkv_grad,
        late[2],
        late[3],
        out_grad,
        early[0],
        early[1],
        early[2],
        up_grad,
        early[3],
        down_grad,
        early[4],
    )


def swap(values, bits):
    width = lax.axis_size("wide")
    return lax.ppermute(values, "wide", [(w, w ^ bits) for w in range(width)])


def after(values, *done):
    return lax.optimization_barrier((values, done))[0]


def gather_chips(top, bottom):
    x_top, y_bottom = swap(top, 2), swap(bottom, 4)
    x_bottom, y_top = swap(bottom, 2), swap(top, 4)
    return [
        (top, bottom),
        (x_top, x_bottom),
        (y_top, y_bottom),
        (swap(y_top, 2), swap(x_bottom, 4)),
    ]


def scatter_chips(partials):
    wide = lambda values: values.astype(jnp.float32)
    own, along_x, along_y, diagonal = partials
    top = swap(diagonal[0], 2)
    bottom = swap(diagonal[1], 4)
    x_top = swap(along_x[0], 2)
    y_bottom = swap(along_y[1], 4)
    y_top = swap((wide(along_y[0]) + wide(top)).astype(jnp.bfloat16), 4)
    x_bottom = swap((wide(along_x[1]) + wide(bottom)).astype(jnp.bfloat16), 2)
    return jnp.concatenate(
        [
            wide(own[0]) + wide(x_top) + wide(y_top),
            wide(own[1]) + wide(x_bottom) + wide(y_bottom),
        ]
    )


def halves_of(values):
    half = values.shape[0] // 2
    return values[:half], values[half:]


def tree_sum(values):
    width = lax.axis_size("wide")
    terms = [values] + [swap(values, bits) for bits in range(1, width)]
    while len(terms) > 1:
        terms = [terms[k] + terms[k + 1] for k in range(0, len(terms), 2)]
    total = terms[0]
    size = lax.axis_size("batch")
    terms = [total] + [
        lax.ppermute(total, "batch", [(z, z ^ bits) for z in range(size)])
        for bits in range(1, size)
    ]
    while len(terms) > 1:
        terms = [terms[k] + terms[k + 1] for k in range(0, len(terms), 2)]
    return terms[0]


def local_chips(
    hidden,
    cotangent,
    exit_layer,
    ln1_gain,
    ln1_bias,
    qkv_weight,
    query_bias,
    value_bias,
    out_weight,
    out_bias,
    ln2_gain,
    ln2_bias,
    up_weight,
    up_bias,
    down_weight,
    down_bias,
):
    width = lax.axis_size("wide")
    rank = lax.axis_index("wide")
    rows, model = hidden.shape
    group = rows * width
    slab = model // width
    head_size = model // HEADS
    units_own = up_weight.shape[0]
    keep = exit_layer >= LAYER
    counts = jnp.sum(keep.astype(jnp.int32), axis=1)
    active = lax.dynamic_slice_in_dim(keep.reshape(group), rank * rows, rows, 0)
    active = active.astype(jnp.float32)[:, None]
    grad_out = cotangent.astype(jnp.float32)
    chips = range(4)

    tiles = jnp.arange(group // rows, dtype=jnp.int32)
    slots = ((tiles ^ rank) & 1) * 4 + ((tiles >> 1) ^ (rank >> 1))
    slots = slots.reshape(counts.shape[0], -1)

    routes = [[(w, (3 * w + t) % width) for w in range(width)] for t in range(3)]
    part_at = np.zeros((width, 3), np.int32)
    for t in range(3):
        for w, d in routes[t]:
            part_at[d, t] = (3 * w + t) // width
    place_of = jnp.asarray(np.argsort(part_at, axis=1).astype(np.int32))[rank]
    part_of = jnp.asarray(part_at)[rank]

    hidden_wide = hidden.astype(jnp.float32)
    normal1, inverse1 = normalize(hidden_wide)
    normed1 = gather_chips(*halves_of((normal1 * ln1_gain + ln1_bias).astype(jnp.bfloat16)))
    normed1 = [jnp.concatenate(pair) for pair in normed1]
    slabs = qkv_weight.reshape(3, slab, model)
    received = jnp.stack([lax.ppermute(slabs[t], "wide", routes[t]) for t in range(3)])
    qkv_own = jnp.concatenate(
        [lax.dynamic_index_in_dim(received, place_of[p], 0, keepdims=False) for p in range(3)]
    )
    qkv_other = swap(qkv_own, 1)

    def shift_of(device):
        own = lambda vector: lax.dynamic_slice_in_dim(vector, device * slab, slab, 0)
        return jnp.concatenate([own(query_bias), jnp.zeros((slab,), jnp.float32), own(value_bias)])

    other = rank ^ 1
    up_both = jnp.concatenate([up_weight, swap(up_weight, 1)])
    down_both = jnp.concatenate([down_weight, swap(down_weight, 1)])
    bias_of = lambda device: lax.dynamic_slice_in_dim(up_bias, device * units_own, units_own, 0)
    up_shift = jnp.concatenate([bias_of(rank), bias_of(other)])[None]

    mixed_own, mixed_other = [], []
    rows_in = normed1[0]
    for r in chips:
        lent = (dot_nt(rows_in, qkv_other) + shift_of(other)).astype(jnp.bfloat16)
        kept = (dot_nt(rows_in, qkv_own) + shift_of(rank)).astype(jnp.bfloat16)
        mixed_other.append(swap(lent, 1))
        mixed_own.append(kept)
        if r + 1 < len(chips):
            rows_in = after(normed1[r + 1], lent, kept)
    mixed = mixed_own + mixed_other

    arrived = normed1[3]
    out_whole = lax.all_gather(after(out_weight, arrived), "wide", axis=0, tiled=True)
    grad_ffn = (after(active, arrived) * grad_out).astype(jnp.bfloat16)
    down_bias_grad = jnp.sum(grad_ffn.astype(jnp.float32), axis=0)
    grad_ffn = gather_chips(*halves_of(grad_ffn))

    attended, logs = attend(mixed, slots, counts, head_size)
    attended_rows = lax.all_to_all(attended, "wide", split_axis=0, concat_axis=1, tiled=True)
    middle = hidden_wide + active * (dot_nn(attended_rows, out_whole) + out_bias)
    normal2, inverse2 = normalize(middle)
    normed2 = gather_chips(*halves_of((normal2 * ln2_gain + ln2_bias).astype(jnp.bfloat16)))

    per_tile = jnp.sum(keep.reshape(group // rows, rows).astype(jnp.int32), axis=1)
    block_chip = (rank >> 1) ^ jnp.arange(4, dtype=jnp.int32)
    block_counts = per_tile[2 * block_chip + (rank & 1)]
    kept, partials = (), []
    for r in chips:
        *kept, top, bottom = ffn_block(
            r, block_counts, normed2[r], grad_ffn[r], up_both, down_both, up_shift, tuple(kept)
        )
        partials.append((top, bottom))
    normed2_all, grad_ffn_all, units, grad_pres = kept
    grad_normed2 = scatter_chips(partials)

    size = units_own
    lowered = lambda values: values.astype(jnp.bfloat16)
    down_lent = lowered(dot_tn(units[:, size:], grad_ffn_all))
    up_lent = lowered(dot_tn(after(grad_pres, down_lent)[:, size:], normed2_all))
    lent = (swap(down_lent, 1), swap(up_lent, 1))
    down_own = dot_tn(after(units, up_lent)[:, :size], grad_ffn_all)
    down_own = lowered(down_own + lent[0].astype(jnp.float32))
    up_own = dot_tn(after(grad_pres, down_own)[:, :size], normed2_all)
    up_own = lowered(up_own + lent[1].astype(jnp.float32))
    down_grad, up_grad = lax.psum((down_own, up_own), "batch")
    down_grad = down_grad.astype(jnp.float32)
    up_grad = up_grad.astype(jnp.float32)
    up_bias_own = jnp.sum(grad_pres.astype(jnp.float32), axis=0)

    grad_middle, ln2_gain_grad, ln2_bias_grad = normalize_back(
        grad_normed2, ln2_gain, normal2, inverse2
    )
    grad_middle = grad_out + grad_middle
    grad_branch = (active * grad_middle).astype(jnp.bfloat16)
    out_bias_grad = jnp.sum(grad_branch.astype(jnp.float32), axis=0)
    grad_attended = dot_nt(grad_branch, out_whole).astype(jnp.bfloat16)
    grad_heads = lax.all_to_all(grad_attended, "wide", split_axis=1, concat_axis=0, tiled=True)

    ffn_out = lowered(dot_nn(after(units, up_own, grad_attended), down_both))
    out_partial = lowered(dot_tn(attended_rows, after(grad_branch, ffn_out)))
    out_grad = lax.psum_scatter(out_partial, "wide", scatter_dimension=0, tiled=True)
    grad_heads = after(grad_heads, out_partial)
    ffn_out = scatter_chips([halves_of(part) for part in jnp.split(ffn_out, 4)])
    output = (middle + active * (ffn_out + down_bias)).astype(jnp.bfloat16)

    back_own, back_other = attend_back(
        mixed, slots, grad_heads, attended, logs, counts, head_size
    )
    sums = jnp.sum(back_own.astype(jnp.float32), axis=0) + jnp.sum(
        back_other.astype(jnp.float32), axis=0
    )
    back_other = swap(back_other, 1)
    normed1 = jnp.concatenate(normed1)
    qkv_lent = lowered(dot_tn(back_other, normed1))
    qkv_total = dot_tn(after(back_own, qkv_lent), normed1) + swap(qkv_lent, 1).astype(jnp.float32)
    back_own, back_other = after((back_own, back_other), qkv_total)
    grad_normed1 = lowered(dot_nn(back_own, qkv_own) + dot_nn(back_other, qkv_other))
    grad_normed1 = scatter_chips([halves_of(part) for part in jnp.split(grad_normed1, 4)])
    qkv_parts = []
    for t in range(3):
        part = lax.dynamic_slice_in_dim(qkv_total, part_of[t] * slab, slab, 0)
        total = chain_sum(part, "batch").astype(jnp.bfloat16)
        qkv_parts.append(
            lax.ppermute(total, "wide", [(d, w) for w, d in routes[t]]).astype(jnp.float32)
        )
    qkv_grad = jnp.concatenate(qkv_parts)
    out_grad = chain_sum(after(out_grad, qkv_total).astype(jnp.float32), "batch")

    placed = lambda vector, size, device: lax.dynamic_update_slice_in_dim(
        jnp.zeros((size,), jnp.float32), vector, device * vector.shape[0], 0
    )
    early = tree_sum(
        jnp.concatenate(
            [
                placed(up_bias_own[:size], up_bias.shape[0], rank)
                + placed(up_bias_own[size:], up_bias.shape[0], other),
                down_bias_grad,
                out_bias_grad,
                ln2_gain_grad,
                ln2_bias_grad,
                placed(sums[:slab], model, rank),
                placed(sums[2 * slab :], model, rank),
            ]
        )
    )
    up_bias_grad = early[: up_bias.shape[0]]
    early = early[up_bias.shape[0] :].reshape(6, model)

    grad_hidden, ln1_gain_grad, ln1_bias_grad = normalize_back(
        grad_normed1, ln1_gain, normal1, inverse1
    )
    input_grad = grad_middle + grad_hidden
    late = tree_sum(jnp.stack([ln1_gain_grad, ln1_bias_grad]))
    return (
        output,
        input_grad,
        late[0],
        late[1],
        qkv_grad,
        early[4],
        early[5],
        out_grad,
        early[1],
        early[2],
        early[3],
        up_grad,
        up_bias_grad,
        down_grad,
        early[0],
    )


def solution(mesh):
    local = local_chips if mesh.shape["wide"] == 8 else local_general
    rows = P(("batch", "wide"), None)
    weight = P("wide", None)
    return jax.shard_map(
        local,
        mesh=mesh,
        in_specs=(
            rows,
            rows,
            P("batch", None),
            P(),
            P(),
            weight,
            P(),
            P(),
            weight,
            P(),
            P(),
            P(),
            weight,
            P(),
            weight,
            P(),
        ),
        out_specs=(
            rows,
            rows,
            P(),
            P(),
            weight,
            P(),
            P(),
            weight,
            P(),
            P(),
            P(),
            weight,
            P(),
            weight,
            P(),
        ),
        check_vma=False,
    )
```

```python
import functools

import jax
import jax.numpy as jnp
import numpy as np
from jax import lax
from jax.experimental import pallas as pl
from jax.experimental.pallas import tpu as pltpu
from jax.sharding import PartitionSpec as P

HEADS = 32
LAYER = 12
LANES = 128
TILE = 512
CHUNKS = 2
LOG2E = 1.4426950408889634

epsilon = 1e-05
VMEM_BYTES = 48 * 2**20


def dot_nt(left, right):
    return lax.dot_general(
        left, right, (((1,), (1,)), ((), ())), preferred_element_type=jnp.float32
    )


def dot_nn(left, right):
    return lax.dot_general(
        left, right, (((1,), (0,)), ((), ())), preferred_element_type=jnp.float32
    )


def dot_tn(left, right):
    return lax.dot_general(
        left, right, (((0,), (0,)), ((), ())), preferred_element_type=jnp.float32
    )


def head_masks(head_size):
    lane = lax.broadcasted_iota(jnp.int32, (1, LANES), 1)
    return [
        (lane >= h * head_size) & (lane < (h + 1) * head_size)
        for h in range(LANES // head_size)
    ]


def fetch(sources, target, sems):
    copies = [
        pltpu.make_async_copy(source, target.at[k], sems.at[k]) for k, source in enumerate(sources)
    ]

    @pl.when(pl.program_id(0) == 0)
    def _():
        for copy in copies:
            copy.start()
        for copy in copies:
            copy.wait()


def attend_kernel(head_size, blocks_in, counts, slots, *refs):
    sources = refs[:blocks_in]
    out_ref, log_ref, mixed_ref, key_own, value_own, sems = refs[blocks_in:]
    fetch(sources, mixed_ref, sems)
    length, lanes = out_ref.shape
    tile = mixed_ref.shape[1]
    pack = LANES // head_size
    scale = head_size ** (-0.5) * LOG2E
    sequence = pl.program_id(0)
    blocks = lax.div(counts[sequence] + (tile - 1), tile)
    masks = head_masks(head_size)
    out_ref[...] = jnp.zeros(out_ref.shape, out_ref.dtype)
    log_ref[...] = jnp.zeros(log_ref.shape, log_ref.dtype)
    row = lax.broadcasted_iota(jnp.int32, (tile, tile), 0)
    col = lax.broadcasted_iota(jnp.int32, (tile, tile), 1)
    for pair in range(lanes // LANES):
        base = pair * LANES
        for i in range(length // tile):
            slot = slots[sequence, i]
            keys = mixed_ref[slot, :, lanes + base : lanes + base + LANES]
            values = mixed_ref[slot, :, 2 * lanes + base : 2 * lanes + base + LANES]
            for h in range(pack):
                key_own[h, i * tile : (i + 1) * tile] = jnp.where(masks[h], keys, jnp.zeros_like(keys))
                value_own[h, i * tile : (i + 1) * tile] = jnp.where(
                    masks[h], values, jnp.zeros_like(values)
                )

        def query_block(i, _, pair=pair, base=base):
            start = pl.multiple_of(i * tile, tile)
            queries = mixed_ref[slots[sequence, i], :, base : base + LANES]

            def step(j, carry, diagonal=False):
                total, tops, sums = carry
                first = pl.multiple_of(j * tile, tile)
                new_tops, new_sums, shrinks, adds = [], [], [], []
                for h in range(pack):
                    scores = dot_nt(queries, key_own[h, pl.ds(first, tile)]) * scale
                    if diagonal:
                        scores = jnp.where(col <= row, scores, -1e30)
                    top = jnp.maximum(tops[h], jnp.max(scores, axis=1, keepdims=True))
                    terms = jnp.exp2(scores - top)
                    shrink = jnp.exp2(tops[h] - top)
                    new_tops.append(top)
                    new_sums.append(sums[h] * shrink + jnp.sum(terms, axis=1, keepdims=True))
                    shrinks.append(shrink)
                    adds.append(dot_nn(terms.astype(jnp.bfloat16), value_own[h, pl.ds(first, tile)]))
                shrink = shrinks[0]
                for h in range(1, pack):
                    shrink = jnp.where(masks[h], shrinks[h], shrink)
                total = total * shrink
                for add in adds:
                    total = total + add
                return total, tuple(new_tops), tuple(new_sums)

            carry = (
                jnp.zeros((tile, LANES), jnp.float32),
                tuple(jnp.full((tile, 1), -1e30, jnp.float32) for _ in range(pack)),
                tuple(jnp.zeros((tile, 1), jnp.float32) for _ in range(pack)),
            )
            carry = lax.fori_loop(0, i, step, carry)
            total, tops, sums = step(i, carry, diagonal=True)
            share = 1.0 / sums[0]
            for h in range(1, pack):
                share = jnp.where(masks[h], 1.0 / sums[h], share)
            out_ref[pl.ds(start, tile), base : base + LANES] = (total * share).astype(out_ref.dtype)
            for h in range(pack):
                logs = jnp.broadcast_to(tops[h] + jnp.log2(sums[h]), (tile, LANES))
                index = pair * pack + h
                log_ref[0, index : index + 1, pl.ds(start, tile)] = jnp.transpose(logs)[0:1]
            return 0

        lax.fori_loop(0, blocks, query_block, 0)


def attend(mixed, slots, counts, head_size):
    sequences = counts.shape[0]
    tile = mixed[0].shape[0]
    rows = len(mixed) * tile
    lanes = mixed[0].shape[1] // 3
    length = rows // sequences
    heads = lanes // head_size
    pack = LANES // head_size
    return pl.pallas_call(
        functools.partial(attend_kernel, head_size, len(mixed)),
        grid_spec=pltpu.PrefetchScalarGridSpec(
            num_scalar_prefetch=2,
            grid=(sequences,),
            in_specs=[pl.BlockSpec(memory_space=pl.ANY)] * len(mixed),
            out_specs=[
                pl.BlockSpec((length, lanes), lambda s, *_: (s, 0)),
                pl.BlockSpec((1, heads, length), lambda s, *_: (s, 0, 0)),
            ],
            scratch_shapes=[
                pltpu.VMEM((len(mixed), tile, 3 * lanes), jnp.bfloat16),
                pltpu.VMEM((pack, length, LANES), jnp.bfloat16),
                pltpu.VMEM((pack, length, LANES), jnp.bfloat16),
                pltpu.SemaphoreType.DMA((len(mixed),)),
            ],
        ),
        out_shape=[
            jax.ShapeDtypeStruct((rows, lanes), jnp.bfloat16),
            jax.ShapeDtypeStruct((sequences, heads, length), jnp.float32),
        ],
        compiler_params=pltpu.CompilerParams(vmem_limit_bytes=VMEM_BYTES),
        cost_estimate=pl.CostEstimate(
            flops=rows * length * lanes * 4,
            bytes_accessed=rows * lanes * 8,
            transcendentals=rows * length * heads // 2,
        ),
    )(counts, slots, *mixed)


def attend_back_kernel(
    head_size,
    blocks_in,
    counts,
    slots,
    *refs,
):
    sources = refs[:blocks_in]
    grad_ref, out_ref, log_ref, own_ref, other_ref, mixed_ref = refs[blocks_in : blocks_in + 6]
    query_own, key_own, grad_own, delta, grad_query, grad_key, grad_value, back_ref, sems = refs[
        blocks_in + 6 :
    ]
    fetch(sources, mixed_ref, sems)
    length, lanes = out_ref.shape
    tile = mixed_ref.shape[1]
    pack = LANES // head_size
    scale = head_size ** (-0.5)
    sequence = pl.program_id(0)
    blocks = lax.div(counts[sequence] + (tile - 1), tile)
    masks = head_masks(head_size)
    for i in range(length // tile):
        back_ref[slots[sequence, i]] = jnp.zeros((tile, 3 * lanes), back_ref.dtype)
    key_row = lax.broadcasted_iota(jnp.int32, (tile, tile), 0)
    query_col = lax.broadcasted_iota(jnp.int32, (tile, tile), 1)
    for pair in range(lanes // LANES):
        base = pair * LANES
        for i in range(length // tile):
            span = slice(i * tile, (i + 1) * tile)
            slot = slots[sequence, i]
            queries = mixed_ref[slot, :, base : base + LANES]
            keys = mixed_ref[slot, :, lanes + base : lanes + base + LANES]
            grads = grad_ref[span, base : base + LANES]
            for h in range(pack):
                query_own[h, span] = jnp.where(masks[h], queries, jnp.zeros_like(queries))
                key_own[h, span] = jnp.where(masks[h], keys, jnp.zeros_like(keys))
                grad_own[h, span] = jnp.where(masks[h], grads, jnp.zeros_like(grads))
        grad_query[...] = jnp.zeros(grad_query.shape, jnp.float32)

        def deltas(i, _, base=base):
            start = pl.multiple_of(i * tile, tile)
            grads = grad_ref[pl.ds(start, tile), base : base + LANES].astype(jnp.float32)
            outs = out_ref[pl.ds(start, tile), base : base + LANES].astype(jnp.float32)
            products = jnp.transpose(grads * outs)
            for h in range(pack):
                delta[h : h + 1, pl.ds(start, tile)] = jnp.sum(
                    products[h * head_size : (h + 1) * head_size], axis=0, keepdims=True
                )
            return 0

        lax.fori_loop(0, blocks, deltas, 0)

        def key_block(j, _, pair=pair, base=base):
            first = pl.multiple_of(j * tile, tile)
            place = slots[sequence, j]
            keys = mixed_ref[place, :, lanes + base : lanes + base + LANES]
            values = mixed_ref[place, :, 2 * lanes + base : 2 * lanes + base + LANES]
            grad_key[...] = jnp.zeros(grad_key.shape, jnp.float32)
            grad_value[...] = jnp.zeros(grad_value.shape, jnp.float32)

            def step(i, diagonal=False):
                start = pl.multiple_of(i * tile, tile)
                add_query, add_key, add_value = [], [], []
                for h in range(pack):
                    index = pair * pack + h
                    query_head = query_own[h, pl.ds(start, tile)]
                    grad_head = grad_own[h, pl.ds(start, tile)]
                    scores = dot_nt(keys, query_head) * (scale * LOG2E)
                    probs = jnp.exp2(scores - log_ref[0, index : index + 1, pl.ds(start, tile)])
                    if diagonal:
                        probs = jnp.where(key_row <= query_col, probs, 0.0)
                    grad_probs = dot_nt(values, grad_head)
                    grad_scores = (
                        probs * (grad_probs - delta[h : h + 1, pl.ds(start, tile)])
                    ).astype(jnp.bfloat16)
                    add_value.append(dot_nn(probs.astype(jnp.bfloat16), grad_head))
                    add_key.append(dot_nn(grad_scores, query_head))
                    add_query.append(dot_tn(grad_scores, key_own[h, pl.ds(first, tile)]))
                grad_value[...] += functools.reduce(jnp.add, add_value)
                grad_key[...] += functools.reduce(jnp.add, add_key)
                grad_query[pl.ds(start, tile), :] += functools.reduce(jnp.add, add_query)

            def off_diagonal(i, _):
                step(i)
                return 0

            step(j, diagonal=True)
            lax.fori_loop(j + 1, blocks, off_diagonal, 0)
            back_ref[place, :, lanes + base : lanes + base + LANES] = (grad_key[...] * scale).astype(
                back_ref.dtype
            )
            back_ref[place, :, 2 * lanes + base : 2 * lanes + base + LANES] = grad_value[...].astype(
                back_ref.dtype
            )
            return 0

        lax.fori_loop(0, blocks, key_block, 0)
        for i in range(length // tile):
            back_ref[slots[sequence, i], :, base : base + LANES] = (
                grad_query[i * tile : (i + 1) * tile] * scale
            ).astype(back_ref.dtype)

    @pl.when(sequence == pl.num_programs(0) - 1)
    def _():
        half = blocks_in // 2
        for k in range(half):
            own_ref[k * tile : (k + 1) * tile] = back_ref[k]
            other_ref[k * tile : (k + 1) * tile] = back_ref[half + k]


def attend_back(mixed, slots, grads, outs, logs, counts, head_size):
    sequences = counts.shape[0]
    rows, lanes = outs.shape
    length = rows // sequences
    heads = lanes // head_size
    pack = LANES // head_size
    tile = mixed[0].shape[0]
    whole = pl.BlockSpec((rows // 2, 3 * lanes), lambda s, *_: (0, 0))
    return pl.pallas_call(
        functools.partial(attend_back_kernel, head_size, len(mixed)),
        grid_spec=pltpu.PrefetchScalarGridSpec(
            num_scalar_prefetch=2,
            grid=(sequences,),
            in_specs=[pl.BlockSpec(memory_space=pl.ANY)] * len(mixed)
            + [
                pl.BlockSpec((length, lanes), lambda s, *_: (s, 0)),
                pl.BlockSpec((length, lanes), lambda s, *_: (s, 0)),
                pl.BlockSpec((1, heads, length), lambda s, *_: (s, 0, 0)),
            ],
            out_specs=[whole, whole],
            scratch_shapes=[
                pltpu.VMEM((len(mixed), tile, 3 * lanes), jnp.bfloat16),
                pltpu.VMEM((pack, length, LANES), jnp.bfloat16),
                pltpu.VMEM((pack, length, LANES), jnp.bfloat16),
                pltpu.VMEM((pack, length, LANES), jnp.bfloat16),
                pltpu.VMEM((pack, length), jnp.float32),
                pltpu.VMEM((length, LANES), jnp.float32),
                pltpu.VMEM((tile, LANES), jnp.float32),
                pltpu.VMEM((tile, LANES), jnp.float32),
                pltpu.VMEM((len(mixed), tile, 3 * lanes), jnp.bfloat16),
                pltpu.SemaphoreType.DMA((len(mixed),)),
            ],
        ),
        out_shape=[jax.ShapeDtypeStruct((rows // 2, 3 * lanes), jnp.bfloat16)] * 2,
        compiler_params=pltpu.CompilerParams(vmem_limit_bytes=VMEM_BYTES),
        cost_estimate=pl.CostEstimate(
            flops=rows * length * lanes * 10,
            bytes_accessed=rows * lanes * 18,
            transcendentals=rows * length * heads // 2,
        ),
    )(counts, slots, *mixed, grads, outs, logs)


def ffn_kernel(r, x_parts, g_parts, counts, *refs):
    xs, refs = refs[:x_parts], refs[x_parts:]
    gs, refs = refs[:g_parts], refs[g_parts:]
    up_turned, down_turned, up, shift = refs[:4]
    x_ref, g_ref, units_ref, back_ref, out_ref, total = refs[-6:]
    step = pl.program_id(0)

    @pl.when(step == 0)
    def _():
        for parts, target in ((xs, x_ref), (gs, g_ref)):
            size = target.shape[0] // len(parts)
            for k, part in enumerate(parts):
                target[k * size : (k + 1) * size] = part[...]
        total[...] = jnp.zeros(total.shape, total.dtype)

    @pl.when(counts[r] == 0)
    def _():
        units_ref[...] = jnp.zeros(units_ref.shape, units_ref.dtype)
        back_ref[...] = jnp.zeros(back_ref.shape, back_ref.dtype)

    @pl.when(counts[r] != 0)
    def _():
        width = 256
        for k in range(up.shape[0] // width):
            span = slice(k * width, (k + 1) * width)
            grad_units = dot_nn(g_ref[...], down_turned[:, span])
            pre = dot_nn(x_ref[...], up_turned[:, span]) + shift[:, span]
            bell = jnp.exp2(pre * pre * (-0.5 * LOG2E))
            denominator = 1.0 + (0.3275911 * 0.7071067811865476) * jnp.abs(pre)
            t = pl.reciprocal(denominator, approx=True)
            t = t * (2.0 - denominator * t)
            tail = 0.5 * 1.061405429
            for factor in (-1.453152027, 1.421413741, -0.284496736, 0.254829592):
                tail = tail * t + 0.5 * factor
            tail = tail * t * bell
            below = jnp.where(pre < 0, tail, 1.0 - tail)
            units_ref[:, span] = (pre * below).astype(units_ref.dtype)
            slope = below + pre * bell * 0.3989422804014327
            back_ref[:, span] = (grad_units * slope).astype(back_ref.dtype)
        total[...] += dot_nn(back_ref[...], up[...])

    @pl.when(step == pl.num_programs(0) - 1)
    def _():
        out_ref[...] = total[...].astype(out_ref.dtype)


def ffn_block(r, counts, xs, gs, up_turned, down_turned, up, shift, kept):
    model = xs[0].shape[1]
    size = sum(x.shape[0] for x in xs)
    units = up.shape[0]
    tile = 512
    parts = [pl.BlockSpec(x.shape, lambda u, *_: (0, 0)) for x in (*xs, *gs)]
    turned = pl.BlockSpec((model, tile), lambda u, *_: (0, u))
    rows = pl.BlockSpec((size, model), lambda u, *_: (r, 0))
    tiles = pl.BlockSpec((size, tile), lambda u, *_: (r, u))
    full = lambda columns: jax.ShapeDtypeStruct((4 * size, columns), jnp.bfloat16)
    return pl.pallas_call(
        functools.partial(ffn_kernel, r, len(xs), len(gs)),
        grid_spec=pltpu.PrefetchScalarGridSpec(
            num_scalar_prefetch=1,
            grid=(units // tile,),
            in_specs=parts
            + [
                turned,
                turned,
                pl.BlockSpec((tile, model), lambda u, *_: (u, 0)),
                pl.BlockSpec((1, tile), lambda u, *_: (0, u)),
            ]
            + [pl.BlockSpec(memory_space=pl.ANY)] * len(kept),
            out_specs=[rows, rows, tiles, tiles, pl.BlockSpec((size, model), lambda u, *_: (0, 0))],
            scratch_shapes=[pltpu.VMEM((size, model), jnp.float32)],
        ),
        out_shape=[full(model), full(model), full(units), full(units)]
        + [jax.ShapeDtypeStruct((size, model), jnp.bfloat16)],
        input_output_aliases={len(parts) + 5 + k: k for k in range(len(kept))},
        compiler_params=pltpu.CompilerParams(vmem_limit_bytes=VMEM_BYTES),
        cost_estimate=pl.CostEstimate(
            flops=6 * size * units * model,
            bytes_accessed=6 * units * model + 12 * size * model,
            transcendentals=2 * size * units,
        ),
    )(counts, *xs, *gs, up_turned, down_turned, up, shift, *kept)


def products_kernel(terms, counts, *refs):
    out_ref = refs[-1]
    active = counts[pl.program_id(0)] != 0

    @pl.when(active)
    def _():
        total = dot_nn(refs[0][...], refs[terms][...])
        for k in range(1, terms):
            total = total + dot_nn(refs[k][...], refs[terms + k][...])
        out_ref[...] = total.astype(out_ref.dtype)

    @pl.when(jnp.logical_not(active))
    def _():
        out_ref[...] = jnp.zeros(out_ref.shape, out_ref.dtype)


def products(counts, lefts, rights):
    blocks = counts.shape[0]
    size = lefts[0].shape[0] // blocks
    columns = rights[0].shape[1]
    depth = sum(right.shape[0] for right in rights)
    return pl.pallas_call(
        functools.partial(products_kernel, len(lefts)),
        grid_spec=pltpu.PrefetchScalarGridSpec(
            num_scalar_prefetch=1,
            grid=(blocks,),
            in_specs=[pl.BlockSpec((size, left.shape[1]), lambda i, *_: (i, 0)) for left in lefts]
            + [pl.BlockSpec(right.shape, lambda i, *_: (0, 0)) for right in rights],
            out_specs=pl.BlockSpec((size, columns), lambda i, *_: (i, 0)),
        ),
        out_shape=jax.ShapeDtypeStruct((blocks * size, columns), jnp.bfloat16),
        compiler_params=pltpu.CompilerParams(vmem_limit_bytes=VMEM_BYTES),
        cost_estimate=pl.CostEstimate(
            flops=2 * blocks * size * depth * columns,
            bytes_accessed=2 * (blocks * size * (depth + columns) + depth * columns),
            transcendentals=0,
        ),
    )(counts, *lefts, *rights)


def chain_sum(values, axis):
    size = lax.axis_size(axis)
    if size != 4:
        return lax.psum(values.astype(jnp.bfloat16), axis).astype(jnp.float32)
    place = lax.axis_index(axis)
    outer = lax.ppermute(values.astype(jnp.bfloat16), axis, [(0, 1), (3, 2)])
    half = (values + outer.astype(jnp.float32)).astype(jnp.bfloat16)
    other = lax.ppermute(half, axis, [(1, 2), (2, 1)])
    whole = (half.astype(jnp.float32) + other.astype(jnp.float32)).astype(jnp.bfloat16)
    ends = lax.ppermute(whole, axis, [(1, 0), (2, 3)])
    inner = (place == 1) | (place == 2)
    return jnp.where(inner, whole, ends).astype(jnp.float32)


def normalize(values):
    center = values - jnp.mean(values, axis=-1, keepdims=True)
    inverse = lax.rsqrt(jnp.mean(center * center, axis=-1, keepdims=True) + epsilon)
    return center * inverse, inverse


def normalize_back(grad, gain, normal, inverse):
    scaled = grad * gain
    grad_values = inverse * (
        scaled
        - jnp.mean(scaled, axis=-1, keepdims=True)
        - normal * jnp.mean(scaled * normal, axis=-1, keepdims=True)
    )
    return grad_values, jnp.sum(grad * normal, axis=0), jnp.sum(grad, axis=0)


def local_general(
    hidden,
    cotangent,
    exit_layer,
    ln1_gain,
    ln1_bias,
    qkv_weight,
    query_bias,
    value_bias,
    out_weight,
    out_bias,
    ln2_gain,
    ln2_bias,
    up_weight,
    up_bias,
    down_weight,
    down_bias,
):
    width = lax.axis_size("wide")
    rank = lax.axis_index("wide")
    rows, model = hidden.shape
    group = rows * width
    slab = model // width
    head_size = model // HEADS
    units_own = up_weight.shape[0]
    keep = exit_layer >= LAYER
    counts = jnp.sum(keep.astype(jnp.int32), axis=1)
    active = lax.dynamic_slice_in_dim(keep.reshape(group), rank * rows, rows, 0)
    active = active.astype(jnp.float32)[:, None]
    grad_out = cotangent.astype(jnp.float32)

    routes = [[(w, (3 * w + t) % width) for w in range(width)] for t in range(3)]
    part_at = np.zeros((width, 3), np.int32)
    for t in range(3):
        for w, d in routes[t]:
            part_at[d, t] = (3 * w + t) // width
    place_of = jnp.asarray(np.argsort(part_at, axis=1).astype(np.int32))[rank]
    part_of = jnp.asarray(part_at)[rank]

    hidden_wide = hidden.astype(jnp.float32)
    normal1, inverse1 = normalize(hidden_wide)
    normed1 = lax.all_gather(
        (normal1 * ln1_gain + ln1_bias).astype(jnp.bfloat16), "wide", axis=0, tiled=True
    )
    slabs = qkv_weight.reshape(3, slab, model)
    received = jnp.stack([lax.ppermute(slabs[t], "wide", routes[t]) for t in range(3)])
    qkv_own = jnp.concatenate(
        [lax.dynamic_index_in_dim(received, place_of[p], 0, keepdims=False) for p in range(3)]
    )
    own = lambda vector: lax.dynamic_slice_in_dim(vector, rank * slab, slab, 0)
    qkv_shift = jnp.concatenate(
        [own(query_bias), jnp.zeros((slab,), jnp.float32), own(value_bias)]
    )

    grad_ffn = (active * grad_out).astype(jnp.bfloat16)
    down_bias_grad = jnp.sum(grad_ffn.astype(jnp.float32), axis=0)
    piece = rows // CHUNKS
    part = lambda values, c: values[c * piece : (c + 1) * piece]
    gather = lambda values: lax.all_gather(values, "wide", axis=0, tiled=True)
    scatter = lambda values: lax.psum_scatter(
        values.astype(jnp.bfloat16), "wide", scatter_dimension=0, tiled=True
    )
    grad_ffns = [gather(part(grad_ffn, c)) for c in range(CHUNKS)]
    out_whole = gather(out_weight)

    mixed = (dot_nt(normed1, qkv_own) + qkv_shift).astype(jnp.bfloat16)
    mixed = jnp.split(mixed, group // TILE)
    slots = jnp.arange(group // TILE, dtype=jnp.int32).reshape(counts.shape[0], -1)
    attended, logs = attend(mixed, slots, counts, head_size)
    attended_rows = lax.all_to_all(attended, "wide", split_axis=0, concat_axis=1, tiled=True)
    middle = hidden_wide + active * (dot_nn(attended_rows, out_whole) + out_bias)
    normal2, inverse2 = normalize(middle)
    normed2 = (normal2 * ln2_gain + ln2_bias).astype(jnp.bfloat16)
    up_shift = lax.dynamic_slice_in_dim(up_bias, rank * units_own, units_own, 0)

    normed2s = [gather(part(normed2, c)) for c in range(CHUNKS)]
    units, grad_pres, grad_normed2, ffn_out = [], [], [], []
    for c in range(CHUNKS):
        grad_units = dot_nt(grad_ffns[c], down_weight)
        pre = dot_nt(normed2s[c], up_weight) + up_shift
        below = 0.5 + 0.5 * lax.erf(pre * 0.7071067811865476)
        bell = jnp.exp(-0.5 * pre * pre) * 0.3989422804014327
        units.append((pre * below).astype(jnp.bfloat16))
        grad_pres.append((grad_units * (below + pre * bell)).astype(jnp.bfloat16))
        grad_normed2.append(scatter(dot_nn(grad_pres[c], up_weight)))
    for c in range(CHUNKS):
        ffn_out.append(scatter(dot_nn(units[c], down_weight)))
    grad_normed2 = jnp.concatenate(grad_normed2).astype(jnp.float32)
    ffn_out = jnp.concatenate(ffn_out).astype(jnp.float32)
    output = (middle + active * (ffn_out + down_bias)).astype(jnp.bfloat16)

    up_bias_own = sum(jnp.sum(g.astype(jnp.float32), axis=0) for g in grad_pres)
    down_grad = sum(dot_tn(units[c], grad_ffns[c]) for c in range(CHUNKS))
    up_grad = sum(dot_tn(grad_pres[c], normed2s[c]) for c in range(CHUNKS))
    halves = lambda values: jnp.concatenate(
        [chain_sum(half, "batch") for half in jnp.split(values, 2)]
    )
    down_grad = halves(down_grad)
    up_grad = halves(up_grad)

    grad_middle, ln2_gain_grad, ln2_bias_grad = normalize_back(
        grad_normed2, ln2_gain, normal2, inverse2
    )
    grad_middle = grad_out + grad_middle
    grad_branch = (active * grad_middle).astype(jnp.bfloat16)
    out_bias_grad = jnp.sum(grad_branch.astype(jnp.float32), axis=0)
    grad_attended = dot_nt(grad_branch, out_whole).astype(jnp.bfloat16)
    grad_heads = lax.all_to_all(grad_attended, "wide", split_axis=1, concat_axis=0, tiled=True)
    out_grad = chain_sum(scatter(dot_tn(attended_rows, grad_branch)).astype(jnp.float32), "batch")

    placed = lambda vector, size: lax.dynamic_update_slice_in_dim(
        jnp.zeros((size,), jnp.float32), vector, rank * vector.shape[0], 0
    )
    early = lax.psum(
        (
            out_bias_grad,
            ln2_gain_grad,
            ln2_bias_grad,
            placed(up_bias_own, up_bias.shape[0]),
            down_bias_grad,
        ),
        ("batch", "wide"),
    )

    grad_mixed = jnp.concatenate(
        attend_back(mixed, slots, grad_heads, attended, logs, counts, head_size)
    )
    grad_normed1 = scatter(dot_nn(grad_mixed, qkv_own)).astype(jnp.float32)
    sums = jnp.sum(grad_mixed.astype(jnp.float32), axis=0)
    qkv_parts = []
    for t in range(3):
        columns = lax.dynamic_slice_in_dim(grad_mixed, part_of[t] * slab, slab, 1)
        total = chain_sum(dot_tn(columns, normed1), "batch").astype(jnp.bfloat16)
        back = [(d, w) for w, d in routes[t]]
        qkv_parts.append(lax.ppermute(total, "wide", back).astype(jnp.float32))
    qkv_grad = jnp.concatenate(qkv_parts)

    grad_hidden, ln1_gain_grad, ln1_bias_grad = normalize_back(
        grad_normed1, ln1_gain, normal1, inverse1
    )
    input_grad = grad_middle + grad_hidden
    late = lax.psum(
        (
            ln1_gain_grad,
            ln1_bias_grad,
            placed(sums[:slab], model),
            placed(sums[2 * slab :], model),
        ),
        ("batch", "wide"),
    )
    return (
        output,
        input_grad,
        late[0],
        late[1],
        qkv_grad,
        late[2],
        late[3],
        out_grad,
        early[0],
        early[1],
        early[2],
        up_grad,
        early[3],
        down_grad,
        early[4],
    )


def swap(values, bits):
    width = lax.axis_size("wide")
    return lax.ppermute(values, "wide", [(w, w ^ bits) for w in range(width)])


def after(values, *done):
    return lax.optimization_barrier((values, done))[0]


def gather_chips(values, *done):
    half = values.shape[0] // 2
    along_x, along_y = swap(values, 2), swap(values, 4)
    relay_x, relay_y = after((along_x, along_y), *done)
    diagonal = [swap(relay_y[:half], 2), swap(relay_x[half:], 4)]
    return [[values], [along_x], [along_y], diagonal]


def scatter_chips(partials):
    wide = lambda values: values.astype(jnp.float32)
    own, along_x, along_y, diagonal = partials
    half = own.shape[0] // 2
    top = swap(diagonal[:half], 2)
    bottom = swap(diagonal[half:], 4)
    x_top = swap(along_x[:half], 2)
    y_bottom = swap(along_y[half:], 4)
    y_top = swap((wide(along_y[:half]) + wide(top)).astype(jnp.bfloat16), 4)
    x_bottom = swap((wide(along_x[half:]) + wide(bottom)).astype(jnp.bfloat16), 2)
    return jnp.concatenate(
        [
            wide(own[:half]) + wide(x_top) + wide(y_top),
            wide(own[half:]) + wide(x_bottom) + wide(y_bottom),
        ]
    )


def tree_sum(values):
    total = values + swap(values, 1)
    total = (total + swap(total, 2)) + (swap(total, 4) + swap(total, 6))
    size = lax.axis_size("batch")
    terms = [total] + [
        lax.ppermute(total, "batch", [(z, z ^ bits) for z in range(size)])
        for bits in range(1, size)
    ]
    while len(terms) > 1:
        terms = [terms[k] + terms[k + 1] for k in range(0, len(terms), 2)]
    return terms[0]


def local_chips(
    hidden,
    cotangent,
    exit_layer,
    ln1_gain,
    ln1_bias,
    qkv_weight,
    query_bias,
    value_bias,
    out_weight,
    out_bias,
    ln2_gain,
    ln2_bias,
    up_weight,
    up_bias,
    down_weight,
    down_bias,
):
    width = lax.axis_size("wide")
    rank = lax.axis_index("wide")
    rows, model = hidden.shape
    group = rows * width
    slab = model // width
    head_size = model // HEADS
    units_own = up_weight.shape[0]
    keep = exit_layer >= LAYER
    counts = jnp.sum(keep.astype(jnp.int32), axis=1)
    active = lax.dynamic_slice_in_dim(keep.reshape(group), rank * rows, rows, 0)
    active = active.astype(jnp.float32)[:, None]
    grad_out = cotangent.astype(jnp.float32)
    chips = range(4)

    tiles = jnp.arange(group // rows, dtype=jnp.int32)
    slots = ((tiles ^ rank) & 1) * 4 + ((tiles >> 1) ^ (rank >> 1))
    slots = slots.reshape(counts.shape[0], -1)

    routes = [[(w, (3 * w + t) % width) for w in range(width)] for t in range(3)]
    part_at = np.zeros((width, 3), np.int32)
    for t in range(3):
        for w, d in routes[t]:
            part_at[d, t] = (3 * w + t) // width
    place_of = jnp.asarray(np.argsort(part_at, axis=1).astype(np.int32))[rank]
    part_of = jnp.asarray(part_at)[rank]

    hidden_wide = hidden.astype(jnp.float32)
    normal1, inverse1 = normalize(hidden_wide)
    slabs = qkv_weight.reshape(3, slab, model)
    slabs = [lax.ppermute(slabs[t], "wide", routes[t]) for t in range(3)]
    normed1 = gather_chips((normal1 * ln1_gain + ln1_bias).astype(jnp.bfloat16))
    slabs = after(slabs, normed1[1], normed1[2])
    received = jnp.stack(slabs)
    qkv_own = jnp.concatenate(
        [lax.dynamic_index_in_dim(received, place_of[p], 0, keepdims=False) for p in range(3)]
    )
    qkv_other = swap(qkv_own, 1)
    own_turned, other_turned = qkv_own.T, qkv_other.T

    def shift_of(device):
        own = lambda vector: lax.dynamic_slice_in_dim(vector, device * slab, slab, 0)
        return jnp.concatenate([own(query_bias), jnp.zeros((slab,), jnp.float32), own(value_bias)])

    other = rank ^ 1
    up_other, down_other = swap(after((up_weight, down_weight), *slabs), 1)
    up_both = jnp.concatenate([up_weight, up_other])
    down_both = jnp.concatenate([down_weight, down_other])
    up_turned, down_turned = up_both.T, down_both.T
    bias_of = lambda device: lax.dynamic_slice_in_dim(up_bias, device * units_own, units_own, 0)
    up_shift = jnp.concatenate([bias_of(rank), bias_of(other)])[None]

    mixed_own, mixed_other = [], []
    rows_in = normed1[0][0]
    blocks_in = []
    for r in chips:
        blocks_in.append(rows_in)
        lent = (dot_nn(rows_in, other_turned) + shift_of(other)).astype(jnp.bfloat16)
        kept = (dot_nn(rows_in, own_turned) + shift_of(rank)).astype(jnp.bfloat16)
        mixed_other.append(swap(lent, 1))
        mixed_own.append(kept)
        if r + 1 < len(chips):
            extra = (up_both, down_both, up_turned, down_turned) if r + 1 == 3 else ()
            rows_in = after(normed1[r + 1], lent, kept, *extra)
            rows_in = jnp.concatenate(rows_in) if len(rows_in) > 1 else rows_in[0]
    mixed = mixed_own + mixed_other

    arrived = blocks_in[3]
    normed1 = jnp.concatenate(blocks_in)
    out_whole = lax.all_gather(after(out_weight, arrived), "wide", axis=0, tiled=True)
    grad_ffn = (after(active, arrived) * grad_out).astype(jnp.bfloat16)
    down_bias_grad = jnp.sum(grad_ffn.astype(jnp.float32), axis=0)

    attended, logs = attend(mixed, slots, counts, head_size)
    attended_rows = lax.all_to_all(attended, "wide", split_axis=0, concat_axis=1, tiled=True)
    grad_ffn = gather_chips(grad_ffn, attended)
    attended_rows = after(attended_rows, grad_ffn[1], grad_ffn[2])
    middle = hidden_wide + active * (dot_nn(attended_rows, out_whole) + out_bias)
    normal2, inverse2 = normalize(middle)
    normed2 = gather_chips((normal2 * ln2_gain + ln2_bias).astype(jnp.bfloat16))

    per_tile = jnp.sum(keep.reshape(group // rows, rows).astype(jnp.int32), axis=1)
    block_chip = (rank >> 1) ^ jnp.arange(4, dtype=jnp.int32)
    block_counts = per_tile[2 * block_chip + (rank & 1)]
    kept, partials = (), []
    for r in chips:
        rows_in = normed2[r]
        if r == 1:
            out_turned = after(out_whole, partials[0]).T
            rows_in = after(rows_in, normed2[2], out_turned)
        *kept, partial = ffn_block(
            r,
            block_counts,
            rows_in,
            grad_ffn[r],
            up_turned,
            down_turned,
            up_both,
            up_shift,
            tuple(kept),
        )
        partials.append(partial)
    normed2_all, grad_ffn_all, units, grad_pres = kept
    grad_normed2 = scatter_chips(partials)

    size = units_own
    lowered = lambda values: values.astype(jnp.bfloat16)
    down_lent = lowered(dot_tn(units[:, size:], grad_ffn_all))
    up_lent = lowered(dot_tn(after(grad_pres, down_lent)[:, size:], normed2_all))
    down_theirs, up_theirs = swap(down_lent, 1), swap(up_lent, 1)
    down_own = dot_tn(after(units, up_lent)[:, :size], grad_ffn_all)
    down_own = lowered(down_own + down_theirs.astype(jnp.float32))
    down_grad = lax.psum(down_own, "batch").astype(jnp.float32)

    grad_middle, ln2_gain_grad, ln2_bias_grad = normalize_back(
        after(grad_normed2, down_own), ln2_gain, normal2, inverse2
    )
    grad_middle = grad_out + grad_middle
    grad_branch = (active * grad_middle).astype(jnp.bfloat16)
    out_bias_grad = jnp.sum(grad_branch.astype(jnp.float32), axis=0)
    grad_attended = dot_nn(grad_branch, out_turned).astype(jnp.bfloat16)
    grad_heads = lax.all_to_all(grad_attended, "wide", split_axis=1, concat_axis=0, tiled=True)

    up_own = dot_tn(after(grad_pres, grad_attended)[:, :size], normed2_all)
    up_own = up_own + up_theirs.astype(jnp.float32)
    ffn_out = products(block_counts, [after(units, up_own)], [down_both])
    out_partial = lowered(dot_tn(attended_rows, after(grad_branch, ffn_out)))
    out_grad = lax.psum_scatter(out_partial, "wide", scatter_dimension=0, tiled=True)
    grad_heads = after(grad_heads, out_partial)
    ffn_out = scatter_chips(jnp.split(ffn_out, 4))
    output = (middle + active * (ffn_out + down_bias)).astype(jnp.bfloat16)

    back_own, back_other = attend_back(
        mixed, slots, grad_heads, attended, logs, counts, head_size
    )
    up_grad = jnp.concatenate([chain_sum(half, "batch") for half in jnp.split(up_own, 2)])
    up_bias_own = jnp.sum(grad_pres.astype(jnp.float32), axis=0)
    sums = jnp.sum(back_own.astype(jnp.float32), axis=0) + jnp.sum(
        back_other.astype(jnp.float32), axis=0
    )
    back_other = swap(back_other, 1)
    qkv_lent = lowered(dot_tn(back_other, normed1))
    qkv_total = dot_tn(after(back_own, qkv_lent), normed1) + swap(qkv_lent, 1).astype(jnp.float32)
    back_own, back_other = after((back_own, back_other), qkv_total)
    grad_normed1 = products(block_counts, [back_own, back_other], [qkv_own, qkv_other])
    grad_normed1 = scatter_chips(jnp.split(grad_normed1, 4))
    qkv_parts = []
    for t in range(3):
        part = lax.dynamic_slice_in_dim(qkv_total, part_of[t] * slab, slab, 0)
        total = chain_sum(part, "batch").astype(jnp.bfloat16)
        qkv_parts.append(
            lax.ppermute(total, "wide", [(d, w) for w, d in routes[t]]).astype(jnp.float32)
        )
    qkv_grad = jnp.concatenate(qkv_parts)
    out_grad = chain_sum(after(out_grad, qkv_total).astype(jnp.float32), "batch")

    placed = lambda vector, size, device: lax.dynamic_update_slice_in_dim(
        jnp.zeros((size,), jnp.float32), vector, device * vector.shape[0], 0
    )
    grad_hidden, ln1_gain_grad, ln1_bias_grad = normalize_back(
        grad_normed1, ln1_gain, normal1, inverse1
    )
    input_grad = grad_middle + grad_hidden
    smalls = tree_sum(
        jnp.concatenate(
            [
                placed(up_bias_own[:size], up_bias.shape[0], rank)
                + placed(up_bias_own[size:], up_bias.shape[0], other),
                down_bias_grad,
                out_bias_grad,
                ln2_gain_grad,
                ln2_bias_grad,
                placed(sums[:slab], model, rank),
                placed(sums[2 * slab :], model, rank),
                ln1_gain_grad,
                ln1_bias_grad,
            ]
        )
    )
    up_bias_grad = smalls[: up_bias.shape[0]]
    smalls = smalls[up_bias.shape[0] :].reshape(8, model)
    return (
        output,
        input_grad,
        smalls[6],
        smalls[7],
        qkv_grad,
        smalls[4],
        smalls[5],
        out_grad,
        smalls[1],
        smalls[2],
        smalls[3],
        up_grad,
        up_bias_grad,
        down_grad,
        smalls[0],
    )


def solution(mesh):
    local = local_chips if mesh.shape["wide"] == 8 else local_general
    rows = P(("batch", "wide"), None)
    weight = P("wide", None)
    return jax.shard_map(
        local,
        mesh=mesh,
        in_specs=(
            rows,
            rows,
            P("batch", None),
            P(),
            P(),
            weight,
            P(),
            P(),
            weight,
            P(),
            P(),
            P(),
            weight,
            P(),
            weight,
            P(),
        ),
        out_specs=(
            rows,
            rows,
            P(),
            P(),
            weight,
            P(),
            P(),
            weight,
            P(),
            P(),
            P(),
            weight,
            P(),
            weight,
            P(),
        ),
        check_vma=False,
    )
```

```python
import functools

import jax
import jax.numpy as jnp
import numpy as np
from jax import lax
from jax.experimental import pallas as pl
from jax.experimental.pallas import tpu as pltpu
from jax.sharding import PartitionSpec as P

HEADS = 32
LAYER = 12
LANES = 128
TILE = 512
CHUNKS = 2
LOG2E = 1.4426950408889634

epsilon = 1e-05
VMEM_BYTES = 48 * 2**20


def dot_nt(left, right):
    return lax.dot_general(
        left, right, (((1,), (1,)), ((), ())), preferred_element_type=jnp.float32
    )


def dot_nn(left, right):
    return lax.dot_general(
        left, right, (((1,), (0,)), ((), ())), preferred_element_type=jnp.float32
    )


def dot_tn(left, right):
    return lax.dot_general(
        left, right, (((0,), (0,)), ((), ())), preferred_element_type=jnp.float32
    )


def head_masks(head_size):
    lane = lax.broadcasted_iota(jnp.int32, (1, LANES), 1)
    return [
        (lane >= h * head_size) & (lane < (h + 1) * head_size)
        for h in range(LANES // head_size)
    ]


def fetch(sources, target, sems, step=0):
    size = target.shape[1]
    pieces = [
        source.at[pl.ds(k * size, size)]
        for source in sources
        for k in range(source.shape[0] // size)
    ]
    copies = [
        pltpu.make_async_copy(piece, target.at[k], sems.at[k]) for k, piece in enumerate(pieces)
    ]

    @pl.when(pl.program_id(0) == step)
    def _():
        for copy in copies:
            copy.start()
        for copy in copies:
            copy.wait()


def attend_kernel(head_size, blocks_in, counts, slots, *refs):
    sources = refs[:blocks_in]
    out_ref, log_ref, mixed_ref, key_own, value_own, sems = refs[blocks_in:]
    fetch(sources, mixed_ref, sems)
    length, lanes = out_ref.shape
    tile = mixed_ref.shape[1]
    pack = LANES // head_size
    scale = head_size ** (-0.5) * LOG2E
    sequence = pl.program_id(0)
    blocks = lax.div(counts[sequence] + (tile - 1), tile)
    masks = head_masks(head_size)
    out_ref[...] = jnp.zeros(out_ref.shape, out_ref.dtype)
    log_ref[...] = jnp.zeros(log_ref.shape, log_ref.dtype)
    row = lax.broadcasted_iota(jnp.int32, (tile, tile), 0)
    col = lax.broadcasted_iota(jnp.int32, (tile, tile), 1)
    for pair in range(lanes // LANES):
        base = pair * LANES
        for i in range(length // tile):
            slot = slots[sequence, i]
            keys = mixed_ref[slot, :, lanes + base : lanes + base + LANES]
            values = mixed_ref[slot, :, 2 * lanes + base : 2 * lanes + base + LANES]
            for h in range(pack):
                key_own[h, i * tile : (i + 1) * tile] = jnp.where(masks[h], keys, jnp.zeros_like(keys))
                value_own[h, i * tile : (i + 1) * tile] = jnp.where(
                    masks[h], values, jnp.zeros_like(values)
                )

        def query_block(i, _, pair=pair, base=base):
            start = pl.multiple_of(i * tile, tile)
            queries = mixed_ref[slots[sequence, i], :, base : base + LANES]

            def step(j, carry, diagonal=False):
                total, tops, sums = carry
                first = pl.multiple_of(j * tile, tile)
                new_tops, new_sums, shrinks, adds = [], [], [], []
                for h in range(pack):
                    scores = dot_nt(queries, key_own[h, pl.ds(first, tile)]) * scale
                    if diagonal:
                        scores = jnp.where(col <= row, scores, -1e30)
                    top = jnp.maximum(tops[h], jnp.max(scores, axis=1, keepdims=True))
                    terms = jnp.exp2(scores - top)
                    shrink = jnp.exp2(tops[h] - top)
                    new_tops.append(top)
                    new_sums.append(sums[h] * shrink + jnp.sum(terms, axis=1, keepdims=True))
                    shrinks.append(shrink)
                    adds.append(dot_nn(terms.astype(jnp.bfloat16), value_own[h, pl.ds(first, tile)]))
                shrink = shrinks[0]
                for h in range(1, pack):
                    shrink = jnp.where(masks[h], shrinks[h], shrink)
                total = total * shrink
                for add in adds:
                    total = total + add
                return total, tuple(new_tops), tuple(new_sums)

            carry = (
                jnp.zeros((tile, LANES), jnp.float32),
                tuple(jnp.full((tile, 1), -1e30, jnp.float32) for _ in range(pack)),
                tuple(jnp.zeros((tile, 1), jnp.float32) for _ in range(pack)),
            )
            carry = lax.fori_loop(0, i, step, carry)
            total, tops, sums = step(i, carry, diagonal=True)
            share = 1.0 / sums[0]
            for h in range(1, pack):
                share = jnp.where(masks[h], 1.0 / sums[h], share)
            out_ref[pl.ds(start, tile), base : base + LANES] = (total * share).astype(out_ref.dtype)
            for h in range(pack):
                logs = jnp.broadcast_to(tops[h] + jnp.log2(sums[h]), (tile, LANES))
                index = pair * pack + h
                log_ref[0, index : index + 1, pl.ds(start, tile)] = jnp.transpose(logs)[0:1]
            return 0

        lax.fori_loop(0, blocks, query_block, 0)


def attend(mixed, slots, counts, head_size):
    sequences = counts.shape[0]
    rows = sum(part.shape[0] for part in mixed)
    tile = rows // slots.size
    blocks = rows // tile
    lanes = mixed[0].shape[1] // 3
    length = rows // sequences
    heads = lanes // head_size
    pack = LANES // head_size
    return pl.pallas_call(
        functools.partial(attend_kernel, head_size, len(mixed)),
        grid_spec=pltpu.PrefetchScalarGridSpec(
            num_scalar_prefetch=2,
            grid=(sequences,),
            in_specs=[pl.BlockSpec(memory_space=pl.ANY)] * len(mixed),
            out_specs=[
                pl.BlockSpec((length, lanes), lambda s, *_: (s, 0)),
                pl.BlockSpec((1, heads, length), lambda s, *_: (s, 0, 0)),
            ],
            scratch_shapes=[
                pltpu.VMEM((blocks, tile, 3 * lanes), jnp.bfloat16),
                pltpu.VMEM((pack, length, LANES), jnp.bfloat16),
                pltpu.VMEM((pack, length, LANES), jnp.bfloat16),
                pltpu.SemaphoreType.DMA((blocks,)),
            ],
        ),
        out_shape=[
            jax.ShapeDtypeStruct((rows, lanes), jnp.bfloat16),
            jax.ShapeDtypeStruct((sequences, heads, length), jnp.float32),
        ],
        compiler_params=pltpu.CompilerParams(vmem_limit_bytes=VMEM_BYTES),
        cost_estimate=pl.CostEstimate(
            flops=rows * length * lanes * 4,
            bytes_accessed=rows * lanes * 8,
            transcendentals=rows * length * heads // 2,
        ),
    )(counts, slots, *mixed)


def attend_back_kernel(
    head_size,
    blocks_in,
    counts,
    slots,
    *refs,
):
    sources = refs[:blocks_in]
    grad_ref, out_ref, log_ref, own_ref, other_ref, mixed_ref = refs[blocks_in : blocks_in + 6]
    query_own, key_own, grad_own, delta, grad_query, grad_key, grad_value, back_ref, sems = refs[
        blocks_in + 6 :
    ]
    fetch(sources, mixed_ref, sems)
    length, lanes = out_ref.shape
    tile = mixed_ref.shape[1]
    pack = LANES // head_size
    scale = head_size ** (-0.5)
    sequence = pl.program_id(0)
    blocks = lax.div(counts[sequence] + (tile - 1), tile)
    masks = head_masks(head_size)
    for i in range(length // tile):
        back_ref[slots[sequence, i]] = jnp.zeros((tile, 3 * lanes), back_ref.dtype)
    key_row = lax.broadcasted_iota(jnp.int32, (tile, tile), 0)
    query_col = lax.broadcasted_iota(jnp.int32, (tile, tile), 1)
    for pair in range(lanes // LANES):
        base = pair * LANES
        for i in range(length // tile):
            span = slice(i * tile, (i + 1) * tile)
            slot = slots[sequence, i]
            queries = mixed_ref[slot, :, base : base + LANES]
            keys = mixed_ref[slot, :, lanes + base : lanes + base + LANES]
            grads = grad_ref[span, base : base + LANES]
            for h in range(pack):
                query_own[h, span] = jnp.where(masks[h], queries, jnp.zeros_like(queries))
                key_own[h, span] = jnp.where(masks[h], keys, jnp.zeros_like(keys))
                grad_own[h, span] = jnp.where(masks[h], grads, jnp.zeros_like(grads))
        grad_query[...] = jnp.zeros(grad_query.shape, jnp.float32)

        def deltas(i, _, base=base):
            start = pl.multiple_of(i * tile, tile)
            grads = grad_ref[pl.ds(start, tile), base : base + LANES].astype(jnp.float32)
            outs = out_ref[pl.ds(start, tile), base : base + LANES].astype(jnp.float32)
            products = jnp.transpose(grads * outs)
            for h in range(pack):
                delta[h : h + 1, pl.ds(start, tile)] = jnp.sum(
                    products[h * head_size : (h + 1) * head_size], axis=0, keepdims=True
                )
            return 0

        lax.fori_loop(0, blocks, deltas, 0)

        def key_block(j, _, pair=pair, base=base):
            first = pl.multiple_of(j * tile, tile)
            place = slots[sequence, j]
            keys = mixed_ref[place, :, lanes + base : lanes + base + LANES]
            values = mixed_ref[place, :, 2 * lanes + base : 2 * lanes + base + LANES]
            grad_key[...] = jnp.zeros(grad_key.shape, jnp.float32)
            grad_value[...] = jnp.zeros(grad_value.shape, jnp.float32)

            def step(i, diagonal=False):
                start = pl.multiple_of(i * tile, tile)
                add_query, add_key, add_value = [], [], []
                for h in range(pack):
                    index = pair * pack + h
                    query_head = query_own[h, pl.ds(start, tile)]
                    grad_head = grad_own[h, pl.ds(start, tile)]
                    scores = dot_nt(keys, query_head) * (scale * LOG2E)
                    probs = jnp.exp2(scores - log_ref[0, index : index + 1, pl.ds(start, tile)])
                    if diagonal:
                        probs = jnp.where(key_row <= query_col, probs, 0.0)
                    grad_probs = dot_nt(values, grad_head)
                    grad_scores = (
                        probs * (grad_probs - delta[h : h + 1, pl.ds(start, tile)])
                    ).astype(jnp.bfloat16)
                    add_value.append(dot_nn(probs.astype(jnp.bfloat16), grad_head))
                    add_key.append(dot_nn(grad_scores, query_head))
                    add_query.append(dot_tn(grad_scores, key_own[h, pl.ds(first, tile)]))
                grad_value[...] += functools.reduce(jnp.add, add_value)
                grad_key[...] += functools.reduce(jnp.add, add_key)
                grad_query[pl.ds(start, tile), :] += functools.reduce(jnp.add, add_query)

            def off_diagonal(i, _):
                step(i)
                return 0

            step(j, diagonal=True)
            lax.fori_loop(j + 1, blocks, off_diagonal, 0)
            back_ref[place, :, lanes + base : lanes + base + LANES] = (grad_key[...] * scale).astype(
                back_ref.dtype
            )
            back_ref[place, :, 2 * lanes + base : 2 * lanes + base + LANES] = grad_value[...].astype(
                back_ref.dtype
            )
            return 0

        lax.fori_loop(0, blocks, key_block, 0)
        for i in range(length // tile):
            back_ref[slots[sequence, i], :, base : base + LANES] = (
                grad_query[i * tile : (i + 1) * tile] * scale
            ).astype(back_ref.dtype)

    @pl.when(sequence == pl.num_programs(0) - 1)
    def _():
        half = back_ref.shape[0] // 2
        for k in range(half):
            own_ref[k * tile : (k + 1) * tile] = back_ref[k]
            other_ref[k * tile : (k + 1) * tile] = back_ref[half + k]


def attend_back(mixed, slots, grads, outs, logs, counts, head_size):
    sequences = counts.shape[0]
    rows, lanes = outs.shape
    length = rows // sequences
    heads = lanes // head_size
    pack = LANES // head_size
    tile = rows // slots.size
    blocks = rows // tile
    whole = pl.BlockSpec((rows // 2, 3 * lanes), lambda s, *_: (0, 0))
    return pl.pallas_call(
        functools.partial(attend_back_kernel, head_size, len(mixed)),
        grid_spec=pltpu.PrefetchScalarGridSpec(
            num_scalar_prefetch=2,
            grid=(sequences,),
            in_specs=[pl.BlockSpec(memory_space=pl.ANY)] * len(mixed)
            + [
                pl.BlockSpec((length, lanes), lambda s, *_: (s, 0)),
                pl.BlockSpec((length, lanes), lambda s, *_: (s, 0)),
                pl.BlockSpec((1, heads, length), lambda s, *_: (s, 0, 0)),
            ],
            out_specs=[whole, whole],
            scratch_shapes=[
                pltpu.VMEM((blocks, tile, 3 * lanes), jnp.bfloat16),
                pltpu.VMEM((pack, length, LANES), jnp.bfloat16),
                pltpu.VMEM((pack, length, LANES), jnp.bfloat16),
                pltpu.VMEM((pack, length, LANES), jnp.bfloat16),
                pltpu.VMEM((pack, length), jnp.float32),
                pltpu.VMEM((length, LANES), jnp.float32),
                pltpu.VMEM((tile, LANES), jnp.float32),
                pltpu.VMEM((tile, LANES), jnp.float32),
                pltpu.VMEM((blocks, tile, 3 * lanes), jnp.bfloat16),
                pltpu.SemaphoreType.DMA((blocks,)),
            ],
        ),
        out_shape=[jax.ShapeDtypeStruct((rows // 2, 3 * lanes), jnp.bfloat16)] * 2,
        compiler_params=pltpu.CompilerParams(vmem_limit_bytes=VMEM_BYTES),
        cost_estimate=pl.CostEstimate(
            flops=rows * length * lanes * 10,
            bytes_accessed=rows * lanes * 18,
            transcendentals=rows * length * heads // 2,
        ),
    )(counts, slots, *mixed, grads, outs, logs)


def ffn_kernel(r, x_parts, g_parts, counts, *refs):
    xs, refs = refs[:x_parts], refs[x_parts:]
    gs, refs = refs[:g_parts], refs[g_parts:]
    up_next, down_next, up_last, shift = refs[:4]
    units_ref, back_ref, out_ref, x, g, pres, grads, backs, total, x_sems, g_sems = refs[-11:]
    fetch(xs, x, x_sems)
    fetch(gs, g, g_sems)
    size = out_ref.shape[0]
    model = out_ref.shape[1]
    step = pl.program_id(0)
    tiles = pl.num_programs(0) - 2
    even = lax.rem(step, 2)

    def multiply():
        pres[even] = dot_nt(x[...].reshape(size, model), up_next[...])
        grads[even] = dot_nt(g[...].reshape(size, model), down_next[...])

    def activate():
        pre = pres[1 - even] + shift[...]
        bell = jnp.exp2(pre * pre * (-0.5 * LOG2E))
        denominator = 1.0 + (0.3275911 * 0.7071067811865476) * jnp.abs(pre)
        t = pl.reciprocal(denominator, approx=True)
        t = t * (2.0 - denominator * t)
        tail = 0.5 * 1.061405429
        for factor in (-1.453152027, 1.421413741, -0.284496736, 0.254829592):
            tail = tail * t + 0.5 * factor
        tail = tail * t * bell
        below = jnp.where(pre < 0, tail, 1.0 - tail)
        units_ref[...] = (pre * below).astype(units_ref.dtype)
        slope = below + pre * bell * 0.3989422804014327
        back = (grads[1 - even] * slope).astype(back_ref.dtype)
        back_ref[...] = back
        backs[1 - even] = back

    def collect():
        total[...] += dot_nn(backs[even], up_last[...])

    active = counts[r] != 0

    @pl.when(step == 0)
    def _():
        total[...] = jnp.zeros(total.shape, total.dtype)

    @pl.when(active & (step == 0))
    def _():
        multiply()

    @pl.when(active & (step == 1))
    def _():
        multiply()
        activate()

    @pl.when(active & (step > 1) & (step < tiles))
    def _():
        collect()
        activate()
        multiply()

    @pl.when(active & (step == tiles))
    def _():
        collect()
        activate()

    @pl.when(active & (step == tiles + 1))
    def _():
        collect()

    @pl.when(jnp.logical_not(active))
    def _():
        units_ref[...] = jnp.zeros(units_ref.shape, units_ref.dtype)
        back_ref[...] = jnp.zeros(back_ref.shape, back_ref.dtype)

    @pl.when(step == tiles + 1)
    def _():
        out_ref[...] = total[...].astype(out_ref.dtype)


def ffn_block(r, counts, xs, gs, up, down, shift, kept):
    model = xs[0].shape[1]
    size = sum(x.shape[0] for x in xs)
    units = up.shape[0]
    tile = 512
    tiles = units // tile
    whole = pl.BlockSpec(memory_space=pl.ANY)
    following = pl.BlockSpec((tile, model), lambda u, *_: (jnp.minimum(u, tiles - 1), 0))
    lagging = pl.BlockSpec((tile, model), lambda u, *_: (jnp.clip(u - 2, 0, tiles - 1), 0))
    current = lambda u, *_: jnp.clip(u - 1, 0, tiles - 1)
    output = pl.BlockSpec((size, tile), lambda u, *_: (r, current(u)))
    full = jax.ShapeDtypeStruct((4 * size, units), jnp.bfloat16)
    half = size // 2
    pieces = lambda parts: (len(parts), parts[0].shape[0], model)
    return pl.pallas_call(
        functools.partial(ffn_kernel, r, len(xs), len(gs)),
        grid_spec=pltpu.PrefetchScalarGridSpec(
            num_scalar_prefetch=1,
            grid=(tiles + 2,),
            in_specs=[whole] * (len(xs) + len(gs))
            + [
                following,
                following,
                lagging,
                pl.BlockSpec((1, tile), lambda u, *_: (0, current(u))),
            ]
            + [whole] * len(kept),
            out_specs=[output, output, pl.BlockSpec((size, model), lambda u, *_: (0, 0))],
            scratch_shapes=[
                pltpu.VMEM(pieces(xs), jnp.bfloat16),
                pltpu.VMEM(pieces(gs), jnp.bfloat16),
                pltpu.VMEM((2, size, tile), jnp.float32),
                pltpu.VMEM((2, size, tile), jnp.float32),
                pltpu.VMEM((2, size, tile), jnp.bfloat16),
                pltpu.VMEM((size, model), jnp.float32),
                pltpu.SemaphoreType.DMA((len(xs),)),
                pltpu.SemaphoreType.DMA((len(gs),)),
            ],
        ),
        out_shape=[full, full, jax.ShapeDtypeStruct((size, model), jnp.bfloat16)],
        input_output_aliases={len(xs) + len(gs) + 5 + k: k for k in range(len(kept))},
        compiler_params=pltpu.CompilerParams(vmem_limit_bytes=VMEM_BYTES),
        cost_estimate=pl.CostEstimate(
            flops=6 * size * units * model,
            bytes_accessed=6 * units * model + 8 * size * model,
            transcendentals=2 * size * units,
        ),
    )(counts, *xs, *gs, up, down, up, shift, *kept)


def products_kernel(active, left, right, out_ref):
    here = active[pl.program_id(0)] != 0

    @pl.when(here)
    def _():
        out_ref[...] = dot_nn(left[...], right[...]).astype(out_ref.dtype)

    @pl.when(jnp.logical_not(here))
    def _():
        out_ref[...] = jnp.zeros(out_ref.shape, out_ref.dtype)


def products(counts, left, right):
    blocks = counts.shape[0]
    size = left.shape[0] // blocks
    depth, columns = right.shape
    return pl.pallas_call(
        products_kernel,
        grid_spec=pltpu.PrefetchScalarGridSpec(
            num_scalar_prefetch=1,
            grid=(blocks,),
            in_specs=[
                pl.BlockSpec((size, depth), lambda i, *_: (i, 0)),
                pl.BlockSpec(right.shape, lambda i, *_: (0, 0)),
            ],
            out_specs=pl.BlockSpec((size, columns), lambda i, *_: (i, 0)),
        ),
        out_shape=jax.ShapeDtypeStruct((blocks * size, columns), jnp.bfloat16),
        compiler_params=pltpu.CompilerParams(vmem_limit_bytes=VMEM_BYTES),
        cost_estimate=pl.CostEstimate(
            flops=2 * blocks * size * depth * columns,
            bytes_accessed=2 * (blocks * size * (depth + columns) + depth * columns),
            transcendentals=0,
        ),
    )(counts, left, right)


def project_kernel(inputs, parts, *refs):
    xs = refs[:inputs]
    weights, shifts, outs = refs[inputs : inputs + 2], refs[inputs + 2], refs[inputs + 3 :]
    slab = weights[0].shape[1]
    for k in range(inputs):

        @pl.when(pl.program_id(0) == k)
        def _(k=k):
            for side in (1, 0):
                for t in range(3):
                    columns = pl.ds(pl.multiple_of(parts[side, t] * slab, slab), slab)
                    outs[side][:, columns] = (
                        dot_nt(xs[k][...], weights[side][t]) + shifts[side : side + 1, columns]
                    ).astype(outs[side].dtype)


def project(parts, xs, own, other, shifts):
    size, model = xs[0].shape
    slab = own.shape[1]
    fixed = pl.BlockSpec(own.shape, lambda i, *_: (0, 0, 0))
    output = pl.BlockSpec((size, 3 * slab), lambda i, *_: (i, 0))
    return pl.pallas_call(
        functools.partial(project_kernel, len(xs)),
        grid_spec=pltpu.PrefetchScalarGridSpec(
            num_scalar_prefetch=1,
            grid=(len(xs),),
            in_specs=[pl.BlockSpec((size, model), lambda i, *_: (0, 0))] * len(xs)
            + [fixed, fixed, pl.BlockSpec(shifts.shape, lambda i, *_: (0, 0))],
            out_specs=[output, output],
        ),
        out_shape=[jax.ShapeDtypeStruct((len(xs) * size, 3 * slab), jnp.bfloat16)] * 2,
        compiler_params=pltpu.CompilerParams(vmem_limit_bytes=VMEM_BYTES),
        cost_estimate=pl.CostEstimate(
            flops=12 * len(xs) * size * slab * model,
            bytes_accessed=12 * slab * model + 2 * len(xs) * size * (model + 6 * slab),
            transcendentals=0,
        ),
    )(parts, *xs, own, other, shifts)


def unproject_kernel(parts, active, mine, theirs, own, other, out_ref):
    slab = own.shape[1]
    here = active[pl.program_id(0)] != 0

    @pl.when(here)
    def _():
        total = None
        for side, (left, right) in enumerate(((mine, own), (theirs, other))):
            for t in range(3):
                columns = pl.ds(pl.multiple_of(parts[side, t] * slab, slab), slab)
                term = dot_nn(left[:, columns], right[t])
                total = term if total is None else total + term
        out_ref[...] = total.astype(out_ref.dtype)

    @pl.when(jnp.logical_not(here))
    def _():
        out_ref[...] = jnp.zeros(out_ref.shape, out_ref.dtype)


def unproject(parts, counts, mine, theirs, own, other):
    blocks = counts.shape[0]
    size = mine.shape[0] // blocks
    slab, model = own.shape[1:]
    left = pl.BlockSpec((size, 3 * slab), lambda i, *_: (i, 0))
    fixed = pl.BlockSpec(own.shape, lambda i, *_: (0, 0, 0))
    return pl.pallas_call(
        unproject_kernel,
        grid_spec=pltpu.PrefetchScalarGridSpec(
            num_scalar_prefetch=2,
            grid=(blocks,),
            in_specs=[left, left, fixed, fixed],
            out_specs=pl.BlockSpec((size, model), lambda i, *_: (i, 0)),
        ),
        out_shape=jax.ShapeDtypeStruct((blocks * size, model), jnp.bfloat16),
        compiler_params=pltpu.CompilerParams(vmem_limit_bytes=VMEM_BYTES),
        cost_estimate=pl.CostEstimate(
            flops=12 * blocks * size * slab * model,
            bytes_accessed=12 * slab * model + 2 * blocks * size * (model + 6 * slab),
            transcendentals=0,
        ),
    )(parts, counts, mine, theirs, own, other)


def weight_grad_kernel(inputs, added, columns, *refs):
    left, rights = refs[0], refs[1 : 1 + inputs]
    out_ref, tokens, sems = refs[-3:]
    fetch(rights, tokens, sems)
    rows, model = left.shape[0], out_ref.shape[1]
    total = dot_tn(left[...], tokens[...].reshape(rows, model))
    if added:
        total = total + refs[1 + inputs][...].astype(jnp.float32)
    out_ref[...] = total.astype(out_ref.dtype)


def weight_grad(left, columns, tile, rights, extra=None):
    rows = left.shape[0]
    model = rights[0].shape[1]
    steps = columns.shape[0]
    least = min(right.shape[0] for right in rights)
    output = pl.BlockSpec((tile, model), lambda i, *_: (i, 0))
    extras = [] if extra is None else [extra]
    return pl.pallas_call(
        functools.partial(weight_grad_kernel, len(rights), len(extras)),
        grid_spec=pltpu.PrefetchScalarGridSpec(
            num_scalar_prefetch=1,
            grid=(steps,),
            in_specs=[pl.BlockSpec((rows, tile), lambda i, columns: (0, columns[i]))]
            + [pl.BlockSpec(memory_space=pl.ANY)] * len(rights)
            + [output] * len(extras),
            out_specs=output,
            scratch_shapes=[
                pltpu.VMEM((rows // least, least, model), jnp.bfloat16),
                pltpu.SemaphoreType.DMA((rows // least,)),
            ],
        ),
        out_shape=jax.ShapeDtypeStruct((steps * tile, model), jnp.bfloat16),
        compiler_params=pltpu.CompilerParams(vmem_limit_bytes=VMEM_BYTES),
        cost_estimate=pl.CostEstimate(
            flops=2 * steps * tile * rows * model,
            bytes_accessed=2 * (rows * model + steps * tile * (rows + 2 * model)),
            transcendentals=0,
        ),
    )(columns, left, *rights, *extras)


def chain_sum(values, axis):
    size = lax.axis_size(axis)
    if size != 4:
        return lax.psum(values.astype(jnp.bfloat16), axis).astype(jnp.float32)
    place = lax.axis_index(axis)
    outer = lax.ppermute(values.astype(jnp.bfloat16), axis, [(0, 1), (3, 2)])
    half = (values + outer.astype(jnp.float32)).astype(jnp.bfloat16)
    other = lax.ppermute(half, axis, [(1, 2), (2, 1)])
    whole = (half.astype(jnp.float32) + other.astype(jnp.float32)).astype(jnp.bfloat16)
    ends = lax.ppermute(whole, axis, [(1, 0), (2, 3)])
    inner = (place == 1) | (place == 2)
    return jnp.where(inner, whole, ends).astype(jnp.float32)


class Chain:
    def __init__(self):
        place = lax.axis_index("batch")
        self.inner = (place == 1) | (place == 2)
        self.first = self.second = self.third = None
        self.outward = self.across = None
        self.totals = []

    def advance(self, block, *done):
        wide = lambda values: values.astype(jnp.float32)
        outward, across = after((self.outward, self.across), *done)
        half = whole = None
        if self.first is not None:
            half = (wide(self.first) + wide(outward)).astype(jnp.bfloat16)
        if self.second is not None:
            whole = (wide(self.second) + wide(across)).astype(jnp.bfloat16)
        if self.third is not None:
            self.totals.append(jnp.where(self.inner, self.third, outward))
        sent = block
        if whole is not None:
            sent = whole if block is None else jnp.where(self.inner, whole, block)
        self.outward = self.across = None
        if sent is not None:
            self.outward = lax.ppermute(sent, "batch", [(0, 1), (1, 0), (2, 3), (3, 2)])
        if half is not None:
            self.across = lax.ppermute(half, "batch", [(1, 2), (2, 1)])
        self.first, self.second, self.third = block, half, whole
        return [value for value in (sent, half) if value is not None]


def normalize(values):
    center = values - jnp.mean(values, axis=-1, keepdims=True)
    inverse = lax.rsqrt(jnp.mean(center * center, axis=-1, keepdims=True) + epsilon)
    return center * inverse, inverse


def normalize_back(grad, gain, normal, inverse):
    scaled = grad * gain
    grad_values = inverse * (
        scaled
        - jnp.mean(scaled, axis=-1, keepdims=True)
        - normal * jnp.mean(scaled * normal, axis=-1, keepdims=True)
    )
    return grad_values, jnp.sum(grad * normal, axis=0), jnp.sum(grad, axis=0)


def local_general(
    hidden,
    cotangent,
    exit_layer,
    ln1_gain,
    ln1_bias,
    qkv_weight,
    query_bias,
    value_bias,
    out_weight,
    out_bias,
    ln2_gain,
    ln2_bias,
    up_weight,
    up_bias,
    down_weight,
    down_bias,
):
    width = lax.axis_size("wide")
    rank = lax.axis_index("wide")
    rows, model = hidden.shape
    group = rows * width
    slab = model // width
    head_size = model // HEADS
    units_own = up_weight.shape[0]
    keep = exit_layer >= LAYER
    counts = jnp.sum(keep.astype(jnp.int32), axis=1)
    active = lax.dynamic_slice_in_dim(keep.reshape(group), rank * rows, rows, 0)
    active = active.astype(jnp.float32)[:, None]
    grad_out = cotangent.astype(jnp.float32)

    routes = [[(w, (3 * w + t) % width) for w in range(width)] for t in range(3)]
    part_at = np.zeros((width, 3), np.int32)
    for t in range(3):
        for w, d in routes[t]:
            part_at[d, t] = (3 * w + t) // width
    place_of = jnp.asarray(np.argsort(part_at, axis=1).astype(np.int32))[rank]
    part_of = jnp.asarray(part_at)[rank]

    hidden_wide = hidden.astype(jnp.float32)
    normal1, inverse1 = normalize(hidden_wide)
    normed1 = lax.all_gather(
        (normal1 * ln1_gain + ln1_bias).astype(jnp.bfloat16), "wide", axis=0, tiled=True
    )
    slabs = qkv_weight.reshape(3, slab, model)
    received = jnp.stack([lax.ppermute(slabs[t], "wide", routes[t]) for t in range(3)])
    qkv_own = jnp.concatenate(
        [lax.dynamic_index_in_dim(received, place_of[p], 0, keepdims=False) for p in range(3)]
    )
    own = lambda vector: lax.dynamic_slice_in_dim(vector, rank * slab, slab, 0)
    qkv_shift = jnp.concatenate(
        [own(query_bias), jnp.zeros((slab,), jnp.float32), own(value_bias)]
    )

    grad_ffn = (active * grad_out).astype(jnp.bfloat16)
    down_bias_grad = jnp.sum(grad_ffn.astype(jnp.float32), axis=0)
    piece = rows // CHUNKS
    part = lambda values, c: values[c * piece : (c + 1) * piece]
    gather = lambda values: lax.all_gather(values, "wide", axis=0, tiled=True)
    scatter = lambda values: lax.psum_scatter(
        values.astype(jnp.bfloat16), "wide", scatter_dimension=0, tiled=True
    )
    grad_ffns = [gather(part(grad_ffn, c)) for c in range(CHUNKS)]
    out_whole = gather(out_weight)

    mixed = (dot_nt(normed1, qkv_own) + qkv_shift).astype(jnp.bfloat16)
    mixed = jnp.split(mixed, group // TILE)
    slots = jnp.arange(group // TILE, dtype=jnp.int32).reshape(counts.shape[0], -1)
    attended, logs = attend(mixed, slots, counts, head_size)
    attended_rows = lax.all_to_all(attended, "wide", split_axis=0, concat_axis=1, tiled=True)
    middle = hidden_wide + active * (dot_nn(attended_rows, out_whole) + out_bias)
    normal2, inverse2 = normalize(middle)
    normed2 = (normal2 * ln2_gain + ln2_bias).astype(jnp.bfloat16)
    up_shift = lax.dynamic_slice_in_dim(up_bias, rank * units_own, units_own, 0)

    normed2s = [gather(part(normed2, c)) for c in range(CHUNKS)]
    units, grad_pres, grad_normed2, ffn_out = [], [], [], []
    for c in range(CHUNKS):
        grad_units = dot_nt(grad_ffns[c], down_weight)
        pre = dot_nt(normed2s[c], up_weight) + up_shift
        below = 0.5 + 0.5 * lax.erf(pre * 0.7071067811865476)
        bell = jnp.exp(-0.5 * pre * pre) * 0.3989422804014327
        units.append((pre * below).astype(jnp.bfloat16))
        grad_pres.append((grad_units * (below + pre * bell)).astype(jnp.bfloat16))
        grad_normed2.append(scatter(dot_nn(grad_pres[c], up_weight)))
    for c in range(CHUNKS):
        ffn_out.append(scatter(dot_nn(units[c], down_weight)))
    grad_normed2 = jnp.concatenate(grad_normed2).astype(jnp.float32)
    ffn_out = jnp.concatenate(ffn_out).astype(jnp.float32)
    output = (middle + active * (ffn_out + down_bias)).astype(jnp.bfloat16)

    up_bias_own = sum(jnp.sum(g.astype(jnp.float32), axis=0) for g in grad_pres)
    down_grad = sum(dot_tn(units[c], grad_ffns[c]) for c in range(CHUNKS))
    up_grad = sum(dot_tn(grad_pres[c], normed2s[c]) for c in range(CHUNKS))
    halves = lambda values: jnp.concatenate(
        [chain_sum(half, "batch") for half in jnp.split(values, 2)]
    )
    down_grad = halves(down_grad)
    up_grad = halves(up_grad)

    grad_middle, ln2_gain_grad, ln2_bias_grad = normalize_back(
        grad_normed2, ln2_gain, normal2, inverse2
    )
    grad_middle = grad_out + grad_middle
    grad_branch = (active * grad_middle).astype(jnp.bfloat16)
    out_bias_grad = jnp.sum(grad_branch.astype(jnp.float32), axis=0)
    grad_attended = dot_nt(grad_branch, out_whole).astype(jnp.bfloat16)
    grad_heads = lax.all_to_all(grad_attended, "wide", split_axis=1, concat_axis=0, tiled=True)
    out_grad = chain_sum(scatter(dot_tn(attended_rows, grad_branch)).astype(jnp.float32), "batch")

    placed = lambda vector, size: lax.dynamic_update_slice_in_dim(
        jnp.zeros((size,), jnp.float32), vector, rank * vector.shape[0], 0
    )
    early = lax.psum(
        (
            out_bias_grad,
            ln2_gain_grad,
            ln2_bias_grad,
            placed(up_bias_own, up_bias.shape[0]),
            down_bias_grad,
        ),
        ("batch", "wide"),
    )

    grad_mixed = jnp.concatenate(
        attend_back(mixed, slots, grad_heads, attended, logs, counts, head_size)
    )
    grad_normed1 = scatter(dot_nn(grad_mixed, qkv_own)).astype(jnp.float32)
    sums = jnp.sum(grad_mixed.astype(jnp.float32), axis=0)
    qkv_parts = []
    for t in range(3):
        columns = lax.dynamic_slice_in_dim(grad_mixed, part_of[t] * slab, slab, 1)
        total = chain_sum(dot_tn(columns, normed1), "batch").astype(jnp.bfloat16)
        back = [(d, w) for w, d in routes[t]]
        qkv_parts.append(lax.ppermute(total, "wide", back).astype(jnp.float32))
    qkv_grad = jnp.concatenate(qkv_parts)

    grad_hidden, ln1_gain_grad, ln1_bias_grad = normalize_back(
        grad_normed1, ln1_gain, normal1, inverse1
    )
    input_grad = grad_middle + grad_hidden
    late = lax.psum(
        (
            ln1_gain_grad,
            ln1_bias_grad,
            placed(sums[:slab], model),
            placed(sums[2 * slab :], model),
        ),
        ("batch", "wide"),
    )
    return (
        output,
        input_grad,
        late[0],
        late[1],
        qkv_grad,
        late[2],
        late[3],
        out_grad,
        early[0],
        early[1],
        early[2],
        up_grad,
        early[3],
        down_grad,
        early[4],
    )


def swap(values, bits):
    width = lax.axis_size("wide")
    return lax.ppermute(values, "wide", [(w, w ^ bits) for w in range(width)])


def after(values, *done):
    return lax.optimization_barrier((values, done))[0]


def relay(along_x, along_y):
    half = along_x.shape[0] // 2
    return [swap(along_y[:half], 2), swap(along_x[half:], 4)]


def scatter_chips(partials):
    wide = lambda values: values.astype(jnp.float32)
    own, along_x, along_y, diagonal = partials
    half = own.shape[0] // 2
    top = swap(diagonal[:half], 2)
    bottom = swap(diagonal[half:], 4)
    x_top = swap(along_x[:half], 2)
    y_bottom = swap(along_y[half:], 4)
    y_top = swap((wide(along_y[:half]) + wide(top)).astype(jnp.bfloat16), 4)
    x_bottom = swap((wide(along_x[half:]) + wide(bottom)).astype(jnp.bfloat16), 2)
    return jnp.concatenate(
        [
            wide(own[:half]) + wide(x_top) + wide(y_top),
            wide(own[half:]) + wide(x_bottom) + wide(y_bottom),
        ]
    )


def tree_sum(values):
    total = values + swap(values, 1)
    total = (total + swap(total, 2)) + (swap(total, 4) + swap(total, 6))
    size = lax.axis_size("batch")
    terms = [total] + [
        lax.ppermute(total, "batch", [(z, z ^ bits) for z in range(size)])
        for bits in range(1, size)
    ]
    while len(terms) > 1:
        terms = [terms[k] + terms[k + 1] for k in range(0, len(terms), 2)]
    return terms[0]


def local_chips(
    hidden,
    cotangent,
    exit_layer,
    ln1_gain,
    ln1_bias,
    qkv_weight,
    query_bias,
    value_bias,
    out_weight,
    out_bias,
    ln2_gain,
    ln2_bias,
    up_weight,
    up_bias,
    down_weight,
    down_bias,
):
    width = lax.axis_size("wide")
    rank = lax.axis_index("wide")
    rows, model = hidden.shape
    group = rows * width
    slab = model // width
    head_size = model // HEADS
    units_own = up_weight.shape[0]
    keep = exit_layer >= LAYER
    counts = jnp.sum(keep.astype(jnp.int32), axis=1)
    active = lax.dynamic_slice_in_dim(keep.reshape(group), rank * rows, rows, 0)
    active = active.astype(jnp.float32)[:, None]
    grad_out = cotangent.astype(jnp.float32)
    chips = range(4)

    tiles = jnp.arange(group // rows, dtype=jnp.int32)
    slots = ((tiles ^ rank) & 1) * 4 + ((tiles >> 1) ^ (rank >> 1))
    slots = slots.reshape(counts.shape[0], -1)

    routes = [[(w, (3 * w + t) % width) for w in range(width)] for t in range(3)]
    part_at = np.zeros((width, 3), np.int32)
    for t in range(3):
        for w, d in routes[t]:
            part_at[d, t] = (3 * w + t) // width
    part_at = jnp.asarray(part_at)
    other = rank ^ 1
    parts = jnp.stack([part_at[rank], part_at[other]])

    hidden_wide = hidden.astype(jnp.float32)
    normal1, inverse1 = normalize(hidden_wide)
    slabs = qkv_weight.reshape(3, slab, model)
    slabs = [lax.ppermute(slabs[t], "wide", routes[t]) for t in range(3)]
    normed1 = (normal1 * ln1_gain + ln1_bias).astype(jnp.bfloat16)
    normed1 = [normed1, swap(normed1, 2), swap(normed1, 4)]
    diagonal1 = relay(normed1[1], normed1[2])
    qkv_own = jnp.stack(after(slabs, normed1[1:]))
    qkv_other = swap(qkv_own, 1)

    def shift_of(device):
        own = lambda vector: lax.dynamic_slice_in_dim(vector, device * slab, slab, 0)
        return jnp.concatenate([own(query_bias), jnp.zeros((slab,), jnp.float32), own(value_bias)])

    shifts = jnp.stack([shift_of(rank), shift_of(other)])
    up_other, down_other = swap(after((up_weight, down_weight), normed1[1:]), 1)
    up_both = jnp.concatenate([up_weight, up_other])
    down_both = jnp.concatenate([down_weight, down_other])
    bias_of = lambda device: lax.dynamic_slice_in_dim(up_bias, device * units_own, units_own, 0)
    up_shift = jnp.concatenate([bias_of(rank), bias_of(other)])[None]

    mixed_near, lent_near = project(parts, normed1, qkv_own, qkv_other, shifts)
    lent_near = swap(lent_near, 1)
    diagonal1 = after(diagonal1, mixed_near, up_both, down_both)
    mixed_far, lent_far = project(parts, diagonal1, qkv_own, qkv_other, shifts)
    mixed = [mixed_near, mixed_far, lent_near, swap(lent_far, 1)]

    out_whole = lax.all_gather(after(out_weight, diagonal1), "wide", axis=0, tiled=True)
    grad_ffn = (after(active, diagonal1) * grad_out).astype(jnp.bfloat16)
    down_bias_grad = jnp.sum(grad_ffn.astype(jnp.float32), axis=0)
    grad_ffn = [grad_ffn, swap(grad_ffn, 2), swap(grad_ffn, 4)]

    attended, logs = attend(mixed, slots, counts, head_size)
    attended_rows = lax.all_to_all(attended, "wide", split_axis=0, concat_axis=1, tiled=True)
    middle = hidden_wide + active * (dot_nn(attended_rows, out_whole) + out_bias)
    normal2, inverse2 = normalize(middle)
    normed2 = (normal2 * ln2_gain + ln2_bias).astype(jnp.bfloat16)
    normed2 = [normed2, swap(normed2, 2), swap(normed2, 4)]
    grad_ffn = after(grad_ffn, normed2[0])
    diagonal_ffn = relay(grad_ffn[1], grad_ffn[2])
    diagonal2 = relay(normed2[1], normed2[2])

    per_tile = jnp.sum(keep.reshape(group // rows, rows).astype(jnp.int32), axis=1)
    block_chip = (rank >> 1) ^ jnp.arange(4, dtype=jnp.int32)
    block_counts = per_tile[2 * block_chip + (rank & 1)]
    inputs2 = [[after(normed2[0], grad_ffn[1:])], None, [normed2[2]], diagonal2]
    gradients = [[grad_ffn[0]], [grad_ffn[1]], [grad_ffn[2]], diagonal_ffn]
    kept, partials = (), []
    for r in chips:
        if r == 1:
            inputs2[1] = [after(normed2[1], normed2[2], partials[0])]
        *kept, partial = ffn_block(
            r, block_counts, inputs2[r], gradients[r], up_both, down_both, up_shift, tuple(kept)
        )
        partials.append(partial)
    units, grad_pres = kept
    grad_normed2 = scatter_chips(partials)
    tokens2 = [*normed2, *diagonal2]
    tokens_ffn = [*grad_ffn, *diagonal_ffn]
    chain = Chain()

    tile = 512
    count = units_own // tile
    mine = jnp.arange(count, dtype=jnp.int32)
    lent = mine + count
    down_lent = weight_grad(units, lent, tile, tokens_ffn)
    up_lent = weight_grad(after(grad_pres, down_lent), lent, tile, tokens2)
    down_theirs, up_theirs = swap(down_lent, 1), swap(up_lent, 1)
    down_own = weight_grad(after(units, up_lent), mine, tile, tokens_ffn, down_theirs)
    wait = chain.advance(down_own[:tile], down_own)

    grad_middle, ln2_gain_grad, ln2_bias_grad = normalize_back(
        after(grad_normed2, wait), ln2_gain, normal2, inverse2
    )
    grad_middle = grad_out + grad_middle
    grad_branch = (active * grad_middle).astype(jnp.bfloat16)
    out_bias_grad = jnp.sum(grad_branch.astype(jnp.float32), axis=0)
    grad_attended = dot_nt(grad_branch, out_whole).astype(jnp.bfloat16)
    grad_heads = lax.all_to_all(grad_attended, "wide", split_axis=1, concat_axis=0, tiled=True)

    up_own = weight_grad(after(grad_pres, grad_attended), mine, tile, tokens2, up_theirs)
    out_partial = dot_tn(attended_rows, after(grad_branch, up_own)).astype(jnp.bfloat16)
    out_grad = lax.psum_scatter(out_partial, "wide", scatter_dimension=0, tiled=True)
    wait = chain.advance(down_own[tile:], out_partial)

    back_own, back_other = attend_back(
        mixed, slots, after(grad_heads, wait), attended, logs, counts, head_size
    )
    wait = chain.advance(up_own[:tile], back_own)
    theirs = swap(back_other, 1)
    tokens1 = [*normed1, *diagonal1]
    qkv_lent = weight_grad(after(theirs, wait), parts[1], slab, tokens1)
    grad_normed1 = unproject(
        parts, block_counts, after(back_own, qkv_lent), theirs, qkv_own, qkv_other
    )
    qkv_total = weight_grad(
        after(back_own, grad_normed1), parts[0], slab, tokens1, swap(qkv_lent, 1)
    )
    grad_normed1 = scatter_chips(jnp.split(grad_normed1, 4))
    wait = chain.advance(up_own[tile:], qkv_total)
    ffn_out = products(block_counts, after(units, wait), down_both)
    wait = chain.advance(qkv_total[: 2 * slab], ffn_out)
    ffn_out = scatter_chips(jnp.split(ffn_out, 4))
    output = (middle + active * (ffn_out + down_bias)).astype(jnp.bfloat16)
    up_bias_own = jnp.sum(grad_pres.astype(jnp.float32), axis=0)
    sums = jnp.sum(back_own.astype(jnp.float32), axis=0) + jnp.sum(
        back_other.astype(jnp.float32), axis=0
    )
    chain.advance(jnp.concatenate([qkv_total[2 * slab :], out_grad]), wait)
    chain.advance(None)
    chain.advance(None)
    chain.advance(None)
    totals = chain.totals
    down_grad = jnp.concatenate(totals[0:2]).astype(jnp.float32)
    up_grad = jnp.concatenate(totals[2:4]).astype(jnp.float32)
    out_grad = totals[5][slab:].astype(jnp.float32)
    qkv_parts = [totals[4][:slab], totals[4][slab:], totals[5][:slab]]
    qkv_grad = jnp.concatenate(
        [
            lax.ppermute(qkv_parts[t], "wide", [(d, w) for w, d in routes[t]]).astype(jnp.float32)
            for t in range(3)
        ]
    )

    placed = lambda vector, size, device: lax.dynamic_update_slice_in_dim(
        jnp.zeros((size,), jnp.float32), vector, device * vector.shape[0], 0
    )
    grad_hidden, ln1_gain_grad, ln1_bias_grad = normalize_back(
        grad_normed1, ln1_gain, normal1, inverse1
    )
    input_grad = grad_middle + grad_hidden
    smalls = tree_sum(
        jnp.concatenate(
            [
                placed(up_bias_own[:units_own], up_bias.shape[0], rank)
                + placed(up_bias_own[units_own:], up_bias.shape[0], other),
                down_bias_grad,
                out_bias_grad,
                ln2_gain_grad,
                ln2_bias_grad,
                placed(sums[:slab], model, rank),
                placed(sums[2 * slab :], model, rank),
                ln1_gain_grad,
                ln1_bias_grad,
            ]
        )
    )
    up_bias_grad = smalls[: up_bias.shape[0]]
    smalls = smalls[up_bias.shape[0] :].reshape(8, model)
    return (
        output,
        input_grad,
        smalls[6],
        smalls[7],
        qkv_grad,
        smalls[4],
        smalls[5],
        out_grad,
        smalls[1],
        smalls[2],
        smalls[3],
        up_grad,
        up_bias_grad,
        down_grad,
        smalls[0],
    )


def solution(mesh):
    chips = mesh.shape["wide"] == 8 and mesh.shape["batch"] == 4
    local = local_chips if chips else local_general
    rows = P(("batch", "wide"), None)
    weight = P("wide", None)
    return jax.shard_map(
        local,
        mesh=mesh,
        in_specs=(
            rows,
            rows,
            P("batch", None),
            P(),
            P(),
            weight,
            P(),
            P(),
            weight,
            P(),
            P(),
            P(),
            weight,
            P(),
            weight,
            P(),
        ),
        out_specs=(
            rows,
            rows,
            P(),
            P(),
            weight,
            P(),
            P(),
            weight,
            P(),
            P(),
            P(),
            weight,
            P(),
            weight,
            P(),
        ),
        check_vma=False,
    )
```

```python
import functools

import jax
import jax.numpy as jnp
import numpy as np
from jax import lax
from jax.experimental import pallas as pl
from jax.experimental.pallas import tpu as pltpu
from jax.sharding import PartitionSpec as P

HEADS = 32
LAYER = 12
LANES = 128
TILE = 512
CHUNKS = 2
LOG2E = 1.4426950408889634

epsilon = 1e-05
VMEM_BYTES = 48 * 2**20


def dot_nt(left, right):
    return lax.dot_general(
        left, right, (((1,), (1,)), ((), ())), preferred_element_type=jnp.float32
    )


def dot_nn(left, right):
    return lax.dot_general(
        left, right, (((1,), (0,)), ((), ())), preferred_element_type=jnp.float32
    )


def dot_tn(left, right):
    return lax.dot_general(
        left, right, (((0,), (0,)), ((), ())), preferred_element_type=jnp.float32
    )


def head_masks(head_size):
    lane = lax.broadcasted_iota(jnp.int32, (1, LANES), 1)
    return [
        (lane >= h * head_size) & (lane < (h + 1) * head_size)
        for h in range(LANES // head_size)
    ]


def fetch(sources, target, sems):
    size = target.shape[1]
    copies = []
    row = 0
    for source in sources:
        rows = source.shape[0]
        least = min(rows, size)
        for k in range(rows // least):
            place = target.at[row // size, pl.ds(row % size, least)]
            copies.append(
                pltpu.make_async_copy(source.at[pl.ds(k * least, least)], place, sems.at[len(copies)])
            )
            row += least

    @pl.when(pl.program_id(0) == 0)
    def _():
        for copy in copies:
            copy.start()
        for copy in copies:
            copy.wait()


def attend_kernel(head_size, blocks_in, counts, slots, *refs):
    sources = refs[:blocks_in]
    out_ref, log_ref, mixed_ref, key_own, value_own, sems = refs[blocks_in:]
    fetch(sources, mixed_ref, sems)
    length, lanes = out_ref.shape
    tile = mixed_ref.shape[1]
    pack = LANES // head_size
    scale = head_size ** (-0.5) * LOG2E
    sequence = pl.program_id(0)
    blocks = lax.div(counts[sequence] + (tile - 1), tile)
    masks = head_masks(head_size)
    out_ref[...] = jnp.zeros(out_ref.shape, out_ref.dtype)
    log_ref[...] = jnp.zeros(log_ref.shape, log_ref.dtype)
    row = lax.broadcasted_iota(jnp.int32, (tile, tile), 0)
    col = lax.broadcasted_iota(jnp.int32, (tile, tile), 1)
    for pair in range(lanes // LANES):
        base = pair * LANES
        for i in range(length // tile):
            slot = slots[sequence, i]
            keys = mixed_ref[slot, :, lanes + base : lanes + base + LANES]
            values = mixed_ref[slot, :, 2 * lanes + base : 2 * lanes + base + LANES]
            for h in range(pack):
                key_own[h, i * tile : (i + 1) * tile] = jnp.where(masks[h], keys, jnp.zeros_like(keys))
                value_own[h, i * tile : (i + 1) * tile] = jnp.where(
                    masks[h], values, jnp.zeros_like(values)
                )

        def query_block(i, _, pair=pair, base=base):
            start = pl.multiple_of(i * tile, tile)
            queries = mixed_ref[slots[sequence, i], :, base : base + LANES]

            def step(j, carry, diagonal=False):
                total, tops, sums = carry
                first = pl.multiple_of(j * tile, tile)
                new_tops, new_sums, shrinks, adds = [], [], [], []
                for h in range(pack):
                    scores = dot_nt(queries, key_own[h, pl.ds(first, tile)]) * scale
                    if diagonal:
                        scores = jnp.where(col <= row, scores, -1e30)
                    top = jnp.maximum(tops[h], jnp.max(scores, axis=1, keepdims=True))
                    terms = jnp.exp2(scores - top)
                    shrink = jnp.exp2(tops[h] - top)
                    new_tops.append(top)
                    new_sums.append(sums[h] * shrink + jnp.sum(terms, axis=1, keepdims=True))
                    shrinks.append(shrink)
                    adds.append(dot_nn(terms.astype(jnp.bfloat16), value_own[h, pl.ds(first, tile)]))
                shrink = shrinks[0]
                for h in range(1, pack):
                    shrink = jnp.where(masks[h], shrinks[h], shrink)
                total = total * shrink
                for add in adds:
                    total = total + add
                return total, tuple(new_tops), tuple(new_sums)

            carry = (
                jnp.zeros((tile, LANES), jnp.float32),
                tuple(jnp.full((tile, 1), -1e30, jnp.float32) for _ in range(pack)),
                tuple(jnp.zeros((tile, 1), jnp.float32) for _ in range(pack)),
            )
            carry = lax.fori_loop(0, i, step, carry)
            total, tops, sums = step(i, carry, diagonal=True)
            share = 1.0 / sums[0]
            for h in range(1, pack):
                share = jnp.where(masks[h], 1.0 / sums[h], share)
            out_ref[pl.ds(start, tile), base : base + LANES] = (total * share).astype(out_ref.dtype)
            for h in range(pack):
                logs = jnp.broadcast_to(tops[h] + jnp.log2(sums[h]), (tile, LANES))
                index = pair * pack + h
                log_ref[0, index : index + 1, pl.ds(start, tile)] = jnp.transpose(logs)[0:1]
            return 0

        lax.fori_loop(0, blocks, query_block, 0)


def attend(mixed, slots, counts, head_size):
    sequences = counts.shape[0]
    rows = sum(part.shape[0] for part in mixed)
    tile = rows // slots.size
    blocks = rows // tile
    lanes = mixed[0].shape[1] // 3
    length = rows // sequences
    heads = lanes // head_size
    pack = LANES // head_size
    return pl.pallas_call(
        functools.partial(attend_kernel, head_size, len(mixed)),
        grid_spec=pltpu.PrefetchScalarGridSpec(
            num_scalar_prefetch=2,
            grid=(sequences,),
            in_specs=[pl.BlockSpec(memory_space=pl.ANY)] * len(mixed),
            out_specs=[
                pl.BlockSpec((length, lanes), lambda s, *_: (s, 0)),
                pl.BlockSpec((1, heads, length), lambda s, *_: (s, 0, 0)),
            ],
            scratch_shapes=[
                pltpu.VMEM((blocks, tile, 3 * lanes), jnp.bfloat16),
                pltpu.VMEM((pack, length, LANES), jnp.bfloat16),
                pltpu.VMEM((pack, length, LANES), jnp.bfloat16),
                pltpu.SemaphoreType.DMA((blocks,)),
            ],
        ),
        out_shape=[
            jax.ShapeDtypeStruct((rows, lanes), jnp.bfloat16),
            jax.ShapeDtypeStruct((sequences, heads, length), jnp.float32),
        ],
        compiler_params=pltpu.CompilerParams(vmem_limit_bytes=VMEM_BYTES),
        cost_estimate=pl.CostEstimate(
            flops=rows * length * lanes * 4,
            bytes_accessed=rows * lanes * 8,
            transcendentals=rows * length * heads // 2,
        ),
    )(counts, slots, *mixed)


def attend_back_kernel(
    head_size,
    blocks_in,
    counts,
    slots,
    *refs,
):
    sources = refs[:blocks_in]
    grad_ref, out_ref, log_ref, own_ref, other_ref, mixed_ref = refs[blocks_in : blocks_in + 6]
    query_own, key_own, grad_own, delta, grad_query, grad_key, grad_value, back_ref, sems = refs[
        blocks_in + 6 :
    ]
    fetch(sources, mixed_ref, sems)
    length, lanes = out_ref.shape
    tile = mixed_ref.shape[1]
    pack = LANES // head_size
    scale = head_size ** (-0.5)
    sequence = pl.program_id(0)
    blocks = lax.div(counts[sequence] + (tile - 1), tile)
    masks = head_masks(head_size)
    for i in range(length // tile):
        back_ref[slots[sequence, i]] = jnp.zeros((tile, 3 * lanes), back_ref.dtype)
    key_row = lax.broadcasted_iota(jnp.int32, (tile, tile), 0)
    query_col = lax.broadcasted_iota(jnp.int32, (tile, tile), 1)
    for pair in range(lanes // LANES):
        base = pair * LANES
        for i in range(length // tile):
            span = slice(i * tile, (i + 1) * tile)
            slot = slots[sequence, i]
            queries = mixed_ref[slot, :, base : base + LANES]
            keys = mixed_ref[slot, :, lanes + base : lanes + base + LANES]
            grads = grad_ref[span, base : base + LANES]
            for h in range(pack):
                query_own[h, span] = jnp.where(masks[h], queries, jnp.zeros_like(queries))
                key_own[h, span] = jnp.where(masks[h], keys, jnp.zeros_like(keys))
                grad_own[h, span] = jnp.where(masks[h], grads, jnp.zeros_like(grads))
        grad_query[...] = jnp.zeros(grad_query.shape, jnp.float32)

        def deltas(i, _, base=base):
            start = pl.multiple_of(i * tile, tile)
            grads = grad_ref[pl.ds(start, tile), base : base + LANES].astype(jnp.float32)
            outs = out_ref[pl.ds(start, tile), base : base + LANES].astype(jnp.float32)
            products = jnp.transpose(grads * outs)
            for h in range(pack):
                delta[h : h + 1, pl.ds(start, tile)] = jnp.sum(
                    products[h * head_size : (h + 1) * head_size], axis=0, keepdims=True
                )
            return 0

        lax.fori_loop(0, blocks, deltas, 0)

        def key_block(j, _, pair=pair, base=base):
            first = pl.multiple_of(j * tile, tile)
            place = slots[sequence, j]
            keys = mixed_ref[place, :, lanes + base : lanes + base + LANES]
            values = mixed_ref[place, :, 2 * lanes + base : 2 * lanes + base + LANES]
            grad_key[...] = jnp.zeros(grad_key.shape, jnp.float32)
            grad_value[...] = jnp.zeros(grad_value.shape, jnp.float32)

            def step(i, diagonal=False):
                start = pl.multiple_of(i * tile, tile)
                add_query, add_key, add_value = [], [], []
                for h in range(pack):
                    index = pair * pack + h
                    query_head = query_own[h, pl.ds(start, tile)]
                    grad_head = grad_own[h, pl.ds(start, tile)]
                    scores = dot_nt(keys, query_head) * (scale * LOG2E)
                    probs = jnp.exp2(scores - log_ref[0, index : index + 1, pl.ds(start, tile)])
                    if diagonal:
                        probs = jnp.where(key_row <= query_col, probs, 0.0)
                    grad_probs = dot_nt(values, grad_head)
                    grad_scores = (
                        probs * (grad_probs - delta[h : h + 1, pl.ds(start, tile)])
                    ).astype(jnp.bfloat16)
                    add_value.append(dot_nn(probs.astype(jnp.bfloat16), grad_head))
                    add_key.append(dot_nn(grad_scores, query_head))
                    add_query.append(dot_tn(grad_scores, key_own[h, pl.ds(first, tile)]))
                grad_value[...] += functools.reduce(jnp.add, add_value)
                grad_key[...] += functools.reduce(jnp.add, add_key)
                grad_query[pl.ds(start, tile), :] += functools.reduce(jnp.add, add_query)

            def off_diagonal(i, _):
                step(i)
                return 0

            step(j, diagonal=True)
            lax.fori_loop(j + 1, blocks, off_diagonal, 0)
            back_ref[place, :, lanes + base : lanes + base + LANES] = (grad_key[...] * scale).astype(
                back_ref.dtype
            )
            back_ref[place, :, 2 * lanes + base : 2 * lanes + base + LANES] = grad_value[...].astype(
                back_ref.dtype
            )
            return 0

        lax.fori_loop(0, blocks, key_block, 0)
        for i in range(length // tile):
            back_ref[slots[sequence, i], :, base : base + LANES] = (
                grad_query[i * tile : (i + 1) * tile] * scale
            ).astype(back_ref.dtype)

    @pl.when(sequence == pl.num_programs(0) - 1)
    def _():
        half = back_ref.shape[0] // 2
        for k in range(half):
            own_ref[k * tile : (k + 1) * tile] = back_ref[k]
            other_ref[k * tile : (k + 1) * tile] = back_ref[half + k]


def attend_back(mixed, slots, grads, outs, logs, counts, head_size):
    sequences = counts.shape[0]
    rows, lanes = outs.shape
    length = rows // sequences
    heads = lanes // head_size
    pack = LANES // head_size
    tile = rows // slots.size
    blocks = rows // tile
    whole = pl.BlockSpec((rows // 2, 3 * lanes), lambda s, *_: (0, 0))
    return pl.pallas_call(
        functools.partial(attend_back_kernel, head_size, len(mixed)),
        grid_spec=pltpu.PrefetchScalarGridSpec(
            num_scalar_prefetch=2,
            grid=(sequences,),
            in_specs=[pl.BlockSpec(memory_space=pl.ANY)] * len(mixed)
            + [
                pl.BlockSpec((length, lanes), lambda s, *_: (s, 0)),
                pl.BlockSpec((length, lanes), lambda s, *_: (s, 0)),
                pl.BlockSpec((1, heads, length), lambda s, *_: (s, 0, 0)),
            ],
            out_specs=[whole, whole],
            scratch_shapes=[
                pltpu.VMEM((blocks, tile, 3 * lanes), jnp.bfloat16),
                pltpu.VMEM((pack, length, LANES), jnp.bfloat16),
                pltpu.VMEM((pack, length, LANES), jnp.bfloat16),
                pltpu.VMEM((pack, length, LANES), jnp.bfloat16),
                pltpu.VMEM((pack, length), jnp.float32),
                pltpu.VMEM((length, LANES), jnp.float32),
                pltpu.VMEM((tile, LANES), jnp.float32),
                pltpu.VMEM((tile, LANES), jnp.float32),
                pltpu.VMEM((blocks, tile, 3 * lanes), jnp.bfloat16),
                pltpu.SemaphoreType.DMA((blocks,)),
            ],
        ),
        out_shape=[jax.ShapeDtypeStruct((rows // 2, 3 * lanes), jnp.bfloat16)] * 2,
        compiler_params=pltpu.CompilerParams(vmem_limit_bytes=VMEM_BYTES),
        cost_estimate=pl.CostEstimate(
            flops=rows * length * lanes * 10,
            bytes_accessed=rows * lanes * 18,
            transcendentals=rows * length * heads // 2,
        ),
    )(counts, slots, *mixed, grads, outs, logs)


def ffn_kernel(block, x_parts, g_parts, counts, *refs):
    xs, refs = refs[:x_parts], refs[x_parts:]
    gs, refs = refs[:g_parts], refs[g_parts:]
    ups, downs, shifts = refs[0:2], refs[2:4], refs[4:6]
    units_ref, back_ref, out_ref, x, g, total, x_sems, g_sems = refs[-8:]
    fetch(xs, x, x_sems)
    fetch(gs, g, g_sems)
    blocks, size, model = x.shape
    width = ups[0].shape[0]
    step = pl.program_id(0)

    @pl.when(step == 0)
    def _():
        total[...] = jnp.zeros(total.shape, total.dtype)

    for k in range(blocks):
        rows = slice(k * size, (k + 1) * size)

        @pl.when(counts[block + k] != 0)
        def _(k=k, rows=rows):
            backs = []
            for side in range(2):
                span = slice(side * width, (side + 1) * width)
                pre = dot_nt(x[k], ups[side][...]) + shifts[side][...]
                grad_units = dot_nt(g[k], downs[side][...])
                bell = jnp.exp2(pre * pre * (-0.5 * LOG2E))
                denominator = 1.0 + (0.3275911 * 0.7071067811865476) * jnp.abs(pre)
                t = pl.reciprocal(denominator, approx=True)
                t = t * (2.0 - denominator * t)
                tail = 0.5 * 1.061405429
                for factor in (-1.453152027, 1.421413741, -0.284496736, 0.254829592):
                    tail = tail * t + 0.5 * factor
                tail = tail * t * bell
                below = jnp.where(pre < 0, tail, 1.0 - tail)
                units_ref[rows, span] = (pre * below).astype(units_ref.dtype)
                slope = below + pre * bell * 0.3989422804014327
                backs.append((grad_units * slope).astype(back_ref.dtype))
                back_ref[rows, span] = backs[-1]
            total[rows] += dot_nn(backs[0], ups[0][...]) + dot_nn(backs[1], ups[1][...])

        @pl.when(counts[block + k] == 0)
        def _(rows=rows):
            units_ref[rows] = jnp.zeros((size, 2 * width), units_ref.dtype)
            back_ref[rows] = jnp.zeros((size, 2 * width), back_ref.dtype)

    @pl.when(step == pl.num_programs(0) - 1)
    def _():
        out_ref[...] = total[...].astype(out_ref.dtype)


def ffn_blocks(place, block, counts, xs, gs, ups, downs, shifts, kept):
    size, width = 512, 256
    model = xs[0].shape[1]
    rows = sum(x.shape[0] for x in xs)
    units = ups[0].shape[0]
    whole = pl.BlockSpec(memory_space=pl.ANY)
    weights = pl.BlockSpec((width, model), lambda u, *_: (u, 0))
    shift = pl.BlockSpec((1, width), lambda u, *_: (0, u))
    output = pl.BlockSpec((rows, 2 * width), lambda u, *_: (place, u))
    full = jax.ShapeDtypeStruct((4 * size, 2 * units), jnp.bfloat16)
    return pl.pallas_call(
        functools.partial(ffn_kernel, block, len(xs), len(gs)),
        grid_spec=pltpu.PrefetchScalarGridSpec(
            num_scalar_prefetch=1,
            grid=(units // width,),
            in_specs=[whole] * (len(xs) + len(gs))
            + [weights] * 4
            + [shift] * 2
            + [whole] * len(kept),
            out_specs=[output, output, pl.BlockSpec((rows, model), lambda u, *_: (0, 0))],
            scratch_shapes=[
                pltpu.VMEM((rows // size, size, model), jnp.bfloat16),
                pltpu.VMEM((rows // size, size, model), jnp.bfloat16),
                pltpu.VMEM((rows, model), jnp.float32),
                pltpu.SemaphoreType.DMA((len(xs),)),
                pltpu.SemaphoreType.DMA((len(gs),)),
            ],
        ),
        out_shape=[full, full, jax.ShapeDtypeStruct((rows, model), jnp.bfloat16)],
        input_output_aliases={len(xs) + len(gs) + 7 + k: k for k in range(len(kept))},
        compiler_params=pltpu.CompilerParams(vmem_limit_bytes=VMEM_BYTES),
        cost_estimate=pl.CostEstimate(
            flops=12 * rows * units * model,
            bytes_accessed=8 * units * model + 8 * rows * model,
            transcendentals=4 * rows * units,
        ),
    )(counts, *xs, *gs, *ups, *downs, *shifts, *kept)


def products_kernel(width, active, left, own, other, out_ref):
    here = active[pl.program_id(0)] != 0

    @pl.when(here)
    def _():
        total = None
        for k in range(own.shape[0] // width):
            rows = slice(k * width, (k + 1) * width)
            for side, right in enumerate((own, other)):
                start = (2 * k + side) * width
                term = dot_nn(left[:, start : start + width], right[rows])
                total = term if total is None else total + term
        out_ref[...] = total.astype(out_ref.dtype)

    @pl.when(jnp.logical_not(here))
    def _():
        out_ref[...] = jnp.zeros(out_ref.shape, out_ref.dtype)


def products(counts, left, own, other):
    blocks = counts.shape[0]
    rows, depth = left.shape
    size = rows // blocks
    columns = own.shape[1]
    return pl.pallas_call(
        functools.partial(products_kernel, 256),
        grid_spec=pltpu.PrefetchScalarGridSpec(
            num_scalar_prefetch=1,
            grid=(blocks,),
            in_specs=[
                pl.BlockSpec((size, depth), lambda i, *_: (i, 0)),
                pl.BlockSpec(own.shape, lambda i, *_: (0, 0)),
                pl.BlockSpec(own.shape, lambda i, *_: (0, 0)),
            ],
            out_specs=pl.BlockSpec((size, columns), lambda i, *_: (i, 0)),
        ),
        out_shape=jax.ShapeDtypeStruct((rows, columns), jnp.bfloat16),
        compiler_params=pltpu.CompilerParams(vmem_limit_bytes=VMEM_BYTES),
        cost_estimate=pl.CostEstimate(
            flops=2 * rows * depth * columns,
            bytes_accessed=2 * (rows * (depth + columns) + depth * columns),
            transcendentals=0,
        ),
    )(counts, left, own, other)


def project_kernel(inputs, parts, *refs):
    xs = refs[:inputs]
    weights, shifts, outs = refs[inputs : inputs + 2], refs[inputs + 2], refs[inputs + 3 :]
    slab = weights[0].shape[1]
    for k in range(inputs):

        @pl.when(pl.program_id(0) == k)
        def _(k=k):
            for side in (1, 0):
                weight = weights[side][...].reshape(3 * slab, weights[side].shape[2])
                mixed = dot_nt(xs[k][...], weight)
                for t in range(3):
                    columns = pl.ds(pl.multiple_of(parts[side, t] * slab, slab), slab)
                    outs[side][:, columns] = (
                        mixed[:, t * slab : (t + 1) * slab] + shifts[side : side + 1, columns]
                    ).astype(outs[side].dtype)


def project(parts, xs, own, other, shifts):
    size, model = xs[0].shape
    slab = own.shape[1]
    fixed = pl.BlockSpec(own.shape, lambda i, *_: (0, 0, 0))
    output = pl.BlockSpec((size, 3 * slab), lambda i, *_: (i, 0))
    return pl.pallas_call(
        functools.partial(project_kernel, len(xs)),
        grid_spec=pltpu.PrefetchScalarGridSpec(
            num_scalar_prefetch=1,
            grid=(len(xs),),
            in_specs=[pl.BlockSpec((size, model), lambda i, *_: (0, 0))] * len(xs)
            + [fixed, fixed, pl.BlockSpec(shifts.shape, lambda i, *_: (0, 0))],
            out_specs=[output, output],
        ),
        out_shape=[jax.ShapeDtypeStruct((len(xs) * size, 3 * slab), jnp.bfloat16)] * 2,
        compiler_params=pltpu.CompilerParams(vmem_limit_bytes=VMEM_BYTES),
        cost_estimate=pl.CostEstimate(
            flops=12 * len(xs) * size * slab * model,
            bytes_accessed=12 * slab * model + 2 * len(xs) * size * (model + 6 * slab),
            transcendentals=0,
        ),
    )(parts, *xs, own, other, shifts)


def unproject_kernel(parts, active, mine, theirs, own, other, out_ref):
    slab = own.shape[1]
    here = active[pl.program_id(0)] != 0

    @pl.when(here)
    def _():
        total = None
        for side, (left, right) in enumerate(((mine, own), (theirs, other))):
            for t in range(3):
                columns = pl.ds(pl.multiple_of(parts[side, t] * slab, slab), slab)
                term = dot_nn(left[:, columns], right[t])
                total = term if total is None else total + term
        out_ref[...] = total.astype(out_ref.dtype)

    @pl.when(jnp.logical_not(here))
    def _():
        out_ref[...] = jnp.zeros(out_ref.shape, out_ref.dtype)


def unproject(parts, counts, mine, theirs, own, other):
    blocks = counts.shape[0]
    size = mine.shape[0] // blocks
    slab, model = own.shape[1:]
    left = pl.BlockSpec((size, 3 * slab), lambda i, *_: (i, 0))
    fixed = pl.BlockSpec(own.shape, lambda i, *_: (0, 0, 0))
    return pl.pallas_call(
        unproject_kernel,
        grid_spec=pltpu.PrefetchScalarGridSpec(
            num_scalar_prefetch=2,
            grid=(blocks,),
            in_specs=[left, left, fixed, fixed],
            out_specs=pl.BlockSpec((size, model), lambda i, *_: (i, 0)),
        ),
        out_shape=jax.ShapeDtypeStruct((blocks * size, model), jnp.bfloat16),
        compiler_params=pltpu.CompilerParams(vmem_limit_bytes=VMEM_BYTES),
        cost_estimate=pl.CostEstimate(
            flops=12 * blocks * size * slab * model,
            bytes_accessed=12 * slab * model + 2 * blocks * size * (model + 6 * slab),
            transcendentals=0,
        ),
    )(parts, counts, mine, theirs, own, other)


def weight_grad_kernel(inputs, added, columns, *refs):
    left, rights = refs[0], refs[1 : 1 + inputs]
    tokens, sems = refs[-2:]
    outs = refs[1 + inputs + added : -2]
    fetch(rights, tokens, sems)
    total = dot_tn(left[...], tokens[0])
    if added:
        total = total + refs[1 + inputs][...].astype(jnp.float32)
    size = outs[0].shape[0]
    for k, out_ref in enumerate(outs):
        out_ref[...] = total[k * size : (k + 1) * size].astype(out_ref.dtype)


def weight_grad(left, columns, tile, rights, extra=None, outputs=1):
    rows = left.shape[0]
    model = rights[0].shape[1]
    steps = columns.shape[0]
    output = pl.BlockSpec((tile // outputs, model), lambda i, *_: (i, 0))
    extras = [] if extra is None else [extra]
    shape = jax.ShapeDtypeStruct((steps * tile // outputs, model), jnp.bfloat16)
    results = pl.pallas_call(
        functools.partial(weight_grad_kernel, len(rights), len(extras)),
        grid_spec=pltpu.PrefetchScalarGridSpec(
            num_scalar_prefetch=1,
            grid=(steps,),
            in_specs=[pl.BlockSpec((rows, tile), lambda i, columns: (0, columns[i]))]
            + [pl.BlockSpec(memory_space=pl.ANY)] * len(rights)
            + [output] * len(extras),
            out_specs=[output] * outputs,
            scratch_shapes=[
                pltpu.VMEM((1, rows, model), jnp.bfloat16),
                pltpu.SemaphoreType.DMA((len(rights),)),
            ],
        ),
        out_shape=[shape] * outputs,
        compiler_params=pltpu.CompilerParams(vmem_limit_bytes=VMEM_BYTES),
        cost_estimate=pl.CostEstimate(
            flops=2 * steps * tile * rows * model,
            bytes_accessed=2 * (rows * model + steps * tile * (rows + 2 * model)),
            transcendentals=0,
        ),
    )(columns, left, *rights, *extras)
    return results[0] if outputs == 1 else results


def chain_sum(values, axis):
    size = lax.axis_size(axis)
    if size != 4:
        return lax.psum(values.astype(jnp.bfloat16), axis).astype(jnp.float32)
    place = lax.axis_index(axis)
    outer = lax.ppermute(values.astype(jnp.bfloat16), axis, [(0, 1), (3, 2)])
    half = (values + outer.astype(jnp.float32)).astype(jnp.bfloat16)
    other = lax.ppermute(half, axis, [(1, 2), (2, 1)])
    whole = (half.astype(jnp.float32) + other.astype(jnp.float32)).astype(jnp.bfloat16)
    ends = lax.ppermute(whole, axis, [(1, 0), (2, 3)])
    inner = (place == 1) | (place == 2)
    return jnp.where(inner, whole, ends).astype(jnp.float32)


class Chain:
    def __init__(self):
        place = lax.axis_index("batch")
        self.inner = (place == 1) | (place == 2)
        self.first = self.second = self.third = None
        self.outward = self.across = None
        self.totals = []

    def advance(self, block, *done):
        wide = lambda values: values.astype(jnp.float32)
        outward, across = after((self.outward, self.across), *done)
        half = whole = None
        if self.first is not None:
            half = (wide(self.first) + wide(outward)).astype(jnp.bfloat16)
        if self.second is not None:
            whole = (wide(self.second) + wide(across)).astype(jnp.bfloat16)
        if self.third is not None:
            self.totals.append(jnp.where(self.inner, self.third, outward))
        sent = block
        if whole is not None:
            sent = whole if block is None else jnp.where(self.inner, whole, block)
        self.outward = self.across = None
        if sent is not None:
            self.outward = lax.ppermute(sent, "batch", [(0, 1), (1, 0), (2, 3), (3, 2)])
        if half is not None:
            self.across = lax.ppermute(half, "batch", [(1, 2), (2, 1)])
        self.first, self.second, self.third = block, half, whole
        return [value for value in (sent, half) if value is not None]


def normalize(values):
    center = values - jnp.mean(values, axis=-1, keepdims=True)
    inverse = lax.rsqrt(jnp.mean(center * center, axis=-1, keepdims=True) + epsilon)
    return center * inverse, inverse


def normalize_back(grad, gain, normal, inverse):
    scaled = grad * gain
    grad_values = inverse * (
        scaled
        - jnp.mean(scaled, axis=-1, keepdims=True)
        - normal * jnp.mean(scaled * normal, axis=-1, keepdims=True)
    )
    return grad_values, jnp.sum(grad * normal, axis=0), jnp.sum(grad, axis=0)


def local_general(
    hidden,
    cotangent,
    exit_layer,
    ln1_gain,
    ln1_bias,
    qkv_weight,
    query_bias,
    value_bias,
    out_weight,
    out_bias,
    ln2_gain,
    ln2_bias,
    up_weight,
    up_bias,
    down_weight,
    down_bias,
):
    width = lax.axis_size("wide")
    rank = lax.axis_index("wide")
    rows, model = hidden.shape
    group = rows * width
    slab = model // width
    head_size = model // HEADS
    units_own = up_weight.shape[0]
    keep = exit_layer >= LAYER
    counts = jnp.sum(keep.astype(jnp.int32), axis=1)
    active = lax.dynamic_slice_in_dim(keep.reshape(group), rank * rows, rows, 0)
    active = active.astype(jnp.float32)[:, None]
    grad_out = cotangent.astype(jnp.float32)

    routes = [[(w, (3 * w + t) % width) for w in range(width)] for t in range(3)]
    part_at = np.zeros((width, 3), np.int32)
    for t in range(3):
        for w, d in routes[t]:
            part_at[d, t] = (3 * w + t) // width
    place_of = jnp.asarray(np.argsort(part_at, axis=1).astype(np.int32))[rank]
    part_of = jnp.asarray(part_at)[rank]

    hidden_wide = hidden.astype(jnp.float32)
    normal1, inverse1 = normalize(hidden_wide)
    normed1 = lax.all_gather(
        (normal1 * ln1_gain + ln1_bias).astype(jnp.bfloat16), "wide", axis=0, tiled=True
    )
    slabs = qkv_weight.reshape(3, slab, model)
    received = jnp.stack([lax.ppermute(slabs[t], "wide", routes[t]) for t in range(3)])
    qkv_own = jnp.concatenate(
        [lax.dynamic_index_in_dim(received, place_of[p], 0, keepdims=False) for p in range(3)]
    )
    own = lambda vector: lax.dynamic_slice_in_dim(vector, rank * slab, slab, 0)
    qkv_shift = jnp.concatenate(
        [own(query_bias), jnp.zeros((slab,), jnp.float32), own(value_bias)]
    )

    grad_ffn = (active * grad_out).astype(jnp.bfloat16)
    down_bias_grad = jnp.sum(grad_ffn.astype(jnp.float32), axis=0)
    piece = rows // CHUNKS
    part = lambda values, c: values[c * piece : (c + 1) * piece]
    gather = lambda values: lax.all_gather(values, "wide", axis=0, tiled=True)
    scatter = lambda values: lax.psum_scatter(
        values.astype(jnp.bfloat16), "wide", scatter_dimension=0, tiled=True
    )
    grad_ffns = [gather(part(grad_ffn, c)) for c in range(CHUNKS)]
    out_whole = gather(out_weight)

    mixed = (dot_nt(normed1, qkv_own) + qkv_shift).astype(jnp.bfloat16)
    mixed = jnp.split(mixed, group // TILE)
    slots = jnp.arange(group // TILE, dtype=jnp.int32).reshape(counts.shape[0], -1)
    attended, logs = attend(mixed, slots, counts, head_size)
    attended_rows = lax.all_to_all(attended, "wide", split_axis=0, concat_axis=1, tiled=True)
    middle = hidden_wide + active * (dot_nn(attended_rows, out_whole) + out_bias)
    normal2, inverse2 = normalize(middle)
    normed2 = (normal2 * ln2_gain + ln2_bias).astype(jnp.bfloat16)
    up_shift = lax.dynamic_slice_in_dim(up_bias, rank * units_own, units_own, 0)

    normed2s = [gather(part(normed2, c)) for c in range(CHUNKS)]
    units, grad_pres, grad_normed2, ffn_out = [], [], [], []
    for c in range(CHUNKS):
        grad_units = dot_nt(grad_ffns[c], down_weight)
        pre = dot_nt(normed2s[c], up_weight) + up_shift
        below = 0.5 + 0.5 * lax.erf(pre * 0.7071067811865476)
        bell = jnp.exp(-0.5 * pre * pre) * 0.3989422804014327
        units.append((pre * below).astype(jnp.bfloat16))
        grad_pres.append((grad_units * (below + pre * bell)).astype(jnp.bfloat16))
        grad_normed2.append(scatter(dot_nn(grad_pres[c], up_weight)))
    for c in range(CHUNKS):
        ffn_out.append(scatter(dot_nn(units[c], down_weight)))
    grad_normed2 = jnp.concatenate(grad_normed2).astype(jnp.float32)
    ffn_out = jnp.concatenate(ffn_out).astype(jnp.float32)
    output = (middle + active * (ffn_out + down_bias)).astype(jnp.bfloat16)

    up_bias_own = sum(jnp.sum(g.astype(jnp.float32), axis=0) for g in grad_pres)
    down_grad = sum(dot_tn(units[c], grad_ffns[c]) for c in range(CHUNKS))
    up_grad = sum(dot_tn(grad_pres[c], normed2s[c]) for c in range(CHUNKS))
    halves = lambda values: jnp.concatenate(
        [chain_sum(half, "batch") for half in jnp.split(values, 2)]
    )
    down_grad = halves(down_grad)
    up_grad = halves(up_grad)

    grad_middle, ln2_gain_grad, ln2_bias_grad = normalize_back(
        grad_normed2, ln2_gain, normal2, inverse2
    )
    grad_middle = grad_out + grad_middle
    grad_branch = (active * grad_middle).astype(jnp.bfloat16)
    out_bias_grad = jnp.sum(grad_branch.astype(jnp.float32), axis=0)
    grad_attended = dot_nt(grad_branch, out_whole).astype(jnp.bfloat16)
    grad_heads = lax.all_to_all(grad_attended, "wide", split_axis=1, concat_axis=0, tiled=True)
    out_grad = chain_sum(scatter(dot_tn(attended_rows, grad_branch)).astype(jnp.float32), "batch")

    placed = lambda vector, size: lax.dynamic_update_slice_in_dim(
        jnp.zeros((size,), jnp.float32), vector, rank * vector.shape[0], 0
    )
    early = lax.psum(
        (
            out_bias_grad,
            ln2_gain_grad,
            ln2_bias_grad,
            placed(up_bias_own, up_bias.shape[0]),
            down_bias_grad,
        ),
        ("batch", "wide"),
    )

    grad_mixed = jnp.concatenate(
        attend_back(mixed, slots, grad_heads, attended, logs, counts, head_size)
    )
    grad_normed1 = scatter(dot_nn(grad_mixed, qkv_own)).astype(jnp.float32)
    sums = jnp.sum(grad_mixed.astype(jnp.float32), axis=0)
    qkv_parts = []
    for t in range(3):
        columns = lax.dynamic_slice_in_dim(grad_mixed, part_of[t] * slab, slab, 1)
        total = chain_sum(dot_tn(columns, normed1), "batch").astype(jnp.bfloat16)
        back = [(d, w) for w, d in routes[t]]
        qkv_parts.append(lax.ppermute(total, "wide", back).astype(jnp.float32))
    qkv_grad = jnp.concatenate(qkv_parts)

    grad_hidden, ln1_gain_grad, ln1_bias_grad = normalize_back(
        grad_normed1, ln1_gain, normal1, inverse1
    )
    input_grad = grad_middle + grad_hidden
    late = lax.psum(
        (
            ln1_gain_grad,
            ln1_bias_grad,
            placed(sums[:slab], model),
            placed(sums[2 * slab :], model),
        ),
        ("batch", "wide"),
    )
    return (
        output,
        input_grad,
        late[0],
        late[1],
        qkv_grad,
        late[2],
        late[3],
        out_grad,
        early[0],
        early[1],
        early[2],
        up_grad,
        early[3],
        down_grad,
        early[4],
    )


def swap(values, bits):
    width = lax.axis_size("wide")
    return lax.ppermute(values, "wide", [(w, w ^ bits) for w in range(width)])


def after(values, *done):
    return lax.optimization_barrier((values, done))[0]


def relay(along_x, along_y):
    half = along_x.shape[0] // 2
    return [swap(along_y[:half], 2), swap(along_x[half:], 4)]


class Scatter:
    def __init__(self, own, along_x, along_y, diagonal):
        self.half = half = own.shape[0] // 2
        self.own, self.along_x, self.along_y = own, along_x, along_y
        self.from_x = swap(jnp.concatenate([diagonal[:half], along_x[:half]]), 2)
        self.from_y = swap(jnp.concatenate([diagonal[half:], along_y[half:]]), 4)

    def second(self, *done):
        half = self.half
        from_x, from_y = after((self.from_x, self.from_y), *done)
        self.near = (from_x[half:], from_y[half:])
        return self.forward(from_x[:half], from_y[:half])

    def forward(self, top, bottom):
        wide = lambda values: values.astype(jnp.float32)
        half = self.half
        y_top = (wide(self.along_y[:half]) + wide(top)).astype(jnp.bfloat16)
        x_bottom = (wide(self.along_x[half:]) + wide(bottom)).astype(jnp.bfloat16)
        self.last = (swap(y_top, 4), swap(x_bottom, 2))
        return y_top, x_bottom

    def finish(self, *done):
        wide = lambda values: values.astype(jnp.float32)
        y_top, x_bottom = after(self.last, *done)
        x_top, y_bottom = self.near
        return jnp.concatenate(
            [
                wide(self.own[: self.half]) + wide(x_top) + wide(y_top),
                wide(self.own[self.half :]) + wide(x_bottom) + wide(y_bottom),
            ]
        )


class EarlyScatter(Scatter):
    def __init__(self, own, along_x, along_y):
        self.half = half = own.shape[0] // 2
        self.own, self.along_x, self.along_y = own, along_x, along_y
        self.near = (swap(along_x[:half], 2), swap(along_y[half:], 4))

    def first(self, diagonal):
        self.from_far = (swap(diagonal[: self.half], 2), swap(diagonal[self.half :], 4))
        self.near = after(self.near, diagonal)
        return self.near

    def second(self, *done):
        return self.forward(*after(self.from_far, *done))


def tree_sum(values):
    total = values + swap(values, 1)
    total = (total + swap(total, 2)) + (swap(total, 4) + swap(total, 6))
    size = lax.axis_size("batch")
    terms = [total] + [
        lax.ppermute(total, "batch", [(z, z ^ bits) for z in range(size)])
        for bits in range(1, size)
    ]
    while len(terms) > 1:
        terms = [terms[k] + terms[k + 1] for k in range(0, len(terms), 2)]
    return terms[0]


def local_chips(
    hidden,
    cotangent,
    exit_layer,
    ln1_gain,
    ln1_bias,
    qkv_weight,
    query_bias,
    value_bias,
    out_weight,
    out_bias,
    ln2_gain,
    ln2_bias,
    up_weight,
    up_bias,
    down_weight,
    down_bias,
):
    width = lax.axis_size("wide")
    rank = lax.axis_index("wide")
    rows, model = hidden.shape
    group = rows * width
    slab = model // width
    head_size = model // HEADS
    units_own = up_weight.shape[0]
    keep = exit_layer >= LAYER
    counts = jnp.sum(keep.astype(jnp.int32), axis=1)
    active = lax.dynamic_slice_in_dim(keep.reshape(group), rank * rows, rows, 0)
    active = active.astype(jnp.float32)[:, None]
    grad_out = cotangent.astype(jnp.float32)

    tiles = jnp.arange(group // rows, dtype=jnp.int32)
    slots = ((tiles ^ rank) & 1) * 4 + ((tiles >> 1) ^ (rank >> 1))
    slots = slots.reshape(counts.shape[0], -1)

    routes = [[(w, (3 * w + t) % width) for w in range(width)] for t in range(3)]
    part_at = np.zeros((width, 3), np.int32)
    for t in range(3):
        for w, d in routes[t]:
            part_at[d, t] = (3 * w + t) // width
    part_at = jnp.asarray(part_at)
    other = rank ^ 1
    parts = jnp.stack([part_at[rank], part_at[other]])

    hidden_wide = hidden.astype(jnp.float32)
    normal1, inverse1 = normalize(hidden_wide)
    slabs = qkv_weight.reshape(3, slab, model)
    slabs = [lax.ppermute(slabs[t], "wide", routes[t]) for t in range(3)]
    normed1 = (normal1 * ln1_gain + ln1_bias).astype(jnp.bfloat16)
    normed1 = [normed1, swap(normed1, 2), swap(normed1, 4)]
    diagonal1 = relay(normed1[1], normed1[2])
    qkv_own = jnp.stack(after(slabs, normed1[1:]))
    qkv_other = swap(qkv_own, 1)

    def shift_of(device):
        own = lambda vector: lax.dynamic_slice_in_dim(vector, device * slab, slab, 0)
        return jnp.concatenate([own(query_bias), jnp.zeros((slab,), jnp.float32), own(value_bias)])

    shifts = jnp.stack([shift_of(rank), shift_of(other)])
    bias_of = lambda device: lax.dynamic_slice_in_dim(up_bias, device * units_own, units_own, 0)
    up_shifts = [bias_of(rank)[None], bias_of(other)[None]]

    mixed_near, lent_near = project(parts, normed1, qkv_own, qkv_other, shifts)
    lent_near = swap(lent_near, 1)
    diagonal1 = after(diagonal1, mixed_near)
    mixed_far, lent_far = project(parts, diagonal1, qkv_own, qkv_other, shifts)
    mixed = [mixed_near, mixed_far, lent_near, swap(lent_far, 1)]

    out_whole = lax.all_gather(after(out_weight, diagonal1), "wide", axis=0, tiled=True)
    grad_ffn = (after(active, diagonal1) * grad_out).astype(jnp.bfloat16)
    down_bias_grad = jnp.sum(grad_ffn.astype(jnp.float32), axis=0)
    grad_ffn = [grad_ffn, swap(grad_ffn, 2), swap(grad_ffn, 4)]

    attended, logs = attend(mixed, slots, counts, head_size)
    attended_rows = lax.all_to_all(attended, "wide", split_axis=0, concat_axis=1, tiled=True)
    up_other, down_other = swap(after((up_weight, down_weight), attended), 1)
    middle = hidden_wide + active * (dot_nn(attended_rows, out_whole) + out_bias)
    normal2, inverse2 = normalize(middle)
    normed2 = (normal2 * ln2_gain + ln2_bias).astype(jnp.bfloat16)
    normed2 = [normed2, swap(normed2, 2), swap(normed2, 4)]

    per_tile = jnp.sum(keep.reshape(group // rows, rows).astype(jnp.int32), axis=1)
    block_chip = (rank >> 1) ^ jnp.arange(4, dtype=jnp.int32)
    block_counts = per_tile[2 * block_chip + (rank & 1)]
    ups, downs = [up_weight, up_other], [down_weight, down_other]

    def ffn(place, block, xs, gs, kept):
        *kept, partial = ffn_blocks(
            place, block, block_counts, xs, gs, ups, downs, up_shifts, tuple(kept)
        )
        return kept, partial

    kept, partial_own = ffn(2, 0, normed2[:1], grad_ffn[:1], ())
    normed2[1:] = after(normed2[1:], partial_own)
    grad_ffn[1:] = after(grad_ffn[1:], normed2[1:])
    diagonal2 = relay(normed2[1], normed2[2])
    diagonal_ffn = relay(grad_ffn[1], grad_ffn[2])
    normed2[1:] = after(normed2[1:], grad_ffn[1:])
    kept, partial_near = ffn(0, 1, normed2[1:], grad_ffn[1:], kept)
    scatter2 = EarlyScatter(partial_own, partial_near[:rows], partial_near[rows:])
    diagonal2 = after(diagonal2, partial_near)
    (units, grad_pres), partial_far = ffn(3, 3, diagonal2, diagonal_ffn, kept)
    wait = scatter2.first(partial_far)
    tokens2 = [*normed2[1:], normed2[0], *diagonal2]
    tokens_ffn = [*grad_ffn[1:], grad_ffn[0], *diagonal_ffn]

    wide = lambda values: values.astype(jnp.float32)
    lowered = lambda values: values.astype(jnp.bfloat16)
    tile = 512
    tiles = jnp.arange(2 * units_own // tile, dtype=jnp.int32)
    down_own, down_lent = weight_grad(after(units, wait), tiles, tile, tokens_ffn, outputs=2)
    wait = scatter2.second(down_lent)
    down_lent = swap(down_lent, 1)
    up_own, up_lent = weight_grad(after(grad_pres, wait), tiles, tile, tokens2, outputs=2)
    up_lent = swap(up_lent, 1)
    grad_normed2 = scatter2.finish(up_own)
    down_sum = lowered(wide(down_own) + wide(after(down_lent, up_own)))
    down_grad = lax.psum(down_sum, "batch")

    grad_middle, ln2_gain_grad, ln2_bias_grad = normalize_back(
        after(grad_normed2, down_sum), ln2_gain, normal2, inverse2
    )
    grad_middle = grad_out + grad_middle
    grad_branch = (active * grad_middle).astype(jnp.bfloat16)
    out_bias_grad = jnp.sum(grad_branch.astype(jnp.float32), axis=0)
    grad_attended = dot_nt(grad_branch, out_whole).astype(jnp.bfloat16)
    grad_heads = lax.all_to_all(grad_attended, "wide", split_axis=1, concat_axis=0, tiled=True)

    owners = 2 * block_chip + (rank & 1)
    grad_branch = after(grad_branch, grad_attended)
    out_lent = weight_grad(attended_rows, owners ^ 1, slab, [grad_branch])
    up_sum = lowered(wide(up_own) + wide(after(up_lent, out_lent)))
    out_lent = swap(out_lent, 1)
    out_own = weight_grad(after(attended_rows, up_sum), owners, slab, [grad_branch], out_lent)
    scatter_out = Scatter(*jnp.split(out_own, 4))

    back_own, back_other = attend_back(
        mixed, slots, after(grad_heads, out_own), attended, logs, counts, head_size
    )
    theirs = swap(back_other, 1)
    wait = scatter_out.second(back_own)
    tokens1 = [*normed1, *diagonal1]
    qkv_own_grad = weight_grad(after(back_own, wait), parts[0], slab, tokens1)
    theirs = after(theirs, qkv_own_grad)
    qkv_lent = weight_grad(theirs, parts[1], slab, tokens1)
    grad_normed1 = unproject(
        parts, block_counts, after(back_own, qkv_lent), theirs, qkv_own, qkv_other
    )
    qkv_lent = swap(qkv_lent, 1)
    scatter1 = Scatter(*jnp.split(grad_normed1, 4))
    qkv_total = lowered(wide(qkv_own_grad) + wide(after(qkv_lent, grad_normed1)))
    out_total = lowered(scatter_out.finish(qkv_total))
    chain = Chain()
    wait = chain.advance(qkv_total[:slab], out_total)
    ffn_counts = block_counts[jnp.array([1, 2, 0, 3])]
    ffn_out = products(ffn_counts, after(units, *wait), *downs)
    up_grad = lax.psum(after(up_sum, after(down_grad, ffn_out)), "batch")
    wait = chain.advance(qkv_total[slab : 2 * slab], ffn_out)
    wait = scatter1.second(*wait)
    wait = chain.advance(qkv_total[2 * slab :], *wait)
    grad_normed1 = scatter1.finish(*wait)
    grad_hidden, ln1_gain_grad, ln1_bias_grad = normalize_back(
        grad_normed1, ln1_gain, normal1, inverse1
    )
    input_grad = grad_middle + grad_hidden
    wait = chain.advance(out_total, grad_normed1)
    along_x, along_y, own, diagonal = jnp.split(after(ffn_out, grad_normed1), 4)
    scatter_ffn = Scatter(own, along_x, along_y, diagonal)
    up_bias_own = jnp.sum(wide(grad_pres), axis=0).reshape(-1, 2, 256)
    up_bias_own = [up_bias_own[:, side].reshape(units_own) for side in range(2)]
    sums = jnp.sum(wide(back_own), axis=0) + jnp.sum(wide(back_other), axis=0)
    wait = chain.advance(None, *wait)
    wait = scatter_ffn.second(*wait)
    wait = chain.advance(None, *wait)
    ffn_out = scatter_ffn.finish(*wait)
    output = (middle + active * (ffn_out + down_bias)).astype(jnp.bfloat16)
    chain.advance(None)
    totals = chain.totals
    down_grad, up_grad, out_grad = wide(down_grad), wide(up_grad), wide(totals[3])
    qkv_grad = jnp.concatenate(
        [
            wide(lax.ppermute(totals[t], "wide", [(d, w) for w, d in routes[t]]))
            for t in range(3)
        ]
    )

    placed = lambda vector, size, device: lax.dynamic_update_slice_in_dim(
        jnp.zeros((size,), jnp.float32), vector, device * vector.shape[0], 0
    )
    smalls = tree_sum(
        jnp.concatenate(
            [
                placed(up_bias_own[0], up_bias.shape[0], rank)
                + placed(up_bias_own[1], up_bias.shape[0], other),
                down_bias_grad,
                out_bias_grad,
                ln2_gain_grad,
                ln2_bias_grad,
                placed(sums[:slab], model, rank),
                placed(sums[2 * slab :], model, rank),
                ln1_gain_grad,
                ln1_bias_grad,
            ]
        )
    )
    up_bias_grad = smalls[: up_bias.shape[0]]
    smalls = smalls[up_bias.shape[0] :].reshape(8, model)
    return (
        output,
        input_grad,
        smalls[6],
        smalls[7],
        qkv_grad,
        smalls[4],
        smalls[5],
        out_grad,
        smalls[1],
        smalls[2],
        smalls[3],
        up_grad,
        up_bias_grad,
        down_grad,
        smalls[0],
    )


def solution(mesh):
    chips = mesh.shape["wide"] == 8 and mesh.shape["batch"] == 4
    local = local_chips if chips else local_general
    rows = P(("batch", "wide"), None)
    weight = P("wide", None)
    return jax.shard_map(
        local,
        mesh=mesh,
        in_specs=(
            rows,
            rows,
            P("batch", None),
            P(),
            P(),
            weight,
            P(),
            P(),
            weight,
            P(),
            P(),
            P(),
            weight,
            P(),
            weight,
            P(),
        ),
        out_specs=(
            rows,
            rows,
            P(),
            P(),
            weight,
            P(),
            P(),
            weight,
            P(),
            P(),
            P(),
            weight,
            P(),
            weight,
            P(),
        ),
        check_vma=False,
    )
```

```python
import functools

import jax
import jax.numpy as jnp
import numpy as np
from jax import lax
from jax.experimental import pallas as pl
from jax.experimental.pallas import tpu as pltpu
from jax.sharding import PartitionSpec as P

HEADS = 32
LAYER = 12
LANES = 128
TILE = 512
CHUNKS = 2
LOG2E = 1.4426950408889634

epsilon = 1e-05
VMEM_BYTES = 48 * 2**20


def dot_nt(left, right):
    return lax.dot_general(
        left, right, (((1,), (1,)), ((), ())), preferred_element_type=jnp.float32
    )


def dot_nn(left, right):
    return lax.dot_general(
        left, right, (((1,), (0,)), ((), ())), preferred_element_type=jnp.float32
    )


def dot_tn(left, right):
    return lax.dot_general(
        left, right, (((0,), (0,)), ((), ())), preferred_element_type=jnp.float32
    )


def head_masks(head_size):
    lane = lax.broadcasted_iota(jnp.int32, (1, LANES), 1)
    return [
        (lane >= h * head_size) & (lane < (h + 1) * head_size)
        for h in range(LANES // head_size)
    ]


def fetch(sources, target, sems):
    size = target.shape[1]
    copies = []
    row = 0
    for source in sources:
        rows = source.shape[0]
        least = min(rows, size)
        for k in range(rows // least):
            place = target.at[row // size, pl.ds(row % size, least)]
            copies.append(
                pltpu.make_async_copy(source.at[pl.ds(k * least, least)], place, sems.at[len(copies)])
            )
            row += least

    @pl.when(pl.program_id(0) == 0)
    def _():
        for copy in copies:
            copy.start()
        for copy in copies:
            copy.wait()


def attend_kernel(head_size, blocks_in, counts, slots, *refs):
    sources = refs[:blocks_in]
    out_ref, log_ref, mixed_ref, key_own, value_own, sems = refs[blocks_in:]
    fetch(sources, mixed_ref, sems)
    length, lanes = out_ref.shape
    tile = mixed_ref.shape[1]
    pack = LANES // head_size
    scale = head_size ** (-0.5) * LOG2E
    sequence = pl.program_id(0)
    blocks = lax.div(counts[sequence] + (tile - 1), tile)
    masks = head_masks(head_size)
    out_ref[...] = jnp.zeros(out_ref.shape, out_ref.dtype)
    log_ref[...] = jnp.zeros(log_ref.shape, log_ref.dtype)
    row = lax.broadcasted_iota(jnp.int32, (tile, tile), 0)
    col = lax.broadcasted_iota(jnp.int32, (tile, tile), 1)
    for pair in range(lanes // LANES):
        base = pair * LANES
        for i in range(length // tile):
            slot = slots[sequence, i]
            keys = mixed_ref[slot, :, lanes + base : lanes + base + LANES]
            values = mixed_ref[slot, :, 2 * lanes + base : 2 * lanes + base + LANES]
            for h in range(pack):
                key_own[h, i * tile : (i + 1) * tile] = jnp.where(masks[h], keys, jnp.zeros_like(keys))
                value_own[h, i * tile : (i + 1) * tile] = jnp.where(
                    masks[h], values, jnp.zeros_like(values)
                )

        def query_block(i, _, pair=pair, base=base):
            start = pl.multiple_of(i * tile, tile)
            queries = mixed_ref[slots[sequence, i], :, base : base + LANES]

            def step(j, carry, diagonal=False):
                total, tops, sums = carry
                first = pl.multiple_of(j * tile, tile)
                new_tops, new_sums, shrinks, adds = [], [], [], []
                for h in range(pack):
                    scores = dot_nt(queries, key_own[h, pl.ds(first, tile)]) * scale
                    if diagonal:
                        scores = jnp.where(col <= row, scores, -1e30)
                    top = jnp.maximum(tops[h], jnp.max(scores, axis=1, keepdims=True))
                    terms = jnp.exp2(scores - top)
                    shrink = jnp.exp2(tops[h] - top)
                    new_tops.append(top)
                    new_sums.append(sums[h] * shrink + jnp.sum(terms, axis=1, keepdims=True))
                    shrinks.append(shrink)
                    adds.append(dot_nn(terms.astype(jnp.bfloat16), value_own[h, pl.ds(first, tile)]))
                shrink = shrinks[0]
                for h in range(1, pack):
                    shrink = jnp.where(masks[h], shrinks[h], shrink)
                total = total * shrink
                for add in adds:
                    total = total + add
                return total, tuple(new_tops), tuple(new_sums)

            carry = (
                jnp.zeros((tile, LANES), jnp.float32),
                tuple(jnp.full((tile, 1), -1e30, jnp.float32) for _ in range(pack)),
                tuple(jnp.zeros((tile, 1), jnp.float32) for _ in range(pack)),
            )
            carry = lax.fori_loop(0, i, step, carry)
            total, tops, sums = step(i, carry, diagonal=True)
            share = 1.0 / sums[0]
            for h in range(1, pack):
                share = jnp.where(masks[h], 1.0 / sums[h], share)
            out_ref[pl.ds(start, tile), base : base + LANES] = (total * share).astype(out_ref.dtype)
            for h in range(pack):
                logs = jnp.broadcast_to(tops[h] + jnp.log2(sums[h]), (tile, LANES))
                index = pair * pack + h
                log_ref[0, index : index + 1, pl.ds(start, tile)] = jnp.transpose(logs)[0:1]
            return 0

        lax.fori_loop(0, blocks, query_block, 0)


def attend(mixed, slots, counts, head_size):
    sequences = counts.shape[0]
    rows = sum(part.shape[0] for part in mixed)
    tile = rows // slots.size
    blocks = rows // tile
    lanes = mixed[0].shape[1] // 3
    length = rows // sequences
    heads = lanes // head_size
    pack = LANES // head_size
    return pl.pallas_call(
        functools.partial(attend_kernel, head_size, len(mixed)),
        grid_spec=pltpu.PrefetchScalarGridSpec(
            num_scalar_prefetch=2,
            grid=(sequences,),
            in_specs=[pl.BlockSpec(memory_space=pl.ANY)] * len(mixed),
            out_specs=[
                pl.BlockSpec((length, lanes), lambda s, *_: (s, 0)),
                pl.BlockSpec((1, heads, length), lambda s, *_: (s, 0, 0)),
            ],
            scratch_shapes=[
                pltpu.VMEM((blocks, tile, 3 * lanes), jnp.bfloat16),
                pltpu.VMEM((pack, length, LANES), jnp.bfloat16),
                pltpu.VMEM((pack, length, LANES), jnp.bfloat16),
                pltpu.SemaphoreType.DMA((blocks,)),
            ],
        ),
        out_shape=[
            jax.ShapeDtypeStruct((rows, lanes), jnp.bfloat16),
            jax.ShapeDtypeStruct((sequences, heads, length), jnp.float32),
        ],
        compiler_params=pltpu.CompilerParams(vmem_limit_bytes=VMEM_BYTES),
        cost_estimate=pl.CostEstimate(
            flops=rows * length * lanes * 4,
            bytes_accessed=rows * lanes * 8,
            transcendentals=rows * length * heads // 2,
        ),
    )(counts, slots, *mixed)


def attend_back_kernel(
    head_size,
    blocks_in,
    counts,
    slots,
    *refs,
):
    sources = refs[:blocks_in]
    grad_ref, out_ref, log_ref, own_ref, other_ref, mixed_ref = refs[blocks_in : blocks_in + 6]
    query_own, key_own, grad_own, delta, grad_query, grad_key, grad_value, back_ref, sems = refs[
        blocks_in + 6 :
    ]
    fetch(sources, mixed_ref, sems)
    length, lanes = out_ref.shape
    tile = mixed_ref.shape[1]
    pack = LANES // head_size
    scale = head_size ** (-0.5)
    sequence = pl.program_id(0)
    blocks = lax.div(counts[sequence] + (tile - 1), tile)
    masks = head_masks(head_size)
    for i in range(length // tile):
        back_ref[slots[sequence, i]] = jnp.zeros((tile, 3 * lanes), back_ref.dtype)
    key_row = lax.broadcasted_iota(jnp.int32, (tile, tile), 0)
    query_col = lax.broadcasted_iota(jnp.int32, (tile, tile), 1)
    for pair in range(lanes // LANES):
        base = pair * LANES
        for i in range(length // tile):
            span = slice(i * tile, (i + 1) * tile)
            slot = slots[sequence, i]
            queries = mixed_ref[slot, :, base : base + LANES]
            keys = mixed_ref[slot, :, lanes + base : lanes + base + LANES]
            grads = grad_ref[span, base : base + LANES]
            for h in range(pack):
                query_own[h, span] = jnp.where(masks[h], queries, jnp.zeros_like(queries))
                key_own[h, span] = jnp.where(masks[h], keys, jnp.zeros_like(keys))
                grad_own[h, span] = jnp.where(masks[h], grads, jnp.zeros_like(grads))
        grad_query[...] = jnp.zeros(grad_query.shape, jnp.float32)

        def deltas(i, _, base=base):
            start = pl.multiple_of(i * tile, tile)
            grads = grad_ref[pl.ds(start, tile), base : base + LANES].astype(jnp.float32)
            outs = out_ref[pl.ds(start, tile), base : base + LANES].astype(jnp.float32)
            products = jnp.transpose(grads * outs)
            for h in range(pack):
                delta[h : h + 1, pl.ds(start, tile)] = jnp.sum(
                    products[h * head_size : (h + 1) * head_size], axis=0, keepdims=True
                )
            return 0

        lax.fori_loop(0, blocks, deltas, 0)

        def key_block(j, _, pair=pair, base=base):
            first = pl.multiple_of(j * tile, tile)
            place = slots[sequence, j]
            keys = mixed_ref[place, :, lanes + base : lanes + base + LANES]
            values = mixed_ref[place, :, 2 * lanes + base : 2 * lanes + base + LANES]
            grad_key[...] = jnp.zeros(grad_key.shape, jnp.float32)
            grad_value[...] = jnp.zeros(grad_value.shape, jnp.float32)

            def step(i, diagonal=False):
                start = pl.multiple_of(i * tile, tile)
                add_query, add_key, add_value = [], [], []
                for h in range(pack):
                    index = pair * pack + h
                    query_head = query_own[h, pl.ds(start, tile)]
                    grad_head = grad_own[h, pl.ds(start, tile)]
                    scores = dot_nt(keys, query_head) * (scale * LOG2E)
                    probs = jnp.exp2(scores - log_ref[0, index : index + 1, pl.ds(start, tile)])
                    if diagonal:
                        probs = jnp.where(key_row <= query_col, probs, 0.0)
                    grad_probs = dot_nt(values, grad_head)
                    grad_scores = (
                        probs * (grad_probs - delta[h : h + 1, pl.ds(start, tile)])
                    ).astype(jnp.bfloat16)
                    add_value.append(dot_nn(probs.astype(jnp.bfloat16), grad_head))
                    add_key.append(dot_nn(grad_scores, query_head))
                    add_query.append(dot_tn(grad_scores, key_own[h, pl.ds(first, tile)]))
                grad_value[...] += functools.reduce(jnp.add, add_value)
                grad_key[...] += functools.reduce(jnp.add, add_key)
                grad_query[pl.ds(start, tile), :] += functools.reduce(jnp.add, add_query)

            def off_diagonal(i, _):
                step(i)
                return 0

            step(j, diagonal=True)
            lax.fori_loop(j + 1, blocks, off_diagonal, 0)
            back_ref[place, :, lanes + base : lanes + base + LANES] = (grad_key[...] * scale).astype(
                back_ref.dtype
            )
            back_ref[place, :, 2 * lanes + base : 2 * lanes + base + LANES] = grad_value[...].astype(
                back_ref.dtype
            )
            return 0

        lax.fori_loop(0, blocks, key_block, 0)
        for i in range(length // tile):
            back_ref[slots[sequence, i], :, base : base + LANES] = (
                grad_query[i * tile : (i + 1) * tile] * scale
            ).astype(back_ref.dtype)

    @pl.when(sequence == pl.num_programs(0) - 1)
    def _():
        half = back_ref.shape[0] // 2
        for k in range(half):
            own_ref[k * tile : (k + 1) * tile] = back_ref[k]
            other_ref[k * tile : (k + 1) * tile] = back_ref[half + k]


def attend_back(mixed, slots, grads, outs, logs, counts, head_size):
    sequences = counts.shape[0]
    rows, lanes = outs.shape
    length = rows // sequences
    heads = lanes // head_size
    pack = LANES // head_size
    tile = rows // slots.size
    blocks = rows // tile
    whole = pl.BlockSpec((rows // 2, 3 * lanes), lambda s, *_: (0, 0))
    return pl.pallas_call(
        functools.partial(attend_back_kernel, head_size, len(mixed)),
        grid_spec=pltpu.PrefetchScalarGridSpec(
            num_scalar_prefetch=2,
            grid=(sequences,),
            in_specs=[pl.BlockSpec(memory_space=pl.ANY)] * len(mixed)
            + [
                pl.BlockSpec((length, lanes), lambda s, *_: (s, 0)),
                pl.BlockSpec((length, lanes), lambda s, *_: (s, 0)),
                pl.BlockSpec((1, heads, length), lambda s, *_: (s, 0, 0)),
            ],
            out_specs=[whole, whole],
            scratch_shapes=[
                pltpu.VMEM((blocks, tile, 3 * lanes), jnp.bfloat16),
                pltpu.VMEM((pack, length, LANES), jnp.bfloat16),
                pltpu.VMEM((pack, length, LANES), jnp.bfloat16),
                pltpu.VMEM((pack, length, LANES), jnp.bfloat16),
                pltpu.VMEM((pack, length), jnp.float32),
                pltpu.VMEM((length, LANES), jnp.float32),
                pltpu.VMEM((tile, LANES), jnp.float32),
                pltpu.VMEM((tile, LANES), jnp.float32),
                pltpu.VMEM((blocks, tile, 3 * lanes), jnp.bfloat16),
                pltpu.SemaphoreType.DMA((blocks,)),
            ],
        ),
        out_shape=[jax.ShapeDtypeStruct((rows // 2, 3 * lanes), jnp.bfloat16)] * 2,
        compiler_params=pltpu.CompilerParams(vmem_limit_bytes=VMEM_BYTES),
        cost_estimate=pl.CostEstimate(
            flops=rows * length * lanes * 10,
            bytes_accessed=rows * lanes * 18,
            transcendentals=rows * length * heads // 2,
        ),
    )(counts, slots, *mixed, grads, outs, logs)


def ffn_kernel(block, x_parts, g_parts, counts, *refs):
    xs, refs = refs[:x_parts], refs[x_parts:]
    gs, refs = refs[:g_parts], refs[g_parts:]
    ups, downs, shifts = refs[0:2], refs[2:4], refs[4:6]
    units_ref, back_ref, out_ref, x, g, total, x_sems, g_sems = refs[-8:]
    fetch(xs, x, x_sems)
    fetch(gs, g, g_sems)
    blocks, size, model = x.shape
    width = ups[0].shape[0]
    step = pl.program_id(0)

    @pl.when(step == 0)
    def _():
        total[...] = jnp.zeros(total.shape, total.dtype)

    for k in range(blocks):
        rows = slice(k * size, (k + 1) * size)

        @pl.when(counts[block + k] != 0)
        def _(k=k, rows=rows):
            backs = []
            for side in range(2):
                span = slice(side * width, (side + 1) * width)
                pre = dot_nt(x[k], ups[side][...]) + shifts[side][...]
                grad_units = dot_nt(g[k], downs[side][...])
                bell = jnp.exp2(pre * pre * (-0.5 * LOG2E))
                denominator = 1.0 + (0.3275911 * 0.7071067811865476) * jnp.abs(pre)
                t = pl.reciprocal(denominator, approx=True)
                t = t * (2.0 - denominator * t)
                tail = 0.5 * 1.061405429
                for factor in (-1.453152027, 1.421413741, -0.284496736, 0.254829592):
                    tail = tail * t + 0.5 * factor
                tail = tail * t * bell
                below = jnp.where(pre < 0, tail, 1.0 - tail)
                units_ref[rows, span] = (pre * below).astype(units_ref.dtype)
                slope = below + pre * bell * 0.3989422804014327
                backs.append((grad_units * slope).astype(back_ref.dtype))
                back_ref[rows, span] = backs[-1]
            total[rows] += dot_nn(backs[0], ups[0][...]) + dot_nn(backs[1], ups[1][...])

        @pl.when(counts[block + k] == 0)
        def _(rows=rows):
            units_ref[rows] = jnp.zeros((size, 2 * width), units_ref.dtype)
            back_ref[rows] = jnp.zeros((size, 2 * width), back_ref.dtype)

    @pl.when(step == pl.num_programs(0) - 1)
    def _():
        out_ref[...] = total[...].astype(out_ref.dtype)


def ffn_blocks(place, block, counts, xs, gs, ups, downs, shifts, kept):
    size, width = 512, 256
    model = xs[0].shape[1]
    rows = sum(x.shape[0] for x in xs)
    units = ups[0].shape[0]
    whole = pl.BlockSpec(memory_space=pl.ANY)
    weights = pl.BlockSpec((width, model), lambda u, *_: (u, 0))
    shift = pl.BlockSpec((1, width), lambda u, *_: (0, u))
    output = pl.BlockSpec((rows, 2 * width), lambda u, *_: (place, u))
    full = jax.ShapeDtypeStruct((4 * size, 2 * units), jnp.bfloat16)
    return pl.pallas_call(
        functools.partial(ffn_kernel, block, len(xs), len(gs)),
        grid_spec=pltpu.PrefetchScalarGridSpec(
            num_scalar_prefetch=1,
            grid=(units // width,),
            in_specs=[whole] * (len(xs) + len(gs))
            + [weights] * 4
            + [shift] * 2
            + [whole] * len(kept),
            out_specs=[output, output, pl.BlockSpec((rows, model), lambda u, *_: (0, 0))],
            scratch_shapes=[
                pltpu.VMEM((rows // size, size, model), jnp.bfloat16),
                pltpu.VMEM((rows // size, size, model), jnp.bfloat16),
                pltpu.VMEM((rows, model), jnp.float32),
                pltpu.SemaphoreType.DMA((len(xs),)),
                pltpu.SemaphoreType.DMA((len(gs),)),
            ],
        ),
        out_shape=[full, full, jax.ShapeDtypeStruct((rows, model), jnp.bfloat16)],
        input_output_aliases={len(xs) + len(gs) + 7 + k: k for k in range(len(kept))},
        compiler_params=pltpu.CompilerParams(vmem_limit_bytes=VMEM_BYTES),
        cost_estimate=pl.CostEstimate(
            flops=12 * rows * units * model,
            bytes_accessed=8 * units * model + 8 * rows * model,
            transcendentals=4 * rows * units,
        ),
    )(counts, *xs, *gs, *ups, *downs, *shifts, *kept)


def products_kernel(width, active, left, own, other, out_ref):
    here = active[pl.program_id(0)] != 0

    @pl.when(here)
    def _():
        total = None
        for k in range(own.shape[0] // width):
            rows = slice(k * width, (k + 1) * width)
            for side, right in enumerate((own, other)):
                start = (2 * k + side) * width
                term = dot_nn(left[:, start : start + width], right[rows])
                total = term if total is None else total + term
        out_ref[...] = total.astype(out_ref.dtype)

    @pl.when(jnp.logical_not(here))
    def _():
        out_ref[...] = jnp.zeros(out_ref.shape, out_ref.dtype)


def products(counts, left, own, other):
    blocks = counts.shape[0]
    rows, depth = left.shape
    size = rows // blocks
    columns = own.shape[1]
    return pl.pallas_call(
        functools.partial(products_kernel, 256),
        grid_spec=pltpu.PrefetchScalarGridSpec(
            num_scalar_prefetch=1,
            grid=(blocks,),
            in_specs=[
                pl.BlockSpec((size, depth), lambda i, *_: (i, 0)),
                pl.BlockSpec(own.shape, lambda i, *_: (0, 0)),
                pl.BlockSpec(own.shape, lambda i, *_: (0, 0)),
            ],
            out_specs=pl.BlockSpec((size, columns), lambda i, *_: (i, 0)),
        ),
        out_shape=jax.ShapeDtypeStruct((rows, columns), jnp.bfloat16),
        compiler_params=pltpu.CompilerParams(vmem_limit_bytes=VMEM_BYTES),
        cost_estimate=pl.CostEstimate(
            flops=2 * rows * depth * columns,
            bytes_accessed=2 * (rows * (depth + columns) + depth * columns),
            transcendentals=0,
        ),
    )(counts, left, own, other)


def project_kernel(inputs, side, parts, *refs):
    xs = refs[:inputs]
    weights, shift, out_ref = refs[inputs:]
    slab = weights.shape[1]
    weight = weights[...].reshape(3 * slab, weights.shape[2])
    for k in range(inputs):

        @pl.when(pl.program_id(0) == k)
        def _(k=k):
            mixed = dot_nt(xs[k][...], weight)
            for t in range(3):
                columns = pl.ds(pl.multiple_of(parts[side, t] * slab, slab), slab)
                out_ref[:, columns] = (
                    mixed[:, t * slab : (t + 1) * slab] + shift[:, columns]
                ).astype(out_ref.dtype)


def project(parts, side, xs, weights, shift):
    size, model = xs[0].shape
    slab = weights.shape[1]
    return pl.pallas_call(
        functools.partial(project_kernel, len(xs), side),
        grid_spec=pltpu.PrefetchScalarGridSpec(
            num_scalar_prefetch=1,
            grid=(len(xs),),
            in_specs=[pl.BlockSpec((size, model), lambda i, *_: (0, 0))] * len(xs)
            + [
                pl.BlockSpec(weights.shape, lambda i, *_: (0, 0, 0)),
                pl.BlockSpec(shift.shape, lambda i, *_: (0, 0)),
            ],
            out_specs=pl.BlockSpec((size, 3 * slab), lambda i, *_: (i, 0)),
        ),
        out_shape=jax.ShapeDtypeStruct((len(xs) * size, 3 * slab), jnp.bfloat16),
        compiler_params=pltpu.CompilerParams(vmem_limit_bytes=VMEM_BYTES),
        cost_estimate=pl.CostEstimate(
            flops=6 * len(xs) * size * slab * model,
            bytes_accessed=6 * slab * model + 2 * len(xs) * size * (model + 3 * slab),
            transcendentals=0,
        ),
    )(parts, *xs, weights, shift)


def unproject_kernel(parts, active, mine, theirs, own, other, out_ref):
    slab = own.shape[1]
    here = active[pl.program_id(0)] != 0

    @pl.when(here)
    def _():
        total = None
        for side, (left, right) in enumerate(((mine, own), (theirs, other))):
            for t in range(3):
                columns = pl.ds(pl.multiple_of(parts[side, t] * slab, slab), slab)
                term = dot_nn(left[:, columns], right[t])
                total = term if total is None else total + term
        out_ref[...] = total.astype(out_ref.dtype)

    @pl.when(jnp.logical_not(here))
    def _():
        out_ref[...] = jnp.zeros(out_ref.shape, out_ref.dtype)


def unproject(parts, counts, mine, theirs, own, other):
    blocks = counts.shape[0]
    size = mine.shape[0] // blocks
    slab, model = own.shape[1:]
    left = pl.BlockSpec((size, 3 * slab), lambda i, *_: (i, 0))
    fixed = pl.BlockSpec(own.shape, lambda i, *_: (0, 0, 0))
    return pl.pallas_call(
        unproject_kernel,
        grid_spec=pltpu.PrefetchScalarGridSpec(
            num_scalar_prefetch=2,
            grid=(blocks,),
            in_specs=[left, left, fixed, fixed],
            out_specs=pl.BlockSpec((size, model), lambda i, *_: (i, 0)),
        ),
        out_shape=jax.ShapeDtypeStruct((blocks * size, model), jnp.bfloat16),
        compiler_params=pltpu.CompilerParams(vmem_limit_bytes=VMEM_BYTES),
        cost_estimate=pl.CostEstimate(
            flops=12 * blocks * size * slab * model,
            bytes_accessed=12 * slab * model + 2 * blocks * size * (model + 6 * slab),
            transcendentals=0,
        ),
    )(parts, counts, mine, theirs, own, other)


def weight_grad_kernel(inputs, added, columns, *refs):
    left, rights = refs[0], refs[1 : 1 + inputs]
    tokens, sems = refs[-2:]
    outs = refs[1 + inputs + added : -2]
    fetch(rights, tokens, sems)
    total = dot_tn(left[...], tokens[0])
    if added:
        total = total + refs[1 + inputs][...].astype(jnp.float32)
    size = outs[0].shape[0]
    for k, out_ref in enumerate(outs):
        out_ref[...] = total[k * size : (k + 1) * size].astype(out_ref.dtype)


def weight_grad(left, columns, tile, rights, extra=None, outputs=1):
    rows = left.shape[0]
    model = rights[0].shape[1]
    steps = columns.shape[0]
    output = pl.BlockSpec((tile // outputs, model), lambda i, *_: (i, 0))
    extras = [] if extra is None else [extra]
    shape = jax.ShapeDtypeStruct((steps * tile // outputs, model), jnp.bfloat16)
    results = pl.pallas_call(
        functools.partial(weight_grad_kernel, len(rights), len(extras)),
        grid_spec=pltpu.PrefetchScalarGridSpec(
            num_scalar_prefetch=1,
            grid=(steps,),
            in_specs=[pl.BlockSpec((rows, tile), lambda i, columns: (0, columns[i]))]
            + [pl.BlockSpec(memory_space=pl.ANY)] * len(rights)
            + [output] * len(extras),
            out_specs=[output] * outputs,
            scratch_shapes=[
                pltpu.VMEM((1, rows, model), jnp.bfloat16),
                pltpu.SemaphoreType.DMA((len(rights),)),
            ],
        ),
        out_shape=[shape] * outputs,
        compiler_params=pltpu.CompilerParams(vmem_limit_bytes=VMEM_BYTES),
        cost_estimate=pl.CostEstimate(
            flops=2 * steps * tile * rows * model,
            bytes_accessed=2 * (rows * model + steps * tile * (rows + 2 * model)),
            transcendentals=0,
        ),
    )(columns, left, *rights, *extras)
    return results[0] if outputs == 1 else results


def chain_sum(values, axis):
    size = lax.axis_size(axis)
    if size != 4:
        return lax.psum(values.astype(jnp.bfloat16), axis).astype(jnp.float32)
    place = lax.axis_index(axis)
    outer = lax.ppermute(values.astype(jnp.bfloat16), axis, [(0, 1), (3, 2)])
    half = (values + outer.astype(jnp.float32)).astype(jnp.bfloat16)
    other = lax.ppermute(half, axis, [(1, 2), (2, 1)])
    whole = (half.astype(jnp.float32) + other.astype(jnp.float32)).astype(jnp.bfloat16)
    ends = lax.ppermute(whole, axis, [(1, 0), (2, 3)])
    inner = (place == 1) | (place == 2)
    return jnp.where(inner, whole, ends).astype(jnp.float32)


class Chain:
    def __init__(self):
        place = lax.axis_index("batch")
        self.inner = (place == 1) | (place == 2)
        self.blocks = (None, None, None)
        self.moved = (None, None, None)
        self.totals = []

    def advance(self, block, *done):
        wide = lambda values: values.astype(jnp.float32)
        first, second, third = self.blocks
        inward, across, outward = after(self.moved, *done)
        half = whole = None
        if first is not None:
            half = (wide(first) + wide(inward)).astype(jnp.bfloat16)
        if second is not None:
            whole = (wide(second) + wide(across)).astype(jnp.bfloat16)
        if third is not None:
            self.totals.append(jnp.where(self.inner, third, outward))
        self.blocks = (block, half, whole)
        pairs = ([(0, 1), (3, 2)], [(1, 2), (2, 1)], [(1, 0), (2, 3)])
        self.moved = tuple(
            None if value is None else lax.ppermute(value, "batch", route)
            for value, route in zip(self.blocks, pairs)
        )
        return [value for value in self.blocks if value is not None]


def normalize(values):
    center = values - jnp.mean(values, axis=-1, keepdims=True)
    inverse = lax.rsqrt(jnp.mean(center * center, axis=-1, keepdims=True) + epsilon)
    return center * inverse, inverse


def normalize_back(grad, gain, normal, inverse):
    scaled = grad * gain
    grad_values = inverse * (
        scaled
        - jnp.mean(scaled, axis=-1, keepdims=True)
        - normal * jnp.mean(scaled * normal, axis=-1, keepdims=True)
    )
    return grad_values, jnp.sum(grad * normal, axis=0), jnp.sum(grad, axis=0)


def local_general(
    hidden,
    cotangent,
    exit_layer,
    ln1_gain,
    ln1_bias,
    qkv_weight,
    query_bias,
    value_bias,
    out_weight,
    out_bias,
    ln2_gain,
    ln2_bias,
    up_weight,
    up_bias,
    down_weight,
    down_bias,
):
    width = lax.axis_size("wide")
    rank = lax.axis_index("wide")
    rows, model = hidden.shape
    group = rows * width
    slab = model // width
    head_size = model // HEADS
    units_own = up_weight.shape[0]
    keep = exit_layer >= LAYER
    counts = jnp.sum(keep.astype(jnp.int32), axis=1)
    active = lax.dynamic_slice_in_dim(keep.reshape(group), rank * rows, rows, 0)
    active = active.astype(jnp.float32)[:, None]
    grad_out = cotangent.astype(jnp.float32)

    routes = [[(w, (3 * w + t) % width) for w in range(width)] for t in range(3)]
    part_at = np.zeros((width, 3), np.int32)
    for t in range(3):
        for w, d in routes[t]:
            part_at[d, t] = (3 * w + t) // width
    place_of = jnp.asarray(np.argsort(part_at, axis=1).astype(np.int32))[rank]
    part_of = jnp.asarray(part_at)[rank]

    hidden_wide = hidden.astype(jnp.float32)
    normal1, inverse1 = normalize(hidden_wide)
    normed1 = lax.all_gather(
        (normal1 * ln1_gain + ln1_bias).astype(jnp.bfloat16), "wide", axis=0, tiled=True
    )
    slabs = qkv_weight.reshape(3, slab, model)
    received = jnp.stack([lax.ppermute(slabs[t], "wide", routes[t]) for t in range(3)])
    qkv_own = jnp.concatenate(
        [lax.dynamic_index_in_dim(received, place_of[p], 0, keepdims=False) for p in range(3)]
    )
    own = lambda vector: lax.dynamic_slice_in_dim(vector, rank * slab, slab, 0)
    qkv_shift = jnp.concatenate(
        [own(query_bias), jnp.zeros((slab,), jnp.float32), own(value_bias)]
    )

    grad_ffn = (active * grad_out).astype(jnp.bfloat16)
    down_bias_grad = jnp.sum(grad_ffn.astype(jnp.float32), axis=0)
    piece = rows // CHUNKS
    part = lambda values, c: values[c * piece : (c + 1) * piece]
    gather = lambda values: lax.all_gather(values, "wide", axis=0, tiled=True)
    scatter = lambda values: lax.psum_scatter(
        values.astype(jnp.bfloat16), "wide", scatter_dimension=0, tiled=True
    )
    grad_ffns = [gather(part(grad_ffn, c)) for c in range(CHUNKS)]
    out_whole = gather(out_weight)

    mixed = (dot_nt(normed1, qkv_own) + qkv_shift).astype(jnp.bfloat16)
    mixed = jnp.split(mixed, group // TILE)
    slots = jnp.arange(group // TILE, dtype=jnp.int32).reshape(counts.shape[0], -1)
    attended, logs = attend(mixed, slots, counts, head_size)
    attended_rows = lax.all_to_all(attended, "wide", split_axis=0, concat_axis=1, tiled=True)
    middle = hidden_wide + active * (dot_nn(attended_rows, out_whole) + out_bias)
    normal2, inverse2 = normalize(middle)
    normed2 = (normal2 * ln2_gain + ln2_bias).astype(jnp.bfloat16)
    up_shift = lax.dynamic_slice_in_dim(up_bias, rank * units_own, units_own, 0)

    normed2s = [gather(part(normed2, c)) for c in range(CHUNKS)]
    units, grad_pres, grad_normed2, ffn_out = [], [], [], []
    for c in range(CHUNKS):
        grad_units = dot_nt(grad_ffns[c], down_weight)
        pre = dot_nt(normed2s[c], up_weight) + up_shift
        below = 0.5 + 0.5 * lax.erf(pre * 0.7071067811865476)
        bell = jnp.exp(-0.5 * pre * pre) * 0.3989422804014327
        units.append((pre * below).astype(jnp.bfloat16))
        grad_pres.append((grad_units * (below + pre * bell)).astype(jnp.bfloat16))
        grad_normed2.append(scatter(dot_nn(grad_pres[c], up_weight)))
    for c in range(CHUNKS):
        ffn_out.append(scatter(dot_nn(units[c], down_weight)))
    grad_normed2 = jnp.concatenate(grad_normed2).astype(jnp.float32)
    ffn_out = jnp.concatenate(ffn_out).astype(jnp.float32)
    output = (middle + active * (ffn_out + down_bias)).astype(jnp.bfloat16)

    up_bias_own = sum(jnp.sum(g.astype(jnp.float32), axis=0) for g in grad_pres)
    down_grad = sum(dot_tn(units[c], grad_ffns[c]) for c in range(CHUNKS))
    up_grad = sum(dot_tn(grad_pres[c], normed2s[c]) for c in range(CHUNKS))
    halves = lambda values: jnp.concatenate(
        [chain_sum(half, "batch") for half in jnp.split(values, 2)]
    )
    down_grad = halves(down_grad)
    up_grad = halves(up_grad)

    grad_middle, ln2_gain_grad, ln2_bias_grad = normalize_back(
        grad_normed2, ln2_gain, normal2, inverse2
    )
    grad_middle = grad_out + grad_middle
    grad_branch = (active * grad_middle).astype(jnp.bfloat16)
    out_bias_grad = jnp.sum(grad_branch.astype(jnp.float32), axis=0)
    grad_attended = dot_nt(grad_branch, out_whole).astype(jnp.bfloat16)
    grad_heads = lax.all_to_all(grad_attended, "wide", split_axis=1, concat_axis=0, tiled=True)
    out_grad = chain_sum(scatter(dot_tn(attended_rows, grad_branch)).astype(jnp.float32), "batch")

    placed = lambda vector, size: lax.dynamic_update_slice_in_dim(
        jnp.zeros((size,), jnp.float32), vector, rank * vector.shape[0], 0
    )
    early = lax.psum(
        (
            out_bias_grad,
            ln2_gain_grad,
            ln2_bias_grad,
            placed(up_bias_own, up_bias.shape[0]),
            down_bias_grad,
        ),
        ("batch", "wide"),
    )

    grad_mixed = jnp.concatenate(
        attend_back(mixed, slots, grad_heads, attended, logs, counts, head_size)
    )
    grad_normed1 = scatter(dot_nn(grad_mixed, qkv_own)).astype(jnp.float32)
    sums = jnp.sum(grad_mixed.astype(jnp.float32), axis=0)
    qkv_parts = []
    for t in range(3):
        columns = lax.dynamic_slice_in_dim(grad_mixed, part_of[t] * slab, slab, 1)
        total = chain_sum(dot_tn(columns, normed1), "batch").astype(jnp.bfloat16)
        back = [(d, w) for w, d in routes[t]]
        qkv_parts.append(lax.ppermute(total, "wide", back).astype(jnp.float32))
    qkv_grad = jnp.concatenate(qkv_parts)

    grad_hidden, ln1_gain_grad, ln1_bias_grad = normalize_back(
        grad_normed1, ln1_gain, normal1, inverse1
    )
    input_grad = grad_middle + grad_hidden
    late = lax.psum(
        (
            ln1_gain_grad,
            ln1_bias_grad,
            placed(sums[:slab], model),
            placed(sums[2 * slab :], model),
        ),
        ("batch", "wide"),
    )
    return (
        output,
        input_grad,
        late[0],
        late[1],
        qkv_grad,
        late[2],
        late[3],
        out_grad,
        early[0],
        early[1],
        early[2],
        up_grad,
        early[3],
        down_grad,
        early[4],
    )


def swap(values, bits):
    width = lax.axis_size("wide")
    return lax.ppermute(values, "wide", [(w, w ^ bits) for w in range(width)])


def after(values, *done):
    return lax.optimization_barrier((values, done))[0]


def relay(along_x, along_y):
    half = along_x.shape[0] // 2
    return [swap(along_y[:half], 2), swap(along_x[half:], 4)]


class Scatter:
    def __init__(self, own, along_x, along_y, diagonal):
        self.half = half = own.shape[0] // 2
        self.own, self.along_x, self.along_y = own, along_x, along_y
        self.from_x = swap(jnp.concatenate([diagonal[:half], along_x[:half]]), 2)
        self.from_y = swap(jnp.concatenate([diagonal[half:], along_y[half:]]), 4)

    def second(self, *done):
        half = self.half
        from_x, from_y = after((self.from_x, self.from_y), *done)
        self.near = (from_x[half:], from_y[half:])
        return self.forward(from_x[:half], from_y[:half])

    def forward(self, top, bottom):
        wide = lambda values: values.astype(jnp.float32)
        half = self.half
        y_top = (wide(self.along_y[:half]) + wide(top)).astype(jnp.bfloat16)
        x_bottom = (wide(self.along_x[half:]) + wide(bottom)).astype(jnp.bfloat16)
        self.last = (swap(y_top, 4), swap(x_bottom, 2))
        return y_top, x_bottom

    def finish(self, *done):
        wide = lambda values: values.astype(jnp.float32)
        y_top, x_bottom = after(self.last, *done)
        x_top, y_bottom = self.near
        return jnp.concatenate(
            [
                wide(self.own[: self.half]) + wide(x_top) + wide(y_top),
                wide(self.own[self.half :]) + wide(x_bottom) + wide(y_bottom),
            ]
        )


class EarlyScatter(Scatter):
    def __init__(self, own, along_x, along_y):
        self.half = half = own.shape[0] // 2
        self.own, self.along_x, self.along_y = own, along_x, along_y
        self.near = (swap(along_x[:half], 2), swap(along_y[half:], 4))

    def first(self, diagonal):
        self.from_far = (swap(diagonal[: self.half], 2), swap(diagonal[self.half :], 4))
        self.near = after(self.near, diagonal)
        return self.near

    def second(self, *done):
        return self.forward(*after(self.from_far, *done))


def tree_sum(values):
    total = values + swap(values, 1)
    total = (total + swap(total, 2)) + (swap(total, 4) + swap(total, 6))
    size = lax.axis_size("batch")
    terms = [total] + [
        lax.ppermute(total, "batch", [(z, z ^ bits) for z in range(size)])
        for bits in range(1, size)
    ]
    while len(terms) > 1:
        terms = [terms[k] + terms[k + 1] for k in range(0, len(terms), 2)]
    return terms[0]


def local_chips(
    hidden,
    cotangent,
    exit_layer,
    ln1_gain,
    ln1_bias,
    qkv_weight,
    query_bias,
    value_bias,
    out_weight,
    out_bias,
    ln2_gain,
    ln2_bias,
    up_weight,
    up_bias,
    down_weight,
    down_bias,
):
    width = lax.axis_size("wide")
    rank = lax.axis_index("wide")
    rows, model = hidden.shape
    group = rows * width
    slab = model // width
    head_size = model // HEADS
    units_own = up_weight.shape[0]
    keep = exit_layer >= LAYER
    counts = jnp.sum(keep.astype(jnp.int32), axis=1)
    active = lax.dynamic_slice_in_dim(keep.reshape(group), rank * rows, rows, 0)
    active = active.astype(jnp.float32)[:, None]
    grad_out = cotangent.astype(jnp.float32)

    tiles = jnp.arange(group // rows, dtype=jnp.int32)
    slots = ((tiles ^ rank) & 1) * 4 + ((tiles >> 1) ^ (rank >> 1))
    slots = slots.reshape(counts.shape[0], -1)

    routes = [[(w, (3 * w + t) % width) for w in range(width)] for t in range(3)]
    part_at = np.zeros((width, 3), np.int32)
    for t in range(3):
        for w, d in routes[t]:
            part_at[d, t] = (3 * w + t) // width
    part_at = jnp.asarray(part_at)
    other = rank ^ 1
    parts = jnp.stack([part_at[rank], part_at[other]])

    hidden_wide = hidden.astype(jnp.float32)
    normal1, inverse1 = normalize(hidden_wide)
    slabs = qkv_weight.reshape(3, slab, model)
    slabs = [lax.ppermute(slabs[t], "wide", routes[t]) for t in range(3)]
    normed1 = (normal1 * ln1_gain + ln1_bias).astype(jnp.bfloat16)
    normed1 = [normed1, swap(normed1, 2), swap(normed1, 4)]
    diagonal1 = relay(normed1[1], normed1[2])
    qkv_own = jnp.stack(after(slabs, normed1[1:]))
    qkv_other = swap(qkv_own, 1)

    def shift_of(device):
        own = lambda vector: lax.dynamic_slice_in_dim(vector, device * slab, slab, 0)
        shift = [own(query_bias), jnp.zeros((slab,), jnp.float32), own(value_bias)]
        return jnp.concatenate(shift)[None]

    bias_of = lambda device: lax.dynamic_slice_in_dim(up_bias, device * units_own, units_own, 0)
    up_shifts = [bias_of(rank)[None], bias_of(other)[None]]

    mixed_near = project(parts, 0, normed1, qkv_own, shift_of(rank))
    qkv_other = after(qkv_other, mixed_near)
    lent_near = project(parts, 1, normed1, qkv_other, shift_of(other))
    diagonal1 = after(diagonal1, lent_near)
    lent_far = project(parts, 1, diagonal1, qkv_other, shift_of(other))
    mixed_far = project(parts, 0, after(diagonal1, lent_far), qkv_own, shift_of(rank))
    mixed = [mixed_near, mixed_far, swap(lent_near, 1), swap(lent_far, 1)]

    out_whole = lax.all_gather(after(out_weight, diagonal1), "wide", axis=0, tiled=True)
    grad_ffn = (after(active, diagonal1) * grad_out).astype(jnp.bfloat16)
    down_bias_grad = jnp.sum(grad_ffn.astype(jnp.float32), axis=0)
    grad_ffn = [grad_ffn, swap(grad_ffn, 2), swap(grad_ffn, 4)]

    attended, logs = attend(mixed, slots, counts, head_size)
    attended_rows = lax.all_to_all(attended, "wide", split_axis=0, concat_axis=1, tiled=True)
    attended_rows = after(attended_rows, grad_ffn[1:])
    up_other, down_other = swap(after((up_weight, down_weight), attended), 1)
    middle = hidden_wide + active * (dot_nn(attended_rows, out_whole) + out_bias)
    normal2, inverse2 = normalize(middle)
    normed2 = (normal2 * ln2_gain + ln2_bias).astype(jnp.bfloat16)
    normed2 = [normed2, swap(normed2, 2), swap(normed2, 4)]

    per_tile = jnp.sum(keep.reshape(group // rows, rows).astype(jnp.int32), axis=1)
    block_chip = (rank >> 1) ^ jnp.arange(4, dtype=jnp.int32)
    block_counts = per_tile[2 * block_chip + (rank & 1)]
    ups, downs = [up_weight, up_other], [down_weight, down_other]

    def ffn(place, block, xs, gs, kept):
        *kept, partial = ffn_blocks(
            place, block, block_counts, xs, gs, ups, downs, up_shifts, tuple(kept)
        )
        return kept, partial

    kept, partial_own = ffn(2, 0, normed2[:1], grad_ffn[:1], ())
    normed2[1:] = after(normed2[1:], partial_own)
    diagonal2 = relay(normed2[1], normed2[2])
    diagonal_ffn = relay(*after(grad_ffn[1:], attended_rows))
    kept, partial_near = ffn(0, 1, normed2[1:], grad_ffn[1:], kept)
    scatter2 = EarlyScatter(partial_own, partial_near[:rows], partial_near[rows:])
    diagonal2 = after(diagonal2, partial_near)
    (units, grad_pres), partial_far = ffn(3, 3, diagonal2, diagonal_ffn, kept)
    wait = scatter2.first(partial_far)
    tokens2 = [*normed2[1:], normed2[0], *diagonal2]
    tokens_ffn = [*grad_ffn[1:], grad_ffn[0], *diagonal_ffn]

    wide = lambda values: values.astype(jnp.float32)
    lowered = lambda values: values.astype(jnp.bfloat16)
    tile = 512
    tiles = jnp.arange(2 * units_own // tile, dtype=jnp.int32)
    half = tiles.shape[0] // 2
    chain = Chain()
    down_own, down_lent = weight_grad(after(units, wait), tiles, tile, tokens_ffn, outputs=2)
    wait = scatter2.second(down_lent)
    down_lent = swap(down_lent, 1)
    grad_pres = after(grad_pres, wait)
    up_own, up_lent = weight_grad(grad_pres, tiles[:half], tile, tokens2, outputs=2)
    down_sum = lowered(wide(down_own) + wide(after(down_lent, up_own)))
    wait = chain.advance(down_sum[:tile], down_sum)
    grad_pres = after(grad_pres, wait)
    up_more, lent_more = weight_grad(grad_pres, tiles[half:], tile, tokens2, outputs=2)
    up_own, up_lent = [up_own, up_more], [swap(up_lent, 1), swap(lent_more, 1)]
    grad_normed2 = scatter2.finish(up_more)

    grad_middle, ln2_gain_grad, ln2_bias_grad = normalize_back(
        grad_normed2, ln2_gain, normal2, inverse2
    )
    grad_middle = grad_out + grad_middle
    grad_branch = (active * grad_middle).astype(jnp.bfloat16)
    out_bias_grad = jnp.sum(grad_branch.astype(jnp.float32), axis=0)
    grad_attended = dot_nt(grad_branch, out_whole).astype(jnp.bfloat16)
    grad_heads = lax.all_to_all(grad_attended, "wide", split_axis=1, concat_axis=0, tiled=True)
    wait = chain.advance(down_sum[tile:], grad_attended)

    owners = 2 * block_chip + (rank & 1)
    grad_branch = after(grad_branch, wait)
    out_lent = weight_grad(attended_rows, owners ^ 1, slab, [grad_branch])
    up_sum = [
        lowered(wide(mine) + wide(lent)) for mine, lent in zip(up_own, after(up_lent, out_lent))
    ]
    out_lent = swap(out_lent, 1)
    out_own = weight_grad(after(attended_rows, up_sum), owners, slab, [grad_branch], out_lent)
    scatter_out = Scatter(*jnp.split(out_own, 4))
    wait = chain.advance(up_sum[0], out_own)

    back_own, back_other = attend_back(
        mixed, slots, after(grad_heads, wait), attended, logs, counts, head_size
    )
    theirs = swap(back_other, 1)
    wait = chain.advance(up_sum[1], back_own)
    tokens1 = [*normed1, *diagonal1]
    qkv_own_grad = weight_grad(after(back_own, wait), parts[0], slab, tokens1)
    wait = scatter_out.second(qkv_own_grad)
    theirs = after(theirs, wait)
    qkv_lent = weight_grad(theirs, parts[1], slab, tokens1)
    grad_normed1 = unproject(
        parts, block_counts, after(back_own, qkv_lent), theirs, qkv_own, qkv_other
    )
    qkv_lent = swap(qkv_lent, 1)
    scatter1 = Scatter(*jnp.split(grad_normed1, 4))
    qkv_total = lowered(wide(qkv_own_grad) + wide(after(qkv_lent, grad_normed1)))
    wait = chain.advance(qkv_total[:slab], qkv_total)
    ffn_counts = block_counts[jnp.array([1, 2, 0, 3])]
    ffn_out = products(ffn_counts, after(units, *wait), *downs)
    wait = chain.advance(qkv_total[slab : 2 * slab], ffn_out)
    wait = scatter1.second(*wait)
    wait = chain.advance(qkv_total[2 * slab :], *wait)
    grad_normed1 = scatter1.finish(*wait)
    grad_hidden, ln1_gain_grad, ln1_bias_grad = normalize_back(
        grad_normed1, ln1_gain, normal1, inverse1
    )
    input_grad = grad_middle + grad_hidden
    out_total = lowered(scatter_out.finish(*wait))
    wait = chain.advance(out_total, grad_normed1)
    along_x, along_y, own, diagonal = jnp.split(after(ffn_out, grad_normed1), 4)
    scatter_ffn = Scatter(own, along_x, along_y, diagonal)
    up_bias_own = jnp.sum(wide(grad_pres), axis=0).reshape(-1, 2, 256)
    up_bias_own = [up_bias_own[:, side].reshape(units_own) for side in range(2)]
    sums = jnp.sum(wide(back_own), axis=0) + jnp.sum(wide(back_other), axis=0)
    wait = chain.advance(None, *wait)
    wait = scatter_ffn.second(*wait)
    wait = chain.advance(None, *wait)
    ffn_out = scatter_ffn.finish(*wait)
    output = (middle + active * (ffn_out + down_bias)).astype(jnp.bfloat16)
    chain.advance(None)
    totals = chain.totals
    down_grad = wide(jnp.concatenate(totals[0:2]))
    up_grad = wide(jnp.concatenate(totals[2:4]))
    qkv_grad = jnp.concatenate(
        [
            wide(lax.ppermute(totals[4 + t], "wide", [(d, w) for w, d in routes[t]]))
            for t in range(3)
        ]
    )
    out_grad = wide(totals[7])

    placed = lambda vector, size, device: lax.dynamic_update_slice_in_dim(
        jnp.zeros((size,), jnp.float32), vector, device * vector.shape[0], 0
    )
    smalls = tree_sum(
        jnp.concatenate(
            [
                placed(up_bias_own[0], up_bias.shape[0], rank)
                + placed(up_bias_own[1], up_bias.shape[0], other),
                down_bias_grad,
                out_bias_grad,
                ln2_gain_grad,
                ln2_bias_grad,
                placed(sums[:slab], model, rank),
                placed(sums[2 * slab :], model, rank),
                ln1_gain_grad,
                ln1_bias_grad,
            ]
        )
    )
    up_bias_grad = smalls[: up_bias.shape[0]]
    smalls = smalls[up_bias.shape[0] :].reshape(8, model)
    return (
        output,
        input_grad,
        smalls[6],
        smalls[7],
        qkv_grad,
        smalls[4],
        smalls[5],
        out_grad,
        smalls[1],
        smalls[2],
        smalls[3],
        up_grad,
        up_bias_grad,
        down_grad,
        smalls[0],
    )


def solution(mesh):
    chips = mesh.shape["wide"] == 8 and mesh.shape["batch"] == 4
    local = local_chips if chips else local_general
    rows = P(("batch", "wide"), None)
    weight = P("wide", None)
    return jax.shard_map(
        local,
        mesh=mesh,
        in_specs=(
            rows,
            rows,
            P("batch", None),
            P(),
            P(),
            weight,
            P(),
            P(),
            weight,
            P(),
            P(),
            P(),
            weight,
            P(),
            weight,
            P(),
        ),
        out_specs=(
            rows,
            rows,
            P(),
            P(),
            weight,
            P(),
            P(),
            weight,
            P(),
            P(),
            P(),
            weight,
            P(),
            weight,
            P(),
        ),
        check_vma=False,
    )
```

```python
import functools

import jax
import jax.numpy as jnp
import numpy as np
from jax import lax
from jax.experimental import pallas as pl
from jax.experimental.pallas import tpu as pltpu
from jax.sharding import PartitionSpec as P

HEADS = 32
LAYER = 12
LANES = 128
TILE = 512
CHUNKS = 2
LOG2E = 1.4426950408889634

epsilon = 1e-05
VMEM_BYTES = 48 * 2**20


def dot_nt(left, right):
    return lax.dot_general(
        left, right, (((1,), (1,)), ((), ())), preferred_element_type=jnp.float32
    )


def dot_nn(left, right):
    return lax.dot_general(
        left, right, (((1,), (0,)), ((), ())), preferred_element_type=jnp.float32
    )


def dot_tn(left, right):
    return lax.dot_general(
        left, right, (((0,), (0,)), ((), ())), preferred_element_type=jnp.float32
    )


def head_masks(head_size):
    lane = lax.broadcasted_iota(jnp.int32, (1, LANES), 1)
    return [
        (lane >= h * head_size) & (lane < (h + 1) * head_size)
        for h in range(LANES // head_size)
    ]


def fetch(sources, target, sems):
    size = target.shape[1]
    copies = []
    row = 0
    for source in sources:
        rows = source.shape[0]
        least = min(rows, size)
        for k in range(rows // least):
            place = target.at[row // size, pl.ds(row % size, least)]
            copies.append(
                pltpu.make_async_copy(source.at[pl.ds(k * least, least)], place, sems.at[len(copies)])
            )
            row += least

    @pl.when(pl.program_id(0) == 0)
    def _():
        for copy in copies:
            copy.start()
        for copy in copies:
            copy.wait()


def attend_kernel(head_size, blocks_in, counts, slots, *refs):
    sources = refs[:blocks_in]
    out_ref, log_ref, mixed_ref, key_own, value_own, sems = refs[blocks_in:]
    fetch(sources, mixed_ref, sems)
    length, lanes = out_ref.shape
    tile = mixed_ref.shape[1]
    pack = LANES // head_size
    scale = head_size ** (-0.5) * LOG2E
    sequence = pl.program_id(0)
    blocks = lax.div(counts[sequence] + (tile - 1), tile)
    masks = head_masks(head_size)
    out_ref[...] = jnp.zeros(out_ref.shape, out_ref.dtype)
    log_ref[...] = jnp.zeros(log_ref.shape, log_ref.dtype)
    row = lax.broadcasted_iota(jnp.int32, (tile, tile), 0)
    col = lax.broadcasted_iota(jnp.int32, (tile, tile), 1)
    for pair in range(lanes // LANES):
        base = pair * LANES
        for i in range(length // tile):
            slot = slots[sequence, i]
            keys = mixed_ref[slot, :, lanes + base : lanes + base + LANES]
            values = mixed_ref[slot, :, 2 * lanes + base : 2 * lanes + base + LANES]
            for h in range(pack):
                key_own[h, i * tile : (i + 1) * tile] = jnp.where(masks[h], keys, jnp.zeros_like(keys))
                value_own[h, i * tile : (i + 1) * tile] = jnp.where(
                    masks[h], values, jnp.zeros_like(values)
                )

        def query_block(i, _, pair=pair, base=base):
            start = pl.multiple_of(i * tile, tile)
            queries = mixed_ref[slots[sequence, i], :, base : base + LANES]

            def step(j, carry, diagonal=False):
                total, tops, sums = carry
                first = pl.multiple_of(j * tile, tile)
                new_tops, new_sums, shrinks, adds = [], [], [], []
                for h in range(pack):
                    scores = dot_nt(queries, key_own[h, pl.ds(first, tile)]) * scale
                    if diagonal:
                        scores = jnp.where(col <= row, scores, -1e30)
                    top = jnp.maximum(tops[h], jnp.max(scores, axis=1, keepdims=True))
                    terms = jnp.exp2(scores - top)
                    shrink = jnp.exp2(tops[h] - top)
                    new_tops.append(top)
                    new_sums.append(sums[h] * shrink + jnp.sum(terms, axis=1, keepdims=True))
                    shrinks.append(shrink)
                    adds.append(dot_nn(terms.astype(jnp.bfloat16), value_own[h, pl.ds(first, tile)]))
                shrink = shrinks[0]
                for h in range(1, pack):
                    shrink = jnp.where(masks[h], shrinks[h], shrink)
                total = total * shrink
                for add in adds:
                    total = total + add
                return total, tuple(new_tops), tuple(new_sums)

            carry = (
                jnp.zeros((tile, LANES), jnp.float32),
                tuple(jnp.full((tile, 1), -1e30, jnp.float32) for _ in range(pack)),
                tuple(jnp.zeros((tile, 1), jnp.float32) for _ in range(pack)),
            )
            carry = lax.fori_loop(0, i, step, carry)
            total, tops, sums = step(i, carry, diagonal=True)
            share = 1.0 / sums[0]
            for h in range(1, pack):
                share = jnp.where(masks[h], 1.0 / sums[h], share)
            out_ref[pl.ds(start, tile), base : base + LANES] = (total * share).astype(out_ref.dtype)
            for h in range(pack):
                logs = jnp.broadcast_to(tops[h] + jnp.log2(sums[h]), (tile, LANES))
                index = pair * pack + h
                log_ref[0, index : index + 1, pl.ds(start, tile)] = jnp.transpose(logs)[0:1]
            return 0

        lax.fori_loop(0, blocks, query_block, 0)


def attend(mixed, slots, counts, head_size):
    sequences = counts.shape[0]
    rows = sum(part.shape[0] for part in mixed)
    tile = rows // slots.size
    blocks = rows // tile
    lanes = mixed[0].shape[1] // 3
    length = rows // sequences
    heads = lanes // head_size
    pack = LANES // head_size
    return pl.pallas_call(
        functools.partial(attend_kernel, head_size, len(mixed)),
        grid_spec=pltpu.PrefetchScalarGridSpec(
            num_scalar_prefetch=2,
            grid=(sequences,),
            in_specs=[pl.BlockSpec(memory_space=pl.ANY)] * len(mixed),
            out_specs=[
                pl.BlockSpec((length, lanes), lambda s, *_: (s, 0)),
                pl.BlockSpec((1, heads, length), lambda s, *_: (s, 0, 0)),
            ],
            scratch_shapes=[
                pltpu.VMEM((blocks, tile, 3 * lanes), jnp.bfloat16),
                pltpu.VMEM((pack, length, LANES), jnp.bfloat16),
                pltpu.VMEM((pack, length, LANES), jnp.bfloat16),
                pltpu.SemaphoreType.DMA((blocks,)),
            ],
        ),
        out_shape=[
            jax.ShapeDtypeStruct((rows, lanes), jnp.bfloat16),
            jax.ShapeDtypeStruct((sequences, heads, length), jnp.float32),
        ],
        compiler_params=pltpu.CompilerParams(vmem_limit_bytes=VMEM_BYTES),
        cost_estimate=pl.CostEstimate(
            flops=rows * length * lanes * 4,
            bytes_accessed=rows * lanes * 8,
            transcendentals=rows * length * heads // 2,
        ),
    )(counts, slots, *mixed)


def attend_back_kernel(
    head_size,
    blocks_in,
    counts,
    slots,
    *refs,
):
    sources = refs[:blocks_in]
    grad_ref, out_ref, log_ref, own_ref, other_ref, mixed_ref = refs[blocks_in : blocks_in + 6]
    query_own, key_own, grad_own, delta, grad_query, grad_key, grad_value, back_ref, sems = refs[
        blocks_in + 6 :
    ]
    fetch(sources, mixed_ref, sems)
    length, lanes = out_ref.shape
    tile = mixed_ref.shape[1]
    pack = LANES // head_size
    scale = head_size ** (-0.5)
    sequence = pl.program_id(0)
    blocks = lax.div(counts[sequence] + (tile - 1), tile)
    masks = head_masks(head_size)
    for i in range(length // tile):
        back_ref[slots[sequence, i]] = jnp.zeros((tile, 3 * lanes), back_ref.dtype)
    key_row = lax.broadcasted_iota(jnp.int32, (tile, tile), 0)
    query_col = lax.broadcasted_iota(jnp.int32, (tile, tile), 1)
    for pair in range(lanes // LANES):
        base = pair * LANES
        for i in range(length // tile):
            span = slice(i * tile, (i + 1) * tile)
            slot = slots[sequence, i]
            queries = mixed_ref[slot, :, base : base + LANES]
            keys = mixed_ref[slot, :, lanes + base : lanes + base + LANES]
            grads = grad_ref[span, base : base + LANES]
            for h in range(pack):
                query_own[h, span] = jnp.where(masks[h], queries, jnp.zeros_like(queries))
                key_own[h, span] = jnp.where(masks[h], keys, jnp.zeros_like(keys))
                grad_own[h, span] = jnp.where(masks[h], grads, jnp.zeros_like(grads))
        grad_query[...] = jnp.zeros(grad_query.shape, jnp.float32)

        def deltas(i, _, base=base):
            start = pl.multiple_of(i * tile, tile)
            grads = grad_ref[pl.ds(start, tile), base : base + LANES].astype(jnp.float32)
            outs = out_ref[pl.ds(start, tile), base : base + LANES].astype(jnp.float32)
            products = jnp.transpose(grads * outs)
            for h in range(pack):
                delta[h : h + 1, pl.ds(start, tile)] = jnp.sum(
                    products[h * head_size : (h + 1) * head_size], axis=0, keepdims=True
                )
            return 0

        lax.fori_loop(0, blocks, deltas, 0)

        def key_block(j, _, pair=pair, base=base):
            first = pl.multiple_of(j * tile, tile)
            place = slots[sequence, j]
            keys = mixed_ref[place, :, lanes + base : lanes + base + LANES]
            values = mixed_ref[place, :, 2 * lanes + base : 2 * lanes + base + LANES]
            grad_key[...] = jnp.zeros(grad_key.shape, jnp.float32)
            grad_value[...] = jnp.zeros(grad_value.shape, jnp.float32)

            def step(i, diagonal=False):
                start = pl.multiple_of(i * tile, tile)
                add_query, add_key, add_value = [], [], []
                for h in range(pack):
                    index = pair * pack + h
                    query_head = query_own[h, pl.ds(start, tile)]
                    grad_head = grad_own[h, pl.ds(start, tile)]
                    scores = dot_nt(keys, query_head) * (scale * LOG2E)
                    probs = jnp.exp2(scores - log_ref[0, index : index + 1, pl.ds(start, tile)])
                    if diagonal:
                        probs = jnp.where(key_row <= query_col, probs, 0.0)
                    grad_probs = dot_nt(values, grad_head)
                    grad_scores = (
                        probs * (grad_probs - delta[h : h + 1, pl.ds(start, tile)])
                    ).astype(jnp.bfloat16)
                    add_value.append(dot_nn(probs.astype(jnp.bfloat16), grad_head))
                    add_key.append(dot_nn(grad_scores, query_head))
                    add_query.append(dot_tn(grad_scores, key_own[h, pl.ds(first, tile)]))
                grad_value[...] += functools.reduce(jnp.add, add_value)
                grad_key[...] += functools.reduce(jnp.add, add_key)
                grad_query[pl.ds(start, tile), :] += functools.reduce(jnp.add, add_query)

            def off_diagonal(i, _):
                step(i)
                return 0

            step(j, diagonal=True)
            lax.fori_loop(j + 1, blocks, off_diagonal, 0)
            back_ref[place, :, lanes + base : lanes + base + LANES] = (grad_key[...] * scale).astype(
                back_ref.dtype
            )
            back_ref[place, :, 2 * lanes + base : 2 * lanes + base + LANES] = grad_value[...].astype(
                back_ref.dtype
            )
            return 0

        lax.fori_loop(0, blocks, key_block, 0)
        for i in range(length // tile):
            back_ref[slots[sequence, i], :, base : base + LANES] = (
                grad_query[i * tile : (i + 1) * tile] * scale
            ).astype(back_ref.dtype)

    @pl.when(sequence == pl.num_programs(0) - 1)
    def _():
        half = back_ref.shape[0] // 2
        for k in range(half):
            own_ref[k * tile : (k + 1) * tile] = back_ref[k]
            other_ref[k * tile : (k + 1) * tile] = back_ref[half + k]


def attend_back(mixed, slots, grads, outs, logs, counts, head_size):
    sequences = counts.shape[0]
    rows, lanes = outs.shape
    length = rows // sequences
    heads = lanes // head_size
    pack = LANES // head_size
    tile = rows // slots.size
    blocks = rows // tile
    whole = pl.BlockSpec((rows // 2, 3 * lanes), lambda s, *_: (0, 0))
    return pl.pallas_call(
        functools.partial(attend_back_kernel, head_size, len(mixed)),
        grid_spec=pltpu.PrefetchScalarGridSpec(
            num_scalar_prefetch=2,
            grid=(sequences,),
            in_specs=[pl.BlockSpec(memory_space=pl.ANY)] * len(mixed)
            + [
                pl.BlockSpec((length, lanes), lambda s, *_: (s, 0)),
                pl.BlockSpec((length, lanes), lambda s, *_: (s, 0)),
                pl.BlockSpec((1, heads, length), lambda s, *_: (s, 0, 0)),
            ],
            out_specs=[whole, whole],
            scratch_shapes=[
                pltpu.VMEM((blocks, tile, 3 * lanes), jnp.bfloat16),
                pltpu.VMEM((pack, length, LANES), jnp.bfloat16),
                pltpu.VMEM((pack, length, LANES), jnp.bfloat16),
                pltpu.VMEM((pack, length, LANES), jnp.bfloat16),
                pltpu.VMEM((pack, length), jnp.float32),
                pltpu.VMEM((length, LANES), jnp.float32),
                pltpu.VMEM((tile, LANES), jnp.float32),
                pltpu.VMEM((tile, LANES), jnp.float32),
                pltpu.VMEM((blocks, tile, 3 * lanes), jnp.bfloat16),
                pltpu.SemaphoreType.DMA((blocks,)),
            ],
        ),
        out_shape=[jax.ShapeDtypeStruct((rows // 2, 3 * lanes), jnp.bfloat16)] * 2,
        compiler_params=pltpu.CompilerParams(vmem_limit_bytes=VMEM_BYTES),
        cost_estimate=pl.CostEstimate(
            flops=rows * length * lanes * 10,
            bytes_accessed=rows * lanes * 18,
            transcendentals=rows * length * heads // 2,
        ),
    )(counts, slots, *mixed, grads, outs, logs)


def ffn_kernel(block, x_parts, g_parts, counts, *refs):
    xs, refs = refs[:x_parts], refs[x_parts:]
    gs, refs = refs[:g_parts], refs[g_parts:]
    ups, downs, shifts = refs[0:2], refs[2:4], refs[4:6]
    units_ref, back_ref, out_ref, x, g, total, x_sems, g_sems = refs[-8:]
    fetch(xs, x, x_sems)
    fetch(gs, g, g_sems)
    blocks, size, model = x.shape
    width = ups[0].shape[0]
    step = pl.program_id(0)

    @pl.when(step == 0)
    def _():
        total[...] = jnp.zeros(total.shape, total.dtype)

    for k in range(blocks):
        rows = slice(k * size, (k + 1) * size)

        @pl.when(counts[block + k] != 0)
        def _(k=k, rows=rows):
            backs = []
            for side in range(2):
                span = slice(side * width, (side + 1) * width)
                pre = dot_nt(x[k], ups[side][...]) + shifts[side][...]
                grad_units = dot_nt(g[k], downs[side][...])
                bell = jnp.exp2(pre * pre * (-0.5 * LOG2E))
                denominator = 1.0 + (0.3275911 * 0.7071067811865476) * jnp.abs(pre)
                t = pl.reciprocal(denominator, approx=True)
                t = t * (2.0 - denominator * t)
                tail = 0.5 * 1.061405429
                for factor in (-1.453152027, 1.421413741, -0.284496736, 0.254829592):
                    tail = tail * t + 0.5 * factor
                tail = tail * t * bell
                below = jnp.where(pre < 0, tail, 1.0 - tail)
                units_ref[rows, span] = (pre * below).astype(units_ref.dtype)
                slope = below + pre * bell * 0.3989422804014327
                backs.append((grad_units * slope).astype(back_ref.dtype))
                back_ref[rows, span] = backs[-1]
            total[rows] += dot_nn(backs[0], ups[0][...]) + dot_nn(backs[1], ups[1][...])

        @pl.when(counts[block + k] == 0)
        def _(rows=rows):
            units_ref[rows] = jnp.zeros((size, 2 * width), units_ref.dtype)
            back_ref[rows] = jnp.zeros((size, 2 * width), back_ref.dtype)

    @pl.when(step == pl.num_programs(0) - 1)
    def _():
        out_ref[...] = total[...].astype(out_ref.dtype)


def ffn_blocks(place, block, counts, xs, gs, ups, downs, shifts, kept):
    size, width = 512, 256
    model = xs[0].shape[1]
    rows = sum(x.shape[0] for x in xs)
    units = ups[0].shape[0]
    whole = pl.BlockSpec(memory_space=pl.ANY)
    weights = pl.BlockSpec((width, model), lambda u, *_: (u, 0))
    shift = pl.BlockSpec((1, width), lambda u, *_: (0, u))
    output = pl.BlockSpec((rows, 2 * width), lambda u, *_: (place, u))
    full = jax.ShapeDtypeStruct((4 * size, 2 * units), jnp.bfloat16)
    return pl.pallas_call(
        functools.partial(ffn_kernel, block, len(xs), len(gs)),
        grid_spec=pltpu.PrefetchScalarGridSpec(
            num_scalar_prefetch=1,
            grid=(units // width,),
            in_specs=[whole] * (len(xs) + len(gs))
            + [weights] * 4
            + [shift] * 2
            + [whole] * len(kept),
            out_specs=[output, output, pl.BlockSpec((rows, model), lambda u, *_: (0, 0))],
            scratch_shapes=[
                pltpu.VMEM((rows // size, size, model), jnp.bfloat16),
                pltpu.VMEM((rows // size, size, model), jnp.bfloat16),
                pltpu.VMEM((rows, model), jnp.float32),
                pltpu.SemaphoreType.DMA((len(xs),)),
                pltpu.SemaphoreType.DMA((len(gs),)),
            ],
        ),
        out_shape=[full, full, jax.ShapeDtypeStruct((rows, model), jnp.bfloat16)],
        input_output_aliases={len(xs) + len(gs) + 7 + k: k for k in range(len(kept))},
        compiler_params=pltpu.CompilerParams(vmem_limit_bytes=VMEM_BYTES),
        cost_estimate=pl.CostEstimate(
            flops=12 * rows * units * model,
            bytes_accessed=8 * units * model + 8 * rows * model,
            transcendentals=4 * rows * units,
        ),
    )(counts, *xs, *gs, *ups, *downs, *shifts, *kept)


def products_kernel(width, active, left, own, other, out_ref):
    here = active[pl.program_id(0)] != 0

    @pl.when(here)
    def _():
        total = None
        for k in range(own.shape[0] // width):
            rows = slice(k * width, (k + 1) * width)
            for side, right in enumerate((own, other)):
                start = (2 * k + side) * width
                term = dot_nn(left[:, start : start + width], right[rows])
                total = term if total is None else total + term
        out_ref[...] = total.astype(out_ref.dtype)

    @pl.when(jnp.logical_not(here))
    def _():
        out_ref[...] = jnp.zeros(out_ref.shape, out_ref.dtype)


def products(counts, left, own, other):
    blocks = counts.shape[0]
    rows, depth = left.shape
    size = rows // blocks
    columns = own.shape[1]
    return pl.pallas_call(
        functools.partial(products_kernel, 256),
        grid_spec=pltpu.PrefetchScalarGridSpec(
            num_scalar_prefetch=1,
            grid=(blocks,),
            in_specs=[
                pl.BlockSpec((size, depth), lambda i, *_: (i, 0)),
                pl.BlockSpec(own.shape, lambda i, *_: (0, 0)),
                pl.BlockSpec(own.shape, lambda i, *_: (0, 0)),
            ],
            out_specs=pl.BlockSpec((size, columns), lambda i, *_: (i, 0)),
        ),
        out_shape=jax.ShapeDtypeStruct((rows, columns), jnp.bfloat16),
        compiler_params=pltpu.CompilerParams(vmem_limit_bytes=VMEM_BYTES),
        cost_estimate=pl.CostEstimate(
            flops=2 * rows * depth * columns,
            bytes_accessed=2 * (rows * (depth + columns) + depth * columns),
            transcendentals=0,
        ),
    )(counts, left, own, other)


def project_kernel(inputs, side, parts, *refs):
    xs = refs[:inputs]
    weights, shift, out_ref = refs[inputs:]
    slab = weights.shape[1]
    weight = weights[...].reshape(3 * slab, weights.shape[2])
    for k in range(inputs):

        @pl.when(pl.program_id(0) == k)
        def _(k=k):
            mixed = dot_nt(xs[k][...], weight)
            for t in range(3):
                columns = pl.ds(pl.multiple_of(parts[side, t] * slab, slab), slab)
                out_ref[:, columns] = (
                    mixed[:, t * slab : (t + 1) * slab] + shift[:, columns]
                ).astype(out_ref.dtype)


def project(parts, side, xs, weights, shift):
    size, model = xs[0].shape
    slab = weights.shape[1]
    return pl.pallas_call(
        functools.partial(project_kernel, len(xs), side),
        grid_spec=pltpu.PrefetchScalarGridSpec(
            num_scalar_prefetch=1,
            grid=(len(xs),),
            in_specs=[pl.BlockSpec((size, model), lambda i, *_: (0, 0))] * len(xs)
            + [
                pl.BlockSpec(weights.shape, lambda i, *_: (0, 0, 0)),
                pl.BlockSpec(shift.shape, lambda i, *_: (0, 0)),
            ],
            out_specs=pl.BlockSpec((size, 3 * slab), lambda i, *_: (i, 0)),
        ),
        out_shape=jax.ShapeDtypeStruct((len(xs) * size, 3 * slab), jnp.bfloat16),
        compiler_params=pltpu.CompilerParams(vmem_limit_bytes=VMEM_BYTES),
        cost_estimate=pl.CostEstimate(
            flops=6 * len(xs) * size * slab * model,
            bytes_accessed=6 * slab * model + 2 * len(xs) * size * (model + 3 * slab),
            transcendentals=0,
        ),
    )(parts, *xs, weights, shift)


def unproject_kernel(parts, active, mine, theirs, own, other, out_ref):
    slab = own.shape[1]
    here = active[pl.program_id(0)] != 0

    @pl.when(here)
    def _():
        total = None
        for side, (left, right) in enumerate(((mine, own), (theirs, other))):
            for t in range(3):
                columns = pl.ds(pl.multiple_of(parts[side, t] * slab, slab), slab)
                term = dot_nn(left[:, columns], right[t])
                total = term if total is None else total + term
        out_ref[...] = total.astype(out_ref.dtype)

    @pl.when(jnp.logical_not(here))
    def _():
        out_ref[...] = jnp.zeros(out_ref.shape, out_ref.dtype)


def unproject(parts, counts, mine, theirs, own, other):
    blocks = counts.shape[0]
    size = mine.shape[0] // blocks
    slab, model = own.shape[1:]
    left = pl.BlockSpec((size, 3 * slab), lambda i, *_: (i, 0))
    fixed = pl.BlockSpec(own.shape, lambda i, *_: (0, 0, 0))
    return pl.pallas_call(
        unproject_kernel,
        grid_spec=pltpu.PrefetchScalarGridSpec(
            num_scalar_prefetch=2,
            grid=(blocks,),
            in_specs=[left, left, fixed, fixed],
            out_specs=pl.BlockSpec((size, model), lambda i, *_: (i, 0)),
        ),
        out_shape=jax.ShapeDtypeStruct((blocks * size, model), jnp.bfloat16),
        compiler_params=pltpu.CompilerParams(vmem_limit_bytes=VMEM_BYTES),
        cost_estimate=pl.CostEstimate(
            flops=12 * blocks * size * slab * model,
            bytes_accessed=12 * slab * model + 2 * blocks * size * (model + 6 * slab),
            transcendentals=0,
        ),
    )(parts, counts, mine, theirs, own, other)


def weight_grad_kernel(inputs, added, columns, *refs):
    left, rights = refs[0], refs[1 : 1 + inputs]
    tokens, sems = refs[-2:]
    outs = refs[1 + inputs + added : -2]
    fetch(rights, tokens, sems)
    total = dot_tn(left[...], tokens[0])
    if added:
        total = total + refs[1 + inputs][...].astype(jnp.float32)
    size = outs[0].shape[0]
    for k, out_ref in enumerate(outs):
        out_ref[...] = total[k * size : (k + 1) * size].astype(out_ref.dtype)


def weight_grad(left, columns, tile, rights, extra=None, outputs=1):
    rows = left.shape[0]
    model = rights[0].shape[1]
    steps = columns.shape[0]
    output = pl.BlockSpec((tile // outputs, model), lambda i, *_: (i, 0))
    extras = [] if extra is None else [extra]
    shape = jax.ShapeDtypeStruct((steps * tile // outputs, model), jnp.bfloat16)
    results = pl.pallas_call(
        functools.partial(weight_grad_kernel, len(rights), len(extras)),
        grid_spec=pltpu.PrefetchScalarGridSpec(
            num_scalar_prefetch=1,
            grid=(steps,),
            in_specs=[pl.BlockSpec((rows, tile), lambda i, columns: (0, columns[i]))]
            + [pl.BlockSpec(memory_space=pl.ANY)] * len(rights)
            + [output] * len(extras),
            out_specs=[output] * outputs,
            scratch_shapes=[
                pltpu.VMEM((1, rows, model), jnp.bfloat16),
                pltpu.SemaphoreType.DMA((len(rights),)),
            ],
        ),
        out_shape=[shape] * outputs,
        compiler_params=pltpu.CompilerParams(vmem_limit_bytes=VMEM_BYTES),
        cost_estimate=pl.CostEstimate(
            flops=2 * steps * tile * rows * model,
            bytes_accessed=2 * (rows * model + steps * tile * (rows + 2 * model)),
            transcendentals=0,
        ),
    )(columns, left, *rights, *extras)
    return results[0] if outputs == 1 else results


def chain_sum(values, axis):
    size = lax.axis_size(axis)
    if size != 4:
        return lax.psum(values.astype(jnp.bfloat16), axis).astype(jnp.float32)
    place = lax.axis_index(axis)
    outer = lax.ppermute(values.astype(jnp.bfloat16), axis, [(0, 1), (3, 2)])
    half = (values + outer.astype(jnp.float32)).astype(jnp.bfloat16)
    other = lax.ppermute(half, axis, [(1, 2), (2, 1)])
    whole = (half.astype(jnp.float32) + other.astype(jnp.float32)).astype(jnp.bfloat16)
    ends = lax.ppermute(whole, axis, [(1, 0), (2, 3)])
    inner = (place == 1) | (place == 2)
    return jnp.where(inner, whole, ends).astype(jnp.float32)


class Chain:
    def __init__(self):
        place = lax.axis_index("batch")
        self.inner = (place == 1) | (place == 2)
        self.blocks = (None, None, None)
        self.moved = (None, None, None)
        self.totals = []

    def advance(self, block, *done):
        wide = lambda values: values.astype(jnp.float32)
        first, second, third = self.blocks
        inward, across, outward = after(self.moved, *done)
        half = whole = None
        if first is not None:
            half = (wide(first) + wide(inward)).astype(jnp.bfloat16)
        if second is not None:
            whole = (wide(second) + wide(across)).astype(jnp.bfloat16)
        if third is not None:
            self.totals.append(jnp.where(self.inner, third, outward))
        self.blocks = (block, half, whole)
        pairs = ([(0, 1), (3, 2)], [(1, 2), (2, 1)], [(1, 0), (2, 3)])
        self.moved = tuple(
            None if value is None else lax.ppermute(value, "batch", route)
            for value, route in zip(self.blocks, pairs)
        )
        return [value for value in self.blocks if value is not None]


def normalize(values):
    center = values - jnp.mean(values, axis=-1, keepdims=True)
    inverse = lax.rsqrt(jnp.mean(center * center, axis=-1, keepdims=True) + epsilon)
    return center * inverse, inverse


def normalize_back(grad, gain, normal, inverse):
    scaled = grad * gain
    grad_values = inverse * (
        scaled
        - jnp.mean(scaled, axis=-1, keepdims=True)
        - normal * jnp.mean(scaled * normal, axis=-1, keepdims=True)
    )
    return grad_values, jnp.sum(grad * normal, axis=0), jnp.sum(grad, axis=0)


def local_general(
    hidden,
    cotangent,
    exit_layer,
    ln1_gain,
    ln1_bias,
    qkv_weight,
    query_bias,
    value_bias,
    out_weight,
    out_bias,
    ln2_gain,
    ln2_bias,
    up_weight,
    up_bias,
    down_weight,
    down_bias,
):
    width = lax.axis_size("wide")
    rank = lax.axis_index("wide")
    rows, model = hidden.shape
    group = rows * width
    slab = model // width
    head_size = model // HEADS
    units_own = up_weight.shape[0]
    keep = exit_layer >= LAYER
    counts = jnp.sum(keep.astype(jnp.int32), axis=1)
    active = lax.dynamic_slice_in_dim(keep.reshape(group), rank * rows, rows, 0)
    active = active.astype(jnp.float32)[:, None]
    grad_out = cotangent.astype(jnp.float32)

    routes = [[(w, (3 * w + t) % width) for w in range(width)] for t in range(3)]
    part_at = np.zeros((width, 3), np.int32)
    for t in range(3):
        for w, d in routes[t]:
            part_at[d, t] = (3 * w + t) // width
    place_of = jnp.asarray(np.argsort(part_at, axis=1).astype(np.int32))[rank]
    part_of = jnp.asarray(part_at)[rank]

    hidden_wide = hidden.astype(jnp.float32)
    normal1, inverse1 = normalize(hidden_wide)
    normed1 = lax.all_gather(
        (normal1 * ln1_gain + ln1_bias).astype(jnp.bfloat16), "wide", axis=0, tiled=True
    )
    slabs = qkv_weight.reshape(3, slab, model)
    received = jnp.stack([lax.ppermute(slabs[t], "wide", routes[t]) for t in range(3)])
    qkv_own = jnp.concatenate(
        [lax.dynamic_index_in_dim(received, place_of[p], 0, keepdims=False) for p in range(3)]
    )
    own = lambda vector: lax.dynamic_slice_in_dim(vector, rank * slab, slab, 0)
    qkv_shift = jnp.concatenate(
        [own(query_bias), jnp.zeros((slab,), jnp.float32), own(value_bias)]
    )

    grad_ffn = (active * grad_out).astype(jnp.bfloat16)
    down_bias_grad = jnp.sum(grad_ffn.astype(jnp.float32), axis=0)
    piece = rows // CHUNKS
    part = lambda values, c: values[c * piece : (c + 1) * piece]
    gather = lambda values: lax.all_gather(values, "wide", axis=0, tiled=True)
    scatter = lambda values: lax.psum_scatter(
        values.astype(jnp.bfloat16), "wide", scatter_dimension=0, tiled=True
    )
    grad_ffns = [gather(part(grad_ffn, c)) for c in range(CHUNKS)]
    out_whole = gather(out_weight)

    mixed = (dot_nt(normed1, qkv_own) + qkv_shift).astype(jnp.bfloat16)
    mixed = jnp.split(mixed, group // TILE)
    slots = jnp.arange(group // TILE, dtype=jnp.int32).reshape(counts.shape[0], -1)
    attended, logs = attend(mixed, slots, counts, head_size)
    attended_rows = lax.all_to_all(attended, "wide", split_axis=0, concat_axis=1, tiled=True)
    middle = hidden_wide + active * (dot_nn(attended_rows, out_whole) + out_bias)
    normal2, inverse2 = normalize(middle)
    normed2 = (normal2 * ln2_gain + ln2_bias).astype(jnp.bfloat16)
    up_shift = lax.dynamic_slice_in_dim(up_bias, rank * units_own, units_own, 0)

    normed2s = [gather(part(normed2, c)) for c in range(CHUNKS)]
    units, grad_pres, grad_normed2, ffn_out = [], [], [], []
    for c in range(CHUNKS):
        grad_units = dot_nt(grad_ffns[c], down_weight)
        pre = dot_nt(normed2s[c], up_weight) + up_shift
        below = 0.5 + 0.5 * lax.erf(pre * 0.7071067811865476)
        bell = jnp.exp(-0.5 * pre * pre) * 0.3989422804014327
        units.append((pre * below).astype(jnp.bfloat16))
        grad_pres.append((grad_units * (below + pre * bell)).astype(jnp.bfloat16))
        grad_normed2.append(scatter(dot_nn(grad_pres[c], up_weight)))
    for c in range(CHUNKS):
        ffn_out.append(scatter(dot_nn(units[c], down_weight)))
    grad_normed2 = jnp.concatenate(grad_normed2).astype(jnp.float32)
    ffn_out = jnp.concatenate(ffn_out).astype(jnp.float32)
    output = (middle + active * (ffn_out + down_bias)).astype(jnp.bfloat16)

    up_bias_own = sum(jnp.sum(g.astype(jnp.float32), axis=0) for g in grad_pres)
    down_grad = sum(dot_tn(units[c], grad_ffns[c]) for c in range(CHUNKS))
    up_grad = sum(dot_tn(grad_pres[c], normed2s[c]) for c in range(CHUNKS))
    halves = lambda values: jnp.concatenate(
        [chain_sum(half, "batch") for half in jnp.split(values, 2)]
    )
    down_grad = halves(down_grad)
    up_grad = halves(up_grad)

    grad_middle, ln2_gain_grad, ln2_bias_grad = normalize_back(
        grad_normed2, ln2_gain, normal2, inverse2
    )
    grad_middle = grad_out + grad_middle
    grad_branch = (active * grad_middle).astype(jnp.bfloat16)
    out_bias_grad = jnp.sum(grad_branch.astype(jnp.float32), axis=0)
    grad_attended = dot_nt(grad_branch, out_whole).astype(jnp.bfloat16)
    grad_heads = lax.all_to_all(grad_attended, "wide", split_axis=1, concat_axis=0, tiled=True)
    out_grad = chain_sum(scatter(dot_tn(attended_rows, grad_branch)).astype(jnp.float32), "batch")

    placed = lambda vector, size: lax.dynamic_update_slice_in_dim(
        jnp.zeros((size,), jnp.float32), vector, rank * vector.shape[0], 0
    )
    early = lax.psum(
        (
            out_bias_grad,
            ln2_gain_grad,
            ln2_bias_grad,
            placed(up_bias_own, up_bias.shape[0]),
            down_bias_grad,
        ),
        ("batch", "wide"),
    )

    grad_mixed = jnp.concatenate(
        attend_back(mixed, slots, grad_heads, attended, logs, counts, head_size)
    )
    grad_normed1 = scatter(dot_nn(grad_mixed, qkv_own)).astype(jnp.float32)
    sums = jnp.sum(grad_mixed.astype(jnp.float32), axis=0)
    qkv_parts = []
    for t in range(3):
        columns = lax.dynamic_slice_in_dim(grad_mixed, part_of[t] * slab, slab, 1)
        total = chain_sum(dot_tn(columns, normed1), "batch").astype(jnp.bfloat16)
        back = [(d, w) for w, d in routes[t]]
        qkv_parts.append(lax.ppermute(total, "wide", back).astype(jnp.float32))
    qkv_grad = jnp.concatenate(qkv_parts)

    grad_hidden, ln1_gain_grad, ln1_bias_grad = normalize_back(
        grad_normed1, ln1_gain, normal1, inverse1
    )
    input_grad = grad_middle + grad_hidden
    late = lax.psum(
        (
            ln1_gain_grad,
            ln1_bias_grad,
            placed(sums[:slab], model),
            placed(sums[2 * slab :], model),
        ),
        ("batch", "wide"),
    )
    return (
        output,
        input_grad,
        late[0],
        late[1],
        qkv_grad,
        late[2],
        late[3],
        out_grad,
        early[0],
        early[1],
        early[2],
        up_grad,
        early[3],
        down_grad,
        early[4],
    )


def swap(values, bits):
    width = lax.axis_size("wide")
    return lax.ppermute(values, "wide", [(w, w ^ bits) for w in range(width)])


def after(values, *done):
    return lax.optimization_barrier((values, done))[0]


def relay(along_x, along_y):
    half = along_x.shape[0] // 2
    return [swap(along_y[:half], 2), swap(along_x[half:], 4)]


class Scatter:
    def __init__(self, own, along_x, along_y, diagonal):
        self.half = half = own.shape[0] // 2
        self.own, self.along_x, self.along_y = own, along_x, along_y
        self.from_x = swap(jnp.concatenate([diagonal[:half], along_x[:half]]), 2)
        self.from_y = swap(jnp.concatenate([diagonal[half:], along_y[half:]]), 4)

    def second(self, *done):
        half = self.half
        from_x, from_y = after((self.from_x, self.from_y), *done)
        self.near = (from_x[half:], from_y[half:])
        return self.forward(from_x[:half], from_y[:half])

    def forward(self, top, bottom):
        wide = lambda values: values.astype(jnp.float32)
        half = self.half
        y_top = (wide(self.along_y[:half]) + wide(top)).astype(jnp.bfloat16)
        x_bottom = (wide(self.along_x[half:]) + wide(bottom)).astype(jnp.bfloat16)
        self.last = (swap(y_top, 4), swap(x_bottom, 2))
        return y_top, x_bottom

    def finish(self, *done):
        wide = lambda values: values.astype(jnp.float32)
        y_top, x_bottom = after(self.last, *done)
        x_top, y_bottom = self.near
        return jnp.concatenate(
            [
                wide(self.own[: self.half]) + wide(x_top) + wide(y_top),
                wide(self.own[self.half :]) + wide(x_bottom) + wide(y_bottom),
            ]
        )


class EarlyScatter(Scatter):
    def __init__(self, own, along_x, along_y):
        self.half = half = own.shape[0] // 2
        self.own, self.along_x, self.along_y = own, along_x, along_y
        self.near = (swap(along_x[:half], 2), swap(along_y[half:], 4))

    def first(self, diagonal):
        self.from_far = (swap(diagonal[: self.half], 2), swap(diagonal[self.half :], 4))
        self.near = after(self.near, diagonal)
        return self.near

    def second(self, *done):
        return self.forward(*after(self.from_far, *done))


def tree_sum(values):
    total = values + swap(values, 1)
    total = (total + swap(total, 2)) + (swap(total, 4) + swap(total, 6))
    size = lax.axis_size("batch")
    terms = [total] + [
        lax.ppermute(total, "batch", [(z, z ^ bits) for z in range(size)])
        for bits in range(1, size)
    ]
    while len(terms) > 1:
        terms = [terms[k] + terms[k + 1] for k in range(0, len(terms), 2)]
    return terms[0]


def local_chips(
    hidden,
    cotangent,
    exit_layer,
    ln1_gain,
    ln1_bias,
    qkv_weight,
    query_bias,
    value_bias,
    out_weight,
    out_bias,
    ln2_gain,
    ln2_bias,
    up_weight,
    up_bias,
    down_weight,
    down_bias,
):
    width = lax.axis_size("wide")
    rank = lax.axis_index("wide")
    rows, model = hidden.shape
    group = rows * width
    slab = model // width
    head_size = model // HEADS
    units_own = up_weight.shape[0]
    keep = exit_layer >= LAYER
    counts = jnp.sum(keep.astype(jnp.int32), axis=1)
    active = lax.dynamic_slice_in_dim(keep.reshape(group), rank * rows, rows, 0)
    active = active.astype(jnp.float32)[:, None]
    grad_out = cotangent.astype(jnp.float32)

    tiles = jnp.arange(group // rows, dtype=jnp.int32)
    slots = ((tiles ^ rank) & 1) * 4 + ((tiles >> 1) ^ (rank >> 1))
    slots = slots.reshape(counts.shape[0], -1)

    routes = [[(w, (3 * w + t) % width) for w in range(width)] for t in range(3)]
    part_at = np.zeros((width, 3), np.int32)
    for t in range(3):
        for w, d in routes[t]:
            part_at[d, t] = (3 * w + t) // width
    part_at = jnp.asarray(part_at)
    other = rank ^ 1
    parts = jnp.stack([part_at[rank], part_at[other]])

    hidden_wide = hidden.astype(jnp.float32)
    normal1, inverse1 = normalize(hidden_wide)
    slabs = qkv_weight.reshape(3, slab, model)
    slabs = [lax.ppermute(slabs[t], "wide", routes[t]) for t in range(3)]
    normed1 = (normal1 * ln1_gain + ln1_bias).astype(jnp.bfloat16)
    normed1 = [normed1, swap(normed1, 2), swap(normed1, 4)]
    diagonal1 = relay(normed1[1], normed1[2])
    qkv_own = jnp.stack(after(slabs, normed1[1:]))
    qkv_other = swap(qkv_own, 1)

    def shift_of(device):
        own = lambda vector: lax.dynamic_slice_in_dim(vector, device * slab, slab, 0)
        shift = [own(query_bias), jnp.zeros((slab,), jnp.float32), own(value_bias)]
        return jnp.concatenate(shift)[None]

    bias_of = lambda device: lax.dynamic_slice_in_dim(up_bias, device * units_own, units_own, 0)
    up_shifts = [bias_of(rank)[None], bias_of(other)[None]]

    mixed_near = project(parts, 0, normed1, qkv_own, shift_of(rank))
    qkv_other = after(qkv_other, mixed_near)
    lent_near = project(parts, 1, normed1, qkv_other, shift_of(other))
    diagonal1 = after(diagonal1, lent_near)
    lent_far = project(parts, 1, diagonal1, qkv_other, shift_of(other))
    mixed_far = project(parts, 0, after(diagonal1, lent_far), qkv_own, shift_of(rank))
    mixed = [mixed_near, mixed_far, swap(lent_near, 1), swap(lent_far, 1)]

    out_whole = lax.all_gather(after(out_weight, diagonal1), "wide", axis=0, tiled=True)
    grad_ffn = (after(active, diagonal1) * grad_out).astype(jnp.bfloat16)
    down_bias_grad = jnp.sum(grad_ffn.astype(jnp.float32), axis=0)
    grad_ffn = [grad_ffn, swap(grad_ffn, 2), swap(grad_ffn, 4)]

    attended, logs = attend(mixed, slots, counts, head_size)
    attended_rows = lax.all_to_all(attended, "wide", split_axis=0, concat_axis=1, tiled=True)
    attended_rows = after(attended_rows, grad_ffn[1:])
    up_other, down_other = swap(after((up_weight, down_weight), attended), 1)
    middle = hidden_wide + active * (dot_nn(attended_rows, out_whole) + out_bias)
    normal2, inverse2 = normalize(middle)
    normed2 = (normal2 * ln2_gain + ln2_bias).astype(jnp.bfloat16)
    normed2 = [normed2, swap(normed2, 2), swap(normed2, 4)]

    per_tile = jnp.sum(keep.reshape(group // rows, rows).astype(jnp.int32), axis=1)
    block_chip = (rank >> 1) ^ jnp.arange(4, dtype=jnp.int32)
    block_counts = per_tile[2 * block_chip + (rank & 1)]
    ups, downs = [up_weight, up_other], [down_weight, down_other]

    def ffn(place, block, xs, gs, kept):
        *kept, partial = ffn_blocks(
            place, block, block_counts, xs, gs, ups, downs, up_shifts, tuple(kept)
        )
        return kept, partial

    kept, partial_own = ffn(2, 0, normed2[:1], grad_ffn[:1], ())
    normed2[1:] = after(normed2[1:], partial_own)
    diagonal2 = relay(normed2[1], normed2[2])
    diagonal_ffn = relay(*after(grad_ffn[1:], attended_rows))
    kept, partial_near = ffn(0, 1, normed2[1:], grad_ffn[1:], kept)
    scatter2 = EarlyScatter(partial_own, partial_near[:rows], partial_near[rows:])
    diagonal2 = after(diagonal2, partial_near)
    (units, grad_pres), partial_far = ffn(3, 3, diagonal2, diagonal_ffn, kept)
    wait = scatter2.first(partial_far)
    tokens2 = [*normed2[1:], normed2[0], *diagonal2]
    tokens_ffn = [*grad_ffn[1:], grad_ffn[0], *diagonal_ffn]

    wide = lambda values: values.astype(jnp.float32)
    lowered = lambda values: values.astype(jnp.bfloat16)
    tile = 512
    tiles = jnp.arange(2 * units_own // tile, dtype=jnp.int32)
    down_own, down_lent = weight_grad(after(units, wait), tiles, tile, tokens_ffn, outputs=2)
    wait = scatter2.second(down_lent)
    down_lent = swap(down_lent, 1)
    up_own, up_lent = weight_grad(after(grad_pres, wait), tiles, tile, tokens2, outputs=2)
    up_lent = swap(up_lent, 1)
    grad_normed2 = scatter2.finish(up_own)
    down_sum = lowered(wide(down_own) + wide(after(down_lent, up_own)))
    up_sum = lowered(wide(up_own) + wide(after(up_lent, down_sum)))
    down_grad, up_grad = lax.psum((down_sum, up_sum), "batch")

    grad_middle, ln2_gain_grad, ln2_bias_grad = normalize_back(
        after(grad_normed2, up_sum), ln2_gain, normal2, inverse2
    )
    grad_middle = grad_out + grad_middle
    grad_branch = (active * grad_middle).astype(jnp.bfloat16)
    out_bias_grad = jnp.sum(grad_branch.astype(jnp.float32), axis=0)
    grad_attended = dot_nt(grad_branch, out_whole).astype(jnp.bfloat16)
    grad_heads = lax.all_to_all(grad_attended, "wide", split_axis=1, concat_axis=0, tiled=True)

    owners = 2 * block_chip + (rank & 1)
    grad_branch = after(grad_branch, grad_attended)
    out_lent = weight_grad(attended_rows, owners ^ 1, slab, [grad_branch])
    out_lent = swap(out_lent, 1)
    out_own = weight_grad(attended_rows, owners, slab, [grad_branch], out_lent)
    scatter_out = Scatter(*jnp.split(out_own, 4))

    back_own, back_other = attend_back(
        mixed, slots, after(grad_heads, out_own), attended, logs, counts, head_size
    )
    theirs = swap(back_other, 1)
    tokens1 = [*normed1, *diagonal1]
    qkv_own_grad = weight_grad(back_own, parts[0], slab, tokens1)
    wait = scatter_out.second(qkv_own_grad)
    theirs = after(theirs, wait)
    qkv_lent = weight_grad(theirs, parts[1], slab, tokens1)
    grad_normed1 = unproject(
        parts, block_counts, after(back_own, qkv_lent), theirs, qkv_own, qkv_other
    )
    qkv_lent = swap(qkv_lent, 1)
    scatter1 = Scatter(*jnp.split(grad_normed1, 4))
    qkv_total = lowered(wide(qkv_own_grad) + wide(after(qkv_lent, grad_normed1)))
    out_total = lowered(scatter_out.finish(qkv_total))
    chain = Chain()
    wait = chain.advance(qkv_total[: 2 * slab], out_total)
    ffn_counts = block_counts[jnp.array([1, 2, 0, 3])]
    ffn_out = products(ffn_counts, after(units, *wait), *downs)
    wait = scatter1.second(ffn_out)
    wait = chain.advance(jnp.concatenate([qkv_total[2 * slab :], out_total]), *wait)
    grad_normed1 = scatter1.finish(*wait)
    grad_hidden, ln1_gain_grad, ln1_bias_grad = normalize_back(
        grad_normed1, ln1_gain, normal1, inverse1
    )
    input_grad = grad_middle + grad_hidden
    grad_pres, back_own, back_other = after((grad_pres, back_own, back_other), grad_normed1)
    up_bias_own = jnp.sum(wide(grad_pres), axis=0).reshape(-1, 2, 256)
    up_bias_own = [up_bias_own[:, side].reshape(units_own) for side in range(2)]
    sums = jnp.sum(wide(back_own), axis=0) + jnp.sum(wide(back_other), axis=0)
    along_x, along_y, own, diagonal = jnp.split(after(ffn_out, grad_normed1), 4)
    scatter_ffn = Scatter(own, along_x, along_y, diagonal)
    wait = chain.advance(None, input_grad)
    wait = scatter_ffn.second(*wait)
    wait = chain.advance(None, *wait)
    ffn_out = scatter_ffn.finish(*wait)
    output = (middle + active * (ffn_out + down_bias)).astype(jnp.bfloat16)
    chain.advance(None, output)
    totals = chain.totals
    qkv_totals = [totals[0][:slab], totals[0][slab:], totals[1][:slab]]
    qkv_grad = jnp.concatenate(
        [
            wide(lax.ppermute(qkv_totals[t], "wide", [(d, w) for w, d in routes[t]]))
            for t in range(3)
        ]
    )
    out_grad = wide(totals[1][slab:])
    down_grad, up_grad = after((down_grad, up_grad), qkv_grad, out_grad, output)
    down_grad, up_grad = wide(down_grad), wide(up_grad)

    placed = lambda vector, size, device: lax.dynamic_update_slice_in_dim(
        jnp.zeros((size,), jnp.float32), vector, device * vector.shape[0], 0
    )
    smalls = tree_sum(
        jnp.concatenate(
            [
                placed(up_bias_own[0], up_bias.shape[0], rank)
                + placed(up_bias_own[1], up_bias.shape[0], other),
                down_bias_grad,
                out_bias_grad,
                ln2_gain_grad,
                ln2_bias_grad,
                placed(sums[:slab], model, rank),
                placed(sums[2 * slab :], model, rank),
                ln1_gain_grad,
                ln1_bias_grad,
            ]
        )
    )
    up_bias_grad = smalls[: up_bias.shape[0]]
    smalls = smalls[up_bias.shape[0] :].reshape(8, model)
    return (
        output,
        input_grad,
        smalls[6],
        smalls[7],
        qkv_grad,
        smalls[4],
        smalls[5],
        out_grad,
        smalls[1],
        smalls[2],
        smalls[3],
        up_grad,
        up_bias_grad,
        down_grad,
        smalls[0],
    )


def solution(mesh):
    chips = mesh.shape["wide"] == 8 and mesh.shape["batch"] == 4
    local = local_chips if chips else local_general
    rows = P(("batch", "wide"), None)
    weight = P("wide", None)
    return jax.shard_map(
        local,
        mesh=mesh,
        in_specs=(
            rows,
            rows,
            P("batch", None),
            P(),
            P(),
            weight,
            P(),
            P(),
            weight,
            P(),
            P(),
            P(),
            weight,
            P(),
            weight,
            P(),
        ),
        out_specs=(
            rows,
            rows,
            P(),
            P(),
            weight,
            P(),
            P(),
            weight,
            P(),
            P(),
            P(),
            weight,
            P(),
            weight,
            P(),
        ),
        check_vma=False,
    )
```

```python
import functools

import jax
import jax.numpy as jnp
import numpy as np
from jax import lax
from jax.experimental import pallas as pl
from jax.experimental.pallas import tpu as pltpu
from jax.sharding import PartitionSpec as P

HEADS = 32
LAYER = 12
LANES = 128
TILE = 512
CHUNKS = 2
LOG2E = 1.4426950408889634

epsilon = 1e-05
VMEM_BYTES = 48 * 2**20
NO_COST = pl.CostEstimate(flops=1, bytes_accessed=1, transcendentals=0)


def dot_nt(left, right):
    return lax.dot_general(
        left, right, (((1,), (1,)), ((), ())), preferred_element_type=jnp.float32
    )


def dot_nn(left, right):
    return lax.dot_general(
        left, right, (((1,), (0,)), ((), ())), preferred_element_type=jnp.float32
    )


def dot_tn(left, right):
    return lax.dot_general(
        left, right, (((0,), (0,)), ((), ())), preferred_element_type=jnp.float32
    )


def head_masks(head_size):
    lane = lax.broadcasted_iota(jnp.int32, (1, LANES), 1)
    return [
        (lane >= h * head_size) & (lane < (h + 1) * head_size)
        for h in range(LANES // head_size)
    ]


def fetch(sources, target, sems):
    size = target.shape[1]
    copies = []
    row = 0
    for source in sources:
        rows = source.shape[0]
        least = min(rows, size)
        for k in range(rows // least):
            place = target.at[row // size, pl.ds(row % size, least)]
            copies.append(
                pltpu.make_async_copy(source.at[pl.ds(k * least, least)], place, sems.at[len(copies)])
            )
            row += least

    @pl.when(pl.program_id(0) == 0)
    def _():
        for copy in copies:
            copy.start()
        for copy in copies:
            copy.wait()


def attend_kernel(head_size, blocks_in, counts, slots, *refs):
    sources = refs[:blocks_in]
    out_ref, log_ref, mixed_ref, key_own, value_own, sems = refs[blocks_in:]
    fetch(sources, mixed_ref, sems)
    length, lanes = out_ref.shape
    tile = mixed_ref.shape[1]
    pack = LANES // head_size
    scale = head_size ** (-0.5) * LOG2E
    sequence = pl.program_id(0)
    blocks = lax.div(counts[sequence] + (tile - 1), tile)
    masks = head_masks(head_size)
    out_ref[...] = jnp.zeros(out_ref.shape, out_ref.dtype)
    log_ref[...] = jnp.zeros(log_ref.shape, log_ref.dtype)
    row = lax.broadcasted_iota(jnp.int32, (tile, tile), 0)
    col = lax.broadcasted_iota(jnp.int32, (tile, tile), 1)
    for pair in range(lanes // LANES):
        base = pair * LANES
        for i in range(length // tile):
            slot = slots[sequence, i]
            keys = mixed_ref[slot, :, lanes + base : lanes + base + LANES]
            values = mixed_ref[slot, :, 2 * lanes + base : 2 * lanes + base + LANES]
            for h in range(pack):
                key_own[h, i * tile : (i + 1) * tile] = jnp.where(masks[h], keys, jnp.zeros_like(keys))
                value_own[h, i * tile : (i + 1) * tile] = jnp.where(
                    masks[h], values, jnp.zeros_like(values)
                )

        def query_block(i, _, pair=pair, base=base):
            start = pl.multiple_of(i * tile, tile)
            queries = mixed_ref[slots[sequence, i], :, base : base + LANES]

            def step(j, carry, diagonal=False):
                total, tops, sums = carry
                first = pl.multiple_of(j * tile, tile)
                new_tops, new_sums, shrinks, adds = [], [], [], []
                for h in range(pack):
                    scores = dot_nt(queries, key_own[h, pl.ds(first, tile)]) * scale
                    if diagonal:
                        scores = jnp.where(col <= row, scores, -1e30)
                    top = jnp.maximum(tops[h], jnp.max(scores, axis=1, keepdims=True))
                    terms = jnp.exp2(scores - top)
                    shrink = jnp.exp2(tops[h] - top)
                    new_tops.append(top)
                    new_sums.append(sums[h] * shrink + jnp.sum(terms, axis=1, keepdims=True))
                    shrinks.append(shrink)
                    adds.append(dot_nn(terms.astype(jnp.bfloat16), value_own[h, pl.ds(first, tile)]))
                shrink = shrinks[0]
                for h in range(1, pack):
                    shrink = jnp.where(masks[h], shrinks[h], shrink)
                total = total * shrink
                for add in adds:
                    total = total + add
                return total, tuple(new_tops), tuple(new_sums)

            carry = (
                jnp.zeros((tile, LANES), jnp.float32),
                tuple(jnp.full((tile, 1), -1e30, jnp.float32) for _ in range(pack)),
                tuple(jnp.zeros((tile, 1), jnp.float32) for _ in range(pack)),
            )
            carry = lax.fori_loop(0, i, step, carry)
            total, tops, sums = step(i, carry, diagonal=True)
            share = 1.0 / sums[0]
            for h in range(1, pack):
                share = jnp.where(masks[h], 1.0 / sums[h], share)
            out_ref[pl.ds(start, tile), base : base + LANES] = (total * share).astype(out_ref.dtype)
            for h in range(pack):
                logs = jnp.broadcast_to(tops[h] + jnp.log2(sums[h]), (tile, LANES))
                index = pair * pack + h
                log_ref[0, index : index + 1, pl.ds(start, tile)] = jnp.transpose(logs)[0:1]
            return 0

        lax.fori_loop(0, blocks, query_block, 0)


def attend(mixed, slots, counts, head_size):
    sequences = counts.shape[0]
    rows = sum(part.shape[0] for part in mixed)
    tile = rows // slots.size
    blocks = rows // tile
    lanes = mixed[0].shape[1] // 3
    length = rows // sequences
    heads = lanes // head_size
    pack = LANES // head_size
    return pl.pallas_call(
        functools.partial(attend_kernel, head_size, len(mixed)),
        grid_spec=pltpu.PrefetchScalarGridSpec(
            num_scalar_prefetch=2,
            grid=(sequences,),
            in_specs=[pl.BlockSpec(memory_space=pl.ANY)] * len(mixed),
            out_specs=[
                pl.BlockSpec((length, lanes), lambda s, *_: (s, 0)),
                pl.BlockSpec((1, heads, length), lambda s, *_: (s, 0, 0)),
            ],
            scratch_shapes=[
                pltpu.VMEM((blocks, tile, 3 * lanes), jnp.bfloat16),
                pltpu.VMEM((pack, length, LANES), jnp.bfloat16),
                pltpu.VMEM((pack, length, LANES), jnp.bfloat16),
                pltpu.SemaphoreType.DMA((blocks,)),
            ],
        ),
        out_shape=[
            jax.ShapeDtypeStruct((rows, lanes), jnp.bfloat16),
            jax.ShapeDtypeStruct((sequences, heads, length), jnp.float32),
        ],
        compiler_params=pltpu.CompilerParams(vmem_limit_bytes=VMEM_BYTES),
        cost_estimate=NO_COST,
    )(counts, slots, *mixed)


def attend_back_kernel(
    head_size,
    blocks_in,
    counts,
    slots,
    *refs,
):
    sources = refs[:blocks_in]
    grad_ref, out_ref, log_ref, own_ref, other_ref, mixed_ref = refs[blocks_in : blocks_in + 6]
    query_own, key_own, grad_own, delta, grad_query, grad_key, grad_value, back_ref, sems = refs[
        blocks_in + 6 :
    ]
    fetch(sources, mixed_ref, sems)
    length, lanes = out_ref.shape
    tile = mixed_ref.shape[1]
    pack = LANES // head_size
    scale = head_size ** (-0.5)
    sequence = pl.program_id(0)
    blocks = lax.div(counts[sequence] + (tile - 1), tile)
    masks = head_masks(head_size)
    for i in range(length // tile):
        back_ref[slots[sequence, i]] = jnp.zeros((tile, 3 * lanes), back_ref.dtype)
    key_row = lax.broadcasted_iota(jnp.int32, (tile, tile), 0)
    query_col = lax.broadcasted_iota(jnp.int32, (tile, tile), 1)
    for pair in range(lanes // LANES):
        base = pair * LANES
        for i in range(length // tile):
            span = slice(i * tile, (i + 1) * tile)
            slot = slots[sequence, i]
            queries = mixed_ref[slot, :, base : base + LANES]
            keys = mixed_ref[slot, :, lanes + base : lanes + base + LANES]
            grads = grad_ref[span, base : base + LANES]
            for h in range(pack):
                query_own[h, span] = jnp.where(masks[h], queries, jnp.zeros_like(queries))
                key_own[h, span] = jnp.where(masks[h], keys, jnp.zeros_like(keys))
                grad_own[h, span] = jnp.where(masks[h], grads, jnp.zeros_like(grads))
        grad_query[...] = jnp.zeros(grad_query.shape, jnp.float32)

        def deltas(i, _, base=base):
            start = pl.multiple_of(i * tile, tile)
            grads = grad_ref[pl.ds(start, tile), base : base + LANES].astype(jnp.float32)
            outs = out_ref[pl.ds(start, tile), base : base + LANES].astype(jnp.float32)
            products = jnp.transpose(grads * outs)
            for h in range(pack):
                delta[h : h + 1, pl.ds(start, tile)] = jnp.sum(
                    products[h * head_size : (h + 1) * head_size], axis=0, keepdims=True
                )
            return 0

        lax.fori_loop(0, blocks, deltas, 0)

        def key_block(j, _, pair=pair, base=base):
            first = pl.multiple_of(j * tile, tile)
            place = slots[sequence, j]
            keys = mixed_ref[place, :, lanes + base : lanes + base + LANES]
            values = mixed_ref[place, :, 2 * lanes + base : 2 * lanes + base + LANES]
            grad_key[...] = jnp.zeros(grad_key.shape, jnp.float32)
            grad_value[...] = jnp.zeros(grad_value.shape, jnp.float32)

            def step(i, diagonal=False):
                start = pl.multiple_of(i * tile, tile)
                add_query, add_key, add_value = [], [], []
                for h in range(pack):
                    index = pair * pack + h
                    query_head = query_own[h, pl.ds(start, tile)]
                    grad_head = grad_own[h, pl.ds(start, tile)]
                    scores = dot_nt(keys, query_head) * (scale * LOG2E)
                    probs = jnp.exp2(scores - log_ref[0, index : index + 1, pl.ds(start, tile)])
                    if diagonal:
                        probs = jnp.where(key_row <= query_col, probs, 0.0)
                    grad_probs = dot_nt(values, grad_head)
                    grad_scores = (
                        probs * (grad_probs - delta[h : h + 1, pl.ds(start, tile)])
                    ).astype(jnp.bfloat16)
                    add_value.append(dot_nn(probs.astype(jnp.bfloat16), grad_head))
                    add_key.append(dot_nn(grad_scores, query_head))
                    add_query.append(dot_tn(grad_scores, key_own[h, pl.ds(first, tile)]))
                grad_value[...] += functools.reduce(jnp.add, add_value)
                grad_key[...] += functools.reduce(jnp.add, add_key)
                grad_query[pl.ds(start, tile), :] += functools.reduce(jnp.add, add_query)

            def off_diagonal(i, _):
                step(i)
                return 0

            step(j, diagonal=True)
            lax.fori_loop(j + 1, blocks, off_diagonal, 0)
            back_ref[place, :, lanes + base : lanes + base + LANES] = (grad_key[...] * scale).astype(
                back_ref.dtype
            )
            back_ref[place, :, 2 * lanes + base : 2 * lanes + base + LANES] = grad_value[...].astype(
                back_ref.dtype
            )
            return 0

        lax.fori_loop(0, blocks, key_block, 0)
        for i in range(length // tile):
            back_ref[slots[sequence, i], :, base : base + LANES] = (
                grad_query[i * tile : (i + 1) * tile] * scale
            ).astype(back_ref.dtype)

    @pl.when(sequence == pl.num_programs(0) - 1)
    def _():
        half = back_ref.shape[0] // 2
        for k in range(half):
            own_ref[k * tile : (k + 1) * tile] = back_ref[k]
            other_ref[k * tile : (k + 1) * tile] = back_ref[half + k]


def attend_back(mixed, slots, grads, outs, logs, counts, head_size):
    sequences = counts.shape[0]
    rows, lanes = outs.shape
    length = rows // sequences
    heads = lanes // head_size
    pack = LANES // head_size
    tile = rows // slots.size
    blocks = rows // tile
    whole = pl.BlockSpec((rows // 2, 3 * lanes), lambda s, *_: (0, 0))
    return pl.pallas_call(
        functools.partial(attend_back_kernel, head_size, len(mixed)),
        grid_spec=pltpu.PrefetchScalarGridSpec(
            num_scalar_prefetch=2,
            grid=(sequences,),
            in_specs=[pl.BlockSpec(memory_space=pl.ANY)] * len(mixed)
            + [
                pl.BlockSpec((length, lanes), lambda s, *_: (s, 0)),
                pl.BlockSpec((length, lanes), lambda s, *_: (s, 0)),
                pl.BlockSpec((1, heads, length), lambda s, *_: (s, 0, 0)),
            ],
            out_specs=[whole, whole],
            scratch_shapes=[
                pltpu.VMEM((blocks, tile, 3 * lanes), jnp.bfloat16),
                pltpu.VMEM((pack, length, LANES), jnp.bfloat16),
                pltpu.VMEM((pack, length, LANES), jnp.bfloat16),
                pltpu.VMEM((pack, length, LANES), jnp.bfloat16),
                pltpu.VMEM((pack, length), jnp.float32),
                pltpu.VMEM((length, LANES), jnp.float32),
                pltpu.VMEM((tile, LANES), jnp.float32),
                pltpu.VMEM((tile, LANES), jnp.float32),
                pltpu.VMEM((blocks, tile, 3 * lanes), jnp.bfloat16),
                pltpu.SemaphoreType.DMA((blocks,)),
            ],
        ),
        out_shape=[jax.ShapeDtypeStruct((rows // 2, 3 * lanes), jnp.bfloat16)] * 2,
        compiler_params=pltpu.CompilerParams(vmem_limit_bytes=VMEM_BYTES),
        cost_estimate=NO_COST,
    )(counts, slots, *mixed, grads, outs, logs)


def ffn_kernel(block, x_parts, g_parts, counts, *refs):
    xs, refs = refs[:x_parts], refs[x_parts:]
    gs, refs = refs[:g_parts], refs[g_parts:]
    ups, downs, shifts = refs[0:2], refs[2:4], refs[4:6]
    units_ref, back_ref, out_ref, x, g, total, x_sems, g_sems = refs[-8:]
    fetch(xs, x, x_sems)
    fetch(gs, g, g_sems)
    blocks, size, model = x.shape
    width = ups[0].shape[0]
    step = pl.program_id(0)

    @pl.when(step == 0)
    def _():
        total[...] = jnp.zeros(total.shape, total.dtype)

    for k in range(blocks):
        rows = slice(k * size, (k + 1) * size)

        @pl.when(counts[block + k] != 0)
        def _(k=k, rows=rows):
            backs = []
            for side in range(2):
                span = slice(side * width, (side + 1) * width)
                pre = dot_nt(x[k], ups[side][...]) + shifts[side][...]
                grad_units = dot_nt(g[k], downs[side][...])
                bell = jnp.exp2(pre * pre * (-0.5 * LOG2E))
                denominator = 1.0 + (0.3275911 * 0.7071067811865476) * jnp.abs(pre)
                t = pl.reciprocal(denominator, approx=True)
                t = t * (2.0 - denominator * t)
                tail = 0.5 * 1.061405429
                for factor in (-1.453152027, 1.421413741, -0.284496736, 0.254829592):
                    tail = tail * t + 0.5 * factor
                tail = tail * t * bell
                below = jnp.where(pre < 0, tail, 1.0 - tail)
                units_ref[rows, span] = (pre * below).astype(units_ref.dtype)
                slope = below + pre * bell * 0.3989422804014327
                backs.append((grad_units * slope).astype(back_ref.dtype))
                back_ref[rows, span] = backs[-1]
            total[rows] += dot_nn(backs[0], ups[0][...]) + dot_nn(backs[1], ups[1][...])

        @pl.when(counts[block + k] == 0)
        def _(rows=rows):
            units_ref[rows] = jnp.zeros((size, 2 * width), units_ref.dtype)
            back_ref[rows] = jnp.zeros((size, 2 * width), back_ref.dtype)

    @pl.when(step == pl.num_programs(0) - 1)
    def _():
        out_ref[...] = total[...].astype(out_ref.dtype)


def ffn_blocks(place, block, counts, xs, gs, ups, downs, shifts, kept):
    size, width = 512, 256
    model = xs[0].shape[1]
    rows = sum(x.shape[0] for x in xs)
    units = ups[0].shape[0]
    whole = pl.BlockSpec(memory_space=pl.ANY)
    weights = pl.BlockSpec((width, model), lambda u, *_: (u, 0))
    shift = pl.BlockSpec((1, width), lambda u, *_: (0, u))
    output = pl.BlockSpec((rows, 2 * width), lambda u, *_: (place, u))
    full = jax.ShapeDtypeStruct((4 * size, 2 * units), jnp.bfloat16)
    return pl.pallas_call(
        functools.partial(ffn_kernel, block, len(xs), len(gs)),
        grid_spec=pltpu.PrefetchScalarGridSpec(
            num_scalar_prefetch=1,
            grid=(units // width,),
            in_specs=[whole] * (len(xs) + len(gs))
            + [weights] * 4
            + [shift] * 2
            + [whole] * len(kept),
            out_specs=[output, output, pl.BlockSpec((rows, model), lambda u, *_: (0, 0))],
            scratch_shapes=[
                pltpu.VMEM((rows // size, size, model), jnp.bfloat16),
                pltpu.VMEM((rows // size, size, model), jnp.bfloat16),
                pltpu.VMEM((rows, model), jnp.float32),
                pltpu.SemaphoreType.DMA((len(xs),)),
                pltpu.SemaphoreType.DMA((len(gs),)),
            ],
        ),
        out_shape=[full, full, jax.ShapeDtypeStruct((rows, model), jnp.bfloat16)],
        input_output_aliases={len(xs) + len(gs) + 7 + k: k for k in range(len(kept))},
        compiler_params=pltpu.CompilerParams(vmem_limit_bytes=VMEM_BYTES),
        cost_estimate=NO_COST,
    )(counts, *xs, *gs, *ups, *downs, *shifts, *kept)


def products_kernel(width, active, left, own, other, out_ref):
    here = active[pl.program_id(0)] != 0

    @pl.when(here)
    def _():
        total = None
        for k in range(own.shape[0] // width):
            rows = slice(k * width, (k + 1) * width)
            for side, right in enumerate((own, other)):
                start = (2 * k + side) * width
                term = dot_nn(left[:, start : start + width], right[rows])
                total = term if total is None else total + term
        out_ref[...] = total.astype(out_ref.dtype)

    @pl.when(jnp.logical_not(here))
    def _():
        out_ref[...] = jnp.zeros(out_ref.shape, out_ref.dtype)


def products(counts, left, own, other):
    blocks = counts.shape[0]
    rows, depth = left.shape
    size = rows // blocks
    columns = own.shape[1]
    return pl.pallas_call(
        functools.partial(products_kernel, 256),
        grid_spec=pltpu.PrefetchScalarGridSpec(
            num_scalar_prefetch=1,
            grid=(blocks,),
            in_specs=[
                pl.BlockSpec((size, depth), lambda i, *_: (i, 0)),
                pl.BlockSpec(own.shape, lambda i, *_: (0, 0)),
                pl.BlockSpec(own.shape, lambda i, *_: (0, 0)),
            ],
            out_specs=pl.BlockSpec((size, columns), lambda i, *_: (i, 0)),
        ),
        out_shape=jax.ShapeDtypeStruct((rows, columns), jnp.bfloat16),
        compiler_params=pltpu.CompilerParams(vmem_limit_bytes=VMEM_BYTES),
        cost_estimate=NO_COST,
    )(counts, left, own, other)


def project_kernel(inputs, side, parts, *refs):
    xs = refs[:inputs]
    weights, shift, out_ref = refs[inputs:]
    slab = weights.shape[1]
    weight = weights[...].reshape(3 * slab, weights.shape[2])
    for k in range(inputs):

        @pl.when(pl.program_id(0) == k)
        def _(k=k):
            mixed = dot_nt(xs[k][...], weight)
            for t in range(3):
                columns = pl.ds(pl.multiple_of(parts[side, t] * slab, slab), slab)
                out_ref[:, columns] = (
                    mixed[:, t * slab : (t + 1) * slab] + shift[:, columns]
                ).astype(out_ref.dtype)


def project(parts, side, xs, weights, shift):
    size, model = xs[0].shape
    slab = weights.shape[1]
    return pl.pallas_call(
        functools.partial(project_kernel, len(xs), side),
        grid_spec=pltpu.PrefetchScalarGridSpec(
            num_scalar_prefetch=1,
            grid=(len(xs),),
            in_specs=[pl.BlockSpec((size, model), lambda i, *_: (0, 0))] * len(xs)
            + [
                pl.BlockSpec(weights.shape, lambda i, *_: (0, 0, 0)),
                pl.BlockSpec(shift.shape, lambda i, *_: (0, 0)),
            ],
            out_specs=pl.BlockSpec((size, 3 * slab), lambda i, *_: (i, 0)),
        ),
        out_shape=jax.ShapeDtypeStruct((len(xs) * size, 3 * slab), jnp.bfloat16),
        compiler_params=pltpu.CompilerParams(vmem_limit_bytes=VMEM_BYTES),
        cost_estimate=NO_COST,
    )(parts, *xs, weights, shift)


def unproject_kernel(parts, active, mine, theirs, own, other, out_ref):
    slab = own.shape[1]
    here = active[pl.program_id(0)] != 0

    @pl.when(here)
    def _():
        total = None
        for side, (left, right) in enumerate(((mine, own), (theirs, other))):
            for t in range(3):
                columns = pl.ds(pl.multiple_of(parts[side, t] * slab, slab), slab)
                term = dot_nn(left[:, columns], right[t])
                total = term if total is None else total + term
        out_ref[...] = total.astype(out_ref.dtype)

    @pl.when(jnp.logical_not(here))
    def _():
        out_ref[...] = jnp.zeros(out_ref.shape, out_ref.dtype)


def unproject(parts, counts, mine, theirs, own, other):
    blocks = counts.shape[0]
    size = mine.shape[0] // blocks
    slab, model = own.shape[1:]
    left = pl.BlockSpec((size, 3 * slab), lambda i, *_: (i, 0))
    fixed = pl.BlockSpec(own.shape, lambda i, *_: (0, 0, 0))
    return pl.pallas_call(
        unproject_kernel,
        grid_spec=pltpu.PrefetchScalarGridSpec(
            num_scalar_prefetch=2,
            grid=(blocks,),
            in_specs=[left, left, fixed, fixed],
            out_specs=pl.BlockSpec((size, model), lambda i, *_: (i, 0)),
        ),
        out_shape=jax.ShapeDtypeStruct((blocks * size, model), jnp.bfloat16),
        compiler_params=pltpu.CompilerParams(vmem_limit_bytes=VMEM_BYTES),
        cost_estimate=NO_COST,
    )(parts, counts, mine, theirs, own, other)


def weight_grad_kernel(inputs, added, columns, *refs):
    left, rights = refs[0], refs[1 : 1 + inputs]
    tokens, sems = refs[-2:]
    outs = refs[1 + inputs + added : -2]
    fetch(rights, tokens, sems)
    total = dot_tn(left[...], tokens[0])
    if added:
        total = total + refs[1 + inputs][...].astype(jnp.float32)
    size = outs[0].shape[0]
    for k, out_ref in enumerate(outs):
        out_ref[...] = total[k * size : (k + 1) * size].astype(out_ref.dtype)


def weight_grad(left, columns, tile, rights, extra=None, outputs=1):
    rows = left.shape[0]
    model = rights[0].shape[1]
    steps = columns.shape[0]
    output = pl.BlockSpec((tile // outputs, model), lambda i, *_: (i, 0))
    extras = [] if extra is None else [extra]
    shape = jax.ShapeDtypeStruct((steps * tile // outputs, model), jnp.bfloat16)
    results = pl.pallas_call(
        functools.partial(weight_grad_kernel, len(rights), len(extras)),
        grid_spec=pltpu.PrefetchScalarGridSpec(
            num_scalar_prefetch=1,
            grid=(steps,),
            in_specs=[pl.BlockSpec((rows, tile), lambda i, columns: (0, columns[i]))]
            + [pl.BlockSpec(memory_space=pl.ANY)] * len(rights)
            + [output] * len(extras),
            out_specs=[output] * outputs,
            scratch_shapes=[
                pltpu.VMEM((1, rows, model), jnp.bfloat16),
                pltpu.SemaphoreType.DMA((len(rights),)),
            ],
        ),
        out_shape=[shape] * outputs,
        compiler_params=pltpu.CompilerParams(vmem_limit_bytes=VMEM_BYTES),
        cost_estimate=NO_COST,
    )(columns, left, *rights, *extras)
    return results[0] if outputs == 1 else results


def chain_sum(values, axis):
    size = lax.axis_size(axis)
    if size != 4:
        return lax.psum(values.astype(jnp.bfloat16), axis).astype(jnp.float32)
    place = lax.axis_index(axis)
    outer = lax.ppermute(values.astype(jnp.bfloat16), axis, [(0, 1), (3, 2)])
    half = (values + outer.astype(jnp.float32)).astype(jnp.bfloat16)
    other = lax.ppermute(half, axis, [(1, 2), (2, 1)])
    whole = (half.astype(jnp.float32) + other.astype(jnp.float32)).astype(jnp.bfloat16)
    ends = lax.ppermute(whole, axis, [(1, 0), (2, 3)])
    inner = (place == 1) | (place == 2)
    return jnp.where(inner, whole, ends).astype(jnp.float32)


class Chain:
    def __init__(self):
        place = lax.axis_index("batch")
        self.inner = (place == 1) | (place == 2)
        self.blocks = (None, None, None)
        self.moved = (None, None, None)
        self.totals = []

    def advance(self, block, *done):
        wide = lambda values: values.astype(jnp.float32)
        first, second, third = self.blocks
        inward, across, outward = after(self.moved, *done)
        half = whole = None
        if first is not None:
            half = (wide(first) + wide(inward)).astype(jnp.bfloat16)
        if second is not None:
            whole = (wide(second) + wide(across)).astype(jnp.bfloat16)
        if third is not None:
            self.totals.append(jnp.where(self.inner, third, outward))
        self.blocks = (block, half, whole)
        pairs = ([(0, 1), (3, 2)], [(1, 2), (2, 1)], [(1, 0), (2, 3)])
        self.moved = tuple(
            None if value is None else lax.ppermute(value, "batch", route)
            for value, route in zip(self.blocks, pairs)
        )
        return [value for value in self.blocks if value is not None]


def normalize(values):
    center = values - jnp.mean(values, axis=-1, keepdims=True)
    inverse = lax.rsqrt(jnp.mean(center * center, axis=-1, keepdims=True) + epsilon)
    return center * inverse, inverse


def normalize_back(grad, gain, normal, inverse):
    scaled = grad * gain
    grad_values = inverse * (
        scaled
        - jnp.mean(scaled, axis=-1, keepdims=True)
        - normal * jnp.mean(scaled * normal, axis=-1, keepdims=True)
    )
    return grad_values, jnp.sum(grad * normal, axis=0), jnp.sum(grad, axis=0)


def local_general(
    hidden,
    cotangent,
    exit_layer,
    ln1_gain,
    ln1_bias,
    qkv_weight,
    query_bias,
    value_bias,
    out_weight,
    out_bias,
    ln2_gain,
    ln2_bias,
    up_weight,
    up_bias,
    down_weight,
    down_bias,
):
    width = lax.axis_size("wide")
    rank = lax.axis_index("wide")
    rows, model = hidden.shape
    group = rows * width
    slab = model // width
    head_size = model // HEADS
    units_own = up_weight.shape[0]
    keep = exit_layer >= LAYER
    counts = jnp.sum(keep.astype(jnp.int32), axis=1)
    active = lax.dynamic_slice_in_dim(keep.reshape(group), rank * rows, rows, 0)
    active = active.astype(jnp.float32)[:, None]
    grad_out = cotangent.astype(jnp.float32)

    routes = [[(w, (3 * w + t) % width) for w in range(width)] for t in range(3)]
    part_at = np.zeros((width, 3), np.int32)
    for t in range(3):
        for w, d in routes[t]:
            part_at[d, t] = (3 * w + t) // width
    place_of = jnp.asarray(np.argsort(part_at, axis=1).astype(np.int32))[rank]
    part_of = jnp.asarray(part_at)[rank]

    hidden_wide = hidden.astype(jnp.float32)
    normal1, inverse1 = normalize(hidden_wide)
    normed1 = lax.all_gather(
        (normal1 * ln1_gain + ln1_bias).astype(jnp.bfloat16), "wide", axis=0, tiled=True
    )
    slabs = qkv_weight.reshape(3, slab, model)
    received = jnp.stack([lax.ppermute(slabs[t], "wide", routes[t]) for t in range(3)])
    qkv_own = jnp.concatenate(
        [lax.dynamic_index_in_dim(received, place_of[p], 0, keepdims=False) for p in range(3)]
    )
    own = lambda vector: lax.dynamic_slice_in_dim(vector, rank * slab, slab, 0)
    qkv_shift = jnp.concatenate(
        [own(query_bias), jnp.zeros((slab,), jnp.float32), own(value_bias)]
    )

    grad_ffn = (active * grad_out).astype(jnp.bfloat16)
    down_bias_grad = jnp.sum(grad_ffn.astype(jnp.float32), axis=0)
    piece = rows // CHUNKS
    part = lambda values, c: values[c * piece : (c + 1) * piece]
    gather = lambda values: lax.all_gather(values, "wide", axis=0, tiled=True)
    scatter = lambda values: lax.psum_scatter(
        values.astype(jnp.bfloat16), "wide", scatter_dimension=0, tiled=True
    )
    grad_ffns = [gather(part(grad_ffn, c)) for c in range(CHUNKS)]
    out_whole = gather(out_weight)

    mixed = (dot_nt(normed1, qkv_own) + qkv_shift).astype(jnp.bfloat16)
    mixed = jnp.split(mixed, group // TILE)
    slots = jnp.arange(group // TILE, dtype=jnp.int32).reshape(counts.shape[0], -1)
    attended, logs = attend(mixed, slots, counts, head_size)
    attended_rows = lax.all_to_all(attended, "wide", split_axis=0, concat_axis=1, tiled=True)
    middle = hidden_wide + active * (dot_nn(attended_rows, out_whole) + out_bias)
    normal2, inverse2 = normalize(middle)
    normed2 = (normal2 * ln2_gain + ln2_bias).astype(jnp.bfloat16)
    up_shift = lax.dynamic_slice_in_dim(up_bias, rank * units_own, units_own, 0)

    normed2s = [gather(part(normed2, c)) for c in range(CHUNKS)]
    units, grad_pres, grad_normed2, ffn_out = [], [], [], []
    for c in range(CHUNKS):
        grad_units = dot_nt(grad_ffns[c], down_weight)
        pre = dot_nt(normed2s[c], up_weight) + up_shift
        below = 0.5 + 0.5 * lax.erf(pre * 0.7071067811865476)
        bell = jnp.exp(-0.5 * pre * pre) * 0.3989422804014327
        units.append((pre * below).astype(jnp.bfloat16))
        grad_pres.append((grad_units * (below + pre * bell)).astype(jnp.bfloat16))
        grad_normed2.append(scatter(dot_nn(grad_pres[c], up_weight)))
    for c in range(CHUNKS):
        ffn_out.append(scatter(dot_nn(units[c], down_weight)))
    grad_normed2 = jnp.concatenate(grad_normed2).astype(jnp.float32)
    ffn_out = jnp.concatenate(ffn_out).astype(jnp.float32)
    output = (middle + active * (ffn_out + down_bias)).astype(jnp.bfloat16)

    up_bias_own = sum(jnp.sum(g.astype(jnp.float32), axis=0) for g in grad_pres)
    down_grad = sum(dot_tn(units[c], grad_ffns[c]) for c in range(CHUNKS))
    up_grad = sum(dot_tn(grad_pres[c], normed2s[c]) for c in range(CHUNKS))
    halves = lambda values: jnp.concatenate(
        [chain_sum(half, "batch") for half in jnp.split(values, 2)]
    )
    down_grad = halves(down_grad)
    up_grad = halves(up_grad)

    grad_middle, ln2_gain_grad, ln2_bias_grad = normalize_back(
        grad_normed2, ln2_gain, normal2, inverse2
    )
    grad_middle = grad_out + grad_middle
    grad_branch = (active * grad_middle).astype(jnp.bfloat16)
    out_bias_grad = jnp.sum(grad_branch.astype(jnp.float32), axis=0)
    grad_attended = dot_nt(grad_branch, out_whole).astype(jnp.bfloat16)
    grad_heads = lax.all_to_all(grad_attended, "wide", split_axis=1, concat_axis=0, tiled=True)
    out_grad = chain_sum(scatter(dot_tn(attended_rows, grad_branch)).astype(jnp.float32), "batch")

    placed = lambda vector, size: lax.dynamic_update_slice_in_dim(
        jnp.zeros((size,), jnp.float32), vector, rank * vector.shape[0], 0
    )
    early = lax.psum(
        (
            out_bias_grad,
            ln2_gain_grad,
            ln2_bias_grad,
            placed(up_bias_own, up_bias.shape[0]),
            down_bias_grad,
        ),
        ("batch", "wide"),
    )

    grad_mixed = jnp.concatenate(
        attend_back(mixed, slots, grad_heads, attended, logs, counts, head_size)
    )
    grad_normed1 = scatter(dot_nn(grad_mixed, qkv_own)).astype(jnp.float32)
    sums = jnp.sum(grad_mixed.astype(jnp.float32), axis=0)
    qkv_parts = []
    for t in range(3):
        columns = lax.dynamic_slice_in_dim(grad_mixed, part_of[t] * slab, slab, 1)
        total = chain_sum(dot_tn(columns, normed1), "batch").astype(jnp.bfloat16)
        back = [(d, w) for w, d in routes[t]]
        qkv_parts.append(lax.ppermute(total, "wide", back).astype(jnp.float32))
    qkv_grad = jnp.concatenate(qkv_parts)

    grad_hidden, ln1_gain_grad, ln1_bias_grad = normalize_back(
        grad_normed1, ln1_gain, normal1, inverse1
    )
    input_grad = grad_middle + grad_hidden
    late = lax.psum(
        (
            ln1_gain_grad,
            ln1_bias_grad,
            placed(sums[:slab], model),
            placed(sums[2 * slab :], model),
        ),
        ("batch", "wide"),
    )
    return (
        output,
        input_grad,
        late[0],
        late[1],
        qkv_grad,
        late[2],
        late[3],
        out_grad,
        early[0],
        early[1],
        early[2],
        up_grad,
        early[3],
        down_grad,
        early[4],
    )


def swap(values, bits):
    width = lax.axis_size("wide")
    return lax.ppermute(values, "wide", [(w, w ^ bits) for w in range(width)])


def after(values, *done):
    return lax.optimization_barrier((values, done))[0]


def relay(along_x, along_y):
    half = along_x.shape[0] // 2
    return [swap(along_y[:half], 2), swap(along_x[half:], 4)]


class Scatter:
    def __init__(self, own, along_x, along_y, diagonal):
        self.half = half = own.shape[0] // 2
        self.own, self.along_x, self.along_y = own, along_x, along_y
        self.sent = (
            jnp.concatenate([diagonal[:half], along_x[:half]]),
            jnp.concatenate([diagonal[half:], along_y[half:]]),
        )
        self.from_x, self.from_y = swap(self.sent[0], 2), swap(self.sent[1], 4)

    def second(self, *done):
        half = self.half
        from_x, from_y = after((self.from_x, self.from_y), *done)
        self.near = (from_x[half:], from_y[half:])
        return self.forward(from_x[:half], from_y[:half])

    def forward(self, top, bottom):
        wide = lambda values: values.astype(jnp.float32)
        half = self.half
        y_top = (wide(self.along_y[:half]) + wide(top)).astype(jnp.bfloat16)
        x_bottom = (wide(self.along_x[half:]) + wide(bottom)).astype(jnp.bfloat16)
        self.last = (swap(y_top, 4), swap(x_bottom, 2))
        return y_top, x_bottom

    def finish(self, *done):
        wide = lambda values: values.astype(jnp.float32)
        y_top, x_bottom = after(self.last, *done)
        x_top, y_bottom = self.near
        return jnp.concatenate(
            [
                wide(self.own[: self.half]) + wide(x_top) + wide(y_top),
                wide(self.own[self.half :]) + wide(x_bottom) + wide(y_bottom),
            ]
        )


class EarlyScatter(Scatter):
    def __init__(self, own, along_x, along_y):
        self.half = half = own.shape[0] // 2
        self.own, self.along_x, self.along_y = own, along_x, along_y
        self.near = (swap(along_x[:half], 2), swap(along_y[half:], 4))

    def first(self, diagonal):
        self.from_far = (swap(diagonal[: self.half], 2), swap(diagonal[self.half :], 4))
        self.near = after(self.near, diagonal)
        return self.near

    def second(self, *done):
        return self.forward(*after(self.from_far, *done))


def tree_sum(values):
    total = values + swap(values, 1)
    total = (total + swap(total, 2)) + (swap(total, 4) + swap(total, 6))
    size = lax.axis_size("batch")
    terms = [total] + [
        lax.ppermute(total, "batch", [(z, z ^ bits) for z in range(size)])
        for bits in range(1, size)
    ]
    while len(terms) > 1:
        terms = [terms[k] + terms[k + 1] for k in range(0, len(terms), 2)]
    return terms[0]


def local_chips(
    hidden,
    cotangent,
    exit_layer,
    ln1_gain,
    ln1_bias,
    qkv_weight,
    query_bias,
    value_bias,
    out_weight,
    out_bias,
    ln2_gain,
    ln2_bias,
    up_weight,
    up_bias,
    down_weight,
    down_bias,
):
    width = lax.axis_size("wide")
    rank = lax.axis_index("wide")
    rows, model = hidden.shape
    group = rows * width
    slab = model // width
    head_size = model // HEADS
    units_own = up_weight.shape[0]
    keep = exit_layer >= LAYER
    counts = jnp.sum(keep.astype(jnp.int32), axis=1)
    active = lax.dynamic_slice_in_dim(keep.reshape(group), rank * rows, rows, 0)
    active = active.astype(jnp.float32)[:, None]
    grad_out = cotangent.astype(jnp.float32)

    tiles = jnp.arange(group // rows, dtype=jnp.int32)
    slots = ((tiles ^ rank) & 1) * 4 + ((tiles >> 1) ^ (rank >> 1))
    slots = slots.reshape(counts.shape[0], -1)

    routes = [[(w, (3 * w + t) % width) for w in range(width)] for t in range(3)]
    part_at = np.zeros((width, 3), np.int32)
    for t in range(3):
        for w, d in routes[t]:
            part_at[d, t] = (3 * w + t) // width
    part_at = jnp.asarray(part_at)
    other = rank ^ 1
    parts = jnp.stack([part_at[rank], part_at[other]])

    hidden_wide = hidden.astype(jnp.float32)
    normal1, inverse1 = normalize(hidden_wide)
    slabs = qkv_weight.reshape(3, slab, model)
    slabs = [lax.ppermute(slabs[t], "wide", routes[t]) for t in range(3)]
    normed1 = (normal1 * ln1_gain + ln1_bias).astype(jnp.bfloat16)
    normed1 = [normed1, swap(normed1, 2), swap(normed1, 4)]
    diagonal1 = relay(normed1[1], normed1[2])
    qkv_own = jnp.stack(after(slabs, normed1[1:]))
    qkv_other = swap(qkv_own, 1)

    def shift_of(device):
        own = lambda vector: lax.dynamic_slice_in_dim(vector, device * slab, slab, 0)
        shift = [own(query_bias), jnp.zeros((slab,), jnp.float32), own(value_bias)]
        return jnp.concatenate(shift)[None]

    bias_of = lambda device: lax.dynamic_slice_in_dim(up_bias, device * units_own, units_own, 0)
    up_shifts = [bias_of(rank)[None], bias_of(other)[None]]

    mixed_near = project(parts, 0, normed1, qkv_own, shift_of(rank))
    qkv_other = after(qkv_other, mixed_near)
    lent_near = project(parts, 1, normed1, qkv_other, shift_of(other))
    diagonal1 = after(diagonal1, lent_near)
    lent_far = project(parts, 1, diagonal1, qkv_other, shift_of(other))
    mixed_far = project(parts, 0, after(diagonal1, lent_far), qkv_own, shift_of(rank))
    mixed = [mixed_near, mixed_far, swap(lent_near, 1), swap(lent_far, 1)]

    out_whole = lax.all_gather(after(out_weight, diagonal1), "wide", axis=0, tiled=True)
    grad_ffn = (after(active, diagonal1) * grad_out).astype(jnp.bfloat16)
    down_bias_grad = jnp.sum(grad_ffn.astype(jnp.float32), axis=0)
    grad_ffn = [grad_ffn, swap(grad_ffn, 2), swap(grad_ffn, 4)]

    attended, logs = attend(mixed, slots, counts, head_size)
    attended_rows = lax.all_to_all(attended, "wide", split_axis=0, concat_axis=1, tiled=True)
    attended_rows = after(attended_rows, grad_ffn[1:])
    up_other, down_other = swap(after((up_weight, down_weight), attended), 1)
    middle = hidden_wide + active * (dot_nn(attended_rows, out_whole) + out_bias)
    normal2, inverse2 = normalize(middle)
    normed2 = (normal2 * ln2_gain + ln2_bias).astype(jnp.bfloat16)
    normed2 = [normed2, swap(normed2, 2), swap(normed2, 4)]

    per_tile = jnp.sum(keep.reshape(group // rows, rows).astype(jnp.int32), axis=1)
    block_chip = (rank >> 1) ^ jnp.arange(4, dtype=jnp.int32)
    block_counts = per_tile[2 * block_chip + (rank & 1)]
    ups, downs = [up_weight, up_other], [down_weight, down_other]

    def ffn(place, block, xs, gs, kept):
        *kept, partial = ffn_blocks(
            place, block, block_counts, xs, gs, ups, downs, up_shifts, tuple(kept)
        )
        return kept, partial

    kept, partial_own = ffn(2, 0, normed2[:1], grad_ffn[:1], ())
    normed2[1:] = after(normed2[1:], partial_own)
    diagonal2 = relay(normed2[1], normed2[2])
    diagonal_ffn = relay(*after(grad_ffn[1:], attended_rows))
    kept, partial_near = ffn(0, 1, normed2[1:], grad_ffn[1:], kept)
    scatter2 = EarlyScatter(partial_own, partial_near[:rows], partial_near[rows:])
    diagonal2 = after(diagonal2, partial_near)
    (units, grad_pres), partial_far = ffn(3, 3, diagonal2, diagonal_ffn, kept)
    wait = scatter2.first(partial_far)
    tokens2 = [*normed2[1:], normed2[0], *diagonal2]
    tokens_ffn = [*grad_ffn[1:], grad_ffn[0], *diagonal_ffn]

    wide = lambda values: values.astype(jnp.float32)
    lowered = lambda values: values.astype(jnp.bfloat16)
    tile = 512
    tiles = jnp.arange(2 * units_own // tile, dtype=jnp.int32)
    chain = Chain()

    down_own, down_lent = weight_grad(after(units, wait), tiles, tile, tokens_ffn, outputs=2)
    wait = scatter2.second(down_lent)
    down_lent = swap(down_lent, 1)
    up_own, up_lent = weight_grad(after(grad_pres, wait), tiles, tile, tokens2, outputs=2)

    up_lent = swap(up_lent, 1)
    down_sum = lowered(wide(down_own) + wide(after(down_lent, up_own)))
    wait = chain.advance(down_sum[:tile], down_sum)
    grad_middle, ln2_gain_grad, ln2_bias_grad = normalize_back(
        scatter2.finish(up_own), ln2_gain, normal2, inverse2
    )
    grad_middle = grad_out + grad_middle
    grad_branch = (active * grad_middle).astype(jnp.bfloat16)
    out_bias_grad = jnp.sum(grad_branch.astype(jnp.float32), axis=0)
    grad_attended = dot_nt(after(grad_branch, wait), out_whole).astype(jnp.bfloat16)
    grad_heads = lax.all_to_all(grad_attended, "wide", split_axis=1, concat_axis=0, tiled=True)
    owners = 2 * block_chip + (rank & 1)
    grad_branch = after(grad_branch, grad_attended)
    out_lent = weight_grad(attended_rows, owners ^ 1, slab, [grad_branch])
    out_lent = swap(out_lent, 1)
    up_sum = lowered(wide(up_own) + wide(after(up_lent, out_lent)))
    out_own = weight_grad(after(attended_rows, up_sum), owners, slab, [grad_branch], out_lent)

    wait = chain.advance(down_sum[tile:], out_own)
    scatter_out = Scatter(*jnp.split(out_own, 4))
    back_own, back_other = attend_back(
        mixed, slots, after(grad_heads, wait, scatter_out.sent), attended, logs, counts, head_size
    )

    theirs = swap(back_other, 1)
    wait = chain.advance(up_sum[:tile], back_own)
    tokens1 = [*normed1, *diagonal1]
    qkv_own_grad = weight_grad(after(back_own, wait), parts[0], slab, tokens1)
    wait = scatter_out.second(qkv_own_grad)
    theirs = after(theirs, wait)
    qkv_lent = weight_grad(theirs, parts[1], slab, tokens1)
    grad_normed1 = unproject(
        parts, block_counts, after(back_own, qkv_lent), theirs, qkv_own, qkv_other
    )
    qkv_lent = swap(qkv_lent, 1)

    scatter1 = Scatter(*jnp.split(grad_normed1, 4))
    wait = chain.advance(up_sum[tile:], grad_normed1)
    ffn_counts = block_counts[jnp.array([1, 2, 0, 3])]
    ffn_out = products(ffn_counts, after(units, wait, scatter1.sent), *downs)

    qkv_total = lowered(wide(qkv_own_grad) + wide(after(qkv_lent, ffn_out)))
    wait = scatter1.second(ffn_out)
    wait = chain.advance(qkv_total[: 2 * slab], ffn_out, wait)
    out_total = lowered(scatter_out.finish(wait))
    grad_pres, back_own, back_other = after((grad_pres, back_own, back_other), wait)
    up_bias_own = jnp.sum(wide(grad_pres), axis=0).reshape(-1, 2, 256)
    up_bias_own = [up_bias_own[:, side].reshape(units_own) for side in range(2)]
    sums = jnp.sum(wide(back_own), axis=0) + jnp.sum(wide(back_other), axis=0)
    along_x, along_y, own, diagonal = jnp.split(after(ffn_out, wait), 4)

    wait = chain.advance(
        jnp.concatenate([qkv_total[2 * slab :], out_total]), up_bias_own, sums, along_x
    )
    grad_normed1 = scatter1.finish(wait)
    scatter_ffn = Scatter(own, along_x, along_y, after(diagonal, grad_normed1))
    grad_hidden, ln1_gain_grad, ln1_bias_grad = normalize_back(
        grad_normed1, ln1_gain, normal1, inverse1
    )
    input_grad = grad_middle + grad_hidden

    wait = chain.advance(None, input_grad, scatter_ffn.sent)
    wait = scatter_ffn.second(wait)
    wait = chain.advance(None, wait)
    ffn_out = scatter_ffn.finish(wait)
    output = (middle + active * (ffn_out + down_bias)).astype(jnp.bfloat16)
    chain.advance(None, output)
    totals = after(chain.totals, output)
    down_grad = wide(jnp.concatenate(totals[0:2]))
    up_grad = wide(jnp.concatenate(totals[2:4]))
    qkv_totals = [totals[4][:slab], totals[4][slab:], totals[5][:slab]]
    qkv_grad = jnp.concatenate(
        [
            wide(lax.ppermute(qkv_totals[t], "wide", [(d, w) for w, d in routes[t]]))
            for t in range(3)
        ]
    )
    out_grad = wide(totals[5][slab:])

    placed = lambda vector, size, device: lax.dynamic_update_slice_in_dim(
        jnp.zeros((size,), jnp.float32), vector, device * vector.shape[0], 0
    )
    smalls = tree_sum(
        jnp.concatenate(
            [
                placed(up_bias_own[0], up_bias.shape[0], rank)
                + placed(up_bias_own[1], up_bias.shape[0], other),
                down_bias_grad,
                out_bias_grad,
                ln2_gain_grad,
                ln2_bias_grad,
                placed(sums[:slab], model, rank),
                placed(sums[2 * slab :], model, rank),
                ln1_gain_grad,
                ln1_bias_grad,
            ]
        )
    )
    up_bias_grad = smalls[: up_bias.shape[0]]
    smalls = smalls[up_bias.shape[0] :].reshape(8, model)
    return (
        output,
        input_grad,
        smalls[6],
        smalls[7],
        qkv_grad,
        smalls[4],
        smalls[5],
        out_grad,
        smalls[1],
        smalls[2],
        smalls[3],
        up_grad,
        up_bias_grad,
        down_grad,
        smalls[0],
    )


def solution(mesh):
    chips = mesh.shape["wide"] == 8 and mesh.shape["batch"] == 4
    local = local_chips if chips else local_general
    rows = P(("batch", "wide"), None)
    weight = P("wide", None)
    return jax.shard_map(
        local,
        mesh=mesh,
        in_specs=(
            rows,
            rows,
            P("batch", None),
            P(),
            P(),
            weight,
            P(),
            P(),
            weight,
            P(),
            P(),
            P(),
            weight,
            P(),
            weight,
            P(),
        ),
        out_specs=(
            rows,
            rows,
            P(),
            P(),
            weight,
            P(),
            P(),
            weight,
            P(),
            P(),
            P(),
            weight,
            P(),
            weight,
            P(),
        ),
        check_vma=False,
    )
```

```python
import functools

import jax
import jax.numpy as jnp
import numpy as np
from jax import lax
from jax.experimental import pallas as pl
from jax.experimental.pallas import tpu as pltpu
from jax.sharding import PartitionSpec as P

HEADS = 32
LAYER = 12
LANES = 128
TILE = 512
CHUNKS = 2
LOG2E = 1.4426950408889634

epsilon = 1e-05
VMEM_BYTES = 48 * 2**20
NO_COST = pl.CostEstimate(flops=1, bytes_accessed=1, transcendentals=0)


def dot_nt(left, right):
    return lax.dot_general(
        left, right, (((1,), (1,)), ((), ())), preferred_element_type=jnp.float32
    )


def dot_nn(left, right):
    return lax.dot_general(
        left, right, (((1,), (0,)), ((), ())), preferred_element_type=jnp.float32
    )


def dot_tn(left, right):
    return lax.dot_general(
        left, right, (((0,), (0,)), ((), ())), preferred_element_type=jnp.float32
    )


def head_masks(head_size):
    lane = lax.broadcasted_iota(jnp.int32, (1, LANES), 1)
    return [
        (lane >= h * head_size) & (lane < (h + 1) * head_size)
        for h in range(LANES // head_size)
    ]


def fetch(sources, target, sems):
    size = target.shape[1]
    copies = []
    row = 0
    for source in sources:
        rows = source.shape[0]
        least = min(rows, size)
        for k in range(rows // least):
            place = target.at[row // size, pl.ds(row % size, least)]
            copies.append(
                pltpu.make_async_copy(source.at[pl.ds(k * least, least)], place, sems.at[len(copies)])
            )
            row += least

    @pl.when(pl.program_id(0) == 0)
    def _():
        for copy in copies:
            copy.start()
        for copy in copies:
            copy.wait()


def attend_kernel(head_size, blocks_in, counts, slots, *refs):
    sources = refs[:blocks_in]
    out_ref, log_ref, mixed_ref, key_own, value_own, sems = refs[blocks_in:]
    fetch(sources, mixed_ref, sems)
    length, lanes = out_ref.shape
    tile = mixed_ref.shape[1]
    pack = LANES // head_size
    scale = head_size ** (-0.5) * LOG2E
    sequence = pl.program_id(0)
    blocks = lax.div(counts[sequence] + (tile - 1), tile)
    masks = head_masks(head_size)
    out_ref[...] = jnp.zeros(out_ref.shape, out_ref.dtype)
    log_ref[...] = jnp.zeros(log_ref.shape, log_ref.dtype)
    row = lax.broadcasted_iota(jnp.int32, (tile, tile), 0)
    col = lax.broadcasted_iota(jnp.int32, (tile, tile), 1)
    for pair in range(lanes // LANES):
        base = pair * LANES
        for i in range(length // tile):
            slot = slots[sequence, i]
            keys = mixed_ref[slot, :, lanes + base : lanes + base + LANES]
            values = mixed_ref[slot, :, 2 * lanes + base : 2 * lanes + base + LANES]
            for h in range(pack):
                key_own[h, i * tile : (i + 1) * tile] = jnp.where(masks[h], keys, jnp.zeros_like(keys))
                value_own[h, i * tile : (i + 1) * tile] = jnp.where(
                    masks[h], values, jnp.zeros_like(values)
                )

        def query_block(i, _, pair=pair, base=base):
            start = pl.multiple_of(i * tile, tile)
            queries = mixed_ref[slots[sequence, i], :, base : base + LANES]

            def step(j, carry, diagonal=False):
                total, tops, sums = carry
                first = pl.multiple_of(j * tile, tile)
                new_tops, new_sums, shrinks, adds = [], [], [], []
                for h in range(pack):
                    scores = dot_nt(queries, key_own[h, pl.ds(first, tile)]) * scale
                    if diagonal:
                        scores = jnp.where(col <= row, scores, -1e30)
                    top = jnp.maximum(tops[h], jnp.max(scores, axis=1, keepdims=True))
                    terms = jnp.exp2(scores - top)
                    shrink = jnp.exp2(tops[h] - top)
                    new_tops.append(top)
                    new_sums.append(sums[h] * shrink + jnp.sum(terms, axis=1, keepdims=True))
                    shrinks.append(shrink)
                    adds.append(dot_nn(terms.astype(jnp.bfloat16), value_own[h, pl.ds(first, tile)]))
                shrink = shrinks[0]
                for h in range(1, pack):
                    shrink = jnp.where(masks[h], shrinks[h], shrink)
                total = total * shrink
                for add in adds:
                    total = total + add
                return total, tuple(new_tops), tuple(new_sums)

            carry = (
                jnp.zeros((tile, LANES), jnp.float32),
                tuple(jnp.full((tile, 1), -1e30, jnp.float32) for _ in range(pack)),
                tuple(jnp.zeros((tile, 1), jnp.float32) for _ in range(pack)),
            )
            carry = lax.fori_loop(0, i, step, carry)
            total, tops, sums = step(i, carry, diagonal=True)
            share = 1.0 / sums[0]
            for h in range(1, pack):
                share = jnp.where(masks[h], 1.0 / sums[h], share)
            out_ref[pl.ds(start, tile), base : base + LANES] = (total * share).astype(out_ref.dtype)
            for h in range(pack):
                logs = jnp.broadcast_to(tops[h] + jnp.log2(sums[h]), (tile, LANES))
                index = pair * pack + h
                log_ref[0, index : index + 1, pl.ds(start, tile)] = jnp.transpose(logs)[0:1]
            return 0

        lax.fori_loop(0, blocks, query_block, 0)


def attend(mixed, slots, counts, head_size):
    sequences = counts.shape[0]
    rows = sum(part.shape[0] for part in mixed)
    tile = rows // slots.size
    blocks = rows // tile
    lanes = mixed[0].shape[1] // 3
    length = rows // sequences
    heads = lanes // head_size
    pack = LANES // head_size
    return pl.pallas_call(
        functools.partial(attend_kernel, head_size, len(mixed)),
        grid_spec=pltpu.PrefetchScalarGridSpec(
            num_scalar_prefetch=2,
            grid=(sequences,),
            in_specs=[pl.BlockSpec(memory_space=pl.ANY)] * len(mixed),
            out_specs=[
                pl.BlockSpec((length, lanes), lambda s, *_: (s, 0)),
                pl.BlockSpec((1, heads, length), lambda s, *_: (s, 0, 0)),
            ],
            scratch_shapes=[
                pltpu.VMEM((blocks, tile, 3 * lanes), jnp.bfloat16),
                pltpu.VMEM((pack, length, LANES), jnp.bfloat16),
                pltpu.VMEM((pack, length, LANES), jnp.bfloat16),
                pltpu.SemaphoreType.DMA((blocks,)),
            ],
        ),
        out_shape=[
            jax.ShapeDtypeStruct((rows, lanes), jnp.bfloat16),
            jax.ShapeDtypeStruct((sequences, heads, length), jnp.float32),
        ],
        compiler_params=pltpu.CompilerParams(vmem_limit_bytes=VMEM_BYTES),
        cost_estimate=NO_COST,
    )(counts, slots, *mixed)


def attend_back_kernel(
    head_size,
    blocks_in,
    counts,
    slots,
    *refs,
):
    sources = refs[:blocks_in]
    grad_ref, out_ref, log_ref, own_ref, other_ref, mixed_ref = refs[blocks_in : blocks_in + 6]
    query_own, key_own, grad_own, delta, grad_query, grad_key, grad_value, back_ref, sems = refs[
        blocks_in + 6 :
    ]
    fetch(sources, mixed_ref, sems)
    length, lanes = out_ref.shape
    tile = mixed_ref.shape[1]
    pack = LANES // head_size
    scale = head_size ** (-0.5)
    sequence = pl.program_id(0)
    blocks = lax.div(counts[sequence] + (tile - 1), tile)
    masks = head_masks(head_size)
    for i in range(length // tile):
        back_ref[slots[sequence, i]] = jnp.zeros((tile, 3 * lanes), back_ref.dtype)
    key_row = lax.broadcasted_iota(jnp.int32, (tile, tile), 0)
    query_col = lax.broadcasted_iota(jnp.int32, (tile, tile), 1)
    for pair in range(lanes // LANES):
        base = pair * LANES
        for i in range(length // tile):
            span = slice(i * tile, (i + 1) * tile)
            slot = slots[sequence, i]
            queries = mixed_ref[slot, :, base : base + LANES]
            keys = mixed_ref[slot, :, lanes + base : lanes + base + LANES]
            grads = grad_ref[span, base : base + LANES]
            for h in range(pack):
                query_own[h, span] = jnp.where(masks[h], queries, jnp.zeros_like(queries))
                key_own[h, span] = jnp.where(masks[h], keys, jnp.zeros_like(keys))
                grad_own[h, span] = jnp.where(masks[h], grads, jnp.zeros_like(grads))
        grad_query[...] = jnp.zeros(grad_query.shape, jnp.float32)

        def deltas(i, _, base=base):
            start = pl.multiple_of(i * tile, tile)
            grads = grad_ref[pl.ds(start, tile), base : base + LANES].astype(jnp.float32)
            outs = out_ref[pl.ds(start, tile), base : base + LANES].astype(jnp.float32)
            products = jnp.transpose(grads * outs)
            for h in range(pack):
                delta[h : h + 1, pl.ds(start, tile)] = jnp.sum(
                    products[h * head_size : (h + 1) * head_size], axis=0, keepdims=True
                )
            return 0

        lax.fori_loop(0, blocks, deltas, 0)

        def key_block(j, _, pair=pair, base=base):
            first = pl.multiple_of(j * tile, tile)
            place = slots[sequence, j]
            keys = mixed_ref[place, :, lanes + base : lanes + base + LANES]
            values = mixed_ref[place, :, 2 * lanes + base : 2 * lanes + base + LANES]
            grad_key[...] = jnp.zeros(grad_key.shape, jnp.float32)
            grad_value[...] = jnp.zeros(grad_value.shape, jnp.float32)

            def step(i, diagonal=False):
                start = pl.multiple_of(i * tile, tile)
                add_query, add_key, add_value = [], [], []
                for h in range(pack):
                    index = pair * pack + h
                    query_head = query_own[h, pl.ds(start, tile)]
                    grad_head = grad_own[h, pl.ds(start, tile)]
                    scores = dot_nt(keys, query_head) * (scale * LOG2E)
                    probs = jnp.exp2(scores - log_ref[0, index : index + 1, pl.ds(start, tile)])
                    if diagonal:
                        probs = jnp.where(key_row <= query_col, probs, 0.0)
                    grad_probs = dot_nt(values, grad_head)
                    grad_scores = (
                        probs * (grad_probs - delta[h : h + 1, pl.ds(start, tile)])
                    ).astype(jnp.bfloat16)
                    add_value.append(dot_nn(probs.astype(jnp.bfloat16), grad_head))
                    add_key.append(dot_nn(grad_scores, query_head))
                    add_query.append(dot_tn(grad_scores, key_own[h, pl.ds(first, tile)]))
                grad_value[...] += functools.reduce(jnp.add, add_value)
                grad_key[...] += functools.reduce(jnp.add, add_key)
                grad_query[pl.ds(start, tile), :] += functools.reduce(jnp.add, add_query)

            def off_diagonal(i, _):
                step(i)
                return 0

            step(j, diagonal=True)
            lax.fori_loop(j + 1, blocks, off_diagonal, 0)
            back_ref[place, :, lanes + base : lanes + base + LANES] = (grad_key[...] * scale).astype(
                back_ref.dtype
            )
            back_ref[place, :, 2 * lanes + base : 2 * lanes + base + LANES] = grad_value[...].astype(
                back_ref.dtype
            )
            return 0

        lax.fori_loop(0, blocks, key_block, 0)
        for i in range(length // tile):
            back_ref[slots[sequence, i], :, base : base + LANES] = (
                grad_query[i * tile : (i + 1) * tile] * scale
            ).astype(back_ref.dtype)

    @pl.when(sequence == pl.num_programs(0) - 1)
    def _():
        half = back_ref.shape[0] // 2
        for k in range(half):
            own_ref[k * tile : (k + 1) * tile] = back_ref[k]
            other_ref[k * tile : (k + 1) * tile] = back_ref[half + k]


def attend_back(mixed, slots, grads, outs, logs, counts, head_size):
    sequences = counts.shape[0]
    rows, lanes = outs.shape
    length = rows // sequences
    heads = lanes // head_size
    pack = LANES // head_size
    tile = rows // slots.size
    blocks = rows // tile
    whole = pl.BlockSpec((rows // 2, 3 * lanes), lambda s, *_: (0, 0))
    return pl.pallas_call(
        functools.partial(attend_back_kernel, head_size, len(mixed)),
        grid_spec=pltpu.PrefetchScalarGridSpec(
            num_scalar_prefetch=2,
            grid=(sequences,),
            in_specs=[pl.BlockSpec(memory_space=pl.ANY)] * len(mixed)
            + [
                pl.BlockSpec((length, lanes), lambda s, *_: (s, 0)),
                pl.BlockSpec((length, lanes), lambda s, *_: (s, 0)),
                pl.BlockSpec((1, heads, length), lambda s, *_: (s, 0, 0)),
            ],
            out_specs=[whole, whole],
            scratch_shapes=[
                pltpu.VMEM((blocks, tile, 3 * lanes), jnp.bfloat16),
                pltpu.VMEM((pack, length, LANES), jnp.bfloat16),
                pltpu.VMEM((pack, length, LANES), jnp.bfloat16),
                pltpu.VMEM((pack, length, LANES), jnp.bfloat16),
                pltpu.VMEM((pack, length), jnp.float32),
                pltpu.VMEM((length, LANES), jnp.float32),
                pltpu.VMEM((tile, LANES), jnp.float32),
                pltpu.VMEM((tile, LANES), jnp.float32),
                pltpu.VMEM((blocks, tile, 3 * lanes), jnp.bfloat16),
                pltpu.SemaphoreType.DMA((blocks,)),
            ],
        ),
        out_shape=[jax.ShapeDtypeStruct((rows // 2, 3 * lanes), jnp.bfloat16)] * 2,
        compiler_params=pltpu.CompilerParams(vmem_limit_bytes=VMEM_BYTES),
        cost_estimate=NO_COST,
    )(counts, slots, *mixed, grads, outs, logs)


def ffn_kernel(block, x_parts, g_parts, counts, *refs):
    xs, refs = refs[:x_parts], refs[x_parts:]
    gs, refs = refs[:g_parts], refs[g_parts:]
    ups, downs, shifts = refs[0:2], refs[2:4], refs[4:6]
    units_ref, back_ref, out_ref, x, g, total, x_sems, g_sems = refs[-8:]
    fetch(xs, x, x_sems)
    fetch(gs, g, g_sems)
    blocks, size, model = x.shape
    width = ups[0].shape[0]
    step = pl.program_id(0)

    @pl.when(step == 0)
    def _():
        total[...] = jnp.zeros(total.shape, total.dtype)

    for k in range(blocks):
        rows = slice(k * size, (k + 1) * size)

        @pl.when(counts[block + k] != 0)
        def _(k=k, rows=rows):
            backs = []
            for side in range(2):
                span = slice(side * width, (side + 1) * width)
                pre = dot_nt(x[k], ups[side][...]) + shifts[side][...]
                grad_units = dot_nt(g[k], downs[side][...])
                bell = jnp.exp2(pre * pre * (-0.5 * LOG2E))
                denominator = 1.0 + (0.3275911 * 0.7071067811865476) * jnp.abs(pre)
                t = pl.reciprocal(denominator, approx=True)
                t = t * (2.0 - denominator * t)
                tail = 0.5 * 1.061405429
                for factor in (-1.453152027, 1.421413741, -0.284496736, 0.254829592):
                    tail = tail * t + 0.5 * factor
                tail = tail * t * bell
                below = jnp.where(pre < 0, tail, 1.0 - tail)
                units_ref[rows, span] = (pre * below).astype(units_ref.dtype)
                slope = below + pre * bell * 0.3989422804014327
                backs.append((grad_units * slope).astype(back_ref.dtype))
                back_ref[rows, span] = backs[-1]
            total[rows] += dot_nn(backs[0], ups[0][...]) + dot_nn(backs[1], ups[1][...])

        @pl.when(counts[block + k] == 0)
        def _(rows=rows):
            units_ref[rows] = jnp.zeros((size, 2 * width), units_ref.dtype)
            back_ref[rows] = jnp.zeros((size, 2 * width), back_ref.dtype)

    @pl.when(step == pl.num_programs(0) - 1)
    def _():
        out_ref[...] = total[...].astype(out_ref.dtype)


def ffn_blocks(place, block, counts, xs, gs, ups, downs, shifts, kept):
    size, width = 512, 256
    model = xs[0].shape[1]
    rows = sum(x.shape[0] for x in xs)
    units = ups[0].shape[0]
    whole = pl.BlockSpec(memory_space=pl.ANY)
    weights = pl.BlockSpec((width, model), lambda u, *_: (u, 0))
    shift = pl.BlockSpec((1, width), lambda u, *_: (0, u))
    output = pl.BlockSpec((rows, 2 * width), lambda u, *_: (place, u))
    full = jax.ShapeDtypeStruct((4 * size, 2 * units), jnp.bfloat16)
    return pl.pallas_call(
        functools.partial(ffn_kernel, block, len(xs), len(gs)),
        grid_spec=pltpu.PrefetchScalarGridSpec(
            num_scalar_prefetch=1,
            grid=(units // width,),
            in_specs=[whole] * (len(xs) + len(gs))
            + [weights] * 4
            + [shift] * 2
            + [whole] * len(kept),
            out_specs=[output, output, pl.BlockSpec((rows, model), lambda u, *_: (0, 0))],
            scratch_shapes=[
                pltpu.VMEM((rows // size, size, model), jnp.bfloat16),
                pltpu.VMEM((rows // size, size, model), jnp.bfloat16),
                pltpu.VMEM((rows, model), jnp.float32),
                pltpu.SemaphoreType.DMA((len(xs),)),
                pltpu.SemaphoreType.DMA((len(gs),)),
            ],
        ),
        out_shape=[full, full, jax.ShapeDtypeStruct((rows, model), jnp.bfloat16)],
        input_output_aliases={len(xs) + len(gs) + 7 + k: k for k in range(len(kept))},
        compiler_params=pltpu.CompilerParams(vmem_limit_bytes=VMEM_BYTES),
        cost_estimate=NO_COST,
    )(counts, *xs, *gs, *ups, *downs, *shifts, *kept)


def arrange(outs, total):
    to_x, to_y, rest = outs
    half = total.shape[0] // 2
    top, bottom = total[:half].astype(to_x.dtype), total[half:].astype(to_x.dtype)
    step = pl.program_id(0)

    @pl.when(step == 0)
    def _():
        to_x[:half] = top
        to_y[:half] = bottom

    @pl.when(step == 1)
    def _():
        to_x[half:] = top
        rest[half : 2 * half] = bottom

    @pl.when(step == 2)
    def _():
        rest[:half] = top
        to_y[half:] = bottom

    @pl.when(step == 3)
    def _():
        rest[2 * half : 3 * half] = top
        rest[3 * half :] = bottom


def arranged(rows, columns):
    sizes = (rows // 4, rows // 4, rows // 2)
    specs = [pl.BlockSpec((size, columns), lambda i, *_: (0, 0)) for size in sizes]
    return specs, [jax.ShapeDtypeStruct((size, columns), jnp.bfloat16) for size in sizes]


def products_kernel(width, order, active, left, own, other, *outs):
    here = active[order[pl.program_id(0)]] != 0

    @pl.when(here)
    def _():
        total = None
        for k in range(own.shape[0] // width):
            rows = slice(k * width, (k + 1) * width)
            for side, right in enumerate((own, other)):
                start = (2 * k + side) * width
                term = dot_nn(left[:, start : start + width], right[rows])
                total = term if total is None else total + term
        arrange(outs, total)

    @pl.when(jnp.logical_not(here))
    def _():
        arrange(outs, jnp.zeros((left.shape[0], own.shape[1]), jnp.float32))


def products(order, counts, left, own, other):
    blocks = counts.shape[0]
    rows, depth = left.shape
    columns = own.shape[1]
    specs, shapes = arranged(rows, columns)
    return pl.pallas_call(
        functools.partial(products_kernel, 256),
        grid_spec=pltpu.PrefetchScalarGridSpec(
            num_scalar_prefetch=2,
            grid=(blocks,),
            in_specs=[
                pl.BlockSpec((rows // blocks, depth), lambda i, order, *_: (order[i], 0)),
                pl.BlockSpec(own.shape, lambda i, *_: (0, 0)),
                pl.BlockSpec(own.shape, lambda i, *_: (0, 0)),
            ],
            out_specs=specs,
        ),
        out_shape=shapes,
        compiler_params=pltpu.CompilerParams(vmem_limit_bytes=VMEM_BYTES),
        cost_estimate=NO_COST,
    )(order, counts, left, own, other)


def attend_out_kernel(left, weight, bias, hidden, active, out_ref):
    out_ref[...] = hidden[...].astype(jnp.float32) + active[...] * (
        dot_nn(left[...], weight[0]) + bias[...]
    )


def attend_out(left, weights, bias, hidden, active):
    rows, depth = left.shape
    blocks, _, width = weights.shape
    column = pl.BlockSpec((rows, width), lambda j: (0, j))
    return pl.pallas_call(
        attend_out_kernel,
        grid=(blocks,),
        in_specs=[
            pl.BlockSpec((rows, depth), lambda j: (0, 0)),
            pl.BlockSpec((1, depth, width), lambda j: (j, 0, 0)),
            pl.BlockSpec((1, width), lambda j: (0, j)),
            column,
            pl.BlockSpec((rows, 1), lambda j: (0, 0)),
        ],
        out_specs=column,
        out_shape=jax.ShapeDtypeStruct((rows, blocks * width), jnp.float32),
        compiler_params=pltpu.CompilerParams(vmem_limit_bytes=VMEM_BYTES),
        cost_estimate=NO_COST,
    )(left, weights, bias[None], hidden, active)


def attend_out_back_kernel(grad, weight, out_ref, total):
    step = pl.program_id(0)

    @pl.when(step == 0)
    def _():
        total[...] = jnp.zeros(total.shape, total.dtype)

    total[...] += dot_nt(grad[...], weight[0])

    @pl.when(step == pl.num_programs(0) - 1)
    def _():
        out_ref[...] = total[...].astype(out_ref.dtype)


def attend_out_back(grad, weights):
    rows = grad.shape[0]
    blocks, depth, width = weights.shape
    return pl.pallas_call(
        attend_out_back_kernel,
        grid=(blocks,),
        in_specs=[
            pl.BlockSpec((rows, width), lambda j: (0, j)),
            pl.BlockSpec((1, depth, width), lambda j: (j, 0, 0)),
        ],
        out_specs=pl.BlockSpec((rows, depth), lambda j: (0, 0)),
        out_shape=jax.ShapeDtypeStruct((rows, depth), jnp.bfloat16),
        scratch_shapes=[pltpu.VMEM((rows, depth), jnp.float32)],
        compiler_params=pltpu.CompilerParams(vmem_limit_bytes=VMEM_BYTES),
        cost_estimate=NO_COST,
    )(grad, weights)


def project_kernel(inputs, side, parts, *refs):
    xs = refs[:inputs]
    weights, shift, out_ref = refs[inputs:]
    slab = weights.shape[1]
    weight = weights[...].reshape(3 * slab, weights.shape[2])
    for k in range(inputs):

        @pl.when(pl.program_id(0) == k)
        def _(k=k):
            mixed = dot_nt(xs[k][...], weight)
            for t in range(3):
                columns = pl.ds(pl.multiple_of(parts[side, t] * slab, slab), slab)
                out_ref[:, columns] = (
                    mixed[:, t * slab : (t + 1) * slab] + shift[:, columns]
                ).astype(out_ref.dtype)


def project(parts, side, xs, weights, shift):
    size, model = xs[0].shape
    slab = weights.shape[1]
    return pl.pallas_call(
        functools.partial(project_kernel, len(xs), side),
        grid_spec=pltpu.PrefetchScalarGridSpec(
            num_scalar_prefetch=1,
            grid=(len(xs),),
            in_specs=[pl.BlockSpec((size, model), lambda i, *_: (0, 0))] * len(xs)
            + [
                pl.BlockSpec(weights.shape, lambda i, *_: (0, 0, 0)),
                pl.BlockSpec(shift.shape, lambda i, *_: (0, 0)),
            ],
            out_specs=pl.BlockSpec((size, 3 * slab), lambda i, *_: (i, 0)),
        ),
        out_shape=jax.ShapeDtypeStruct((len(xs) * size, 3 * slab), jnp.bfloat16),
        compiler_params=pltpu.CompilerParams(vmem_limit_bytes=VMEM_BYTES),
        cost_estimate=pl.CostEstimate(
            flops=6 * len(xs) * size * slab * model,
            bytes_accessed=6 * slab * model + 2 * len(xs) * size * (model + 3 * slab),
            transcendentals=0,
        ),
    )(parts, *xs, weights, shift)


def unproject_kernel(order, parts, active, mine, theirs, own, other, *outs):
    slab = own.shape[1]
    here = active[order[pl.program_id(0)]] != 0

    @pl.when(here)
    def _():
        total = None
        for side, (left, right) in enumerate(((mine, own), (theirs, other))):
            for t in range(3):
                columns = pl.ds(pl.multiple_of(parts[side, t] * slab, slab), slab)
                term = dot_nn(left[:, columns], right[t])
                total = term if total is None else total + term
        arrange(outs, total)

    @pl.when(jnp.logical_not(here))
    def _():
        arrange(outs, jnp.zeros((mine.shape[0], own.shape[2]), jnp.float32))


def unproject(order, parts, counts, mine, theirs, own, other):
    blocks = counts.shape[0]
    rows = mine.shape[0]
    slab, model = own.shape[1:]
    left = pl.BlockSpec((rows // blocks, 3 * slab), lambda i, order, *_: (order[i], 0))
    fixed = pl.BlockSpec(own.shape, lambda i, *_: (0, 0, 0))
    specs, shapes = arranged(rows, model)
    return pl.pallas_call(
        unproject_kernel,
        grid_spec=pltpu.PrefetchScalarGridSpec(
            num_scalar_prefetch=3,
            grid=(blocks,),
            in_specs=[left, left, fixed, fixed],
            out_specs=specs,
        ),
        out_shape=shapes,
        compiler_params=pltpu.CompilerParams(vmem_limit_bytes=VMEM_BYTES),
        cost_estimate=NO_COST,
    )(order, parts, counts, mine, theirs, own, other)


def weight_grad_kernel(inputs, added, columns, *refs):
    left, rights = refs[0], refs[1 : 1 + inputs]
    tokens, sems = refs[-2:]
    outs = refs[1 + inputs + added : -2]
    fetch(rights, tokens, sems)
    total = dot_tn(left[...], tokens[0])
    if added:
        total = total + refs[1 + inputs][...].astype(jnp.float32)
    size = outs[0].shape[0]
    for k, out_ref in enumerate(outs):
        out_ref[...] = total[k * size : (k + 1) * size].astype(out_ref.dtype)


def weight_grad(left, columns, tile, rights, extra=None, outputs=1):
    rows = left.shape[0]
    model = rights[0].shape[1]
    steps = columns.shape[0]
    output = pl.BlockSpec((tile // outputs, model), lambda i, *_: (i, 0))
    extras = [] if extra is None else [extra]
    shape = jax.ShapeDtypeStruct((steps * tile // outputs, model), jnp.bfloat16)
    results = pl.pallas_call(
        functools.partial(weight_grad_kernel, len(rights), len(extras)),
        grid_spec=pltpu.PrefetchScalarGridSpec(
            num_scalar_prefetch=1,
            grid=(steps,),
            in_specs=[pl.BlockSpec((rows, tile), lambda i, columns: (0, columns[i]))]
            + [pl.BlockSpec(memory_space=pl.ANY)] * len(rights)
            + [output] * len(extras),
            out_specs=[output] * outputs,
            scratch_shapes=[
                pltpu.VMEM((1, rows, model), jnp.bfloat16),
                pltpu.SemaphoreType.DMA((len(rights),)),
            ],
        ),
        out_shape=[shape] * outputs,
        compiler_params=pltpu.CompilerParams(vmem_limit_bytes=VMEM_BYTES),
        cost_estimate=NO_COST,
    )(columns, left, *rights, *extras)
    return results[0] if outputs == 1 else results


def chain_sum(values, axis):
    size = lax.axis_size(axis)
    if size != 4:
        return lax.psum(values.astype(jnp.bfloat16), axis).astype(jnp.float32)
    place = lax.axis_index(axis)
    outer = lax.ppermute(values.astype(jnp.bfloat16), axis, [(0, 1), (3, 2)])
    half = (values + outer.astype(jnp.float32)).astype(jnp.bfloat16)
    other = lax.ppermute(half, axis, [(1, 2), (2, 1)])
    whole = (half.astype(jnp.float32) + other.astype(jnp.float32)).astype(jnp.bfloat16)
    ends = lax.ppermute(whole, axis, [(1, 0), (2, 3)])
    inner = (place == 1) | (place == 2)
    return jnp.where(inner, whole, ends).astype(jnp.float32)


class Chain:
    routes = ([(0, 1), (3, 2)], [(1, 2), (2, 1)], [(1, 0), (2, 3)])

    def __init__(self, block):
        self.leg = 0
        self.block = block
        self.moved = lax.ppermute(block, "batch", self.routes[0])

    def advance(self, *done):
        moved = after(self.moved, *done)
        wide = lambda values: values.astype(jnp.float32)
        self.block = (wide(self.block) + wide(moved)).astype(jnp.bfloat16)
        self.leg += 1
        self.moved = lax.ppermute(self.block, "batch", self.routes[self.leg])
        return self.block

    def total(self, *done):
        place = lax.axis_index("batch")
        moved = after(self.moved, *done)
        return jnp.where((place == 1) | (place == 2), self.block, moved)


def normalize(values):
    center = values - jnp.mean(values, axis=-1, keepdims=True)
    inverse = lax.rsqrt(jnp.mean(center * center, axis=-1, keepdims=True) + epsilon)
    return center * inverse, inverse


def normalize_back(grad, gain, normal, inverse):
    scaled = grad * gain
    grad_values = inverse * (
        scaled
        - jnp.mean(scaled, axis=-1, keepdims=True)
        - normal * jnp.mean(scaled * normal, axis=-1, keepdims=True)
    )
    return grad_values, jnp.sum(grad * normal, axis=0), jnp.sum(grad, axis=0)


def local_general(
    hidden,
    cotangent,
    exit_layer,
    ln1_gain,
    ln1_bias,
    qkv_weight,
    query_bias,
    value_bias,
    out_weight,
    out_bias,
    ln2_gain,
    ln2_bias,
    up_weight,
    up_bias,
    down_weight,
    down_bias,
):
    width = lax.axis_size("wide")
    rank = lax.axis_index("wide")
    rows, model = hidden.shape
    group = rows * width
    slab = model // width
    head_size = model // HEADS
    units_own = up_weight.shape[0]
    keep = exit_layer >= LAYER
    counts = jnp.sum(keep.astype(jnp.int32), axis=1)
    active = lax.dynamic_slice_in_dim(keep.reshape(group), rank * rows, rows, 0)
    active = active.astype(jnp.float32)[:, None]
    grad_out = cotangent.astype(jnp.float32)

    routes = [[(w, (3 * w + t) % width) for w in range(width)] for t in range(3)]
    part_at = np.zeros((width, 3), np.int32)
    for t in range(3):
        for w, d in routes[t]:
            part_at[d, t] = (3 * w + t) // width
    place_of = jnp.asarray(np.argsort(part_at, axis=1).astype(np.int32))[rank]
    part_of = jnp.asarray(part_at)[rank]

    hidden_wide = hidden.astype(jnp.float32)
    normal1, inverse1 = normalize(hidden_wide)
    normed1 = lax.all_gather(
        (normal1 * ln1_gain + ln1_bias).astype(jnp.bfloat16), "wide", axis=0, tiled=True
    )
    slabs = qkv_weight.reshape(3, slab, model)
    received = jnp.stack([lax.ppermute(slabs[t], "wide", routes[t]) for t in range(3)])
    qkv_own = jnp.concatenate(
        [lax.dynamic_index_in_dim(received, place_of[p], 0, keepdims=False) for p in range(3)]
    )
    own = lambda vector: lax.dynamic_slice_in_dim(vector, rank * slab, slab, 0)
    qkv_shift = jnp.concatenate(
        [own(query_bias), jnp.zeros((slab,), jnp.float32), own(value_bias)]
    )

    grad_ffn = (active * grad_out).astype(jnp.bfloat16)
    down_bias_grad = jnp.sum(grad_ffn.astype(jnp.float32), axis=0)
    piece = rows // CHUNKS
    part = lambda values, c: values[c * piece : (c + 1) * piece]
    gather = lambda values: lax.all_gather(values, "wide", axis=0, tiled=True)
    scatter = lambda values: lax.psum_scatter(
        values.astype(jnp.bfloat16), "wide", scatter_dimension=0, tiled=True
    )
    grad_ffns = [gather(part(grad_ffn, c)) for c in range(CHUNKS)]
    out_whole = gather(out_weight)

    mixed = (dot_nt(normed1, qkv_own) + qkv_shift).astype(jnp.bfloat16)
    mixed = jnp.split(mixed, group // TILE)
    slots = jnp.arange(group // TILE, dtype=jnp.int32).reshape(counts.shape[0], -1)
    attended, logs = attend(mixed, slots, counts, head_size)
    attended_rows = lax.all_to_all(attended, "wide", split_axis=0, concat_axis=1, tiled=True)
    middle = hidden_wide + active * (dot_nn(attended_rows, out_whole) + out_bias)
    normal2, inverse2 = normalize(middle)
    normed2 = (normal2 * ln2_gain + ln2_bias).astype(jnp.bfloat16)
    up_shift = lax.dynamic_slice_in_dim(up_bias, rank * units_own, units_own, 0)

    normed2s = [gather(part(normed2, c)) for c in range(CHUNKS)]
    units, grad_pres, grad_normed2, ffn_out = [], [], [], []
    for c in range(CHUNKS):
        grad_units = dot_nt(grad_ffns[c], down_weight)
        pre = dot_nt(normed2s[c], up_weight) + up_shift
        below = 0.5 + 0.5 * lax.erf(pre * 0.7071067811865476)
        bell = jnp.exp(-0.5 * pre * pre) * 0.3989422804014327
        units.append((pre * below).astype(jnp.bfloat16))
        grad_pres.append((grad_units * (below + pre * bell)).astype(jnp.bfloat16))
        grad_normed2.append(scatter(dot_nn(grad_pres[c], up_weight)))
    for c in range(CHUNKS):
        ffn_out.append(scatter(dot_nn(units[c], down_weight)))
    grad_normed2 = jnp.concatenate(grad_normed2).astype(jnp.float32)
    ffn_out = jnp.concatenate(ffn_out).astype(jnp.float32)
    output = (middle + active * (ffn_out + down_bias)).astype(jnp.bfloat16)

    up_bias_own = sum(jnp.sum(g.astype(jnp.float32), axis=0) for g in grad_pres)
    down_grad = sum(dot_tn(units[c], grad_ffns[c]) for c in range(CHUNKS))
    up_grad = sum(dot_tn(grad_pres[c], normed2s[c]) for c in range(CHUNKS))
    halves = lambda values: jnp.concatenate(
        [chain_sum(half, "batch") for half in jnp.split(values, 2)]
    )
    down_grad = halves(down_grad)
    up_grad = halves(up_grad)

    grad_middle, ln2_gain_grad, ln2_bias_grad = normalize_back(
        grad_normed2, ln2_gain, normal2, inverse2
    )
    grad_middle = grad_out + grad_middle
    grad_branch = (active * grad_middle).astype(jnp.bfloat16)
    out_bias_grad = jnp.sum(grad_branch.astype(jnp.float32), axis=0)
    grad_attended = dot_nt(grad_branch, out_whole).astype(jnp.bfloat16)
    grad_heads = lax.all_to_all(grad_attended, "wide", split_axis=1, concat_axis=0, tiled=True)
    out_grad = chain_sum(scatter(dot_tn(attended_rows, grad_branch)).astype(jnp.float32), "batch")

    placed = lambda vector, size: lax.dynamic_update_slice_in_dim(
        jnp.zeros((size,), jnp.float32), vector, rank * vector.shape[0], 0
    )
    early = lax.psum(
        (
            out_bias_grad,
            ln2_gain_grad,
            ln2_bias_grad,
            placed(up_bias_own, up_bias.shape[0]),
            down_bias_grad,
        ),
        ("batch", "wide"),
    )

    grad_mixed = jnp.concatenate(
        attend_back(mixed, slots, grad_heads, attended, logs, counts, head_size)
    )
    grad_normed1 = scatter(dot_nn(grad_mixed, qkv_own)).astype(jnp.float32)
    sums = jnp.sum(grad_mixed.astype(jnp.float32), axis=0)
    qkv_parts = []
    for t in range(3):
        columns = lax.dynamic_slice_in_dim(grad_mixed, part_of[t] * slab, slab, 1)
        total = chain_sum(dot_tn(columns, normed1), "batch").astype(jnp.bfloat16)
        back = [(d, w) for w, d in routes[t]]
        qkv_parts.append(lax.ppermute(total, "wide", back).astype(jnp.float32))
    qkv_grad = jnp.concatenate(qkv_parts)

    grad_hidden, ln1_gain_grad, ln1_bias_grad = normalize_back(
        grad_normed1, ln1_gain, normal1, inverse1
    )
    input_grad = grad_middle + grad_hidden
    late = lax.psum(
        (
            ln1_gain_grad,
            ln1_bias_grad,
            placed(sums[:slab], model),
            placed(sums[2 * slab :], model),
        ),
        ("batch", "wide"),
    )
    return (
        output,
        input_grad,
        late[0],
        late[1],
        qkv_grad,
        late[2],
        late[3],
        out_grad,
        early[0],
        early[1],
        early[2],
        up_grad,
        early[3],
        down_grad,
        early[4],
    )


def swap(values, bits):
    width = lax.axis_size("wide")
    return lax.ppermute(values, "wide", [(w, w ^ bits) for w in range(width)])


def after(values, *done):
    return lax.optimization_barrier((values, done))[0]


def relay(along_x, along_y):
    half = along_x.shape[0] // 2
    return [swap(along_y[:half], 2), swap(along_x[half:], 4)]


class Scatter:
    def __init__(self, to_x, to_y, rest):
        self.half = half = to_x.shape[0] // 2
        self.sent = (to_x, to_y)
        self.rest = rest
        self.from_x, self.from_y = swap(to_x, 2), swap(to_y, 4)

    def second(self, *done):
        half = self.half
        from_x, from_y = after((self.from_x, self.from_y), *done)
        self.near = (from_x[half:], from_y[half:])
        self.own = self.rest[2 * half :]
        return self.forward(self.rest[:half], self.rest[half : 2 * half], from_x[:half], from_y[:half])

    def forward(self, along_y, along_x, top, bottom):
        wide = lambda values: values.astype(jnp.float32)
        y_top = (wide(along_y) + wide(top)).astype(jnp.bfloat16)
        x_bottom = (wide(along_x) + wide(bottom)).astype(jnp.bfloat16)
        self.last = (swap(y_top, 4), swap(x_bottom, 2))
        return y_top, x_bottom

    def finish(self, *done):
        wide = lambda values: values.astype(jnp.float32)
        y_top, x_bottom = after(self.last, *done)
        x_top, y_bottom = self.near
        return jnp.concatenate(
            [
                wide(self.own[: self.half]) + wide(x_top) + wide(y_top),
                wide(self.own[self.half :]) + wide(x_bottom) + wide(y_bottom),
            ]
        )


def split_for_scatter(own, along_x, along_y, diagonal):
    half = own.shape[0] // 2
    return (
        jnp.concatenate([diagonal[:half], along_x[:half]]),
        jnp.concatenate([diagonal[half:], along_y[half:]]),
        jnp.concatenate([along_y[:half], along_x[half:], own]),
    )


class EarlyScatter(Scatter):
    def __init__(self, own, along_x, along_y):
        self.half = half = own.shape[0] // 2
        self.own, self.along_x, self.along_y = own, along_x, along_y
        self.near = (swap(along_x[:half], 2), swap(along_y[half:], 4))

    def first(self, diagonal):
        self.from_far = (swap(diagonal[: self.half], 2), swap(diagonal[self.half :], 4))
        self.near = after(self.near, diagonal)
        return self.near

    def second(self, *done):
        half = self.half
        far = after(self.from_far, *done)
        return self.forward(self.along_y[:half], self.along_x[half:], *far)


def tree_sum(values):
    total = values + swap(values, 1)
    total = (total + swap(total, 2)) + (swap(total, 4) + swap(total, 6))
    size = lax.axis_size("batch")
    terms = [total] + [
        lax.ppermute(total, "batch", [(z, z ^ bits) for z in range(size)])
        for bits in range(1, size)
    ]
    while len(terms) > 1:
        terms = [terms[k] + terms[k + 1] for k in range(0, len(terms), 2)]
    return terms[0]


def local_chips(
    hidden,
    cotangent,
    exit_layer,
    ln1_gain,
    ln1_bias,
    qkv_weight,
    query_bias,
    value_bias,
    out_weight,
    out_bias,
    ln2_gain,
    ln2_bias,
    up_weight,
    up_bias,
    down_weight,
    down_bias,
):
    width = lax.axis_size("wide")
    rank = lax.axis_index("wide")
    rows, model = hidden.shape
    group = rows * width
    slab = model // width
    head_size = model // HEADS
    units_own = up_weight.shape[0]
    keep = exit_layer >= LAYER
    counts = jnp.sum(keep.astype(jnp.int32), axis=1)
    active = lax.dynamic_slice_in_dim(keep.reshape(group), rank * rows, rows, 0)
    active = active.astype(jnp.float32)[:, None]
    grad_out = cotangent.astype(jnp.float32)

    tiles = jnp.arange(group // rows, dtype=jnp.int32)
    slots = ((tiles ^ rank) & 1) * 4 + ((tiles >> 1) ^ (rank >> 1))
    slots = slots.reshape(counts.shape[0], -1)

    routes = [[(w, (3 * w + t) % width) for w in range(width)] for t in range(3)]
    part_at = np.zeros((width, 3), np.int32)
    for t in range(3):
        for w, d in routes[t]:
            part_at[d, t] = (3 * w + t) // width
    part_at = jnp.asarray(part_at)
    other = rank ^ 1
    parts = jnp.stack([part_at[rank], part_at[other]])

    hidden_wide = hidden.astype(jnp.float32)
    normal1, inverse1 = normalize(hidden_wide)
    slabs = qkv_weight.reshape(3, slab, model)
    slabs = [lax.ppermute(slabs[t], "wide", routes[t]) for t in range(3)]
    normed1 = (normal1 * ln1_gain + ln1_bias).astype(jnp.bfloat16)
    normed1 = [normed1, swap(normed1, 2), swap(normed1, 4)]
    diagonal1 = relay(normed1[1], normed1[2])
    qkv_own = jnp.stack(after(slabs, normed1[1:]))
    qkv_other = swap(qkv_own, 1)

    def shift_of(device):
        own = lambda vector: lax.dynamic_slice_in_dim(vector, device * slab, slab, 0)
        shift = [own(query_bias), jnp.zeros((slab,), jnp.float32), own(value_bias)]
        return jnp.concatenate(shift)[None]

    bias_of = lambda device: lax.dynamic_slice_in_dim(up_bias, device * units_own, units_own, 0)
    up_shifts = [bias_of(rank)[None], bias_of(other)[None]]

    mixed_near = project(parts, 0, normed1, qkv_own, shift_of(rank))
    qkv_other = after(qkv_other, mixed_near, diagonal1)
    lent_near = project(parts, 1, normed1, qkv_other, shift_of(other))
    diagonal1 = after(diagonal1, lent_near)
    lent_far = project(parts, 1, diagonal1, qkv_other, shift_of(other))
    mixed_far = project(parts, 0, after(diagonal1, lent_far), qkv_own, shift_of(rank))
    mixed = [mixed_near, mixed_far, swap(lent_near, 1), swap(lent_far, 1)]

    quarter = model // lax.axis_size("batch")
    start = lax.axis_index("batch") * quarter
    out_quarter = lax.dynamic_slice_in_dim(out_weight, start, quarter, 1)
    out_quarter = lax.all_gather(out_quarter, "wide", axis=0, tiled=True)
    out_blocks = lax.all_gather(after(out_quarter, normed1[1:]), "batch", axis=0)
    grad_ffn = (after(active, diagonal1) * grad_out).astype(jnp.bfloat16)
    down_bias_grad = jnp.sum(grad_ffn.astype(jnp.float32), axis=0)
    grad_ffn = [grad_ffn, swap(grad_ffn, 2), swap(grad_ffn, 4)]

    attended, logs = attend(mixed, slots, counts, head_size)
    attended_rows = lax.all_to_all(attended, "wide", split_axis=0, concat_axis=1, tiled=True)
    attended_rows = after(attended_rows, grad_ffn[1:])
    up_other, down_other = swap(after((up_weight, down_weight), attended), 1)
    middle = attend_out(attended_rows, out_blocks, out_bias, hidden, active)
    normal2, inverse2 = normalize(middle)
    normed2 = (normal2 * ln2_gain + ln2_bias).astype(jnp.bfloat16)
    normed2 = [normed2, swap(normed2, 2), swap(normed2, 4)]

    per_tile = jnp.sum(keep.reshape(group // rows, rows).astype(jnp.int32), axis=1)
    block_chip = (rank >> 1) ^ jnp.arange(4, dtype=jnp.int32)
    block_counts = per_tile[2 * block_chip + (rank & 1)]
    ups, downs = [up_weight, up_other], [down_weight, down_other]

    def ffn(place, block, xs, gs, kept):
        *kept, partial = ffn_blocks(
            place, block, block_counts, xs, gs, ups, downs, up_shifts, tuple(kept)
        )
        return kept, partial

    kept, partial_own = ffn(2, 0, normed2[:1], grad_ffn[:1], ())
    normed2[1:] = after(normed2[1:], partial_own)
    diagonal2 = relay(normed2[1], normed2[2])
    diagonal_ffn = relay(*after(grad_ffn[1:], attended_rows))
    kept, partial_near = ffn(0, 1, normed2[1:], grad_ffn[1:], kept)
    scatter2 = EarlyScatter(partial_own, partial_near[:rows], partial_near[rows:])
    diagonal2 = after(diagonal2, partial_near)
    (units, grad_pres), partial_far = ffn(3, 3, diagonal2, diagonal_ffn, kept)
    wait = scatter2.first(partial_far)
    tokens2 = [*normed2[1:], normed2[0], *diagonal2]
    tokens_ffn = [*grad_ffn[1:], grad_ffn[0], *diagonal_ffn]

    wide = lambda values: values.astype(jnp.float32)
    lowered = lambda values: values.astype(jnp.bfloat16)
    tile = 512
    tiles = jnp.arange(2 * units_own // tile, dtype=jnp.int32)

    down_own, down_lent = weight_grad(after(units, wait), tiles, tile, tokens_ffn, outputs=2)
    wait = scatter2.second(down_lent)
    down_lent = swap(down_lent, 1)
    up_own, up_lent = weight_grad(after(grad_pres, wait), tiles, tile, tokens2, outputs=2)

    up_lent = swap(up_lent, 1)
    down_sum = lowered(wide(down_own) + wide(after(down_lent, up_own)))
    chain_a = Chain(down_sum[:tile])
    grad_middle, ln2_gain_grad, ln2_bias_grad = normalize_back(
        scatter2.finish(up_own), ln2_gain, normal2, inverse2
    )
    grad_middle = grad_out + grad_middle
    grad_branch = (active * grad_middle).astype(jnp.bfloat16)
    out_bias_grad = jnp.sum(grad_branch.astype(jnp.float32), axis=0)
    grad_branch = after(grad_branch, chain_a.block)
    grad_attended = attend_out_back(grad_branch, out_blocks)
    grad_heads = lax.all_to_all(grad_attended, "wide", split_axis=1, concat_axis=0, tiled=True)
    owners = 2 * block_chip + (rank & 1)
    grad_branch = after(grad_branch, grad_attended)
    out_lent = weight_grad(attended_rows, owners ^ 1, slab, [grad_branch])
    out_lent = swap(out_lent, 1)
    up_sum = lowered(wide(up_own) + wide(after(up_lent, out_lent)))
    out_own = weight_grad(after(attended_rows, up_sum), owners, slab, [grad_branch], out_lent)

    wait = chain_a.advance(out_own, grad_heads)
    down_rest, up_first = after((down_sum[tile:], up_sum[:tile]), out_own)
    chain_b = Chain(jnp.concatenate([down_rest, up_first]))
    wait = (wait, chain_b.block)
    scatter_out = Scatter(*split_for_scatter(*jnp.split(after(out_own, wait), 4)))
    back_own, back_other = attend_back(
        mixed, slots, after(grad_heads, scatter_out.sent), attended, logs, counts, head_size
    )

    theirs = swap(back_other, 1)
    wait = scatter_out.second(back_own)
    wait = (wait, chain_a.advance(back_own), chain_b.advance(back_own))
    up_rest = after(up_sum[tile:], back_own)
    chain_c = Chain(up_rest)
    wait = (wait, up_rest)
    order = jnp.array([3, 0, 1, 2], jnp.int32)
    ffn_counts = block_counts[jnp.array([1, 2, 0, 3])]
    ffn_parts = products(order, ffn_counts, after(units, wait), *downs)
    tokens1 = [*normed1, *diagonal1]
    theirs = after(theirs, ffn_parts[0])
    qkv_lent = weight_grad(theirs, parts[1], slab, tokens1)
    grad_parts = unproject(
        jnp.array([3, 1, 2, 0], jnp.int32),
        parts,
        block_counts,
        after(back_own, qkv_lent),
        theirs,
        qkv_own,
        qkv_other,
    )
    qkv_lent = swap(qkv_lent, 1)
    scatter1 = Scatter(*grad_parts)
    qkv_total = weight_grad(
        after(back_own, grad_parts[0]), parts[0], slab, tokens1, after(qkv_lent, grad_parts[0])
    )

    wait = (chain_b.advance(qkv_total), chain_c.advance(qkv_total))
    chain_p = Chain(after(qkv_total[: 2 * slab], wait))
    down_first = wide(chain_a.total(chain_p.block))
    grad_pres, back_own, back_other = after((grad_pres, back_own, back_other), chain_p.block)
    up_bias_own = jnp.sum(wide(grad_pres), axis=0).reshape(-1, 2, 256)
    up_bias_own = [up_bias_own[:, side].reshape(units_own) for side in range(2)]
    sums = jnp.sum(wide(back_own), axis=0) + jnp.sum(wide(back_other), axis=0)
    out_total = lowered(scatter_out.finish(chain_p.block))
    last = jnp.concatenate([qkv_total[2 * slab :], out_total])

    wait = (scatter1.second(last, up_bias_own, sums, down_first), chain_p.advance(last))
    chain_q = Chain(after(last, wait))
    grad_normed1 = scatter1.finish(wait, chain_q.block)
    grad_hidden, ln1_gain_grad, ln1_bias_grad = normalize_back(
        grad_normed1, ln1_gain, normal1, inverse1
    )
    input_grad = grad_middle + grad_hidden

    wait = (chain_c.advance(input_grad), chain_p.advance(input_grad), chain_q.advance(input_grad))
    scatter_ffn = Scatter(*after(ffn_parts, wait))
    total_b = wide(chain_b.total(wait))
    wait = (scatter_ffn.second(total_b), chain_q.advance(total_b))
    ffn_out = scatter_ffn.finish(wait)
    output = (middle + active * (ffn_out + down_bias)).astype(jnp.bfloat16)
    down_grad = jnp.concatenate([down_first, total_b[:tile]])
    up_grad = jnp.concatenate([total_b[tile:], wide(chain_c.total(output))])
    total_p, total_q = chain_p.total(output), chain_q.total(output)
    qkv_totals = [total_p[:slab], total_p[slab:], total_q[:slab]]
    qkv_grad = jnp.concatenate(
        [
            wide(lax.ppermute(qkv_totals[t], "wide", [(d, w) for w, d in routes[t]]))
            for t in range(3)
        ]
    )
    out_grad = wide(total_q[slab:])

    placed = lambda vector, size, device: lax.dynamic_update_slice_in_dim(
        jnp.zeros((size,), jnp.float32), vector, device * vector.shape[0], 0
    )
    smalls = tree_sum(
        jnp.concatenate(
            [
                placed(up_bias_own[0], up_bias.shape[0], rank)
                + placed(up_bias_own[1], up_bias.shape[0], other),
                down_bias_grad,
                out_bias_grad,
                ln2_gain_grad,
                ln2_bias_grad,
                placed(sums[:slab], model, rank),
                placed(sums[2 * slab :], model, rank),
                ln1_gain_grad,
                ln1_bias_grad,
            ]
        )
    )
    up_bias_grad = smalls[: up_bias.shape[0]]
    smalls = smalls[up_bias.shape[0] :].reshape(8, model)
    return (
        output,
        input_grad,
        smalls[6],
        smalls[7],
        qkv_grad,
        smalls[4],
        smalls[5],
        out_grad,
        smalls[1],
        smalls[2],
        smalls[3],
        up_grad,
        up_bias_grad,
        down_grad,
        smalls[0],
    )


def solution(mesh):
    chips = mesh.shape["wide"] == 8 and mesh.shape["batch"] == 4
    local = local_chips if chips else local_general
    rows = P(("batch", "wide"), None)
    weight = P("wide", None)
    return jax.shard_map(
        local,
        mesh=mesh,
        in_specs=(
            rows,
            rows,
            P("batch", None),
            P(),
            P(),
            weight,
            P(),
            P(),
            weight,
            P(),
            P(),
            P(),
            weight,
            P(),
            weight,
            P(),
        ),
        out_specs=(
            rows,
            rows,
            P(),
            P(),
            weight,
            P(),
            P(),
            weight,
            P(),
            P(),
            P(),
            weight,
            P(),
            weight,
            P(),
        ),
        check_vma=False,
    )
```

```python
import functools

import jax
import jax.numpy as jnp
import numpy as np
from jax import lax
from jax.experimental import pallas as pl
from jax.experimental.pallas import tpu as pltpu
from jax.sharding import PartitionSpec as P

HEADS = 32
LAYER = 12
LANES = 128
TILE = 512
CHUNKS = 2
LOG2E = 1.4426950408889634

epsilon = 1e-05
VMEM_BYTES = 48 * 2**20


def cost(flops, size, exponentials=0):
    return pl.CostEstimate(flops=flops, bytes_accessed=size, transcendentals=exponentials)


def dot_nt(left, right):
    return lax.dot_general(
        left, right, (((1,), (1,)), ((), ())), preferred_element_type=jnp.float32
    )


def dot_nn(left, right):
    return lax.dot_general(
        left, right, (((1,), (0,)), ((), ())), preferred_element_type=jnp.float32
    )


def dot_tn(left, right):
    return lax.dot_general(
        left, right, (((0,), (0,)), ((), ())), preferred_element_type=jnp.float32
    )


def head_masks(head_size):
    lane = lax.broadcasted_iota(jnp.int32, (1, LANES), 1)
    return [
        (lane >= h * head_size) & (lane < (h + 1) * head_size)
        for h in range(LANES // head_size)
    ]


def fetch(sources, target, sems):
    size = target.shape[1]
    copies = []
    row = 0
    for source in sources:
        rows = source.shape[0]
        least = min(rows, size)
        for k in range(rows // least):
            place = target.at[row // size, pl.ds(row % size, least)]
            copies.append(
                pltpu.make_async_copy(source.at[pl.ds(k * least, least)], place, sems.at[len(copies)])
            )
            row += least

    @pl.when(pl.program_id(0) == 0)
    def _():
        for copy in copies:
            copy.start()
        for copy in copies:
            copy.wait()


def attend_kernel(head_size, blocks_in, counts, slots, *refs):
    sources = refs[:blocks_in]
    out_ref, log_ref, mixed_ref, key_own, value_own, sems = refs[blocks_in:]
    fetch(sources, mixed_ref, sems)
    length, lanes = out_ref.shape
    tile = mixed_ref.shape[1]
    pack = LANES // head_size
    scale = head_size ** (-0.5) * LOG2E
    sequence = pl.program_id(0)
    blocks = lax.div(counts[sequence] + (tile - 1), tile)
    masks = head_masks(head_size)
    out_ref[...] = jnp.zeros(out_ref.shape, out_ref.dtype)
    log_ref[...] = jnp.zeros(log_ref.shape, log_ref.dtype)
    row = lax.broadcasted_iota(jnp.int32, (tile, tile), 0)
    col = lax.broadcasted_iota(jnp.int32, (tile, tile), 1)
    for pair in range(lanes // LANES):
        base = pair * LANES
        for i in range(length // tile):
            slot = slots[sequence, i]
            keys = mixed_ref[slot, :, lanes + base : lanes + base + LANES]
            values = mixed_ref[slot, :, 2 * lanes + base : 2 * lanes + base + LANES]
            for h in range(pack):
                key_own[h, i * tile : (i + 1) * tile] = jnp.where(masks[h], keys, jnp.zeros_like(keys))
                value_own[h, i * tile : (i + 1) * tile] = jnp.where(
                    masks[h], values, jnp.zeros_like(values)
                )

        def query_block(i, _, pair=pair, base=base):
            start = pl.multiple_of(i * tile, tile)
            queries = mixed_ref[slots[sequence, i], :, base : base + LANES]

            def step(j, carry, diagonal=False):
                total, tops, sums = carry
                first = pl.multiple_of(j * tile, tile)
                new_tops, new_sums, shrinks, adds = [], [], [], []
                for h in range(pack):
                    scores = dot_nt(queries, key_own[h, pl.ds(first, tile)]) * scale
                    if diagonal:
                        scores = jnp.where(col <= row, scores, -1e30)
                    top = jnp.maximum(tops[h], jnp.max(scores, axis=1, keepdims=True))
                    terms = jnp.exp2(scores - top)
                    shrink = jnp.exp2(tops[h] - top)
                    new_tops.append(top)
                    new_sums.append(sums[h] * shrink + jnp.sum(terms, axis=1, keepdims=True))
                    shrinks.append(shrink)
                    adds.append(dot_nn(terms.astype(jnp.bfloat16), value_own[h, pl.ds(first, tile)]))
                shrink = shrinks[0]
                for h in range(1, pack):
                    shrink = jnp.where(masks[h], shrinks[h], shrink)
                total = total * shrink
                for add in adds:
                    total = total + add
                return total, tuple(new_tops), tuple(new_sums)

            carry = (
                jnp.zeros((tile, LANES), jnp.float32),
                tuple(jnp.full((tile, 1), -1e30, jnp.float32) for _ in range(pack)),
                tuple(jnp.zeros((tile, 1), jnp.float32) for _ in range(pack)),
            )
            carry = lax.fori_loop(0, i, step, carry)
            total, tops, sums = step(i, carry, diagonal=True)
            share = 1.0 / sums[0]
            for h in range(1, pack):
                share = jnp.where(masks[h], 1.0 / sums[h], share)
            out_ref[pl.ds(start, tile), base : base + LANES] = (total * share).astype(out_ref.dtype)
            for h in range(pack):
                logs = jnp.broadcast_to(tops[h] + jnp.log2(sums[h]), (tile, LANES))
                index = pair * pack + h
                log_ref[0, index : index + 1, pl.ds(start, tile)] = jnp.transpose(logs)[0:1]
            return 0

        lax.fori_loop(0, blocks, query_block, 0)


def attend(mixed, slots, counts, head_size):
    sequences = counts.shape[0]
    rows = sum(part.shape[0] for part in mixed)
    tile = rows // slots.size
    blocks = rows // tile
    lanes = mixed[0].shape[1] // 3
    length = rows // sequences
    heads = lanes // head_size
    pack = LANES // head_size
    return pl.pallas_call(
        functools.partial(attend_kernel, head_size, len(mixed)),
        grid_spec=pltpu.PrefetchScalarGridSpec(
            num_scalar_prefetch=2,
            grid=(sequences,),
            in_specs=[pl.BlockSpec(memory_space=pl.ANY)] * len(mixed),
            out_specs=[
                pl.BlockSpec((length, lanes), lambda s, *_: (s, 0)),
                pl.BlockSpec((1, heads, length), lambda s, *_: (s, 0, 0)),
            ],
            scratch_shapes=[
                pltpu.VMEM((blocks, tile, 3 * lanes), jnp.bfloat16),
                pltpu.VMEM((pack, length, LANES), jnp.bfloat16),
                pltpu.VMEM((pack, length, LANES), jnp.bfloat16),
                pltpu.SemaphoreType.DMA((blocks,)),
            ],
        ),
        out_shape=[
            jax.ShapeDtypeStruct((rows, lanes), jnp.bfloat16),
            jax.ShapeDtypeStruct((sequences, heads, length), jnp.float32),
        ],
        compiler_params=pltpu.CompilerParams(vmem_limit_bytes=VMEM_BYTES),
        cost_estimate=cost(rows * length * lanes * 2, rows * lanes * 8, rows * length * heads // 2),
    )(counts, slots, *mixed)


def attend_back_kernel(
    head_size,
    blocks_in,
    counts,
    slots,
    *refs,
):
    sources = refs[:blocks_in]
    grad_ref, out_ref, log_ref, own_ref, other_ref, mixed_ref = refs[blocks_in : blocks_in + 6]
    query_own, key_own, grad_own, delta, grad_query, grad_key, grad_value, back_ref, sems = refs[
        blocks_in + 6 :
    ]
    fetch(sources, mixed_ref, sems)
    length, lanes = out_ref.shape
    tile = mixed_ref.shape[1]
    pack = LANES // head_size
    scale = head_size ** (-0.5)
    sequence = pl.program_id(0)
    blocks = lax.div(counts[sequence] + (tile - 1), tile)
    masks = head_masks(head_size)
    for i in range(length // tile):
        back_ref[slots[sequence, i]] = jnp.zeros((tile, 3 * lanes), back_ref.dtype)
    key_row = lax.broadcasted_iota(jnp.int32, (tile, tile), 0)
    query_col = lax.broadcasted_iota(jnp.int32, (tile, tile), 1)
    for pair in range(lanes // LANES):
        base = pair * LANES
        for i in range(length // tile):
            span = slice(i * tile, (i + 1) * tile)
            slot = slots[sequence, i]
            queries = mixed_ref[slot, :, base : base + LANES]
            keys = mixed_ref[slot, :, lanes + base : lanes + base + LANES]
            grads = grad_ref[span, base : base + LANES]
            for h in range(pack):
                query_own[h, span] = jnp.where(masks[h], queries, jnp.zeros_like(queries))
                key_own[h, span] = jnp.where(masks[h], keys, jnp.zeros_like(keys))
                grad_own[h, span] = jnp.where(masks[h], grads, jnp.zeros_like(grads))
        grad_query[...] = jnp.zeros(grad_query.shape, jnp.float32)

        def deltas(i, _, base=base):
            start = pl.multiple_of(i * tile, tile)
            grads = grad_ref[pl.ds(start, tile), base : base + LANES].astype(jnp.float32)
            outs = out_ref[pl.ds(start, tile), base : base + LANES].astype(jnp.float32)
            products = jnp.transpose(grads * outs)
            for h in range(pack):
                delta[h : h + 1, pl.ds(start, tile)] = jnp.sum(
                    products[h * head_size : (h + 1) * head_size], axis=0, keepdims=True
                )
            return 0

        lax.fori_loop(0, blocks, deltas, 0)

        def key_block(j, _, pair=pair, base=base):
            first = pl.multiple_of(j * tile, tile)
            place = slots[sequence, j]
            keys = mixed_ref[place, :, lanes + base : lanes + base + LANES]
            values = mixed_ref[place, :, 2 * lanes + base : 2 * lanes + base + LANES]
            grad_key[...] = jnp.zeros(grad_key.shape, jnp.float32)
            grad_value[...] = jnp.zeros(grad_value.shape, jnp.float32)

            def step(i, diagonal=False):
                start = pl.multiple_of(i * tile, tile)
                add_query, add_key, add_value = [], [], []
                for h in range(pack):
                    index = pair * pack + h
                    query_head = query_own[h, pl.ds(start, tile)]
                    grad_head = grad_own[h, pl.ds(start, tile)]
                    scores = dot_nt(keys, query_head) * (scale * LOG2E)
                    probs = jnp.exp2(scores - log_ref[0, index : index + 1, pl.ds(start, tile)])
                    if diagonal:
                        probs = jnp.where(key_row <= query_col, probs, 0.0)
                    grad_probs = dot_nt(values, grad_head)
                    grad_scores = (
                        probs * (grad_probs - delta[h : h + 1, pl.ds(start, tile)])
                    ).astype(jnp.bfloat16)
                    add_value.append(dot_nn(probs.astype(jnp.bfloat16), grad_head))
                    add_key.append(dot_nn(grad_scores, query_head))
                    add_query.append(dot_tn(grad_scores, key_own[h, pl.ds(first, tile)]))
                grad_value[...] += functools.reduce(jnp.add, add_value)
                grad_key[...] += functools.reduce(jnp.add, add_key)
                grad_query[pl.ds(start, tile), :] += functools.reduce(jnp.add, add_query)

            def off_diagonal(i, _):
                step(i)
                return 0

            step(j, diagonal=True)
            lax.fori_loop(j + 1, blocks, off_diagonal, 0)
            back_ref[place, :, lanes + base : lanes + base + LANES] = (grad_key[...] * scale).astype(
                back_ref.dtype
            )
            back_ref[place, :, 2 * lanes + base : 2 * lanes + base + LANES] = grad_value[...].astype(
                back_ref.dtype
            )
            return 0

        lax.fori_loop(0, blocks, key_block, 0)
        for i in range(length // tile):
            back_ref[slots[sequence, i], :, base : base + LANES] = (
                grad_query[i * tile : (i + 1) * tile] * scale
            ).astype(back_ref.dtype)

    @pl.when(sequence == pl.num_programs(0) - 1)
    def _():
        half = back_ref.shape[0] // 2
        for k in range(half):
            own_ref[k * tile : (k + 1) * tile] = back_ref[k]
            other_ref[k * tile : (k + 1) * tile] = back_ref[half + k]


def attend_back(mixed, slots, grads, outs, logs, counts, head_size):
    sequences = counts.shape[0]
    rows, lanes = outs.shape
    length = rows // sequences
    heads = lanes // head_size
    pack = LANES // head_size
    tile = rows // slots.size
    blocks = rows // tile
    whole = pl.BlockSpec((rows // 2, 3 * lanes), lambda s, *_: (0, 0))
    return pl.pallas_call(
        functools.partial(attend_back_kernel, head_size, len(mixed)),
        grid_spec=pltpu.PrefetchScalarGridSpec(
            num_scalar_prefetch=2,
            grid=(sequences,),
            in_specs=[pl.BlockSpec(memory_space=pl.ANY)] * len(mixed)
            + [
                pl.BlockSpec((length, lanes), lambda s, *_: (s, 0)),
                pl.BlockSpec((length, lanes), lambda s, *_: (s, 0)),
                pl.BlockSpec((1, heads, length), lambda s, *_: (s, 0, 0)),
            ],
            out_specs=[whole, whole],
            scratch_shapes=[
                pltpu.VMEM((blocks, tile, 3 * lanes), jnp.bfloat16),
                pltpu.VMEM((pack, length, LANES), jnp.bfloat16),
                pltpu.VMEM((pack, length, LANES), jnp.bfloat16),
                pltpu.VMEM((pack, length, LANES), jnp.bfloat16),
                pltpu.VMEM((pack, length), jnp.float32),
                pltpu.VMEM((length, LANES), jnp.float32),
                pltpu.VMEM((tile, LANES), jnp.float32),
                pltpu.VMEM((tile, LANES), jnp.float32),
                pltpu.VMEM((blocks, tile, 3 * lanes), jnp.bfloat16),
                pltpu.SemaphoreType.DMA((blocks,)),
            ],
        ),
        out_shape=[jax.ShapeDtypeStruct((rows // 2, 3 * lanes), jnp.bfloat16)] * 2,
        compiler_params=pltpu.CompilerParams(vmem_limit_bytes=VMEM_BYTES),
        cost_estimate=cost(1, 1),
    )(counts, slots, *mixed, grads, outs, logs)


def ffn_kernel(block, x_parts, g_parts, counts, *refs):
    xs, refs = refs[:x_parts], refs[x_parts:]
    gs, refs = refs[:g_parts], refs[g_parts:]
    ups, downs, shifts = refs[0:2], refs[2:4], refs[4:6]
    units_ref, back_ref, out_ref, x, g, total, x_sems, g_sems = refs[-8:]
    fetch(xs, x, x_sems)
    fetch(gs, g, g_sems)
    blocks, size, model = x.shape
    width = ups[0].shape[0]
    step = pl.program_id(0)

    @pl.when(step == 0)
    def _():
        total[...] = jnp.zeros(total.shape, total.dtype)

    for k in range(blocks):
        rows = slice(k * size, (k + 1) * size)

        @pl.when(counts[block + k] != 0)
        def _(k=k, rows=rows):
            backs = []
            for side in range(2):
                span = slice(side * width, (side + 1) * width)
                pre = dot_nt(x[k], ups[side][...]) + shifts[side][...]
                grad_units = dot_nt(g[k], downs[side][...])
                bell = jnp.exp2(pre * pre * (-0.5 * LOG2E))
                denominator = 1.0 + (0.3275911 * 0.7071067811865476) * jnp.abs(pre)
                t = pl.reciprocal(denominator, approx=True)
                t = t * (2.0 - denominator * t)
                tail = 0.5 * 1.061405429
                for factor in (-1.453152027, 1.421413741, -0.284496736, 0.254829592):
                    tail = tail * t + 0.5 * factor
                tail = tail * t * bell
                below = jnp.where(pre < 0, tail, 1.0 - tail)
                units_ref[rows, span] = (pre * below).astype(units_ref.dtype)
                slope = below + pre * bell * 0.3989422804014327
                backs.append((grad_units * slope).astype(back_ref.dtype))
                back_ref[rows, span] = backs[-1]
            total[rows] += dot_nn(backs[0], ups[0][...]) + dot_nn(backs[1], ups[1][...])

        @pl.when(counts[block + k] == 0)
        def _(rows=rows):
            units_ref[rows] = jnp.zeros((size, 2 * width), units_ref.dtype)
            back_ref[rows] = jnp.zeros((size, 2 * width), back_ref.dtype)

    @pl.when(step == pl.num_programs(0) - 1)
    def _():
        out_ref[...] = total[...].astype(out_ref.dtype)


def ffn_blocks(place, block, counts, xs, gs, ups, downs, shifts, kept):
    size, width = 512, 256
    model = xs[0].shape[1]
    rows = sum(x.shape[0] for x in xs)
    units = ups[0].shape[0]
    whole = pl.BlockSpec(memory_space=pl.ANY)
    weights = pl.BlockSpec((width, model), lambda u, *_: (u, 0))
    shift = pl.BlockSpec((1, width), lambda u, *_: (0, u))
    output = pl.BlockSpec((rows, 2 * width), lambda u, *_: (place, u))
    full = jax.ShapeDtypeStruct((4 * size, 2 * units), jnp.bfloat16)
    return pl.pallas_call(
        functools.partial(ffn_kernel, block, len(xs), len(gs)),
        grid_spec=pltpu.PrefetchScalarGridSpec(
            num_scalar_prefetch=1,
            grid=(units // width,),
            in_specs=[whole] * (len(xs) + len(gs))
            + [weights] * 4
            + [shift] * 2
            + [whole] * len(kept),
            out_specs=[output, output, pl.BlockSpec((rows, model), lambda u, *_: (0, 0))],
            scratch_shapes=[
                pltpu.VMEM((rows // size, size, model), jnp.bfloat16),
                pltpu.VMEM((rows // size, size, model), jnp.bfloat16),
                pltpu.VMEM((rows, model), jnp.float32),
                pltpu.SemaphoreType.DMA((len(xs),)),
                pltpu.SemaphoreType.DMA((len(gs),)),
            ],
        ),
        out_shape=[full, full, jax.ShapeDtypeStruct((rows, model), jnp.bfloat16)],
        input_output_aliases={len(xs) + len(gs) + 7 + k: k for k in range(len(kept))},
        compiler_params=pltpu.CompilerParams(vmem_limit_bytes=VMEM_BYTES),
        cost_estimate=cost(12 * rows * units * model, 8 * units * model + 8 * rows * model, 4 * rows * units),
    )(counts, *xs, *gs, *ups, *downs, *shifts, *kept)


def arrange(outs, total):
    to_x, to_y, rest = outs
    half = total.shape[0] // 2
    top, bottom = total[:half].astype(to_x.dtype), total[half:].astype(to_x.dtype)
    step = pl.program_id(0)

    @pl.when(step == 0)
    def _():
        to_x[:half] = top
        to_y[:half] = bottom

    @pl.when(step == 1)
    def _():
        to_x[half:] = top
        rest[half : 2 * half] = bottom

    @pl.when(step == 2)
    def _():
        rest[:half] = top
        to_y[half:] = bottom

    @pl.when(step == 3)
    def _():
        rest[2 * half : 3 * half] = top
        rest[3 * half :] = bottom


def arranged(rows, columns):
    sizes = (rows // 4, rows // 4, rows // 2)
    specs = [pl.BlockSpec((size, columns), lambda i, *_: (0, 0)) for size in sizes]
    return specs, [jax.ShapeDtypeStruct((size, columns), jnp.bfloat16) for size in sizes]


def products_kernel(width, order, active, left, own, other, *outs):
    here = active[order[pl.program_id(0)]] != 0

    @pl.when(here)
    def _():
        total = None
        for k in range(own.shape[0] // width):
            rows = slice(k * width, (k + 1) * width)
            for side, right in enumerate((own, other)):
                start = (2 * k + side) * width
                term = dot_nn(left[:, start : start + width], right[rows])
                total = term if total is None else total + term
        arrange(outs, total)

    @pl.when(jnp.logical_not(here))
    def _():
        arrange(outs, jnp.zeros((left.shape[0], own.shape[1]), jnp.float32))


def products(order, counts, left, own, other):
    blocks = counts.shape[0]
    rows, depth = left.shape
    columns = own.shape[1]
    specs, shapes = arranged(rows, columns)
    return pl.pallas_call(
        functools.partial(products_kernel, 256),
        grid_spec=pltpu.PrefetchScalarGridSpec(
            num_scalar_prefetch=2,
            grid=(blocks,),
            in_specs=[
                pl.BlockSpec((rows // blocks, depth), lambda i, order, *_: (order[i], 0)),
                pl.BlockSpec(own.shape, lambda i, *_: (0, 0)),
                pl.BlockSpec(own.shape, lambda i, *_: (0, 0)),
            ],
            out_specs=specs,
        ),
        out_shape=shapes,
        compiler_params=pltpu.CompilerParams(vmem_limit_bytes=VMEM_BYTES),
        cost_estimate=cost(1, 1),
    )(order, counts, left, own, other)


def attend_out_kernel(left, weight, bias, hidden, active, out_ref):
    out_ref[...] = hidden[...].astype(jnp.float32) + active[...] * (
        dot_nn(left[...], weight[0]) + bias[...]
    )


def attend_out(left, weights, bias, hidden, active):
    rows, depth = left.shape
    blocks, _, width = weights.shape
    column = pl.BlockSpec((rows, width), lambda j: (0, j))
    return pl.pallas_call(
        attend_out_kernel,
        grid=(blocks,),
        in_specs=[
            pl.BlockSpec((rows, depth), lambda j: (0, 0)),
            pl.BlockSpec((1, depth, width), lambda j: (j, 0, 0)),
            pl.BlockSpec((1, width), lambda j: (0, j)),
            column,
            pl.BlockSpec((rows, 1), lambda j: (0, 0)),
        ],
        out_specs=column,
        out_shape=jax.ShapeDtypeStruct((rows, blocks * width), jnp.float32),
        compiler_params=pltpu.CompilerParams(vmem_limit_bytes=VMEM_BYTES),
        cost_estimate=cost(2 * rows * depth * blocks * width, 2 * depth * blocks * width + 8 * rows * blocks * width),
    )(left, weights, bias[None], hidden, active)


def attend_out_back_kernel(grad, weight, out_ref, total):
    step = pl.program_id(0)

    @pl.when(step == 0)
    def _():
        total[...] = jnp.zeros(total.shape, total.dtype)

    total[...] += dot_nt(grad[...], weight[0])

    @pl.when(step == pl.num_programs(0) - 1)
    def _():
        out_ref[...] = total[...].astype(out_ref.dtype)


def attend_out_back(grad, weights):
    rows = grad.shape[0]
    blocks, depth, width = weights.shape
    return pl.pallas_call(
        attend_out_back_kernel,
        grid=(blocks,),
        in_specs=[
            pl.BlockSpec((rows, width), lambda j: (0, j)),
            pl.BlockSpec((1, depth, width), lambda j: (j, 0, 0)),
        ],
        out_specs=pl.BlockSpec((rows, depth), lambda j: (0, 0)),
        out_shape=jax.ShapeDtypeStruct((rows, depth), jnp.bfloat16),
        scratch_shapes=[pltpu.VMEM((rows, depth), jnp.float32)],
        compiler_params=pltpu.CompilerParams(vmem_limit_bytes=VMEM_BYTES),
        cost_estimate=cost(1, 1),
    )(grad, weights)


def project_kernel(inputs, side, parts, *refs):
    xs = refs[:inputs]
    weights, shift, out_ref = refs[inputs:]
    slab = weights.shape[1]
    weight = weights[...].reshape(3 * slab, weights.shape[2])
    for k in range(inputs):

        @pl.when(pl.program_id(0) == k)
        def _(k=k):
            mixed = dot_nt(xs[k][...], weight)
            for t in range(3):
                columns = pl.ds(pl.multiple_of(parts[side, t] * slab, slab), slab)
                out_ref[:, columns] = (
                    mixed[:, t * slab : (t + 1) * slab] + shift[:, columns]
                ).astype(out_ref.dtype)


def project(parts, side, xs, weights, shift):
    size, model = xs[0].shape
    slab = weights.shape[1]
    return pl.pallas_call(
        functools.partial(project_kernel, len(xs), side),
        grid_spec=pltpu.PrefetchScalarGridSpec(
            num_scalar_prefetch=1,
            grid=(len(xs),),
            in_specs=[pl.BlockSpec((size, model), lambda i, *_: (0, 0))] * len(xs)
            + [
                pl.BlockSpec(weights.shape, lambda i, *_: (0, 0, 0)),
                pl.BlockSpec(shift.shape, lambda i, *_: (0, 0)),
            ],
            out_specs=pl.BlockSpec((size, 3 * slab), lambda i, *_: (i, 0)),
        ),
        out_shape=jax.ShapeDtypeStruct((len(xs) * size, 3 * slab), jnp.bfloat16),
        compiler_params=pltpu.CompilerParams(vmem_limit_bytes=VMEM_BYTES),
        cost_estimate=pl.CostEstimate(
            flops=6 * len(xs) * size * slab * model,
            bytes_accessed=6 * slab * model + 2 * len(xs) * size * (model + 3 * slab),
            transcendentals=0,
        ),
    )(parts, *xs, weights, shift)


def unproject_kernel(order, parts, active, mine, theirs, own, other, *outs):
    slab = own.shape[1]
    here = active[order[pl.program_id(0)]] != 0

    @pl.when(here)
    def _():
        total = None
        for side, (left, right) in enumerate(((mine, own), (theirs, other))):
            for t in range(3):
                columns = pl.ds(pl.multiple_of(parts[side, t] * slab, slab), slab)
                term = dot_nn(left[:, columns], right[t])
                total = term if total is None else total + term
        arrange(outs, total)

    @pl.when(jnp.logical_not(here))
    def _():
        arrange(outs, jnp.zeros((mine.shape[0], own.shape[2]), jnp.float32))


def unproject(order, parts, counts, mine, theirs, own, other):
    blocks = counts.shape[0]
    rows = mine.shape[0]
    slab, model = own.shape[1:]
    left = pl.BlockSpec((rows // blocks, 3 * slab), lambda i, order, *_: (order[i], 0))
    fixed = pl.BlockSpec(own.shape, lambda i, *_: (0, 0, 0))
    specs, shapes = arranged(rows, model)
    return pl.pallas_call(
        unproject_kernel,
        grid_spec=pltpu.PrefetchScalarGridSpec(
            num_scalar_prefetch=3,
            grid=(blocks,),
            in_specs=[left, left, fixed, fixed],
            out_specs=specs,
        ),
        out_shape=shapes,
        compiler_params=pltpu.CompilerParams(vmem_limit_bytes=VMEM_BYTES),
        cost_estimate=cost(1, 1),
    )(order, parts, counts, mine, theirs, own, other)


def weight_grad_kernel(inputs, added, columns, *refs):
    left, rights = refs[0], refs[1 : 1 + inputs]
    tokens, sems = refs[-2:]
    outs = refs[1 + inputs + added : -2]
    fetch(rights, tokens, sems)
    total = dot_tn(left[...], tokens[0])
    if added:
        total = total + refs[1 + inputs][...].astype(jnp.float32)
    size = outs[0].shape[0]
    for k, out_ref in enumerate(outs):
        out_ref[...] = total[k * size : (k + 1) * size].astype(out_ref.dtype)


def weight_grad(left, columns, tile, rights, extra=None, outputs=1):
    rows = left.shape[0]
    model = rights[0].shape[1]
    steps = columns.shape[0]
    output = pl.BlockSpec((tile // outputs, model), lambda i, *_: (i, 0))
    extras = [] if extra is None else [extra]
    shape = jax.ShapeDtypeStruct((steps * tile // outputs, model), jnp.bfloat16)
    results = pl.pallas_call(
        functools.partial(weight_grad_kernel, len(rights), len(extras)),
        grid_spec=pltpu.PrefetchScalarGridSpec(
            num_scalar_prefetch=1,
            grid=(steps,),
            in_specs=[pl.BlockSpec((rows, tile), lambda i, columns: (0, columns[i]))]
            + [pl.BlockSpec(memory_space=pl.ANY)] * len(rights)
            + [output] * len(extras),
            out_specs=[output] * outputs,
            scratch_shapes=[
                pltpu.VMEM((1, rows, model), jnp.bfloat16),
                pltpu.SemaphoreType.DMA((len(rights),)),
            ],
        ),
        out_shape=[shape] * outputs,
        compiler_params=pltpu.CompilerParams(vmem_limit_bytes=VMEM_BYTES),
        cost_estimate=cost(1, 1),
    )(columns, left, *rights, *extras)
    return results[0] if outputs == 1 else results


def chain_sum(values, axis):
    size = lax.axis_size(axis)
    if size != 4:
        return lax.psum(values.astype(jnp.bfloat16), axis).astype(jnp.float32)
    place = lax.axis_index(axis)
    outer = lax.ppermute(values.astype(jnp.bfloat16), axis, [(0, 1), (3, 2)])
    half = (values + outer.astype(jnp.float32)).astype(jnp.bfloat16)
    other = lax.ppermute(half, axis, [(1, 2), (2, 1)])
    whole = (half.astype(jnp.float32) + other.astype(jnp.float32)).astype(jnp.bfloat16)
    ends = lax.ppermute(whole, axis, [(1, 0), (2, 3)])
    inner = (place == 1) | (place == 2)
    return jnp.where(inner, whole, ends).astype(jnp.float32)


def normalize(values):
    center = values - jnp.mean(values, axis=-1, keepdims=True)
    inverse = lax.rsqrt(jnp.mean(center * center, axis=-1, keepdims=True) + epsilon)
    return center * inverse, inverse


def normalize_back(grad, gain, normal, inverse):
    scaled = grad * gain
    grad_values = inverse * (
        scaled
        - jnp.mean(scaled, axis=-1, keepdims=True)
        - normal * jnp.mean(scaled * normal, axis=-1, keepdims=True)
    )
    return grad_values, jnp.sum(grad * normal, axis=0), jnp.sum(grad, axis=0)


def local_general(
    hidden,
    cotangent,
    exit_layer,
    ln1_gain,
    ln1_bias,
    qkv_weight,
    query_bias,
    value_bias,
    out_weight,
    out_bias,
    ln2_gain,
    ln2_bias,
    up_weight,
    up_bias,
    down_weight,
    down_bias,
):
    width = lax.axis_size("wide")
    rank = lax.axis_index("wide")
    rows, model = hidden.shape
    group = rows * width
    slab = model // width
    head_size = model // HEADS
    units_own = up_weight.shape[0]
    keep = exit_layer >= LAYER
    counts = jnp.sum(keep.astype(jnp.int32), axis=1)
    active = lax.dynamic_slice_in_dim(keep.reshape(group), rank * rows, rows, 0)
    active = active.astype(jnp.float32)[:, None]
    grad_out = cotangent.astype(jnp.float32)

    routes = [[(w, (3 * w + t) % width) for w in range(width)] for t in range(3)]
    part_at = np.zeros((width, 3), np.int32)
    for t in range(3):
        for w, d in routes[t]:
            part_at[d, t] = (3 * w + t) // width
    place_of = jnp.asarray(np.argsort(part_at, axis=1).astype(np.int32))[rank]
    part_of = jnp.asarray(part_at)[rank]

    hidden_wide = hidden.astype(jnp.float32)
    normal1, inverse1 = normalize(hidden_wide)
    normed1 = lax.all_gather(
        (normal1 * ln1_gain + ln1_bias).astype(jnp.bfloat16), "wide", axis=0, tiled=True
    )
    slabs = qkv_weight.reshape(3, slab, model)
    received = jnp.stack([lax.ppermute(slabs[t], "wide", routes[t]) for t in range(3)])
    qkv_own = jnp.concatenate(
        [lax.dynamic_index_in_dim(received, place_of[p], 0, keepdims=False) for p in range(3)]
    )
    own = lambda vector: lax.dynamic_slice_in_dim(vector, rank * slab, slab, 0)
    qkv_shift = jnp.concatenate(
        [own(query_bias), jnp.zeros((slab,), jnp.float32), own(value_bias)]
    )

    grad_ffn = (active * grad_out).astype(jnp.bfloat16)
    down_bias_grad = jnp.sum(grad_ffn.astype(jnp.float32), axis=0)
    piece = rows // CHUNKS
    part = lambda values, c: values[c * piece : (c + 1) * piece]
    gather = lambda values: lax.all_gather(values, "wide", axis=0, tiled=True)
    scatter = lambda values: lax.psum_scatter(
        values.astype(jnp.bfloat16), "wide", scatter_dimension=0, tiled=True
    )
    grad_ffns = [gather(part(grad_ffn, c)) for c in range(CHUNKS)]
    out_whole = gather(out_weight)

    mixed = (dot_nt(normed1, qkv_own) + qkv_shift).astype(jnp.bfloat16)
    mixed = jnp.split(mixed, group // TILE)
    slots = jnp.arange(group // TILE, dtype=jnp.int32).reshape(counts.shape[0], -1)
    attended, logs = attend(mixed, slots, counts, head_size)
    attended_rows = lax.all_to_all(attended, "wide", split_axis=0, concat_axis=1, tiled=True)
    middle = hidden_wide + active * (dot_nn(attended_rows, out_whole) + out_bias)
    normal2, inverse2 = normalize(middle)
    normed2 = (normal2 * ln2_gain + ln2_bias).astype(jnp.bfloat16)
    up_shift = lax.dynamic_slice_in_dim(up_bias, rank * units_own, units_own, 0)

    normed2s = [gather(part(normed2, c)) for c in range(CHUNKS)]
    units, grad_pres, grad_normed2, ffn_out = [], [], [], []
    for c in range(CHUNKS):
        grad_units = dot_nt(grad_ffns[c], down_weight)
        pre = dot_nt(normed2s[c], up_weight) + up_shift
        below = 0.5 + 0.5 * lax.erf(pre * 0.7071067811865476)
        bell = jnp.exp(-0.5 * pre * pre) * 0.3989422804014327
        units.append((pre * below).astype(jnp.bfloat16))
        grad_pres.append((grad_units * (below + pre * bell)).astype(jnp.bfloat16))
        grad_normed2.append(scatter(dot_nn(grad_pres[c], up_weight)))
    for c in range(CHUNKS):
        ffn_out.append(scatter(dot_nn(units[c], down_weight)))
    grad_normed2 = jnp.concatenate(grad_normed2).astype(jnp.float32)
    ffn_out = jnp.concatenate(ffn_out).astype(jnp.float32)
    output = (middle + active * (ffn_out + down_bias)).astype(jnp.bfloat16)

    up_bias_own = sum(jnp.sum(g.astype(jnp.float32), axis=0) for g in grad_pres)
    down_grad = sum(dot_tn(units[c], grad_ffns[c]) for c in range(CHUNKS))
    up_grad = sum(dot_tn(grad_pres[c], normed2s[c]) for c in range(CHUNKS))
    halves = lambda values: jnp.concatenate(
        [chain_sum(half, "batch") for half in jnp.split(values, 2)]
    )
    down_grad = halves(down_grad)
    up_grad = halves(up_grad)

    grad_middle, ln2_gain_grad, ln2_bias_grad = normalize_back(
        grad_normed2, ln2_gain, normal2, inverse2
    )
    grad_middle = grad_out + grad_middle
    grad_branch = (active * grad_middle).astype(jnp.bfloat16)
    out_bias_grad = jnp.sum(grad_branch.astype(jnp.float32), axis=0)
    grad_attended = dot_nt(grad_branch, out_whole).astype(jnp.bfloat16)
    grad_heads = lax.all_to_all(grad_attended, "wide", split_axis=1, concat_axis=0, tiled=True)
    out_grad = chain_sum(scatter(dot_tn(attended_rows, grad_branch)).astype(jnp.float32), "batch")

    placed = lambda vector, size: lax.dynamic_update_slice_in_dim(
        jnp.zeros((size,), jnp.float32), vector, rank * vector.shape[0], 0
    )
    early = lax.psum(
        (
            out_bias_grad,
            ln2_gain_grad,
            ln2_bias_grad,
            placed(up_bias_own, up_bias.shape[0]),
            down_bias_grad,
        ),
        ("batch", "wide"),
    )

    grad_mixed = jnp.concatenate(
        attend_back(mixed, slots, grad_heads, attended, logs, counts, head_size)
    )
    grad_normed1 = scatter(dot_nn(grad_mixed, qkv_own)).astype(jnp.float32)
    sums = jnp.sum(grad_mixed.astype(jnp.float32), axis=0)
    qkv_parts = []
    for t in range(3):
        columns = lax.dynamic_slice_in_dim(grad_mixed, part_of[t] * slab, slab, 1)
        total = chain_sum(dot_tn(columns, normed1), "batch").astype(jnp.bfloat16)
        back = [(d, w) for w, d in routes[t]]
        qkv_parts.append(lax.ppermute(total, "wide", back).astype(jnp.float32))
    qkv_grad = jnp.concatenate(qkv_parts)

    grad_hidden, ln1_gain_grad, ln1_bias_grad = normalize_back(
        grad_normed1, ln1_gain, normal1, inverse1
    )
    input_grad = grad_middle + grad_hidden
    late = lax.psum(
        (
            ln1_gain_grad,
            ln1_bias_grad,
            placed(sums[:slab], model),
            placed(sums[2 * slab :], model),
        ),
        ("batch", "wide"),
    )
    return (
        output,
        input_grad,
        late[0],
        late[1],
        qkv_grad,
        late[2],
        late[3],
        out_grad,
        early[0],
        early[1],
        early[2],
        up_grad,
        early[3],
        down_grad,
        early[4],
    )


def swap(values, bits):
    width = lax.axis_size("wide")
    return lax.ppermute(values, "wide", [(w, w ^ bits) for w in range(width)])


def after(values, *done):
    return lax.optimization_barrier((values, done))[0]


def relay(along_x, along_y):
    half = along_x.shape[0] // 2
    return [swap(along_y[:half], 2), swap(along_x[half:], 4)]


class Scatter:
    def __init__(self, to_x, to_y, rest):
        self.half = half = to_x.shape[0] // 2
        self.sent = (to_x, to_y)
        self.rest = rest
        self.from_x, self.from_y = swap(to_x, 2), swap(to_y, 4)

    def second(self, *done):
        half = self.half
        from_x, from_y = after((self.from_x, self.from_y), *done)
        self.near = (from_x[half:], from_y[half:])
        self.own = self.rest[2 * half :]
        return self.forward(self.rest[:half], self.rest[half : 2 * half], from_x[:half], from_y[:half])

    def forward(self, along_y, along_x, top, bottom):
        wide = lambda values: values.astype(jnp.float32)
        y_top = (wide(along_y) + wide(top)).astype(jnp.bfloat16)
        x_bottom = (wide(along_x) + wide(bottom)).astype(jnp.bfloat16)
        self.last = (swap(y_top, 4), swap(x_bottom, 2))
        return y_top, x_bottom

    def finish(self, *done):
        wide = lambda values: values.astype(jnp.float32)
        y_top, x_bottom = after(self.last, *done)
        x_top, y_bottom = self.near
        return jnp.concatenate(
            [
                wide(self.own[: self.half]) + wide(x_top) + wide(y_top),
                wide(self.own[self.half :]) + wide(x_bottom) + wide(y_bottom),
            ]
        )


def split_for_scatter(own, along_x, along_y, diagonal):
    half = own.shape[0] // 2
    return (
        jnp.concatenate([diagonal[:half], along_x[:half]]),
        jnp.concatenate([diagonal[half:], along_y[half:]]),
        jnp.concatenate([along_y[:half], along_x[half:], own]),
    )


class EarlyScatter(Scatter):
    def __init__(self, own, along_x, along_y):
        self.half = half = own.shape[0] // 2
        self.own, self.along_x, self.along_y = own, along_x, along_y
        self.near = (swap(along_x[:half], 2), swap(along_y[half:], 4))

    def first(self, diagonal):
        self.from_far = (swap(diagonal[: self.half], 2), swap(diagonal[self.half :], 4))
        self.near = after(self.near, diagonal)
        return self.near

    def second(self, *done):
        half = self.half
        far = after(self.from_far, *done)
        return self.forward(self.along_y[:half], self.along_x[half:], *far)


def tree_sum(values):
    total = values + swap(values, 1)
    total = (total + swap(total, 2)) + (swap(total, 4) + swap(total, 6))
    size = lax.axis_size("batch")
    terms = [total] + [
        lax.ppermute(total, "batch", [(z, z ^ bits) for z in range(size)])
        for bits in range(1, size)
    ]
    while len(terms) > 1:
        terms = [terms[k] + terms[k + 1] for k in range(0, len(terms), 2)]
    return terms[0]


def local_chips(
    hidden,
    cotangent,
    exit_layer,
    ln1_gain,
    ln1_bias,
    qkv_weight,
    query_bias,
    value_bias,
    out_weight,
    out_bias,
    ln2_gain,
    ln2_bias,
    up_weight,
    up_bias,
    down_weight,
    down_bias,
):
    width = lax.axis_size("wide")
    rank = lax.axis_index("wide")
    rows, model = hidden.shape
    group = rows * width
    slab = model // width
    head_size = model // HEADS
    units_own = up_weight.shape[0]
    keep = exit_layer >= LAYER
    counts = jnp.sum(keep.astype(jnp.int32), axis=1)
    active = lax.dynamic_slice_in_dim(keep.reshape(group), rank * rows, rows, 0)
    active = active.astype(jnp.float32)[:, None]
    grad_out = cotangent.astype(jnp.float32)

    tiles = jnp.arange(group // rows, dtype=jnp.int32)
    slots = ((tiles ^ rank) & 1) * 4 + ((tiles >> 1) ^ (rank >> 1))
    slots = slots.reshape(counts.shape[0], -1)

    routes = [[(w, (3 * w + t) % width) for w in range(width)] for t in range(3)]
    part_at = np.zeros((width, 3), np.int32)
    for t in range(3):
        for w, d in routes[t]:
            part_at[d, t] = (3 * w + t) // width
    part_at = jnp.asarray(part_at)
    other = rank ^ 1
    parts = jnp.stack([part_at[rank], part_at[other]])

    hidden_wide = hidden.astype(jnp.float32)
    normal1, inverse1 = normalize(hidden_wide)
    slabs = qkv_weight.reshape(3, slab, model)
    slabs = [lax.ppermute(slabs[t], "wide", routes[t]) for t in range(3)]
    normed1 = (normal1 * ln1_gain + ln1_bias).astype(jnp.bfloat16)
    normed1 = [normed1, swap(normed1, 2), swap(normed1, 4)]
    diagonal1 = relay(normed1[1], normed1[2])
    qkv_own = jnp.stack(after(slabs, normed1[1:]))
    qkv_other = swap(qkv_own, 1)

    def shift_of(device):
        own = lambda vector: lax.dynamic_slice_in_dim(vector, device * slab, slab, 0)
        shift = [own(query_bias), jnp.zeros((slab,), jnp.float32), own(value_bias)]
        return jnp.concatenate(shift)[None]

    bias_of = lambda device: lax.dynamic_slice_in_dim(up_bias, device * units_own, units_own, 0)
    up_shifts = [bias_of(rank)[None], bias_of(other)[None]]

    mixed_near = project(parts, 0, normed1, qkv_own, shift_of(rank))
    qkv_other = after(qkv_other, mixed_near, diagonal1)
    lent_near = project(parts, 1, normed1, qkv_other, shift_of(other))
    diagonal1 = after(diagonal1, lent_near)
    lent_far = project(parts, 1, diagonal1, qkv_other, shift_of(other))
    mixed_far = project(parts, 0, after(diagonal1, lent_far), qkv_own, shift_of(rank))
    mixed = [mixed_near, mixed_far, swap(lent_near, 1), swap(lent_far, 1)]

    quarter = model // lax.axis_size("batch")
    start = lax.axis_index("batch") * quarter
    out_quarter = lax.dynamic_slice_in_dim(out_weight, start, quarter, 1)
    out_quarter = lax.all_gather(out_quarter, "wide", axis=0, tiled=True)
    out_blocks = lax.all_gather(after(out_quarter, qkv_own), "batch", axis=0)
    grad_ffn = (after(active, diagonal1) * grad_out).astype(jnp.bfloat16)
    down_bias_grad = jnp.sum(grad_ffn.astype(jnp.float32), axis=0)
    grad_ffn = [grad_ffn, swap(grad_ffn, 2), swap(grad_ffn, 4)]

    attended, logs = attend(mixed, slots, counts, head_size)
    attended_rows = lax.all_to_all(attended, "wide", split_axis=0, concat_axis=1, tiled=True)
    attended_rows = after(attended_rows, grad_ffn[1:])
    up_other, down_other = swap(after((up_weight, down_weight), attended), 1)
    middle = attend_out(attended_rows, out_blocks, out_bias, hidden, active)
    normal2, inverse2 = normalize(middle)
    normed2 = (normal2 * ln2_gain + ln2_bias).astype(jnp.bfloat16)
    normed2 = [normed2, swap(normed2, 2), swap(normed2, 4)]

    per_tile = jnp.sum(keep.reshape(group // rows, rows).astype(jnp.int32), axis=1)
    block_chip = (rank >> 1) ^ jnp.arange(4, dtype=jnp.int32)
    block_counts = per_tile[2 * block_chip + (rank & 1)]
    ups, downs = [up_weight, up_other], [down_weight, down_other]

    def ffn(place, block, xs, gs, kept):
        *kept, partial = ffn_blocks(
            place, block, block_counts, xs, gs, ups, downs, up_shifts, tuple(kept)
        )
        return kept, partial

    kept, partial_own = ffn(2, 0, normed2[:1], grad_ffn[:1], ())
    normed2[1:] = after(normed2[1:], partial_own)
    diagonal2 = relay(normed2[1], normed2[2])
    diagonal_ffn = relay(*after(grad_ffn[1:], attended_rows))
    kept, partial_near = ffn(0, 1, normed2[1:], grad_ffn[1:], kept)
    scatter2 = EarlyScatter(partial_own, partial_near[:rows], partial_near[rows:])
    diagonal2 = after(diagonal2, partial_near)
    (units, grad_pres), partial_far = ffn(3, 3, diagonal2, diagonal_ffn, kept)
    wait = scatter2.first(partial_far)
    tokens2 = [*normed2[1:], normed2[0], *diagonal2]
    tokens_ffn = [*grad_ffn[1:], grad_ffn[0], *diagonal_ffn]

    wide = lambda values: values.astype(jnp.float32)
    lowered = lambda values: values.astype(jnp.bfloat16)
    tile = 512
    tiles = jnp.arange(2 * units_own // tile, dtype=jnp.int32)

    down_own, down_lent = weight_grad(after(units, wait), tiles, tile, tokens_ffn, outputs=2)
    wait = scatter2.second(down_lent)
    down_lent = swap(down_lent, 1)
    up_own, up_lent = weight_grad(after(grad_pres, wait), tiles, tile, tokens2, outputs=2)

    up_lent = swap(up_lent, 1)
    down_sum = lowered(wide(down_own) + wide(after(down_lent, up_own)))
    down_grad = lax.psum(down_sum, "batch")
    grad_middle, ln2_gain_grad, ln2_bias_grad = normalize_back(
        scatter2.finish(up_own), ln2_gain, normal2, inverse2
    )
    grad_middle = grad_out + grad_middle
    grad_branch = (active * grad_middle).astype(jnp.bfloat16)
    out_bias_grad = jnp.sum(grad_branch.astype(jnp.float32), axis=0)
    grad_branch = after(grad_branch, down_sum)
    grad_attended = attend_out_back(grad_branch, out_blocks)
    grad_heads = lax.all_to_all(grad_attended, "wide", split_axis=1, concat_axis=0, tiled=True)
    owners = 2 * block_chip + (rank & 1)
    grad_branch = after(grad_branch, grad_attended)
    out_lent = weight_grad(attended_rows, owners ^ 1, slab, [grad_branch])
    out_lent = swap(out_lent, 1)
    out_own = weight_grad(after(attended_rows, out_lent), owners, slab, [grad_branch], out_lent)

    back_own, back_other = attend_back(
        mixed, slots, after(grad_heads, out_own), attended, logs, counts, head_size
    )

    theirs = swap(back_other, 1)
    out_own = after(out_own, back_own)
    scatter_out = Scatter(*split_for_scatter(*jnp.split(out_own, 4)))
    down_grad = after(down_grad, back_own)
    up_sum = lowered(wide(up_own) + wide(after(up_lent, back_own)))
    up_grad = lax.psum(after(up_sum, down_grad), "batch")
    order = jnp.array([3, 0, 1, 2], jnp.int32)
    ffn_counts = block_counts[jnp.array([1, 2, 0, 3])]
    ffn_parts = products(order, ffn_counts, after(units, up_sum, down_grad, scatter_out.sent), *downs)
    tokens1 = [*normed1, *diagonal1]
    theirs = after(theirs, ffn_parts[0])
    qkv_lent = weight_grad(theirs, parts[1], slab, tokens1)
    wait = scatter_out.second(qkv_lent)
    grad_parts = unproject(
        jnp.array([3, 1, 2, 0], jnp.int32),
        parts,
        block_counts,
        after(back_own, wait),
        theirs,
        qkv_own,
        qkv_other,
    )
    qkv_lent = swap(qkv_lent, 1)
    scatter1 = Scatter(*grad_parts)
    qkv_total = weight_grad(
        after(back_own, grad_parts[0]), parts[0], slab, tokens1, after(qkv_lent, grad_parts[0])
    )
    out_total = lowered(scatter_out.finish(qkv_total))

    up_grad = after(up_grad, out_total)
    qkv_grad, out_grad = lax.psum(after((qkv_total, out_total), up_grad), "batch")
    wait = scatter1.second(out_total, up_grad)
    scatter_ffn = Scatter(*after(ffn_parts, wait))
    grad_normed1 = scatter1.finish(wait, scatter_ffn.sent)
    grad_hidden, ln1_gain_grad, ln1_bias_grad = normalize_back(
        grad_normed1, ln1_gain, normal1, inverse1
    )
    input_grad = grad_middle + grad_hidden
    grad_pres, back_own, back_other = after((grad_pres, back_own, back_other), wait)
    up_bias_own = jnp.sum(wide(grad_pres), axis=0).reshape(-1, 2, 256)
    up_bias_own = [up_bias_own[:, side].reshape(units_own) for side in range(2)]
    sums = jnp.sum(wide(back_own), axis=0) + jnp.sum(wide(back_other), axis=0)
    wait = scatter_ffn.second(input_grad)
    down_grad, up_grad = wide(after(down_grad, wait)), wide(after(up_grad, wait))
    ffn_out = scatter_ffn.finish(down_grad, up_grad)
    output = (middle + active * (ffn_out + down_bias)).astype(jnp.bfloat16)
    qkv_grad = after(qkv_grad, output)
    qkv_grad = jnp.concatenate(
        [
            wide(
                lax.ppermute(
                    qkv_grad[t * slab : (t + 1) * slab], "wide", [(d, w) for w, d in routes[t]]
                )
            )
            for t in range(3)
        ]
    )
    out_grad = wide(out_grad)

    placed = lambda vector, size, device: lax.dynamic_update_slice_in_dim(
        jnp.zeros((size,), jnp.float32), vector, device * vector.shape[0], 0
    )
    smalls = tree_sum(
        jnp.concatenate(
            [
                placed(up_bias_own[0], up_bias.shape[0], rank)
                + placed(up_bias_own[1], up_bias.shape[0], other),
                down_bias_grad,
                out_bias_grad,
                ln2_gain_grad,
                ln2_bias_grad,
                placed(sums[:slab], model, rank),
                placed(sums[2 * slab :], model, rank),
                ln1_gain_grad,
                ln1_bias_grad,
            ]
        )
    )
    up_bias_grad = smalls[: up_bias.shape[0]]
    smalls = smalls[up_bias.shape[0] :].reshape(8, model)
    return (
        output,
        input_grad,
        smalls[6],
        smalls[7],
        qkv_grad,
        smalls[4],
        smalls[5],
        out_grad,
        smalls[1],
        smalls[2],
        smalls[3],
        up_grad,
        up_bias_grad,
        down_grad,
        smalls[0],
    )


def solution(mesh):
    chips = mesh.shape["wide"] == 8 and mesh.shape["batch"] == 4
    local = local_chips if chips else local_general
    rows = P(("batch", "wide"), None)
    weight = P("wide", None)
    return jax.shard_map(
        local,
        mesh=mesh,
        in_specs=(
            rows,
            rows,
            P("batch", None),
            P(),
            P(),
            weight,
            P(),
            P(),
            weight,
            P(),
            P(),
            P(),
            weight,
            P(),
            weight,
            P(),
        ),
        out_specs=(
            rows,
            rows,
            P(),
            P(),
            weight,
            P(),
            P(),
            weight,
            P(),
            P(),
            P(),
            weight,
            P(),
            weight,
            P(),
        ),
        check_vma=False,
    )
```

```python
import functools

import jax
import jax.numpy as jnp
import numpy as np
from jax import lax
from jax.experimental import pallas as pl
from jax.experimental.pallas import tpu as pltpu
from jax.sharding import PartitionSpec as P

HEADS = 32
LAYER = 12
LANES = 128
TILE = 512
CHUNKS = 2
LOG2E = 1.4426950408889634

epsilon = 1e-05
VMEM_BYTES = 48 * 2**20


def cost(flops, size, exponentials=0):
    return pl.CostEstimate(flops=flops, bytes_accessed=size, transcendentals=exponentials)


def dot_nt(left, right):
    return lax.dot_general(
        left, right, (((1,), (1,)), ((), ())), preferred_element_type=jnp.float32
    )


def dot_nn(left, right):
    return lax.dot_general(
        left, right, (((1,), (0,)), ((), ())), preferred_element_type=jnp.float32
    )


def dot_tn(left, right):
    return lax.dot_general(
        left, right, (((0,), (0,)), ((), ())), preferred_element_type=jnp.float32
    )


def head_masks(head_size):
    lane = lax.broadcasted_iota(jnp.int32, (1, LANES), 1)
    return [
        (lane >= h * head_size) & (lane < (h + 1) * head_size)
        for h in range(LANES // head_size)
    ]


def fetch(sources, target, sems):
    size = target.shape[1]
    copies = []
    row = 0
    for source in sources:
        rows = source.shape[0]
        least = min(rows, size)
        for k in range(rows // least):
            place = target.at[row // size, pl.ds(row % size, least)]
            copies.append(
                pltpu.make_async_copy(source.at[pl.ds(k * least, least)], place, sems.at[len(copies)])
            )
            row += least

    @pl.when(pl.program_id(0) == 0)
    def _():
        for copy in copies:
            copy.start()
        for copy in copies:
            copy.wait()


def attend_kernel(head_size, blocks_in, counts, slots, *refs):
    sources = refs[:blocks_in]
    out_ref, log_ref, mixed_ref, key_own, value_own, sems = refs[blocks_in:]
    fetch(sources, mixed_ref, sems)
    length, lanes = out_ref.shape
    tile = mixed_ref.shape[1]
    pack = LANES // head_size
    scale = head_size ** (-0.5) * LOG2E
    sequence = pl.program_id(0)
    blocks = lax.div(counts[sequence] + (tile - 1), tile)
    masks = head_masks(head_size)
    out_ref[...] = jnp.zeros(out_ref.shape, out_ref.dtype)
    log_ref[...] = jnp.zeros(log_ref.shape, log_ref.dtype)
    row = lax.broadcasted_iota(jnp.int32, (tile, tile), 0)
    col = lax.broadcasted_iota(jnp.int32, (tile, tile), 1)
    for pair in range(lanes // LANES):
        base = pair * LANES
        for i in range(length // tile):
            slot = slots[sequence, i]
            keys = mixed_ref[slot, :, lanes + base : lanes + base + LANES]
            values = mixed_ref[slot, :, 2 * lanes + base : 2 * lanes + base + LANES]
            for h in range(pack):
                key_own[h, i * tile : (i + 1) * tile] = jnp.where(masks[h], keys, jnp.zeros_like(keys))
                value_own[h, i * tile : (i + 1) * tile] = jnp.where(
                    masks[h], values, jnp.zeros_like(values)
                )

        def query_block(i, _, pair=pair, base=base):
            start = pl.multiple_of(i * tile, tile)
            queries = mixed_ref[slots[sequence, i], :, base : base + LANES]

            def step(j, carry, diagonal=False):
                total, tops, sums = carry
                first = pl.multiple_of(j * tile, tile)
                new_tops, new_sums, shrinks, adds = [], [], [], []
                for h in range(pack):
                    scores = dot_nt(queries, key_own[h, pl.ds(first, tile)]) * scale
                    if diagonal:
                        scores = jnp.where(col <= row, scores, -1e30)
                    top = jnp.maximum(tops[h], jnp.max(scores, axis=1, keepdims=True))
                    terms = jnp.exp2(scores - top)
                    shrink = jnp.exp2(tops[h] - top)
                    new_tops.append(top)
                    new_sums.append(sums[h] * shrink + jnp.sum(terms, axis=1, keepdims=True))
                    shrinks.append(shrink)
                    adds.append(dot_nn(terms.astype(jnp.bfloat16), value_own[h, pl.ds(first, tile)]))
                shrink = shrinks[0]
                for h in range(1, pack):
                    shrink = jnp.where(masks[h], shrinks[h], shrink)
                total = total * shrink
                for add in adds:
                    total = total + add
                return total, tuple(new_tops), tuple(new_sums)

            carry = (
                jnp.zeros((tile, LANES), jnp.float32),
                tuple(jnp.full((tile, 1), -1e30, jnp.float32) for _ in range(pack)),
                tuple(jnp.zeros((tile, 1), jnp.float32) for _ in range(pack)),
            )
            carry = lax.fori_loop(0, i, step, carry)
            total, tops, sums = step(i, carry, diagonal=True)
            share = 1.0 / sums[0]
            for h in range(1, pack):
                share = jnp.where(masks[h], 1.0 / sums[h], share)
            out_ref[pl.ds(start, tile), base : base + LANES] = (total * share).astype(out_ref.dtype)
            for h in range(pack):
                logs = jnp.broadcast_to(tops[h] + jnp.log2(sums[h]), (tile, LANES))
                index = pair * pack + h
                log_ref[0, index : index + 1, pl.ds(start, tile)] = jnp.transpose(logs)[0:1]
            return 0

        lax.fori_loop(0, blocks, query_block, 0)


def attend(mixed, slots, counts, head_size):
    sequences = counts.shape[0]
    rows = sum(part.shape[0] for part in mixed)
    tile = rows // slots.size
    blocks = rows // tile
    lanes = mixed[0].shape[1] // 3
    length = rows // sequences
    heads = lanes // head_size
    pack = LANES // head_size
    return pl.pallas_call(
        functools.partial(attend_kernel, head_size, len(mixed)),
        grid_spec=pltpu.PrefetchScalarGridSpec(
            num_scalar_prefetch=2,
            grid=(sequences,),
            in_specs=[pl.BlockSpec(memory_space=pl.ANY)] * len(mixed),
            out_specs=[
                pl.BlockSpec((length, lanes), lambda s, *_: (s, 0)),
                pl.BlockSpec((1, heads, length), lambda s, *_: (s, 0, 0)),
            ],
            scratch_shapes=[
                pltpu.VMEM((blocks, tile, 3 * lanes), jnp.bfloat16),
                pltpu.VMEM((pack, length, LANES), jnp.bfloat16),
                pltpu.VMEM((pack, length, LANES), jnp.bfloat16),
                pltpu.SemaphoreType.DMA((blocks,)),
            ],
        ),
        out_shape=[
            jax.ShapeDtypeStruct((rows, lanes), jnp.bfloat16),
            jax.ShapeDtypeStruct((sequences, heads, length), jnp.float32),
        ],
        compiler_params=pltpu.CompilerParams(vmem_limit_bytes=VMEM_BYTES),
        cost_estimate=cost(rows * length * lanes * 2, rows * lanes * 8, rows * length * heads // 2),
    )(counts, slots, *mixed)


def attend_back_kernel(
    head_size,
    blocks_in,
    counts,
    slots,
    *refs,
):
    sources = refs[:blocks_in]
    grad_ref, out_ref, log_ref, own_ref, other_ref, mixed_ref = refs[blocks_in : blocks_in + 6]
    query_own, key_own, grad_own, delta, grad_query, grad_key, grad_value, back_ref, sems = refs[
        blocks_in + 6 :
    ]
    fetch(sources, mixed_ref, sems)
    length, lanes = out_ref.shape
    tile = mixed_ref.shape[1]
    pack = LANES // head_size
    scale = head_size ** (-0.5)
    sequence = pl.program_id(0)
    blocks = lax.div(counts[sequence] + (tile - 1), tile)
    masks = head_masks(head_size)
    for i in range(length // tile):
        back_ref[slots[sequence, i]] = jnp.zeros((tile, 3 * lanes), back_ref.dtype)
    key_row = lax.broadcasted_iota(jnp.int32, (tile, tile), 0)
    query_col = lax.broadcasted_iota(jnp.int32, (tile, tile), 1)
    for pair in range(lanes // LANES):
        base = pair * LANES
        for i in range(length // tile):
            span = slice(i * tile, (i + 1) * tile)
            slot = slots[sequence, i]
            queries = mixed_ref[slot, :, base : base + LANES]
            keys = mixed_ref[slot, :, lanes + base : lanes + base + LANES]
            grads = grad_ref[span, base : base + LANES]
            for h in range(pack):
                query_own[h, span] = jnp.where(masks[h], queries, jnp.zeros_like(queries))
                key_own[h, span] = jnp.where(masks[h], keys, jnp.zeros_like(keys))
                grad_own[h, span] = jnp.where(masks[h], grads, jnp.zeros_like(grads))
        grad_query[...] = jnp.zeros(grad_query.shape, jnp.float32)

        def deltas(i, _, base=base):
            start = pl.multiple_of(i * tile, tile)
            grads = grad_ref[pl.ds(start, tile), base : base + LANES].astype(jnp.float32)
            outs = out_ref[pl.ds(start, tile), base : base + LANES].astype(jnp.float32)
            products = jnp.transpose(grads * outs)
            for h in range(pack):
                delta[h : h + 1, pl.ds(start, tile)] = jnp.sum(
                    products[h * head_size : (h + 1) * head_size], axis=0, keepdims=True
                )
            return 0

        lax.fori_loop(0, blocks, deltas, 0)

        def key_block(j, _, pair=pair, base=base):
            first = pl.multiple_of(j * tile, tile)
            place = slots[sequence, j]
            keys = mixed_ref[place, :, lanes + base : lanes + base + LANES]
            values = mixed_ref[place, :, 2 * lanes + base : 2 * lanes + base + LANES]
            grad_key[...] = jnp.zeros(grad_key.shape, jnp.float32)
            grad_value[...] = jnp.zeros(grad_value.shape, jnp.float32)

            def step(i, diagonal=False):
                start = pl.multiple_of(i * tile, tile)
                add_query, add_key, add_value = [], [], []
                for h in range(pack):
                    index = pair * pack + h
                    query_head = query_own[h, pl.ds(start, tile)]
                    grad_head = grad_own[h, pl.ds(start, tile)]
                    scores = dot_nt(keys, query_head) * (scale * LOG2E)
                    probs = jnp.exp2(scores - log_ref[0, index : index + 1, pl.ds(start, tile)])
                    if diagonal:
                        probs = jnp.where(key_row <= query_col, probs, 0.0)
                    grad_probs = dot_nt(values, grad_head)
                    grad_scores = (
                        probs * (grad_probs - delta[h : h + 1, pl.ds(start, tile)])
                    ).astype(jnp.bfloat16)
                    add_value.append(dot_nn(probs.astype(jnp.bfloat16), grad_head))
                    add_key.append(dot_nn(grad_scores, query_head))
                    add_query.append(dot_tn(grad_scores, key_own[h, pl.ds(first, tile)]))
                grad_value[...] += functools.reduce(jnp.add, add_value)
                grad_key[...] += functools.reduce(jnp.add, add_key)
                grad_query[pl.ds(start, tile), :] += functools.reduce(jnp.add, add_query)

            def off_diagonal(i, _):
                step(i)
                return 0

            step(j, diagonal=True)
            lax.fori_loop(j + 1, blocks, off_diagonal, 0)
            back_ref[place, :, lanes + base : lanes + base + LANES] = (grad_key[...] * scale).astype(
                back_ref.dtype
            )
            back_ref[place, :, 2 * lanes + base : 2 * lanes + base + LANES] = grad_value[...].astype(
                back_ref.dtype
            )
            return 0

        lax.fori_loop(0, blocks, key_block, 0)
        for i in range(length // tile):
            back_ref[slots[sequence, i], :, base : base + LANES] = (
                grad_query[i * tile : (i + 1) * tile] * scale
            ).astype(back_ref.dtype)

    @pl.when(sequence == pl.num_programs(0) - 1)
    def _():
        half = back_ref.shape[0] // 2
        for k in range(half):
            own_ref[k * tile : (k + 1) * tile] = back_ref[k]
            other_ref[k * tile : (k + 1) * tile] = back_ref[half + k]


def attend_back(mixed, slots, grads, outs, logs, counts, head_size):
    sequences = counts.shape[0]
    rows, lanes = outs.shape
    length = rows // sequences
    heads = lanes // head_size
    pack = LANES // head_size
    tile = rows // slots.size
    blocks = rows // tile
    whole = pl.BlockSpec((rows // 2, 3 * lanes), lambda s, *_: (0, 0))
    return pl.pallas_call(
        functools.partial(attend_back_kernel, head_size, len(mixed)),
        grid_spec=pltpu.PrefetchScalarGridSpec(
            num_scalar_prefetch=2,
            grid=(sequences,),
            in_specs=[pl.BlockSpec(memory_space=pl.ANY)] * len(mixed)
            + [
                pl.BlockSpec((length, lanes), lambda s, *_: (s, 0)),
                pl.BlockSpec((length, lanes), lambda s, *_: (s, 0)),
                pl.BlockSpec((1, heads, length), lambda s, *_: (s, 0, 0)),
            ],
            out_specs=[whole, whole],
            scratch_shapes=[
                pltpu.VMEM((blocks, tile, 3 * lanes), jnp.bfloat16),
                pltpu.VMEM((pack, length, LANES), jnp.bfloat16),
                pltpu.VMEM((pack, length, LANES), jnp.bfloat16),
                pltpu.VMEM((pack, length, LANES), jnp.bfloat16),
                pltpu.VMEM((pack, length), jnp.float32),
                pltpu.VMEM((length, LANES), jnp.float32),
                pltpu.VMEM((tile, LANES), jnp.float32),
                pltpu.VMEM((tile, LANES), jnp.float32),
                pltpu.VMEM((blocks, tile, 3 * lanes), jnp.bfloat16),
                pltpu.SemaphoreType.DMA((blocks,)),
            ],
        ),
        out_shape=[jax.ShapeDtypeStruct((rows // 2, 3 * lanes), jnp.bfloat16)] * 2,
        compiler_params=pltpu.CompilerParams(vmem_limit_bytes=VMEM_BYTES),
        cost_estimate=cost(1, 1),
    )(counts, slots, *mixed, grads, outs, logs)


def ffn_kernel(block, x_parts, g_parts, counts, *refs):
    xs, refs = refs[:x_parts], refs[x_parts:]
    gs, refs = refs[:g_parts], refs[g_parts:]
    ups, downs, shifts = refs[0:2], refs[2:4], refs[4:6]
    units_ref, back_ref, out_ref, x, g, total, x_sems, g_sems = refs[-8:]
    fetch(xs, x, x_sems)
    fetch(gs, g, g_sems)
    blocks, size, model = x.shape
    width = ups[0].shape[0]
    step = pl.program_id(0)

    @pl.when(step == 0)
    def _():
        total[...] = jnp.zeros(total.shape, total.dtype)

    for k in range(blocks):
        rows = slice(k * size, (k + 1) * size)

        @pl.when(counts[block + k] != 0)
        def _(k=k, rows=rows):
            backs = []
            for side in range(2):
                span = slice(side * width, (side + 1) * width)
                pre = dot_nt(x[k], ups[side][...]) + shifts[side][...]
                grad_units = dot_nt(g[k], downs[side][...])
                size_of = jnp.abs(pre)
                bell = jnp.exp2(pre * pre * (-0.5 * LOG2E))
                denominator = 1.0 + (0.3275911 * 0.7071067811865476) * size_of
                t = pl.reciprocal(denominator, approx=True)
                t = t * (2.0 - denominator * t)
                tail = 0.5 * 1.061405429
                for factor in (-1.453152027, 1.421413741, -0.284496736, 0.254829592):
                    tail = tail * t + 0.5 * factor
                tail = tail * t
                units = jnp.maximum(pre, 0.0) - size_of * (tail * bell)
                units_ref[rows, span] = units.astype(units_ref.dtype)
                slope = (tail - size_of * 0.3989422804014327) * bell
                slope = jnp.where(pre < 0, slope, 1.0 - slope)
                backs.append((grad_units * slope).astype(back_ref.dtype))
                back_ref[rows, span] = backs[-1]
            total[rows] += dot_nn(backs[0], ups[0][...]) + dot_nn(backs[1], ups[1][...])

        @pl.when(counts[block + k] == 0)
        def _(rows=rows):
            units_ref[rows] = jnp.zeros((size, 2 * width), units_ref.dtype)
            back_ref[rows] = jnp.zeros((size, 2 * width), back_ref.dtype)

    @pl.when(step == pl.num_programs(0) - 1)
    def _():
        out_ref[...] = total[...].astype(out_ref.dtype)


def ffn_blocks(place, block, counts, xs, gs, ups, downs, shifts, kept):
    size, width = 512, 256
    model = xs[0].shape[1]
    rows = sum(x.shape[0] for x in xs)
    units = ups[0].shape[0]
    whole = pl.BlockSpec(memory_space=pl.ANY)
    weights = pl.BlockSpec((width, model), lambda u, *_: (u, 0))
    shift = pl.BlockSpec((1, width), lambda u, *_: (0, u))
    output = pl.BlockSpec((rows, 2 * width), lambda u, *_: (place, u))
    full = jax.ShapeDtypeStruct((4 * size, 2 * units), jnp.bfloat16)
    return pl.pallas_call(
        functools.partial(ffn_kernel, block, len(xs), len(gs)),
        grid_spec=pltpu.PrefetchScalarGridSpec(
            num_scalar_prefetch=1,
            grid=(units // width,),
            in_specs=[whole] * (len(xs) + len(gs))
            + [weights] * 4
            + [shift] * 2
            + [whole] * len(kept),
            out_specs=[output, output, pl.BlockSpec((rows, model), lambda u, *_: (0, 0))],
            scratch_shapes=[
                pltpu.VMEM((rows // size, size, model), jnp.bfloat16),
                pltpu.VMEM((rows // size, size, model), jnp.bfloat16),
                pltpu.VMEM((rows, model), jnp.float32),
                pltpu.SemaphoreType.DMA((len(xs),)),
                pltpu.SemaphoreType.DMA((len(gs),)),
            ],
        ),
        out_shape=[full, full, jax.ShapeDtypeStruct((rows, model), jnp.bfloat16)],
        input_output_aliases={len(xs) + len(gs) + 7 + k: k for k in range(len(kept))},
        compiler_params=pltpu.CompilerParams(vmem_limit_bytes=VMEM_BYTES),
        cost_estimate=cost(12 * rows * units * model, 8 * units * model + 8 * rows * model, 4 * rows * units),
    )(counts, *xs, *gs, *ups, *downs, *shifts, *kept)


def arrange(outs, total):
    to_x, to_y, rest = outs
    half = total.shape[0] // 2
    top, bottom = total[:half].astype(to_x.dtype), total[half:].astype(to_x.dtype)
    step = pl.program_id(0)

    @pl.when(step == 0)
    def _():
        to_x[:half] = top
        to_y[:half] = bottom

    @pl.when(step == 1)
    def _():
        to_x[half:] = top
        rest[half : 2 * half] = bottom

    @pl.when(step == 2)
    def _():
        rest[:half] = top
        to_y[half:] = bottom

    @pl.when(step == 3)
    def _():
        rest[2 * half : 3 * half] = top
        rest[3 * half :] = bottom


def arranged(rows, columns):
    sizes = (rows // 4, rows // 4, rows // 2)
    specs = [pl.BlockSpec((size, columns), lambda i, *_: (0, 0)) for size in sizes]
    return specs, [jax.ShapeDtypeStruct((size, columns), jnp.bfloat16) for size in sizes]


def products_kernel(width, order, active, left, own, other, *outs):
    here = active[order[pl.program_id(0)]] != 0

    @pl.when(here)
    def _():
        total = None
        for k in range(own.shape[0] // width):
            rows = slice(k * width, (k + 1) * width)
            for side, right in enumerate((own, other)):
                start = (2 * k + side) * width
                term = dot_nn(left[:, start : start + width], right[rows])
                total = term if total is None else total + term
        arrange(outs, total)

    @pl.when(jnp.logical_not(here))
    def _():
        arrange(outs, jnp.zeros((left.shape[0], own.shape[1]), jnp.float32))


def products(order, counts, left, own, other):
    blocks = counts.shape[0]
    rows, depth = left.shape
    columns = own.shape[1]
    specs, shapes = arranged(rows, columns)
    return pl.pallas_call(
        functools.partial(products_kernel, 256),
        grid_spec=pltpu.PrefetchScalarGridSpec(
            num_scalar_prefetch=2,
            grid=(blocks,),
            in_specs=[
                pl.BlockSpec((rows // blocks, depth), lambda i, order, *_: (order[i], 0)),
                pl.BlockSpec(own.shape, lambda i, *_: (0, 0)),
                pl.BlockSpec(own.shape, lambda i, *_: (0, 0)),
            ],
            out_specs=specs,
        ),
        out_shape=shapes,
        compiler_params=pltpu.CompilerParams(vmem_limit_bytes=VMEM_BYTES),
        cost_estimate=cost(1, 1),
    )(order, counts, left, own, other)


def attend_out_kernel(left, weight, bias, hidden, active, out_ref):
    out_ref[...] = hidden[...].astype(jnp.float32) + active[...] * (
        dot_nn(left[...], weight[...]) + bias[...]
    )


def attend_out(left, weight, bias, hidden, active):
    rows, depth = left.shape
    columns = weight.shape[1]
    width = 512
    column = pl.BlockSpec((rows, width), lambda j: (0, j))
    return pl.pallas_call(
        attend_out_kernel,
        grid=(columns // width,),
        in_specs=[
            pl.BlockSpec((rows, depth), lambda j: (0, 0)),
            pl.BlockSpec((depth, width), lambda j: (0, j)),
            pl.BlockSpec((1, width), lambda j: (0, j)),
            column,
            pl.BlockSpec((rows, 1), lambda j: (0, 0)),
        ],
        out_specs=column,
        out_shape=jax.ShapeDtypeStruct((rows, columns), jnp.float32),
        compiler_params=pltpu.CompilerParams(vmem_limit_bytes=VMEM_BYTES),
        cost_estimate=cost(2 * rows * depth * columns, 2 * depth * columns + 8 * rows * columns),
    )(left, weight, bias[None], hidden, active)


def attend_out_back_kernel(grad, weight, out_ref):
    out_ref[...] = dot_nt(grad[...], weight[...]).astype(out_ref.dtype)


def attend_out_back(grad, weight):
    rows, columns = grad.shape
    depth = weight.shape[0]
    width = 512
    return pl.pallas_call(
        attend_out_back_kernel,
        grid=(depth // width,),
        in_specs=[
            pl.BlockSpec((rows, columns), lambda j: (0, 0)),
            pl.BlockSpec((width, columns), lambda j: (j, 0)),
        ],
        out_specs=pl.BlockSpec((rows, width), lambda j: (0, j)),
        out_shape=jax.ShapeDtypeStruct((rows, depth), jnp.bfloat16),
        compiler_params=pltpu.CompilerParams(vmem_limit_bytes=VMEM_BYTES),
        cost_estimate=cost(1, 1),
    )(grad, weight)


def project_kernel(inputs, side, parts, *refs):
    xs = refs[:inputs]
    weights, shift, out_ref = refs[inputs:]
    slab = weights.shape[1]
    weight = weights[...].reshape(3 * slab, weights.shape[2])
    for k in range(inputs):

        @pl.when(pl.program_id(0) == k)
        def _(k=k):
            mixed = dot_nt(xs[k][...], weight)
            for t in range(3):
                columns = pl.ds(pl.multiple_of(parts[side, t] * slab, slab), slab)
                out_ref[:, columns] = (
                    mixed[:, t * slab : (t + 1) * slab] + shift[:, columns]
                ).astype(out_ref.dtype)


def project(parts, side, xs, weights, shift):
    size, model = xs[0].shape
    slab = weights.shape[1]
    return pl.pallas_call(
        functools.partial(project_kernel, len(xs), side),
        grid_spec=pltpu.PrefetchScalarGridSpec(
            num_scalar_prefetch=1,
            grid=(len(xs),),
            in_specs=[pl.BlockSpec((size, model), lambda i, *_: (0, 0))] * len(xs)
            + [
                pl.BlockSpec(weights.shape, lambda i, *_: (0, 0, 0)),
                pl.BlockSpec(shift.shape, lambda i, *_: (0, 0)),
            ],
            out_specs=pl.BlockSpec((size, 3 * slab), lambda i, *_: (i, 0)),
        ),
        out_shape=jax.ShapeDtypeStruct((len(xs) * size, 3 * slab), jnp.bfloat16),
        compiler_params=pltpu.CompilerParams(vmem_limit_bytes=VMEM_BYTES),
        cost_estimate=pl.CostEstimate(
            flops=6 * len(xs) * size * slab * model,
            bytes_accessed=6 * slab * model + 2 * len(xs) * size * (model + 3 * slab),
            transcendentals=0,
        ),
    )(parts, *xs, weights, shift)


def unproject_kernel(order, parts, active, mine, theirs, own, other, *outs):
    slab = own.shape[1]
    here = active[order[pl.program_id(0)]] != 0

    @pl.when(here)
    def _():
        total = None
        for side, (left, right) in enumerate(((mine, own), (theirs, other))):
            for t in range(3):
                columns = pl.ds(pl.multiple_of(parts[side, t] * slab, slab), slab)
                term = dot_nn(left[:, columns], right[t])
                total = term if total is None else total + term
        arrange(outs, total)

    @pl.when(jnp.logical_not(here))
    def _():
        arrange(outs, jnp.zeros((mine.shape[0], own.shape[2]), jnp.float32))


def unproject(order, parts, counts, mine, theirs, own, other):
    blocks = counts.shape[0]
    rows = mine.shape[0]
    slab, model = own.shape[1:]
    left = pl.BlockSpec((rows // blocks, 3 * slab), lambda i, order, *_: (order[i], 0))
    fixed = pl.BlockSpec(own.shape, lambda i, *_: (0, 0, 0))
    specs, shapes = arranged(rows, model)
    return pl.pallas_call(
        unproject_kernel,
        grid_spec=pltpu.PrefetchScalarGridSpec(
            num_scalar_prefetch=3,
            grid=(blocks,),
            in_specs=[left, left, fixed, fixed],
            out_specs=specs,
        ),
        out_shape=shapes,
        compiler_params=pltpu.CompilerParams(vmem_limit_bytes=VMEM_BYTES),
        cost_estimate=cost(1, 1),
    )(order, parts, counts, mine, theirs, own, other)


def weight_grad_kernel(inputs, added, columns, *refs):
    left, rights = refs[0], refs[1 : 1 + inputs]
    tokens, sems = refs[-2:]
    outs = refs[1 + inputs + added : -2]
    fetch(rights, tokens, sems)
    total = dot_tn(left[...], tokens[0])
    if added:
        total = total + refs[1 + inputs][...].astype(jnp.float32)
    size = outs[0].shape[0]
    for k, out_ref in enumerate(outs):
        out_ref[...] = total[k * size : (k + 1) * size].astype(out_ref.dtype)


def weight_grad(left, columns, tile, rights, extra=None, outputs=1):
    rows = left.shape[0]
    model = rights[0].shape[1]
    steps = columns.shape[0]
    output = pl.BlockSpec((tile // outputs, model), lambda i, *_: (i, 0))
    extras = [] if extra is None else [extra]
    shape = jax.ShapeDtypeStruct((steps * tile // outputs, model), jnp.bfloat16)
    results = pl.pallas_call(
        functools.partial(weight_grad_kernel, len(rights), len(extras)),
        grid_spec=pltpu.PrefetchScalarGridSpec(
            num_scalar_prefetch=1,
            grid=(steps,),
            in_specs=[pl.BlockSpec((rows, tile), lambda i, columns: (0, columns[i]))]
            + [pl.BlockSpec(memory_space=pl.ANY)] * len(rights)
            + [output] * len(extras),
            out_specs=[output] * outputs,
            scratch_shapes=[
                pltpu.VMEM((1, rows, model), jnp.bfloat16),
                pltpu.SemaphoreType.DMA((len(rights),)),
            ],
        ),
        out_shape=[shape] * outputs,
        compiler_params=pltpu.CompilerParams(vmem_limit_bytes=VMEM_BYTES),
        cost_estimate=cost(1, 1),
    )(columns, left, *rights, *extras)
    return results[0] if outputs == 1 else results


def chain_sum(values, axis):
    size = lax.axis_size(axis)
    if size != 4:
        return lax.psum(values.astype(jnp.bfloat16), axis).astype(jnp.float32)
    place = lax.axis_index(axis)
    outer = lax.ppermute(values.astype(jnp.bfloat16), axis, [(0, 1), (3, 2)])
    half = (values + outer.astype(jnp.float32)).astype(jnp.bfloat16)
    other = lax.ppermute(half, axis, [(1, 2), (2, 1)])
    whole = (half.astype(jnp.float32) + other.astype(jnp.float32)).astype(jnp.bfloat16)
    ends = lax.ppermute(whole, axis, [(1, 0), (2, 3)])
    inner = (place == 1) | (place == 2)
    return jnp.where(inner, whole, ends).astype(jnp.float32)


def normalize(values):
    center = values - jnp.mean(values, axis=-1, keepdims=True)
    inverse = lax.rsqrt(jnp.mean(center * center, axis=-1, keepdims=True) + epsilon)
    return center * inverse, inverse


def normalize_back(grad, gain, normal, inverse):
    scaled = grad * gain
    grad_values = inverse * (
        scaled
        - jnp.mean(scaled, axis=-1, keepdims=True)
        - normal * jnp.mean(scaled * normal, axis=-1, keepdims=True)
    )
    return grad_values, jnp.sum(grad * normal, axis=0), jnp.sum(grad, axis=0)


def local_general(
    hidden,
    cotangent,
    exit_layer,
    ln1_gain,
    ln1_bias,
    qkv_weight,
    query_bias,
    value_bias,
    out_weight,
    out_bias,
    ln2_gain,
    ln2_bias,
    up_weight,
    up_bias,
    down_weight,
    down_bias,
):
    width = lax.axis_size("wide")
    rank = lax.axis_index("wide")
    rows, model = hidden.shape
    group = rows * width
    slab = model // width
    head_size = model // HEADS
    units_own = up_weight.shape[0]
    keep = exit_layer >= LAYER
    counts = jnp.sum(keep.astype(jnp.int32), axis=1)
    active = lax.dynamic_slice_in_dim(keep.reshape(group), rank * rows, rows, 0)
    active = active.astype(jnp.float32)[:, None]
    grad_out = cotangent.astype(jnp.float32)

    routes = [[(w, (3 * w + t) % width) for w in range(width)] for t in range(3)]
    part_at = np.zeros((width, 3), np.int32)
    for t in range(3):
        for w, d in routes[t]:
            part_at[d, t] = (3 * w + t) // width
    place_of = jnp.asarray(np.argsort(part_at, axis=1).astype(np.int32))[rank]
    part_of = jnp.asarray(part_at)[rank]

    hidden_wide = hidden.astype(jnp.float32)
    normal1, inverse1 = normalize(hidden_wide)
    normed1 = lax.all_gather(
        (normal1 * ln1_gain + ln1_bias).astype(jnp.bfloat16), "wide", axis=0, tiled=True
    )
    slabs = qkv_weight.reshape(3, slab, model)
    received = jnp.stack([lax.ppermute(slabs[t], "wide", routes[t]) for t in range(3)])
    qkv_own = jnp.concatenate(
        [lax.dynamic_index_in_dim(received, place_of[p], 0, keepdims=False) for p in range(3)]
    )
    own = lambda vector: lax.dynamic_slice_in_dim(vector, rank * slab, slab, 0)
    qkv_shift = jnp.concatenate(
        [own(query_bias), jnp.zeros((slab,), jnp.float32), own(value_bias)]
    )

    grad_ffn = (active * grad_out).astype(jnp.bfloat16)
    down_bias_grad = jnp.sum(grad_ffn.astype(jnp.float32), axis=0)
    piece = rows // CHUNKS
    part = lambda values, c: values[c * piece : (c + 1) * piece]
    gather = lambda values: lax.all_gather(values, "wide", axis=0, tiled=True)
    scatter = lambda values: lax.psum_scatter(
        values.astype(jnp.bfloat16), "wide", scatter_dimension=0, tiled=True
    )
    grad_ffns = [gather(part(grad_ffn, c)) for c in range(CHUNKS)]
    out_whole = gather(out_weight)

    mixed = (dot_nt(normed1, qkv_own) + qkv_shift).astype(jnp.bfloat16)
    mixed = jnp.split(mixed, group // TILE)
    slots = jnp.arange(group // TILE, dtype=jnp.int32).reshape(counts.shape[0], -1)
    attended, logs = attend(mixed, slots, counts, head_size)
    attended_rows = lax.all_to_all(attended, "wide", split_axis=0, concat_axis=1, tiled=True)
    middle = hidden_wide + active * (dot_nn(attended_rows, out_whole) + out_bias)
    normal2, inverse2 = normalize(middle)
    normed2 = (normal2 * ln2_gain + ln2_bias).astype(jnp.bfloat16)
    up_shift = lax.dynamic_slice_in_dim(up_bias, rank * units_own, units_own, 0)

    normed2s = [gather(part(normed2, c)) for c in range(CHUNKS)]
    units, grad_pres, grad_normed2, ffn_out = [], [], [], []
    for c in range(CHUNKS):
        grad_units = dot_nt(grad_ffns[c], down_weight)
        pre = dot_nt(normed2s[c], up_weight) + up_shift
        below = 0.5 + 0.5 * lax.erf(pre * 0.7071067811865476)
        bell = jnp.exp(-0.5 * pre * pre) * 0.3989422804014327
        units.append((pre * below).astype(jnp.bfloat16))
        grad_pres.append((grad_units * (below + pre * bell)).astype(jnp.bfloat16))
        grad_normed2.append(scatter(dot_nn(grad_pres[c], up_weight)))
    for c in range(CHUNKS):
        ffn_out.append(scatter(dot_nn(units[c], down_weight)))
    grad_normed2 = jnp.concatenate(grad_normed2).astype(jnp.float32)
    ffn_out = jnp.concatenate(ffn_out).astype(jnp.float32)
    output = (middle + active * (ffn_out + down_bias)).astype(jnp.bfloat16)

    up_bias_own = sum(jnp.sum(g.astype(jnp.float32), axis=0) for g in grad_pres)
    down_grad = sum(dot_tn(units[c], grad_ffns[c]) for c in range(CHUNKS))
    up_grad = sum(dot_tn(grad_pres[c], normed2s[c]) for c in range(CHUNKS))
    halves = lambda values: jnp.concatenate(
        [chain_sum(half, "batch") for half in jnp.split(values, 2)]
    )
    down_grad = halves(down_grad)
    up_grad = halves(up_grad)

    grad_middle, ln2_gain_grad, ln2_bias_grad = normalize_back(
        grad_normed2, ln2_gain, normal2, inverse2
    )
    grad_middle = grad_out + grad_middle
    grad_branch = (active * grad_middle).astype(jnp.bfloat16)
    out_bias_grad = jnp.sum(grad_branch.astype(jnp.float32), axis=0)
    grad_attended = dot_nt(grad_branch, out_whole).astype(jnp.bfloat16)
    grad_heads = lax.all_to_all(grad_attended, "wide", split_axis=1, concat_axis=0, tiled=True)
    out_grad = chain_sum(scatter(dot_tn(attended_rows, grad_branch)).astype(jnp.float32), "batch")

    placed = lambda vector, size: lax.dynamic_update_slice_in_dim(
        jnp.zeros((size,), jnp.float32), vector, rank * vector.shape[0], 0
    )
    early = lax.psum(
        (
            out_bias_grad,
            ln2_gain_grad,
            ln2_bias_grad,
            placed(up_bias_own, up_bias.shape[0]),
            down_bias_grad,
        ),
        ("batch", "wide"),
    )

    grad_mixed = jnp.concatenate(
        attend_back(mixed, slots, grad_heads, attended, logs, counts, head_size)
    )
    grad_normed1 = scatter(dot_nn(grad_mixed, qkv_own)).astype(jnp.float32)
    sums = jnp.sum(grad_mixed.astype(jnp.float32), axis=0)
    qkv_parts = []
    for t in range(3):
        columns = lax.dynamic_slice_in_dim(grad_mixed, part_of[t] * slab, slab, 1)
        total = chain_sum(dot_tn(columns, normed1), "batch").astype(jnp.bfloat16)
        back = [(d, w) for w, d in routes[t]]
        qkv_parts.append(lax.ppermute(total, "wide", back).astype(jnp.float32))
    qkv_grad = jnp.concatenate(qkv_parts)

    grad_hidden, ln1_gain_grad, ln1_bias_grad = normalize_back(
        grad_normed1, ln1_gain, normal1, inverse1
    )
    input_grad = grad_middle + grad_hidden
    late = lax.psum(
        (
            ln1_gain_grad,
            ln1_bias_grad,
            placed(sums[:slab], model),
            placed(sums[2 * slab :], model),
        ),
        ("batch", "wide"),
    )
    return (
        output,
        input_grad,
        late[0],
        late[1],
        qkv_grad,
        late[2],
        late[3],
        out_grad,
        early[0],
        early[1],
        early[2],
        up_grad,
        early[3],
        down_grad,
        early[4],
    )


def swap(values, bits):
    width = lax.axis_size("wide")
    return lax.ppermute(values, "wide", [(w, w ^ bits) for w in range(width)])


def after(values, *done):
    return lax.optimization_barrier((values, done))[0]


def relay(along_x, along_y):
    half = along_x.shape[0] // 2
    return [swap(along_y[:half], 2), swap(along_x[half:], 4)]


class Scatter:
    def __init__(self, to_x, to_y, rest):
        self.half = half = to_x.shape[0] // 2
        self.sent = (to_x, to_y)
        self.rest = rest
        self.from_x, self.from_y = swap(to_x, 2), swap(to_y, 4)

    def second(self, *done):
        half = self.half
        from_x, from_y = after((self.from_x, self.from_y), *done)
        self.near = (from_x[half:], from_y[half:])
        self.own = self.rest[2 * half :]
        return self.forward(self.rest[:half], self.rest[half : 2 * half], from_x[:half], from_y[:half])

    def forward(self, along_y, along_x, top, bottom):
        wide = lambda values: values.astype(jnp.float32)
        y_top = (wide(along_y) + wide(top)).astype(jnp.bfloat16)
        x_bottom = (wide(along_x) + wide(bottom)).astype(jnp.bfloat16)
        self.last = (swap(y_top, 4), swap(x_bottom, 2))
        return y_top, x_bottom

    def finish(self, *done):
        wide = lambda values: values.astype(jnp.float32)
        y_top, x_bottom = after(self.last, *done)
        x_top, y_bottom = self.near
        return jnp.concatenate(
            [
                wide(self.own[: self.half]) + wide(x_top) + wide(y_top),
                wide(self.own[self.half :]) + wide(x_bottom) + wide(y_bottom),
            ]
        )


def split_for_scatter(own, along_x, along_y, diagonal):
    half = own.shape[0] // 2
    return (
        jnp.concatenate([diagonal[:half], along_x[:half]]),
        jnp.concatenate([diagonal[half:], along_y[half:]]),
        jnp.concatenate([along_y[:half], along_x[half:], own]),
    )


class EarlyScatter(Scatter):
    def __init__(self, own, along_x, along_y):
        self.half = half = own.shape[0] // 2
        self.own, self.along_x, self.along_y = own, along_x, along_y
        self.near = (swap(along_x[:half], 2), swap(along_y[half:], 4))

    def first(self, diagonal):
        self.from_far = (swap(diagonal[: self.half], 2), swap(diagonal[self.half :], 4))
        self.near = after(self.near, diagonal)
        return self.near

    def second(self, *done):
        half = self.half
        far = after(self.from_far, *done)
        return self.forward(self.along_y[:half], self.along_x[half:], *far)


def tree_sum(values):
    total = values + swap(values, 1)
    total = (total + swap(total, 2)) + (swap(total, 4) + swap(total, 6))
    size = lax.axis_size("batch")
    terms = [total] + [
        lax.ppermute(total, "batch", [(z, z ^ bits) for z in range(size)])
        for bits in range(1, size)
    ]
    while len(terms) > 1:
        terms = [terms[k] + terms[k + 1] for k in range(0, len(terms), 2)]
    return terms[0]


def local_chips(
    hidden,
    cotangent,
    exit_layer,
    ln1_gain,
    ln1_bias,
    qkv_weight,
    query_bias,
    value_bias,
    out_weight,
    out_bias,
    ln2_gain,
    ln2_bias,
    up_weight,
    up_bias,
    down_weight,
    down_bias,
):
    width = lax.axis_size("wide")
    rank = lax.axis_index("wide")
    rows, model = hidden.shape
    group = rows * width
    slab = model // width
    head_size = model // HEADS
    units_own = up_weight.shape[0]
    keep = exit_layer >= LAYER
    counts = jnp.sum(keep.astype(jnp.int32), axis=1)
    active = lax.dynamic_slice_in_dim(keep.reshape(group), rank * rows, rows, 0)
    active = active.astype(jnp.float32)[:, None]
    grad_out = cotangent.astype(jnp.float32)

    tiles = jnp.arange(group // rows, dtype=jnp.int32)
    slots = ((tiles ^ rank) & 1) * 4 + ((tiles >> 1) ^ (rank >> 1))
    slots = slots.reshape(counts.shape[0], -1)

    routes = [[(w, (3 * w + t) % width) for w in range(width)] for t in range(3)]
    part_at = np.zeros((width, 3), np.int32)
    for t in range(3):
        for w, d in routes[t]:
            part_at[d, t] = (3 * w + t) // width
    part_at = jnp.asarray(part_at)
    other = rank ^ 1
    parts = jnp.stack([part_at[rank], part_at[other]])

    hidden_wide = hidden.astype(jnp.float32)
    normal1, inverse1 = normalize(hidden_wide)
    slabs = qkv_weight.reshape(3, slab, model)
    slabs = [lax.ppermute(slabs[t], "wide", routes[t]) for t in range(3)]
    normed1 = (normal1 * ln1_gain + ln1_bias).astype(jnp.bfloat16)
    normed1 = [normed1, swap(normed1, 2), swap(normed1, 4)]
    diagonal1 = relay(normed1[1], normed1[2])
    qkv_own = jnp.stack(after(slabs, normed1[1:]))
    qkv_other = swap(qkv_own, 1)

    def shift_of(device):
        own = lambda vector: lax.dynamic_slice_in_dim(vector, device * slab, slab, 0)
        shift = [own(query_bias), jnp.zeros((slab,), jnp.float32), own(value_bias)]
        return jnp.concatenate(shift)[None]

    bias_of = lambda device: lax.dynamic_slice_in_dim(up_bias, device * units_own, units_own, 0)
    up_shifts = [bias_of(rank)[None], bias_of(other)[None]]

    mixed_near = project(parts, 0, normed1, qkv_own, shift_of(rank))
    qkv_other = after(qkv_other, mixed_near, diagonal1)
    lent_near = project(parts, 1, normed1, qkv_other, shift_of(other))
    diagonal1 = after(diagonal1, lent_near)
    lent_far = project(parts, 1, diagonal1, qkv_other, shift_of(other))
    mixed_far = project(parts, 0, after(diagonal1, lent_far), qkv_own, shift_of(rank))
    mixed = [mixed_near, mixed_far, swap(lent_near, 1), swap(lent_far, 1)]

    out_whole = lax.all_gather(after(out_weight, diagonal1), "wide", axis=0, tiled=True)
    grad_ffn = (after(active, diagonal1) * grad_out).astype(jnp.bfloat16)
    down_bias_grad = jnp.sum(grad_ffn.astype(jnp.float32), axis=0)
    grad_ffn = [grad_ffn, swap(grad_ffn, 2), swap(grad_ffn, 4)]

    attended, logs = attend(mixed, slots, counts, head_size)
    attended_rows = lax.all_to_all(attended, "wide", split_axis=0, concat_axis=1, tiled=True)
    attended_rows = after(attended_rows, grad_ffn[1:])
    up_other, down_other = swap(after((up_weight, down_weight), attended), 1)
    middle = attend_out(attended_rows, out_whole, out_bias, hidden, active)
    normal2, inverse2 = normalize(middle)
    normed2 = (normal2 * ln2_gain + ln2_bias).astype(jnp.bfloat16)
    normed2 = [normed2, swap(normed2, 2), swap(normed2, 4)]

    per_tile = jnp.sum(keep.reshape(group // rows, rows).astype(jnp.int32), axis=1)
    block_chip = (rank >> 1) ^ jnp.arange(4, dtype=jnp.int32)
    block_counts = per_tile[2 * block_chip + (rank & 1)]
    ups, downs = [up_weight, up_other], [down_weight, down_other]

    def ffn(place, block, xs, gs, kept):
        *kept, partial = ffn_blocks(
            place, block, block_counts, xs, gs, ups, downs, up_shifts, tuple(kept)
        )
        return kept, partial

    kept, partial_own = ffn(2, 0, normed2[:1], grad_ffn[:1], ())
    normed2[1:] = after(normed2[1:], partial_own)
    diagonal2 = relay(normed2[1], normed2[2])
    diagonal_ffn = relay(*after(grad_ffn[1:], attended_rows))
    kept, partial_near = ffn(0, 1, normed2[1:], grad_ffn[1:], kept)
    scatter2 = EarlyScatter(partial_own, partial_near[:rows], partial_near[rows:])
    diagonal2 = after(diagonal2, partial_near)
    (units, grad_pres), partial_far = ffn(3, 3, diagonal2, diagonal_ffn, kept)
    wait = scatter2.first(partial_far)
    tokens2 = [*normed2[1:], normed2[0], *diagonal2]
    tokens_ffn = [*grad_ffn[1:], grad_ffn[0], *diagonal_ffn]

    wide = lambda values: values.astype(jnp.float32)
    lowered = lambda values: values.astype(jnp.bfloat16)
    tile = 512
    tiles = jnp.arange(2 * units_own // tile, dtype=jnp.int32)

    down_own, down_lent = weight_grad(after(units, wait), tiles, tile, tokens_ffn, outputs=2)
    wait = scatter2.second(down_lent)
    down_lent = swap(down_lent, 1)
    up_own, up_lent = weight_grad(after(grad_pres, wait), tiles, tile, tokens2, outputs=2)

    up_lent = swap(up_lent, 1)
    down_sum = lowered(wide(down_own) + wide(after(down_lent, up_own)))
    down_grad = lax.psum(down_sum, "batch")
    grad_middle, ln2_gain_grad, ln2_bias_grad = normalize_back(
        scatter2.finish(up_own), ln2_gain, normal2, inverse2
    )
    grad_middle = grad_out + grad_middle
    grad_branch = (active * grad_middle).astype(jnp.bfloat16)
    out_bias_grad = jnp.sum(grad_branch.astype(jnp.float32), axis=0)
    grad_branch = after(grad_branch, down_sum)
    grad_attended = attend_out_back(grad_branch, out_whole)
    grad_heads = lax.all_to_all(grad_attended, "wide", split_axis=1, concat_axis=0, tiled=True)
    owners = 2 * block_chip + (rank & 1)
    grad_branch = after(grad_branch, grad_attended)
    out_lent = weight_grad(attended_rows, owners ^ 1, slab, [grad_branch])
    out_lent = swap(out_lent, 1)
    out_own = weight_grad(after(attended_rows, out_lent), owners, slab, [grad_branch], out_lent)

    back_own, back_other = attend_back(
        mixed, slots, after(grad_heads, out_own), attended, logs, counts, head_size
    )

    theirs = swap(back_other, 1)
    out_own = after(out_own, back_own)
    scatter_out = Scatter(*split_for_scatter(*jnp.split(out_own, 4)))
    down_grad = after(down_grad, back_own)
    up_sum = lowered(wide(up_own) + wide(after(up_lent, back_own)))
    up_grad = lax.psum(after(up_sum, down_grad), "batch")
    order = jnp.array([3, 0, 1, 2], jnp.int32)
    ffn_counts = block_counts[jnp.array([1, 2, 0, 3])]
    ffn_parts = products(order, ffn_counts, after(units, up_sum, down_grad, scatter_out.sent), *downs)
    tokens1 = [*normed1, *diagonal1]
    theirs = after(theirs, ffn_parts[0])
    qkv_lent = weight_grad(theirs, parts[1], slab, tokens1)
    wait = scatter_out.second(qkv_lent)
    grad_parts = unproject(
        jnp.array([3, 1, 2, 0], jnp.int32),
        parts,
        block_counts,
        after(back_own, wait),
        theirs,
        qkv_own,
        qkv_other,
    )
    qkv_lent = swap(qkv_lent, 1)
    scatter1 = Scatter(*grad_parts)
    qkv_total = weight_grad(
        after(back_own, grad_parts[0]), parts[0], slab, tokens1, after(qkv_lent, grad_parts[0])
    )
    out_total = lowered(scatter_out.finish(qkv_total))

    up_grad = after(up_grad, out_total)
    qkv_grad, out_grad = lax.psum(after((qkv_total, out_total), up_grad), "batch")
    wait = scatter1.second(out_total, up_grad)
    scatter_ffn = Scatter(*after(ffn_parts, wait))
    grad_normed1 = scatter1.finish(wait, scatter_ffn.sent)
    grad_hidden, ln1_gain_grad, ln1_bias_grad = normalize_back(
        grad_normed1, ln1_gain, normal1, inverse1
    )
    input_grad = grad_middle + grad_hidden
    grad_pres, back_own, back_other = after((grad_pres, back_own, back_other), wait)
    up_bias_own = jnp.sum(wide(grad_pres), axis=0).reshape(-1, 2, 256)
    up_bias_own = [up_bias_own[:, side].reshape(units_own) for side in range(2)]
    sums = jnp.sum(wide(back_own), axis=0) + jnp.sum(wide(back_other), axis=0)
    wait = scatter_ffn.second(input_grad)
    down_grad, up_grad = wide(after(down_grad, wait)), wide(after(up_grad, wait))
    ffn_out = scatter_ffn.finish(down_grad, up_grad)
    output = (middle + active * (ffn_out + down_bias)).astype(jnp.bfloat16)
    placed = lambda vector, size, device: lax.dynamic_update_slice_in_dim(
        jnp.zeros((size,), jnp.float32), vector, device * vector.shape[0], 0
    )
    smalls = tree_sum(
        jnp.concatenate(
            [
                placed(up_bias_own[0], up_bias.shape[0], rank)
                + placed(up_bias_own[1], up_bias.shape[0], other),
                down_bias_grad,
                out_bias_grad,
                ln2_gain_grad,
                ln2_bias_grad,
                placed(sums[:slab], model, rank),
                placed(sums[2 * slab :], model, rank),
                ln1_gain_grad,
                ln1_bias_grad,
            ]
        )
    )
    up_bias_grad = smalls[: up_bias.shape[0]]
    smalls = smalls[up_bias.shape[0] :].reshape(8, model)
    qkv_grad, out_grad = after((qkv_grad, out_grad), output, smalls)
    qkv_grad = jnp.concatenate(
        [
            wide(
                lax.ppermute(
                    qkv_grad[t * slab : (t + 1) * slab], "wide", [(d, w) for w, d in routes[t]]
                )
            )
            for t in range(3)
        ]
    )
    out_grad = wide(out_grad)
    return (
        output,
        input_grad,
        smalls[6],
        smalls[7],
        qkv_grad,
        smalls[4],
        smalls[5],
        out_grad,
        smalls[1],
        smalls[2],
        smalls[3],
        up_grad,
        up_bias_grad,
        down_grad,
        smalls[0],
    )


def solution(mesh):
    chips = mesh.shape["wide"] == 8 and mesh.shape["batch"] == 4
    local = local_chips if chips else local_general
    rows = P(("batch", "wide"), None)
    weight = P("wide", None)
    return jax.shard_map(
        local,
        mesh=mesh,
        in_specs=(
            rows,
            rows,
            P("batch", None),
            P(),
            P(),
            weight,
            P(),
            P(),
            weight,
            P(),
            P(),
            P(),
            weight,
            P(),
            weight,
            P(),
        ),
        out_specs=(
            rows,
            rows,
            P(),
            P(),
            weight,
            P(),
            P(),
            weight,
            P(),
            P(),
            P(),
            weight,
            P(),
            weight,
            P(),
        ),
        check_vma=False,
    )
```

```python
import functools

import jax
import jax.numpy as jnp
import numpy as np
from jax import lax
from jax.experimental import pallas as pl
from jax.experimental.pallas import tpu as pltpu
from jax.sharding import PartitionSpec as P

HEADS = 32
LAYER = 12
LANES = 128
TILE = 512
CHUNKS = 2
LOG2E = 1.4426950408889634

epsilon = 1e-05
VMEM_BYTES = 48 * 2**20


def cost(flops, size, exponentials=0):
    return pl.CostEstimate(flops=flops, bytes_accessed=size, transcendentals=exponentials)


def dot_nt(left, right):
    return lax.dot_general(
        left, right, (((1,), (1,)), ((), ())), preferred_element_type=jnp.float32
    )


def dot_nn(left, right):
    return lax.dot_general(
        left, right, (((1,), (0,)), ((), ())), preferred_element_type=jnp.float32
    )


def dot_tn(left, right):
    return lax.dot_general(
        left, right, (((0,), (0,)), ((), ())), preferred_element_type=jnp.float32
    )


def head_masks(head_size):
    lane = lax.broadcasted_iota(jnp.int32, (1, LANES), 1)
    return [
        (lane >= h * head_size) & (lane < (h + 1) * head_size)
        for h in range(LANES // head_size)
    ]


def fetch(sources, target, sems):
    size = target.shape[1]
    copies = []
    row = 0
    for source in sources:
        rows = source.shape[0]
        least = min(rows, size)
        for k in range(rows // least):
            place = target.at[row // size, pl.ds(row % size, least)]
            copies.append(
                pltpu.make_async_copy(source.at[pl.ds(k * least, least)], place, sems.at[len(copies)])
            )
            row += least

    @pl.when(pl.program_id(0) == 0)
    def _():
        for copy in copies:
            copy.start()
        for copy in copies:
            copy.wait()


def attend_kernel(head_size, blocks_in, counts, slots, *refs):
    sources = refs[:blocks_in]
    out_ref, log_ref, mixed_ref, key_own, value_own, sems = refs[blocks_in:]
    fetch(sources, mixed_ref, sems)
    length, lanes = out_ref.shape
    tile = mixed_ref.shape[1]
    pack = LANES // head_size
    scale = head_size ** (-0.5) * LOG2E
    sequence = pl.program_id(0)
    blocks = lax.div(counts[sequence] + (tile - 1), tile)
    masks = head_masks(head_size)
    out_ref[...] = jnp.zeros(out_ref.shape, out_ref.dtype)
    log_ref[...] = jnp.zeros(log_ref.shape, log_ref.dtype)
    row = lax.broadcasted_iota(jnp.int32, (tile, tile), 0)
    col = lax.broadcasted_iota(jnp.int32, (tile, tile), 1)
    for pair in range(lanes // LANES):
        base = pair * LANES
        for i in range(length // tile):
            slot = slots[sequence, i]
            keys = mixed_ref[slot, :, lanes + base : lanes + base + LANES]
            values = mixed_ref[slot, :, 2 * lanes + base : 2 * lanes + base + LANES]
            for h in range(pack):
                key_own[h, i * tile : (i + 1) * tile] = jnp.where(masks[h], keys, jnp.zeros_like(keys))
                value_own[h, i * tile : (i + 1) * tile] = jnp.where(
                    masks[h], values, jnp.zeros_like(values)
                )

        def query_block(i, _, pair=pair, base=base):
            start = pl.multiple_of(i * tile, tile)
            queries = mixed_ref[slots[sequence, i], :, base : base + LANES]

            def step(j, carry, diagonal=False):
                total, tops, sums = carry
                first = pl.multiple_of(j * tile, tile)
                new_tops, new_sums, shrinks, adds = [], [], [], []
                for h in range(pack):
                    scores = dot_nt(queries, key_own[h, pl.ds(first, tile)]) * scale
                    if diagonal:
                        scores = jnp.where(col <= row, scores, -1e30)
                    top = jnp.maximum(tops[h], jnp.max(scores, axis=1, keepdims=True))
                    terms = jnp.exp2(scores - top)
                    shrink = jnp.exp2(tops[h] - top)
                    new_tops.append(top)
                    new_sums.append(sums[h] * shrink + jnp.sum(terms, axis=1, keepdims=True))
                    shrinks.append(shrink)
                    adds.append(dot_nn(terms.astype(jnp.bfloat16), value_own[h, pl.ds(first, tile)]))
                shrink = shrinks[0]
                for h in range(1, pack):
                    shrink = jnp.where(masks[h], shrinks[h], shrink)
                total = total * shrink
                for add in adds:
                    total = total + add
                return total, tuple(new_tops), tuple(new_sums)

            carry = (
                jnp.zeros((tile, LANES), jnp.float32),
                tuple(jnp.full((tile, 1), -1e30, jnp.float32) for _ in range(pack)),
                tuple(jnp.zeros((tile, 1), jnp.float32) for _ in range(pack)),
            )
            carry = lax.fori_loop(0, i, step, carry)
            total, tops, sums = step(i, carry, diagonal=True)
            share = 1.0 / sums[0]
            for h in range(1, pack):
                share = jnp.where(masks[h], 1.0 / sums[h], share)
            out_ref[pl.ds(start, tile), base : base + LANES] = (total * share).astype(out_ref.dtype)
            for h in range(pack):
                logs = jnp.broadcast_to(tops[h] + jnp.log2(sums[h]), (tile, LANES))
                index = pair * pack + h
                log_ref[0, index : index + 1, pl.ds(start, tile)] = jnp.transpose(logs)[0:1]
            return 0

        lax.fori_loop(0, blocks, query_block, 0)


def attend(mixed, slots, counts, head_size):
    sequences = counts.shape[0]
    rows = sum(part.shape[0] for part in mixed)
    tile = rows // slots.size
    blocks = rows // tile
    lanes = mixed[0].shape[1] // 3
    length = rows // sequences
    heads = lanes // head_size
    pack = LANES // head_size
    return pl.pallas_call(
        functools.partial(attend_kernel, head_size, len(mixed)),
        grid_spec=pltpu.PrefetchScalarGridSpec(
            num_scalar_prefetch=2,
            grid=(sequences,),
            in_specs=[pl.BlockSpec(memory_space=pl.ANY)] * len(mixed),
            out_specs=[
                pl.BlockSpec((length, lanes), lambda s, *_: (s, 0)),
                pl.BlockSpec((1, heads, length), lambda s, *_: (s, 0, 0)),
            ],
            scratch_shapes=[
                pltpu.VMEM((blocks, tile, 3 * lanes), jnp.bfloat16),
                pltpu.VMEM((pack, length, LANES), jnp.bfloat16),
                pltpu.VMEM((pack, length, LANES), jnp.bfloat16),
                pltpu.SemaphoreType.DMA((blocks,)),
            ],
        ),
        out_shape=[
            jax.ShapeDtypeStruct((rows, lanes), jnp.bfloat16),
            jax.ShapeDtypeStruct((sequences, heads, length), jnp.float32),
        ],
        compiler_params=pltpu.CompilerParams(vmem_limit_bytes=VMEM_BYTES),
        cost_estimate=cost(rows * length * lanes * 2, rows * lanes * 8, rows * length * heads // 2),
    )(counts, slots, *mixed)


def attend_back_kernel(
    head_size,
    blocks_in,
    counts,
    slots,
    *refs,
):
    sources = refs[:blocks_in]
    grad_ref, out_ref, log_ref, own_ref, other_ref, mixed_ref = refs[blocks_in : blocks_in + 6]
    query_own, key_own, grad_own, delta, grad_query, grad_key, grad_value, back_ref, sems = refs[
        blocks_in + 6 :
    ]
    fetch(sources, mixed_ref, sems)
    length, lanes = out_ref.shape
    tile = mixed_ref.shape[1]
    pack = LANES // head_size
    scale = head_size ** (-0.5)
    sequence = pl.program_id(0)
    blocks = lax.div(counts[sequence] + (tile - 1), tile)
    masks = head_masks(head_size)
    for i in range(length // tile):
        back_ref[slots[sequence, i]] = jnp.zeros((tile, 3 * lanes), back_ref.dtype)
    key_row = lax.broadcasted_iota(jnp.int32, (tile, tile), 0)
    query_col = lax.broadcasted_iota(jnp.int32, (tile, tile), 1)
    for pair in range(lanes // LANES):
        base = pair * LANES
        for i in range(length // tile):
            span = slice(i * tile, (i + 1) * tile)
            slot = slots[sequence, i]
            queries = mixed_ref[slot, :, base : base + LANES]
            keys = mixed_ref[slot, :, lanes + base : lanes + base + LANES]
            grads = grad_ref[span, base : base + LANES]
            for h in range(pack):
                query_own[h, span] = jnp.where(masks[h], queries, jnp.zeros_like(queries))
                key_own[h, span] = jnp.where(masks[h], keys, jnp.zeros_like(keys))
                grad_own[h, span] = jnp.where(masks[h], grads, jnp.zeros_like(grads))
        grad_query[...] = jnp.zeros(grad_query.shape, jnp.float32)

        def deltas(i, _, base=base):
            start = pl.multiple_of(i * tile, tile)
            grads = grad_ref[pl.ds(start, tile), base : base + LANES].astype(jnp.float32)
            outs = out_ref[pl.ds(start, tile), base : base + LANES].astype(jnp.float32)
            products = jnp.transpose(grads * outs)
            for h in range(pack):
                delta[h : h + 1, pl.ds(start, tile)] = jnp.sum(
                    products[h * head_size : (h + 1) * head_size], axis=0, keepdims=True
                )
            return 0

        lax.fori_loop(0, blocks, deltas, 0)

        def key_block(j, _, pair=pair, base=base):
            first = pl.multiple_of(j * tile, tile)
            place = slots[sequence, j]
            keys = mixed_ref[place, :, lanes + base : lanes + base + LANES]
            values = mixed_ref[place, :, 2 * lanes + base : 2 * lanes + base + LANES]
            grad_key[...] = jnp.zeros(grad_key.shape, jnp.float32)
            grad_value[...] = jnp.zeros(grad_value.shape, jnp.float32)

            def step(i, diagonal=False):
                start = pl.multiple_of(i * tile, tile)
                add_query, add_key, add_value = [], [], []
                for h in range(pack):
                    index = pair * pack + h
                    query_head = query_own[h, pl.ds(start, tile)]
                    grad_head = grad_own[h, pl.ds(start, tile)]
                    scores = dot_nt(keys, query_head) * (scale * LOG2E)
                    probs = jnp.exp2(scores - log_ref[0, index : index + 1, pl.ds(start, tile)])
                    if diagonal:
                        probs = jnp.where(key_row <= query_col, probs, 0.0)
                    grad_probs = dot_nt(values, grad_head)
                    grad_scores = (
                        probs * (grad_probs - delta[h : h + 1, pl.ds(start, tile)])
                    ).astype(jnp.bfloat16)
                    add_value.append(dot_nn(probs.astype(jnp.bfloat16), grad_head))
                    add_key.append(dot_nn(grad_scores, query_head))
                    add_query.append(dot_tn(grad_scores, key_own[h, pl.ds(first, tile)]))
                grad_value[...] += functools.reduce(jnp.add, add_value)
                grad_key[...] += functools.reduce(jnp.add, add_key)
                grad_query[pl.ds(start, tile), :] += functools.reduce(jnp.add, add_query)

            def off_diagonal(i, _):
                step(i)
                return 0

            step(j, diagonal=True)
            lax.fori_loop(j + 1, blocks, off_diagonal, 0)
            back_ref[place, :, lanes + base : lanes + base + LANES] = (grad_key[...] * scale).astype(
                back_ref.dtype
            )
            back_ref[place, :, 2 * lanes + base : 2 * lanes + base + LANES] = grad_value[...].astype(
                back_ref.dtype
            )
            return 0

        lax.fori_loop(0, blocks, key_block, 0)
        for i in range(length // tile):
            back_ref[slots[sequence, i], :, base : base + LANES] = (
                grad_query[i * tile : (i + 1) * tile] * scale
            ).astype(back_ref.dtype)

    @pl.when(sequence == pl.num_programs(0) - 1)
    def _():
        half = back_ref.shape[0] // 2
        for k in range(half):
            own_ref[k * tile : (k + 1) * tile] = back_ref[k]
            other_ref[k * tile : (k + 1) * tile] = back_ref[half + k]


def attend_back(mixed, slots, grads, outs, logs, counts, head_size):
    sequences = counts.shape[0]
    rows, lanes = outs.shape
    length = rows // sequences
    heads = lanes // head_size
    pack = LANES // head_size
    tile = rows // slots.size
    blocks = rows // tile
    whole = pl.BlockSpec((rows // 2, 3 * lanes), lambda s, *_: (0, 0))
    return pl.pallas_call(
        functools.partial(attend_back_kernel, head_size, len(mixed)),
        grid_spec=pltpu.PrefetchScalarGridSpec(
            num_scalar_prefetch=2,
            grid=(sequences,),
            in_specs=[pl.BlockSpec(memory_space=pl.ANY)] * len(mixed)
            + [
                pl.BlockSpec((length, lanes), lambda s, *_: (s, 0)),
                pl.BlockSpec((length, lanes), lambda s, *_: (s, 0)),
                pl.BlockSpec((1, heads, length), lambda s, *_: (s, 0, 0)),
            ],
            out_specs=[whole, whole],
            scratch_shapes=[
                pltpu.VMEM((blocks, tile, 3 * lanes), jnp.bfloat16),
                pltpu.VMEM((pack, length, LANES), jnp.bfloat16),
                pltpu.VMEM((pack, length, LANES), jnp.bfloat16),
                pltpu.VMEM((pack, length, LANES), jnp.bfloat16),
                pltpu.VMEM((pack, length), jnp.float32),
                pltpu.VMEM((length, LANES), jnp.float32),
                pltpu.VMEM((tile, LANES), jnp.float32),
                pltpu.VMEM((tile, LANES), jnp.float32),
                pltpu.VMEM((blocks, tile, 3 * lanes), jnp.bfloat16),
                pltpu.SemaphoreType.DMA((blocks,)),
            ],
        ),
        out_shape=[jax.ShapeDtypeStruct((rows // 2, 3 * lanes), jnp.bfloat16)] * 2,
        compiler_params=pltpu.CompilerParams(vmem_limit_bytes=VMEM_BYTES),
        cost_estimate=cost(1, 1),
    )(counts, slots, *mixed, grads, outs, logs)


def ffn_kernel(block, x_parts, g_parts, counts, *refs):
    xs, refs = refs[:x_parts], refs[x_parts:]
    gs, refs = refs[:g_parts], refs[g_parts:]
    ups, downs, shifts = refs[0:2], refs[2:4], refs[4:6]
    units_ref, back_ref, out_ref, x, g, total, x_sems, g_sems = refs[-8:]
    fetch(xs, x, x_sems)
    fetch(gs, g, g_sems)
    blocks, size, model = x.shape
    width = ups[0].shape[0]
    step = pl.program_id(0)

    @pl.when(step == 0)
    def _():
        total[...] = jnp.zeros(total.shape, total.dtype)

    for k in range(blocks):
        rows = slice(k * size, (k + 1) * size)

        @pl.when(counts[block + k] != 0)
        def _(k=k, rows=rows):
            backs = []
            for side in range(2):
                span = slice(side * width, (side + 1) * width)
                pre = dot_nt(x[k], ups[side][...]) + shifts[side][...]
                grad_units = dot_nt(g[k], downs[side][...])
                size_of = jnp.abs(pre)
                bell = jnp.exp2(pre * pre * (-0.5 * LOG2E))
                denominator = 1.0 + (0.3275911 * 0.7071067811865476) * size_of
                t = pl.reciprocal(denominator, approx=True)
                t = t * (2.0 - denominator * t)
                tail = 0.5 * 1.061405429
                for factor in (-1.453152027, 1.421413741, -0.284496736, 0.254829592):
                    tail = tail * t + 0.5 * factor
                tail = tail * t
                units = jnp.maximum(pre, 0.0) - size_of * (tail * bell)
                units_ref[rows, span] = units.astype(units_ref.dtype)
                slope = (tail - size_of * 0.3989422804014327) * bell
                slope = jnp.where(pre < 0, slope, 1.0 - slope)
                backs.append((grad_units * slope).astype(back_ref.dtype))
                back_ref[rows, span] = backs[-1]
            total[rows] += dot_nn(backs[0], ups[0][...]) + dot_nn(backs[1], ups[1][...])

        @pl.when(counts[block + k] == 0)
        def _(rows=rows):
            units_ref[rows] = jnp.zeros((size, 2 * width), units_ref.dtype)
            back_ref[rows] = jnp.zeros((size, 2 * width), back_ref.dtype)

    @pl.when(step == pl.num_programs(0) - 1)
    def _():
        out_ref[...] = total[...].astype(out_ref.dtype)


def ffn_blocks(place, block, counts, xs, gs, ups, downs, shifts, kept):
    size, width = 512, 256
    model = xs[0].shape[1]
    rows = sum(x.shape[0] for x in xs)
    units = ups[0].shape[0]
    whole = pl.BlockSpec(memory_space=pl.ANY)
    weights = pl.BlockSpec((width, model), lambda u, *_: (u, 0))
    shift = pl.BlockSpec((1, width), lambda u, *_: (0, u))
    output = pl.BlockSpec((rows, 2 * width), lambda u, *_: (place, u))
    full = jax.ShapeDtypeStruct((4 * size, 2 * units), jnp.bfloat16)
    return pl.pallas_call(
        functools.partial(ffn_kernel, block, len(xs), len(gs)),
        grid_spec=pltpu.PrefetchScalarGridSpec(
            num_scalar_prefetch=1,
            grid=(units // width,),
            in_specs=[whole] * (len(xs) + len(gs))
            + [weights] * 4
            + [shift] * 2
            + [whole] * len(kept),
            out_specs=[output, output, pl.BlockSpec((rows, model), lambda u, *_: (0, 0))],
            scratch_shapes=[
                pltpu.VMEM((rows // size, size, model), jnp.bfloat16),
                pltpu.VMEM((rows // size, size, model), jnp.bfloat16),
                pltpu.VMEM((rows, model), jnp.float32),
                pltpu.SemaphoreType.DMA((len(xs),)),
                pltpu.SemaphoreType.DMA((len(gs),)),
            ],
        ),
        out_shape=[full, full, jax.ShapeDtypeStruct((rows, model), jnp.bfloat16)],
        input_output_aliases={len(xs) + len(gs) + 7 + k: k for k in range(len(kept))},
        compiler_params=pltpu.CompilerParams(vmem_limit_bytes=VMEM_BYTES),
        cost_estimate=cost(12 * rows * units * model, 8 * units * model + 8 * rows * model, 4 * rows * units),
    )(counts, *xs, *gs, *ups, *downs, *shifts, *kept)


def arrange(outs, total):
    to_x, to_y, rest = outs
    half = total.shape[0] // 2
    top, bottom = total[:half].astype(to_x.dtype), total[half:].astype(to_x.dtype)
    step = pl.program_id(0)

    @pl.when(step == 0)
    def _():
        to_x[:half] = top
        to_y[:half] = bottom

    @pl.when(step == 1)
    def _():
        to_x[half:] = top
        rest[half : 2 * half] = bottom

    @pl.when(step == 2)
    def _():
        rest[:half] = top
        to_y[half:] = bottom

    @pl.when(step == 3)
    def _():
        rest[2 * half : 3 * half] = top
        rest[3 * half :] = bottom


def arranged(rows, columns):
    sizes = (rows // 4, rows // 4, rows // 2)
    specs = [pl.BlockSpec((size, columns), lambda i, *_: (0, 0)) for size in sizes]
    return specs, [jax.ShapeDtypeStruct((size, columns), jnp.bfloat16) for size in sizes]


def products_kernel(width, order, active, left, own, other, *outs):
    here = active[order[pl.program_id(0)]] != 0

    @pl.when(here)
    def _():
        total = None
        for k in range(own.shape[0] // width):
            rows = slice(k * width, (k + 1) * width)
            for side, right in enumerate((own, other)):
                start = (2 * k + side) * width
                term = dot_nn(left[:, start : start + width], right[rows])
                total = term if total is None else total + term
        arrange(outs, total)

    @pl.when(jnp.logical_not(here))
    def _():
        arrange(outs, jnp.zeros((left.shape[0], own.shape[1]), jnp.float32))


def products(order, counts, left, own, other):
    blocks = counts.shape[0]
    rows, depth = left.shape
    columns = own.shape[1]
    specs, shapes = arranged(rows, columns)
    return pl.pallas_call(
        functools.partial(products_kernel, 256),
        grid_spec=pltpu.PrefetchScalarGridSpec(
            num_scalar_prefetch=2,
            grid=(blocks,),
            in_specs=[
                pl.BlockSpec((rows // blocks, depth), lambda i, order, *_: (order[i], 0)),
                pl.BlockSpec(own.shape, lambda i, *_: (0, 0)),
                pl.BlockSpec(own.shape, lambda i, *_: (0, 0)),
            ],
            out_specs=specs,
        ),
        out_shape=shapes,
        compiler_params=pltpu.CompilerParams(vmem_limit_bytes=VMEM_BYTES),
        cost_estimate=cost(1, 1),
    )(order, counts, left, own, other)


def attend_out_kernel(left, weight, bias, hidden, active, out_ref):
    out_ref[...] = hidden[...].astype(jnp.float32) + active[...] * (
        dot_nn(left[...], weight[...]) + bias[...]
    )


def attend_out(left, weight, bias, hidden, active):
    rows, depth = left.shape
    columns = weight.shape[1]
    width = 512
    column = pl.BlockSpec((rows, width), lambda j: (0, j))
    return pl.pallas_call(
        attend_out_kernel,
        grid=(columns // width,),
        in_specs=[
            pl.BlockSpec((rows, depth), lambda j: (0, 0)),
            pl.BlockSpec((depth, width), lambda j: (0, j)),
            pl.BlockSpec((1, width), lambda j: (0, j)),
            column,
            pl.BlockSpec((rows, 1), lambda j: (0, 0)),
        ],
        out_specs=column,
        out_shape=jax.ShapeDtypeStruct((rows, columns), jnp.float32),
        compiler_params=pltpu.CompilerParams(vmem_limit_bytes=VMEM_BYTES),
        cost_estimate=cost(2 * rows * depth * columns, 2 * depth * columns + 8 * rows * columns),
    )(left, weight, bias[None], hidden, active)


def attend_out_back_kernel(grad, weight, out_ref):
    out_ref[...] = dot_nt(grad[...], weight[...]).astype(out_ref.dtype)


def attend_out_back(grad, weight):
    rows, columns = grad.shape
    depth = weight.shape[0]
    width = 512
    return pl.pallas_call(
        attend_out_back_kernel,
        grid=(depth // width,),
        in_specs=[
            pl.BlockSpec((rows, columns), lambda j: (0, 0)),
            pl.BlockSpec((width, columns), lambda j: (j, 0)),
        ],
        out_specs=pl.BlockSpec((rows, width), lambda j: (0, j)),
        out_shape=jax.ShapeDtypeStruct((rows, depth), jnp.bfloat16),
        compiler_params=pltpu.CompilerParams(vmem_limit_bytes=VMEM_BYTES),
        cost_estimate=cost(1, 1),
    )(grad, weight)


def project_kernel(inputs, side, parts, *refs):
    xs = refs[:inputs]
    weights, shift, out_ref = refs[inputs:]
    slab = weights.shape[1]
    weight = weights[...].reshape(3 * slab, weights.shape[2])
    for k in range(inputs):

        @pl.when(pl.program_id(0) == k)
        def _(k=k):
            mixed = dot_nt(xs[k][...], weight)
            for t in range(3):
                columns = pl.ds(pl.multiple_of(parts[side, t] * slab, slab), slab)
                out_ref[:, columns] = (
                    mixed[:, t * slab : (t + 1) * slab] + shift[:, columns]
                ).astype(out_ref.dtype)


def project(parts, side, xs, weights, shift):
    size, model = xs[0].shape
    slab = weights.shape[1]
    return pl.pallas_call(
        functools.partial(project_kernel, len(xs), side),
        grid_spec=pltpu.PrefetchScalarGridSpec(
            num_scalar_prefetch=1,
            grid=(len(xs),),
            in_specs=[pl.BlockSpec((size, model), lambda i, *_: (0, 0))] * len(xs)
            + [
                pl.BlockSpec(weights.shape, lambda i, *_: (0, 0, 0)),
                pl.BlockSpec(shift.shape, lambda i, *_: (0, 0)),
            ],
            out_specs=pl.BlockSpec((size, 3 * slab), lambda i, *_: (i, 0)),
        ),
        out_shape=jax.ShapeDtypeStruct((len(xs) * size, 3 * slab), jnp.bfloat16),
        compiler_params=pltpu.CompilerParams(vmem_limit_bytes=VMEM_BYTES),
        cost_estimate=pl.CostEstimate(
            flops=6 * len(xs) * size * slab * model,
            bytes_accessed=6 * slab * model + 2 * len(xs) * size * (model + 3 * slab),
            transcendentals=0,
        ),
    )(parts, *xs, weights, shift)


def unproject_kernel(order, parts, active, mine, theirs, own, other, *outs):
    slab = own.shape[1]
    here = active[order[pl.program_id(0)]] != 0

    @pl.when(here)
    def _():
        total = None
        for side, (left, right) in enumerate(((mine, own), (theirs, other))):
            for t in range(3):
                columns = pl.ds(pl.multiple_of(parts[side, t] * slab, slab), slab)
                term = dot_nn(left[:, columns], right[t])
                total = term if total is None else total + term
        arrange(outs, total)

    @pl.when(jnp.logical_not(here))
    def _():
        arrange(outs, jnp.zeros((mine.shape[0], own.shape[2]), jnp.float32))


def unproject(order, parts, counts, mine, theirs, own, other):
    blocks = counts.shape[0]
    rows = mine.shape[0]
    slab, model = own.shape[1:]
    left = pl.BlockSpec((rows // blocks, 3 * slab), lambda i, order, *_: (order[i], 0))
    fixed = pl.BlockSpec(own.shape, lambda i, *_: (0, 0, 0))
    specs, shapes = arranged(rows, model)
    return pl.pallas_call(
        unproject_kernel,
        grid_spec=pltpu.PrefetchScalarGridSpec(
            num_scalar_prefetch=3,
            grid=(blocks,),
            in_specs=[left, left, fixed, fixed],
            out_specs=specs,
        ),
        out_shape=shapes,
        compiler_params=pltpu.CompilerParams(vmem_limit_bytes=VMEM_BYTES),
        cost_estimate=cost(1, 1),
    )(order, parts, counts, mine, theirs, own, other)


def weight_grad_kernel(inputs, added, columns, *refs):
    left, rights = refs[0], refs[1 : 1 + inputs]
    tokens, sems = refs[-2:]
    outs = refs[1 + inputs + added : -2]
    fetch(rights, tokens, sems)
    total = dot_tn(left[...], tokens[0])
    if added:
        total = total + refs[1 + inputs][...].astype(jnp.float32)
    size = outs[0].shape[0]
    if size == total.shape[0]:
        for k, out_ref in enumerate(outs):

            @pl.when((len(outs) == 1) | (pl.program_id(0) == k))
            def _(out_ref=out_ref):
                out_ref[...] = total.astype(out_ref.dtype)

    else:
        for k, out_ref in enumerate(outs):
            out_ref[...] = total[k * size : (k + 1) * size].astype(out_ref.dtype)


def weight_grad(left, columns, tile, rights, extra=None, outputs=1, apart=False):
    rows = left.shape[0]
    model = rights[0].shape[1]
    steps = columns.shape[0]
    output = pl.BlockSpec((tile // outputs, model), lambda i, *_: (i, 0))
    extras = [] if extra is None else [extra]
    shape = jax.ShapeDtypeStruct((steps * tile // outputs, model), jnp.bfloat16)
    added = [output] * len(extras)
    if apart:
        outputs = steps
        output = pl.BlockSpec((tile, model), lambda i, *_: (0, 0))
        shape = jax.ShapeDtypeStruct((tile, model), jnp.bfloat16)
    results = pl.pallas_call(
        functools.partial(weight_grad_kernel, len(rights), len(extras)),
        grid_spec=pltpu.PrefetchScalarGridSpec(
            num_scalar_prefetch=1,
            grid=(steps,),
            in_specs=[pl.BlockSpec((rows, tile), lambda i, columns: (0, columns[i]))]
            + [pl.BlockSpec(memory_space=pl.ANY)] * len(rights)
            + added,
            out_specs=[output] * outputs,
            scratch_shapes=[
                pltpu.VMEM((1, rows, model), jnp.bfloat16),
                pltpu.SemaphoreType.DMA((len(rights),)),
            ],
        ),
        out_shape=[shape] * outputs,
        compiler_params=pltpu.CompilerParams(vmem_limit_bytes=VMEM_BYTES),
        cost_estimate=cost(1, 1),
    )(columns, left, *rights, *extras)
    return results[0] if outputs == 1 else results


def chain_sum(values, axis):
    size = lax.axis_size(axis)
    if size != 4:
        return lax.psum(values.astype(jnp.bfloat16), axis).astype(jnp.float32)
    place = lax.axis_index(axis)
    outer = lax.ppermute(values.astype(jnp.bfloat16), axis, [(0, 1), (3, 2)])
    half = (values + outer.astype(jnp.float32)).astype(jnp.bfloat16)
    other = lax.ppermute(half, axis, [(1, 2), (2, 1)])
    whole = (half.astype(jnp.float32) + other.astype(jnp.float32)).astype(jnp.bfloat16)
    ends = lax.ppermute(whole, axis, [(1, 0), (2, 3)])
    inner = (place == 1) | (place == 2)
    return jnp.where(inner, whole, ends).astype(jnp.float32)


def normalize(values):
    center = values - jnp.mean(values, axis=-1, keepdims=True)
    inverse = lax.rsqrt(jnp.mean(center * center, axis=-1, keepdims=True) + epsilon)
    return center * inverse, inverse


def normalize_back(grad, gain, normal, inverse):
    scaled = grad * gain
    grad_values = inverse * (
        scaled
        - jnp.mean(scaled, axis=-1, keepdims=True)
        - normal * jnp.mean(scaled * normal, axis=-1, keepdims=True)
    )
    return grad_values, jnp.sum(grad * normal, axis=0), jnp.sum(grad, axis=0)


def local_general(
    hidden,
    cotangent,
    exit_layer,
    ln1_gain,
    ln1_bias,
    qkv_weight,
    query_bias,
    value_bias,
    out_weight,
    out_bias,
    ln2_gain,
    ln2_bias,
    up_weight,
    up_bias,
    down_weight,
    down_bias,
):
    width = lax.axis_size("wide")
    rank = lax.axis_index("wide")
    rows, model = hidden.shape
    group = rows * width
    slab = model // width
    head_size = model // HEADS
    units_own = up_weight.shape[0]
    keep = exit_layer >= LAYER
    counts = jnp.sum(keep.astype(jnp.int32), axis=1)
    active = lax.dynamic_slice_in_dim(keep.reshape(group), rank * rows, rows, 0)
    active = active.astype(jnp.float32)[:, None]
    grad_out = cotangent.astype(jnp.float32)

    routes = [[(w, (3 * w + t) % width) for w in range(width)] for t in range(3)]
    part_at = np.zeros((width, 3), np.int32)
    for t in range(3):
        for w, d in routes[t]:
            part_at[d, t] = (3 * w + t) // width
    place_of = jnp.asarray(np.argsort(part_at, axis=1).astype(np.int32))[rank]
    part_of = jnp.asarray(part_at)[rank]

    hidden_wide = hidden.astype(jnp.float32)
    normal1, inverse1 = normalize(hidden_wide)
    normed1 = lax.all_gather(
        (normal1 * ln1_gain + ln1_bias).astype(jnp.bfloat16), "wide", axis=0, tiled=True
    )
    slabs = qkv_weight.reshape(3, slab, model)
    received = jnp.stack([lax.ppermute(slabs[t], "wide", routes[t]) for t in range(3)])
    qkv_own = jnp.concatenate(
        [lax.dynamic_index_in_dim(received, place_of[p], 0, keepdims=False) for p in range(3)]
    )
    own = lambda vector: lax.dynamic_slice_in_dim(vector, rank * slab, slab, 0)
    qkv_shift = jnp.concatenate(
        [own(query_bias), jnp.zeros((slab,), jnp.float32), own(value_bias)]
    )

    grad_ffn = (active * grad_out).astype(jnp.bfloat16)
    down_bias_grad = jnp.sum(grad_ffn.astype(jnp.float32), axis=0)
    piece = rows // CHUNKS
    part = lambda values, c: values[c * piece : (c + 1) * piece]
    gather = lambda values: lax.all_gather(values, "wide", axis=0, tiled=True)
    scatter = lambda values: lax.psum_scatter(
        values.astype(jnp.bfloat16), "wide", scatter_dimension=0, tiled=True
    )
    grad_ffns = [gather(part(grad_ffn, c)) for c in range(CHUNKS)]
    out_whole = gather(out_weight)

    mixed = (dot_nt(normed1, qkv_own) + qkv_shift).astype(jnp.bfloat16)
    mixed = jnp.split(mixed, group // TILE)
    slots = jnp.arange(group // TILE, dtype=jnp.int32).reshape(counts.shape[0], -1)
    attended, logs = attend(mixed, slots, counts, head_size)
    attended_rows = lax.all_to_all(attended, "wide", split_axis=0, concat_axis=1, tiled=True)
    middle = hidden_wide + active * (dot_nn(attended_rows, out_whole) + out_bias)
    normal2, inverse2 = normalize(middle)
    normed2 = (normal2 * ln2_gain + ln2_bias).astype(jnp.bfloat16)
    up_shift = lax.dynamic_slice_in_dim(up_bias, rank * units_own, units_own, 0)

    normed2s = [gather(part(normed2, c)) for c in range(CHUNKS)]
    units, grad_pres, grad_normed2, ffn_out = [], [], [], []
    for c in range(CHUNKS):
        grad_units = dot_nt(grad_ffns[c], down_weight)
        pre = dot_nt(normed2s[c], up_weight) + up_shift
        below = 0.5 + 0.5 * lax.erf(pre * 0.7071067811865476)
        bell = jnp.exp(-0.5 * pre * pre) * 0.3989422804014327
        units.append((pre * below).astype(jnp.bfloat16))
        grad_pres.append((grad_units * (below + pre * bell)).astype(jnp.bfloat16))
        grad_normed2.append(scatter(dot_nn(grad_pres[c], up_weight)))
    for c in range(CHUNKS):
        ffn_out.append(scatter(dot_nn(units[c], down_weight)))
    grad_normed2 = jnp.concatenate(grad_normed2).astype(jnp.float32)
    ffn_out = jnp.concatenate(ffn_out).astype(jnp.float32)
    output = (middle + active * (ffn_out + down_bias)).astype(jnp.bfloat16)

    up_bias_own = sum(jnp.sum(g.astype(jnp.float32), axis=0) for g in grad_pres)
    down_grad = sum(dot_tn(units[c], grad_ffns[c]) for c in range(CHUNKS))
    up_grad = sum(dot_tn(grad_pres[c], normed2s[c]) for c in range(CHUNKS))
    halves = lambda values: jnp.concatenate(
        [chain_sum(half, "batch") for half in jnp.split(values, 2)]
    )
    down_grad = halves(down_grad)
    up_grad = halves(up_grad)

    grad_middle, ln2_gain_grad, ln2_bias_grad = normalize_back(
        grad_normed2, ln2_gain, normal2, inverse2
    )
    grad_middle = grad_out + grad_middle
    grad_branch = (active * grad_middle).astype(jnp.bfloat16)
    out_bias_grad = jnp.sum(grad_branch.astype(jnp.float32), axis=0)
    grad_attended = dot_nt(grad_branch, out_whole).astype(jnp.bfloat16)
    grad_heads = lax.all_to_all(grad_attended, "wide", split_axis=1, concat_axis=0, tiled=True)
    out_grad = chain_sum(scatter(dot_tn(attended_rows, grad_branch)).astype(jnp.float32), "batch")

    placed = lambda vector, size: lax.dynamic_update_slice_in_dim(
        jnp.zeros((size,), jnp.float32), vector, rank * vector.shape[0], 0
    )
    early = lax.psum(
        (
            out_bias_grad,
            ln2_gain_grad,
            ln2_bias_grad,
            placed(up_bias_own, up_bias.shape[0]),
            down_bias_grad,
        ),
        ("batch", "wide"),
    )

    grad_mixed = jnp.concatenate(
        attend_back(mixed, slots, grad_heads, attended, logs, counts, head_size)
    )
    grad_normed1 = scatter(dot_nn(grad_mixed, qkv_own)).astype(jnp.float32)
    sums = jnp.sum(grad_mixed.astype(jnp.float32), axis=0)
    qkv_parts = []
    for t in range(3):
        columns = lax.dynamic_slice_in_dim(grad_mixed, part_of[t] * slab, slab, 1)
        total = chain_sum(dot_tn(columns, normed1), "batch").astype(jnp.bfloat16)
        back = [(d, w) for w, d in routes[t]]
        qkv_parts.append(lax.ppermute(total, "wide", back).astype(jnp.float32))
    qkv_grad = jnp.concatenate(qkv_parts)

    grad_hidden, ln1_gain_grad, ln1_bias_grad = normalize_back(
        grad_normed1, ln1_gain, normal1, inverse1
    )
    input_grad = grad_middle + grad_hidden
    late = lax.psum(
        (
            ln1_gain_grad,
            ln1_bias_grad,
            placed(sums[:slab], model),
            placed(sums[2 * slab :], model),
        ),
        ("batch", "wide"),
    )
    return (
        output,
        input_grad,
        late[0],
        late[1],
        qkv_grad,
        late[2],
        late[3],
        out_grad,
        early[0],
        early[1],
        early[2],
        up_grad,
        early[3],
        down_grad,
        early[4],
    )


def swap(values, bits):
    width = lax.axis_size("wide")
    return lax.ppermute(values, "wide", [(w, w ^ bits) for w in range(width)])


def after(values, *done):
    return lax.optimization_barrier((values, done))[0]


def relay(along_x, along_y):
    half = along_x.shape[0] // 2
    return [swap(along_y[:half], 2), swap(along_x[half:], 4)]


class Scatter:
    def __init__(self, to_x, to_y, rest):
        self.half = half = to_x.shape[0] // 2
        self.sent = (to_x, to_y)
        self.rest = rest
        self.from_x, self.from_y = swap(to_x, 2), swap(to_y, 4)

    def second(self, *done):
        half = self.half
        from_x, from_y = after((self.from_x, self.from_y), *done)
        self.near = (from_x[half:], from_y[half:])
        self.own = self.rest[2 * half :]
        return self.forward(self.rest[:half], self.rest[half : 2 * half], from_x[:half], from_y[:half])

    def forward(self, along_y, along_x, top, bottom):
        wide = lambda values: values.astype(jnp.float32)
        y_top = (wide(along_y) + wide(top)).astype(jnp.bfloat16)
        x_bottom = (wide(along_x) + wide(bottom)).astype(jnp.bfloat16)
        self.last = (swap(y_top, 4), swap(x_bottom, 2))
        return y_top, x_bottom

    def finish(self, *done):
        wide = lambda values: values.astype(jnp.float32)
        y_top, x_bottom = after(self.last, *done)
        x_top, y_bottom = self.near
        return jnp.concatenate(
            [
                wide(self.own[: self.half]) + wide(x_top) + wide(y_top),
                wide(self.own[self.half :]) + wide(x_bottom) + wide(y_bottom),
            ]
        )


def split_for_scatter(own, along_x, along_y, diagonal):
    half = own.shape[0] // 2
    return (
        jnp.concatenate([diagonal[:half], along_x[:half]]),
        jnp.concatenate([diagonal[half:], along_y[half:]]),
        jnp.concatenate([along_y[:half], along_x[half:], own]),
    )


class EarlyScatter(Scatter):
    def __init__(self, own, along_x, along_y):
        self.half = half = own.shape[0] // 2
        self.own, self.along_x, self.along_y = own, along_x, along_y
        self.near = (swap(along_x[:half], 2), swap(along_y[half:], 4))

    def first(self, diagonal):
        self.from_far = (swap(diagonal[: self.half], 2), swap(diagonal[self.half :], 4))
        self.near = after(self.near, diagonal)
        return self.near

    def second(self, *done):
        half = self.half
        far = after(self.from_far, *done)
        return self.forward(self.along_y[:half], self.along_x[half:], *far)


def tree_sum(values):
    total = values + swap(values, 1)
    total = (total + swap(total, 2)) + (swap(total, 4) + swap(total, 6))
    size = lax.axis_size("batch")
    terms = [total] + [
        lax.ppermute(total, "batch", [(z, z ^ bits) for z in range(size)])
        for bits in range(1, size)
    ]
    while len(terms) > 1:
        terms = [terms[k] + terms[k + 1] for k in range(0, len(terms), 2)]
    return terms[0]


def local_chips(
    hidden,
    cotangent,
    exit_layer,
    ln1_gain,
    ln1_bias,
    qkv_weight,
    query_bias,
    value_bias,
    out_weight,
    out_bias,
    ln2_gain,
    ln2_bias,
    up_weight,
    up_bias,
    down_weight,
    down_bias,
):
    width = lax.axis_size("wide")
    rank = lax.axis_index("wide")
    rows, model = hidden.shape
    group = rows * width
    slab = model // width
    head_size = model // HEADS
    units_own = up_weight.shape[0]
    keep = exit_layer >= LAYER
    counts = jnp.sum(keep.astype(jnp.int32), axis=1)
    active = lax.dynamic_slice_in_dim(keep.reshape(group), rank * rows, rows, 0)
    active = active.astype(jnp.float32)[:, None]
    grad_out = cotangent.astype(jnp.float32)

    tiles = jnp.arange(group // rows, dtype=jnp.int32)
    slots = ((tiles ^ rank) & 1) * 4 + ((tiles >> 1) ^ (rank >> 1))
    slots = slots.reshape(counts.shape[0], -1)

    routes = [[(w, (3 * w + t) % width) for w in range(width)] for t in range(3)]
    part_at = np.zeros((width, 3), np.int32)
    for t in range(3):
        for w, d in routes[t]:
            part_at[d, t] = (3 * w + t) // width
    part_at = jnp.asarray(part_at)
    other = rank ^ 1
    parts = jnp.stack([part_at[rank], part_at[other]])

    hidden_wide = hidden.astype(jnp.float32)
    normal1, inverse1 = normalize(hidden_wide)
    slabs = qkv_weight.reshape(3, slab, model)
    slabs = [lax.ppermute(slabs[t], "wide", routes[t]) for t in range(3)]
    normed1 = (normal1 * ln1_gain + ln1_bias).astype(jnp.bfloat16)
    normed1 = [normed1, swap(normed1, 2), swap(normed1, 4)]
    diagonal1 = relay(normed1[1], normed1[2])
    qkv_own = jnp.stack(after(slabs, normed1[1:]))
    qkv_other = swap(qkv_own, 1)

    def shift_of(device):
        own = lambda vector: lax.dynamic_slice_in_dim(vector, device * slab, slab, 0)
        shift = [own(query_bias), jnp.zeros((slab,), jnp.float32), own(value_bias)]
        return jnp.concatenate(shift)[None]

    bias_of = lambda device: lax.dynamic_slice_in_dim(up_bias, device * units_own, units_own, 0)
    up_shifts = [bias_of(rank)[None], bias_of(other)[None]]

    mixed_near = project(parts, 0, normed1, qkv_own, shift_of(rank))
    qkv_other = after(qkv_other, mixed_near, diagonal1)
    lent_near = project(parts, 1, normed1, qkv_other, shift_of(other))
    diagonal1 = after(diagonal1, lent_near)
    lent_far = project(parts, 1, diagonal1, qkv_other, shift_of(other))
    mixed_far = project(parts, 0, after(diagonal1, lent_far), qkv_own, shift_of(rank))
    mixed = [mixed_near, mixed_far, swap(lent_near, 1), swap(lent_far, 1)]

    out_whole = lax.all_gather(after(out_weight, diagonal1), "wide", axis=0, tiled=True)
    grad_ffn = (after(active, diagonal1) * grad_out).astype(jnp.bfloat16)
    down_bias_grad = jnp.sum(grad_ffn.astype(jnp.float32), axis=0)

    attended, logs = attend(mixed, slots, counts, head_size)
    attended_rows = lax.all_to_all(attended, "wide", split_axis=0, concat_axis=1, tiled=True)
    grad_ffn = after(grad_ffn, attended_rows)
    grad_ffn = [grad_ffn, swap(grad_ffn, 2), swap(grad_ffn, 4)]
    up_other, down_other = swap(after((up_weight, down_weight), attended), 1)
    middle = attend_out(attended_rows, out_whole, out_bias, hidden, active)
    normal2, inverse2 = normalize(middle)
    normed2 = (normal2 * ln2_gain + ln2_bias).astype(jnp.bfloat16)
    normed2 = [normed2, swap(normed2, 2), swap(normed2, 4)]

    per_tile = jnp.sum(keep.reshape(group // rows, rows).astype(jnp.int32), axis=1)
    block_chip = (rank >> 1) ^ jnp.arange(4, dtype=jnp.int32)
    block_counts = per_tile[2 * block_chip + (rank & 1)]
    ups, downs = [up_weight, up_other], [down_weight, down_other]

    def ffn(place, block, xs, gs, kept):
        *kept, partial = ffn_blocks(
            place, block, block_counts, xs, gs, ups, downs, up_shifts, tuple(kept)
        )
        return kept, partial

    kept, partial_own = ffn(2, 0, [after(normed2[0], grad_ffn[1:])], grad_ffn[:1], ())
    normed2[1:] = after(normed2[1:], partial_own)
    diagonal2 = relay(normed2[1], normed2[2])
    diagonal_ffn = relay(*after(grad_ffn[1:], attended_rows))
    kept, partial_near = ffn(0, 1, normed2[1:], grad_ffn[1:], kept)
    scatter2 = EarlyScatter(partial_own, partial_near[:rows], partial_near[rows:])
    diagonal2 = after(diagonal2, partial_near)
    (units, grad_pres), partial_far = ffn(3, 3, diagonal2, diagonal_ffn, kept)
    wait = scatter2.first(partial_far)
    tokens2 = [*normed2[1:], normed2[0], *diagonal2]
    tokens_ffn = [*grad_ffn[1:], grad_ffn[0], *diagonal_ffn]

    wide = lambda values: values.astype(jnp.float32)
    lowered = lambda values: values.astype(jnp.bfloat16)
    tile = 512
    tiles = jnp.arange(2 * units_own // tile, dtype=jnp.int32)

    down_own, down_lent = weight_grad(after(units, wait), tiles, tile, tokens_ffn, outputs=2)
    wait = scatter2.second(down_lent)
    down_lent = swap(down_lent, 1)
    up_own, up_lent = weight_grad(after(grad_pres, wait), tiles, tile, tokens2, outputs=2)

    up_lent = swap(up_lent, 1)
    down_sum = lowered(wide(down_own) + wide(after(down_lent, up_own)))
    down_grad = lax.psum(down_sum, "batch")
    grad_middle, ln2_gain_grad, ln2_bias_grad = normalize_back(
        scatter2.finish(up_own), ln2_gain, normal2, inverse2
    )
    grad_middle = grad_out + grad_middle
    grad_branch = (active * grad_middle).astype(jnp.bfloat16)
    out_bias_grad = jnp.sum(grad_branch.astype(jnp.float32), axis=0)
    grad_branch = after(grad_branch, down_sum)
    grad_attended = attend_out_back(grad_branch, out_whole)
    grad_heads = lax.all_to_all(grad_attended, "wide", split_axis=1, concat_axis=0, tiled=True)
    owners = 2 * block_chip + (rank & 1)
    grad_branch = after(grad_branch, grad_attended)
    out_lent = weight_grad(attended_rows, owners ^ 1, slab, [grad_branch])
    out_lent = swap(out_lent, 1)
    out_own = weight_grad(after(attended_rows, out_lent), owners, slab, [grad_branch], out_lent)

    back_own, back_other = attend_back(
        mixed, slots, after(grad_heads, out_own), attended, logs, counts, head_size
    )

    theirs = swap(back_other, 1)
    out_own = after(out_own, back_own)
    scatter_out = Scatter(*split_for_scatter(*jnp.split(out_own, 4)))
    down_grad = after(down_grad, back_own)
    up_sum = lowered(wide(up_own) + wide(after(up_lent, back_own)))
    up_grad = lax.psum(after(up_sum, down_grad), "batch")
    order = jnp.array([3, 0, 1, 2], jnp.int32)
    ffn_counts = block_counts[jnp.array([1, 2, 0, 3])]
    ffn_parts = products(order, ffn_counts, after(units, up_sum, down_grad, scatter_out.sent), *downs)
    tokens1 = [*normed1, *diagonal1]
    theirs = after(theirs, ffn_parts[0])
    qkv_lent = weight_grad(theirs, parts[1], slab, tokens1)
    wait = scatter_out.second(qkv_lent)
    grad_parts = unproject(
        jnp.array([3, 1, 2, 0], jnp.int32),
        parts,
        block_counts,
        after(back_own, wait),
        theirs,
        qkv_own,
        qkv_other,
    )
    qkv_lent = swap(qkv_lent, 1)
    scatter1 = Scatter(*grad_parts)
    qkv_total = weight_grad(
        after(back_own, grad_parts[0]),
        parts[0],
        slab,
        tokens1,
        after(qkv_lent, grad_parts[0]),
        apart=True,
    )

    up_grad = after(up_grad, qkv_total)
    returned = [
        lax.ppermute(total, "wide", [(d, w) for w, d in route])
        for total, route in zip(after(qkv_total, up_grad), routes)
    ]
    out_total = lowered(scatter_out.finish(up_grad))
    *qkv_grad, out_grad = lax.psum(after((*returned, out_total), up_grad), "batch")
    wait = scatter1.second(out_total, up_grad)
    scatter_ffn = Scatter(*after(ffn_parts, wait))
    grad_normed1 = scatter1.finish(wait, scatter_ffn.sent)
    grad_hidden, ln1_gain_grad, ln1_bias_grad = normalize_back(
        grad_normed1, ln1_gain, normal1, inverse1
    )
    input_grad = grad_middle + grad_hidden
    grad_pres, back_own, back_other = after((grad_pres, back_own, back_other), wait)
    up_bias_own = jnp.sum(wide(grad_pres), axis=0).reshape(-1, 2, 256)
    up_bias_own = [up_bias_own[:, side].reshape(units_own) for side in range(2)]
    sums = jnp.sum(wide(back_own), axis=0) + jnp.sum(wide(back_other), axis=0)
    wait = scatter_ffn.second(input_grad)
    down_grad, up_grad = wide(after(down_grad, wait)), wide(after(up_grad, wait))
    ffn_out = scatter_ffn.finish(down_grad, up_grad)
    output = (middle + active * (ffn_out + down_bias)).astype(jnp.bfloat16)
    placed = lambda vector, size, device: lax.dynamic_update_slice_in_dim(
        jnp.zeros((size,), jnp.float32), vector, device * vector.shape[0], 0
    )
    smalls = tree_sum(
        jnp.concatenate(
            [
                placed(up_bias_own[0], up_bias.shape[0], rank)
                + placed(up_bias_own[1], up_bias.shape[0], other),
                down_bias_grad,
                out_bias_grad,
                ln2_gain_grad,
                ln2_bias_grad,
                placed(sums[:slab], model, rank),
                placed(sums[2 * slab :], model, rank),
                ln1_gain_grad,
                ln1_bias_grad,
            ]
        )
    )
    up_bias_grad = smalls[: up_bias.shape[0]]
    smalls = smalls[up_bias.shape[0] :].reshape(8, model)
    qkv_grad = wide(jnp.concatenate(qkv_grad))
    out_grad = wide(out_grad)
    return (
        output,
        input_grad,
        smalls[6],
        smalls[7],
        qkv_grad,
        smalls[4],
        smalls[5],
        out_grad,
        smalls[1],
        smalls[2],
        smalls[3],
        up_grad,
        up_bias_grad,
        down_grad,
        smalls[0],
    )


def solution(mesh):
    chips = mesh.shape["wide"] == 8 and mesh.shape["batch"] == 4
    local = local_chips if chips else local_general
    rows = P(("batch", "wide"), None)
    weight = P("wide", None)
    return jax.shard_map(
        local,
        mesh=mesh,
        in_specs=(
            rows,
            rows,
            P("batch", None),
            P(),
            P(),
            weight,
            P(),
            P(),
            weight,
            P(),
            P(),
            P(),
            weight,
            P(),
            weight,
            P(),
        ),
        out_specs=(
            rows,
            rows,
            P(),
            P(),
            weight,
            P(),
            P(),
            weight,
            P(),
            P(),
            P(),
            weight,
            P(),
            weight,
            P(),
        ),
        check_vma=False,
    )
```

```python
import functools

import jax
import jax.numpy as jnp
import numpy as np
from jax import lax
from jax.experimental import pallas as pl
from jax.experimental.pallas import tpu as pltpu
from jax.sharding import PartitionSpec as P

HEADS = 32
LAYER = 12
LANES = 128
TILE = 512
CHUNKS = 2
LOG2E = 1.4426950408889634

epsilon = 1e-05
VMEM_BYTES = 48 * 2**20


def cost(flops, size, exponentials=0):
    return pl.CostEstimate(flops=flops, bytes_accessed=size, transcendentals=exponentials)


def dot_nt(left, right):
    return lax.dot_general(
        left, right, (((1,), (1,)), ((), ())), preferred_element_type=jnp.float32
    )


def dot_nn(left, right):
    return lax.dot_general(
        left, right, (((1,), (0,)), ((), ())), preferred_element_type=jnp.float32
    )


def dot_tn(left, right):
    return lax.dot_general(
        left, right, (((0,), (0,)), ((), ())), preferred_element_type=jnp.float32
    )


def head_masks(head_size):
    lane = lax.broadcasted_iota(jnp.int32, (1, LANES), 1)
    return [
        (lane >= h * head_size) & (lane < (h + 1) * head_size)
        for h in range(LANES // head_size)
    ]


def fetch(sources, target, sems):
    size = target.shape[1]
    copies = []
    row = 0
    for source in sources:
        rows = source.shape[0]
        least = min(rows, size)
        for k in range(rows // least):
            place = target.at[row // size, pl.ds(row % size, least)]
            copies.append(
                pltpu.make_async_copy(source.at[pl.ds(k * least, least)], place, sems.at[len(copies)])
            )
            row += least

    @pl.when(pl.program_id(0) == 0)
    def _():
        for copy in copies:
            copy.start()
        for copy in copies:
            copy.wait()


def attend_kernel(head_size, blocks_in, counts, slots, *refs):
    sources = refs[:blocks_in]
    out_ref, log_ref, mixed_ref, key_own, value_own, sems = refs[blocks_in:]
    fetch(sources, mixed_ref, sems)
    length, lanes = out_ref.shape
    tile = mixed_ref.shape[1]
    pack = LANES // head_size
    scale = head_size ** (-0.5) * LOG2E
    sequence = pl.program_id(0)
    blocks = lax.div(counts[sequence] + (tile - 1), tile)
    masks = head_masks(head_size)
    out_ref[...] = jnp.zeros(out_ref.shape, out_ref.dtype)
    log_ref[...] = jnp.zeros(log_ref.shape, log_ref.dtype)
    row = lax.broadcasted_iota(jnp.int32, (tile, tile), 0)
    col = lax.broadcasted_iota(jnp.int32, (tile, tile), 1)
    for pair in range(lanes // LANES):
        base = pair * LANES
        for i in range(length // tile):
            slot = slots[sequence, i]
            keys = mixed_ref[slot, :, lanes + base : lanes + base + LANES]
            values = mixed_ref[slot, :, 2 * lanes + base : 2 * lanes + base + LANES]
            for h in range(pack):
                key_own[h, i * tile : (i + 1) * tile] = jnp.where(masks[h], keys, jnp.zeros_like(keys))
                value_own[h, i * tile : (i + 1) * tile] = jnp.where(
                    masks[h], values, jnp.zeros_like(values)
                )

        def query_block(i, _, pair=pair, base=base):
            start = pl.multiple_of(i * tile, tile)
            queries = mixed_ref[slots[sequence, i], :, base : base + LANES]

            def step(j, carry, diagonal=False):
                total, tops, sums = carry
                first = pl.multiple_of(j * tile, tile)
                new_tops, new_sums, shrinks, adds = [], [], [], []
                for h in range(pack):
                    scores = dot_nt(queries, key_own[h, pl.ds(first, tile)]) * scale
                    if diagonal:
                        scores = jnp.where(col <= row, scores, -1e30)
                    top = jnp.maximum(tops[h], jnp.max(scores, axis=1, keepdims=True))
                    terms = jnp.exp2(scores - top)
                    shrink = jnp.exp2(tops[h] - top)
                    new_tops.append(top)
                    new_sums.append(sums[h] * shrink + jnp.sum(terms, axis=1, keepdims=True))
                    shrinks.append(shrink)
                    adds.append(dot_nn(terms.astype(jnp.bfloat16), value_own[h, pl.ds(first, tile)]))
                shrink = shrinks[0]
                for h in range(1, pack):
                    shrink = jnp.where(masks[h], shrinks[h], shrink)
                total = total * shrink
                for add in adds:
                    total = total + add
                return total, tuple(new_tops), tuple(new_sums)

            carry = (
                jnp.zeros((tile, LANES), jnp.float32),
                tuple(jnp.full((tile, 1), -1e30, jnp.float32) for _ in range(pack)),
                tuple(jnp.zeros((tile, 1), jnp.float32) for _ in range(pack)),
            )
            carry = lax.fori_loop(0, i, step, carry)
            total, tops, sums = step(i, carry, diagonal=True)
            share = 1.0 / sums[0]
            for h in range(1, pack):
                share = jnp.where(masks[h], 1.0 / sums[h], share)
            out_ref[pl.ds(start, tile), base : base + LANES] = (total * share).astype(out_ref.dtype)
            for h in range(pack):
                logs = jnp.broadcast_to(tops[h] + jnp.log2(sums[h]), (tile, LANES))
                index = pair * pack + h
                log_ref[0, index : index + 1, pl.ds(start, tile)] = jnp.transpose(logs)[0:1]
            return 0

        lax.fori_loop(0, blocks, query_block, 0)


def attend(mixed, slots, counts, head_size):
    sequences = counts.shape[0]
    rows = sum(part.shape[0] for part in mixed)
    tile = rows // slots.size
    blocks = rows // tile
    lanes = mixed[0].shape[1] // 3
    length = rows // sequences
    heads = lanes // head_size
    pack = LANES // head_size
    return pl.pallas_call(
        functools.partial(attend_kernel, head_size, len(mixed)),
        grid_spec=pltpu.PrefetchScalarGridSpec(
            num_scalar_prefetch=2,
            grid=(sequences,),
            in_specs=[pl.BlockSpec(memory_space=pl.ANY)] * len(mixed),
            out_specs=[
                pl.BlockSpec((length, lanes), lambda s, *_: (s, 0)),
                pl.BlockSpec((1, heads, length), lambda s, *_: (s, 0, 0)),
            ],
            scratch_shapes=[
                pltpu.VMEM((blocks, tile, 3 * lanes), jnp.bfloat16),
                pltpu.VMEM((pack, length, LANES), jnp.bfloat16),
                pltpu.VMEM((pack, length, LANES), jnp.bfloat16),
                pltpu.SemaphoreType.DMA((blocks,)),
            ],
        ),
        out_shape=[
            jax.ShapeDtypeStruct((rows, lanes), jnp.bfloat16),
            jax.ShapeDtypeStruct((sequences, heads, length), jnp.float32),
        ],
        compiler_params=pltpu.CompilerParams(vmem_limit_bytes=VMEM_BYTES),
        cost_estimate=cost(rows * length * lanes * 2, rows * lanes * 8, rows * length * heads // 2),
    )(counts, slots, *mixed)


def attend_back_kernel(
    head_size,
    blocks_in,
    counts,
    slots,
    *refs,
):
    sources = refs[:blocks_in]
    grad_ref, out_ref, log_ref, own_ref, other_ref, mixed_ref = refs[blocks_in : blocks_in + 6]
    query_own, key_own, grad_own, delta, grad_query, grad_key, grad_value, back_ref, sems = refs[
        blocks_in + 6 :
    ]
    fetch(sources, mixed_ref, sems)
    length, lanes = out_ref.shape
    tile = mixed_ref.shape[1]
    pack = LANES // head_size
    scale = head_size ** (-0.5)
    sequence = pl.program_id(0)
    blocks = lax.div(counts[sequence] + (tile - 1), tile)
    masks = head_masks(head_size)
    for i in range(length // tile):
        back_ref[slots[sequence, i]] = jnp.zeros((tile, 3 * lanes), back_ref.dtype)
    key_row = lax.broadcasted_iota(jnp.int32, (tile, tile), 0)
    query_col = lax.broadcasted_iota(jnp.int32, (tile, tile), 1)
    for pair in range(lanes // LANES):
        base = pair * LANES
        for i in range(length // tile):
            span = slice(i * tile, (i + 1) * tile)
            slot = slots[sequence, i]
            queries = mixed_ref[slot, :, base : base + LANES]
            keys = mixed_ref[slot, :, lanes + base : lanes + base + LANES]
            grads = grad_ref[span, base : base + LANES]
            for h in range(pack):
                query_own[h, span] = jnp.where(masks[h], queries, jnp.zeros_like(queries))
                key_own[h, span] = jnp.where(masks[h], keys, jnp.zeros_like(keys))
                grad_own[h, span] = jnp.where(masks[h], grads, jnp.zeros_like(grads))
        grad_query[...] = jnp.zeros(grad_query.shape, jnp.float32)

        def deltas(i, _, base=base):
            start = pl.multiple_of(i * tile, tile)
            grads = grad_ref[pl.ds(start, tile), base : base + LANES].astype(jnp.float32)
            outs = out_ref[pl.ds(start, tile), base : base + LANES].astype(jnp.float32)
            products = jnp.transpose(grads * outs)
            for h in range(pack):
                delta[h : h + 1, pl.ds(start, tile)] = jnp.sum(
                    products[h * head_size : (h + 1) * head_size], axis=0, keepdims=True
                )
            return 0

        lax.fori_loop(0, blocks, deltas, 0)

        def key_block(j, _, pair=pair, base=base):
            first = pl.multiple_of(j * tile, tile)
            place = slots[sequence, j]
            keys = mixed_ref[place, :, lanes + base : lanes + base + LANES]
            values = mixed_ref[place, :, 2 * lanes + base : 2 * lanes + base + LANES]
            grad_key[...] = jnp.zeros(grad_key.shape, jnp.float32)
            grad_value[...] = jnp.zeros(grad_value.shape, jnp.float32)

            def step(i, diagonal=False):
                start = pl.multiple_of(i * tile, tile)
                add_query, add_key, add_value = [], [], []
                for h in range(pack):
                    index = pair * pack + h
                    query_head = query_own[h, pl.ds(start, tile)]
                    grad_head = grad_own[h, pl.ds(start, tile)]
                    scores = dot_nt(keys, query_head) * (scale * LOG2E)
                    probs = jnp.exp2(scores - log_ref[0, index : index + 1, pl.ds(start, tile)])
                    if diagonal:
                        probs = jnp.where(key_row <= query_col, probs, 0.0)
                    grad_probs = dot_nt(values, grad_head)
                    grad_scores = (
                        probs * (grad_probs - delta[h : h + 1, pl.ds(start, tile)])
                    ).astype(jnp.bfloat16)
                    add_value.append(dot_nn(probs.astype(jnp.bfloat16), grad_head))
                    add_key.append(dot_nn(grad_scores, query_head))
                    add_query.append(dot_tn(grad_scores, key_own[h, pl.ds(first, tile)]))
                grad_value[...] += functools.reduce(jnp.add, add_value)
                grad_key[...] += functools.reduce(jnp.add, add_key)
                grad_query[pl.ds(start, tile), :] += functools.reduce(jnp.add, add_query)

            def off_diagonal(i, _):
                step(i)
                return 0

            step(j, diagonal=True)
            lax.fori_loop(j + 1, blocks, off_diagonal, 0)
            back_ref[place, :, lanes + base : lanes + base + LANES] = (grad_key[...] * scale).astype(
                back_ref.dtype
            )
            back_ref[place, :, 2 * lanes + base : 2 * lanes + base + LANES] = grad_value[...].astype(
                back_ref.dtype
            )
            return 0

        lax.fori_loop(0, blocks, key_block, 0)
        for i in range(length // tile):
            back_ref[slots[sequence, i], :, base : base + LANES] = (
                grad_query[i * tile : (i + 1) * tile] * scale
            ).astype(back_ref.dtype)

    @pl.when(sequence == pl.num_programs(0) - 1)
    def _():
        half = back_ref.shape[0] // 2
        for k in range(half):
            own_ref[k * tile : (k + 1) * tile] = back_ref[k]
            other_ref[k * tile : (k + 1) * tile] = back_ref[half + k]


def attend_back(mixed, slots, grads, outs, logs, counts, head_size):
    sequences = counts.shape[0]
    rows, lanes = outs.shape
    length = rows // sequences
    heads = lanes // head_size
    pack = LANES // head_size
    tile = rows // slots.size
    blocks = rows // tile
    whole = pl.BlockSpec((rows // 2, 3 * lanes), lambda s, *_: (0, 0))
    return pl.pallas_call(
        functools.partial(attend_back_kernel, head_size, len(mixed)),
        grid_spec=pltpu.PrefetchScalarGridSpec(
            num_scalar_prefetch=2,
            grid=(sequences,),
            in_specs=[pl.BlockSpec(memory_space=pl.ANY)] * len(mixed)
            + [
                pl.BlockSpec((length, lanes), lambda s, *_: (s, 0)),
                pl.BlockSpec((length, lanes), lambda s, *_: (s, 0)),
                pl.BlockSpec((1, heads, length), lambda s, *_: (s, 0, 0)),
            ],
            out_specs=[whole, whole],
            scratch_shapes=[
                pltpu.VMEM((blocks, tile, 3 * lanes), jnp.bfloat16),
                pltpu.VMEM((pack, length, LANES), jnp.bfloat16),
                pltpu.VMEM((pack, length, LANES), jnp.bfloat16),
                pltpu.VMEM((pack, length, LANES), jnp.bfloat16),
                pltpu.VMEM((pack, length), jnp.float32),
                pltpu.VMEM((length, LANES), jnp.float32),
                pltpu.VMEM((tile, LANES), jnp.float32),
                pltpu.VMEM((tile, LANES), jnp.float32),
                pltpu.VMEM((blocks, tile, 3 * lanes), jnp.bfloat16),
                pltpu.SemaphoreType.DMA((blocks,)),
            ],
        ),
        out_shape=[jax.ShapeDtypeStruct((rows // 2, 3 * lanes), jnp.bfloat16)] * 2,
        compiler_params=pltpu.CompilerParams(vmem_limit_bytes=VMEM_BYTES),
        cost_estimate=cost(1, 1),
    )(counts, slots, *mixed, grads, outs, logs)


def ffn_kernel(block, x_parts, g_parts, counts, *refs):
    xs, refs = refs[:x_parts], refs[x_parts:]
    gs, refs = refs[:g_parts], refs[g_parts:]
    ups, downs, shifts = refs[0:2], refs[2:4], refs[4:6]
    units_ref, back_ref, out_ref, x, g, total, x_sems, g_sems = refs[-8:]
    fetch(xs, x, x_sems)
    fetch(gs, g, g_sems)
    blocks, size, model = x.shape
    width = ups[0].shape[0]
    step = pl.program_id(0)

    @pl.when(step == 0)
    def _():
        total[...] = jnp.zeros(total.shape, total.dtype)

    for k in range(blocks):
        rows = slice(k * size, (k + 1) * size)

        @pl.when(counts[block + k] != 0)
        def _(k=k, rows=rows):
            backs = []
            for side in range(2):
                span = slice(side * width, (side + 1) * width)
                pre = dot_nt(x[k], ups[side][...]) + shifts[side][...]
                grad_units = dot_nt(g[k], downs[side][...])
                size_of = jnp.abs(pre)
                bell = jnp.exp2(pre * pre * (-0.5 * LOG2E))
                denominator = 1.0 + (0.3275911 * 0.7071067811865476) * size_of
                t = pl.reciprocal(denominator, approx=True)
                t = t * (2.0 - denominator * t)
                tail = 0.5 * 1.061405429
                for factor in (-1.453152027, 1.421413741, -0.284496736, 0.254829592):
                    tail = tail * t + 0.5 * factor
                tail = tail * t
                units = jnp.maximum(pre, 0.0) - size_of * (tail * bell)
                units_ref[rows, span] = units.astype(units_ref.dtype)
                slope = (tail - size_of * 0.3989422804014327) * bell
                slope = jnp.where(pre < 0, slope, 1.0 - slope)
                backs.append((grad_units * slope).astype(back_ref.dtype))
                back_ref[rows, span] = backs[-1]
            total[rows] += dot_nn(backs[0], ups[0][...]) + dot_nn(backs[1], ups[1][...])

        @pl.when(counts[block + k] == 0)
        def _(rows=rows):
            units_ref[rows] = jnp.zeros((size, 2 * width), units_ref.dtype)
            back_ref[rows] = jnp.zeros((size, 2 * width), back_ref.dtype)

    @pl.when(step == pl.num_programs(0) - 1)
    def _():
        out_ref[...] = total[...].astype(out_ref.dtype)


def ffn_blocks(place, block, counts, xs, gs, ups, downs, shifts, kept):
    size, width = 512, 256
    model = xs[0].shape[1]
    rows = sum(x.shape[0] for x in xs)
    units = ups[0].shape[0]
    whole = pl.BlockSpec(memory_space=pl.ANY)
    weights = pl.BlockSpec((width, model), lambda u, *_: (u, 0))
    shift = pl.BlockSpec((1, width), lambda u, *_: (0, u))
    output = pl.BlockSpec((rows, 2 * width), lambda u, *_: (place, u))
    full = jax.ShapeDtypeStruct((4 * size, 2 * units), jnp.bfloat16)
    return pl.pallas_call(
        functools.partial(ffn_kernel, block, len(xs), len(gs)),
        grid_spec=pltpu.PrefetchScalarGridSpec(
            num_scalar_prefetch=1,
            grid=(units // width,),
            in_specs=[whole] * (len(xs) + len(gs))
            + [weights] * 4
            + [shift] * 2
            + [whole] * len(kept),
            out_specs=[output, output, pl.BlockSpec((rows, model), lambda u, *_: (0, 0))],
            scratch_shapes=[
                pltpu.VMEM((rows // size, size, model), jnp.bfloat16),
                pltpu.VMEM((rows // size, size, model), jnp.bfloat16),
                pltpu.VMEM((rows, model), jnp.float32),
                pltpu.SemaphoreType.DMA((len(xs),)),
                pltpu.SemaphoreType.DMA((len(gs),)),
            ],
        ),
        out_shape=[full, full, jax.ShapeDtypeStruct((rows, model), jnp.bfloat16)],
        input_output_aliases={len(xs) + len(gs) + 7 + k: k for k in range(len(kept))},
        compiler_params=pltpu.CompilerParams(vmem_limit_bytes=VMEM_BYTES),
        cost_estimate=cost(12 * rows * units * model, 8 * units * model + 8 * rows * model, 4 * rows * units),
    )(counts, *xs, *gs, *ups, *downs, *shifts, *kept)


def arrange(outs, total):
    to_x, to_y, rest = outs
    half = total.shape[0] // 2
    top, bottom = total[:half].astype(to_x.dtype), total[half:].astype(to_x.dtype)
    step = pl.program_id(0)

    @pl.when(step == 0)
    def _():
        to_x[:half] = top
        to_y[:half] = bottom

    @pl.when(step == 1)
    def _():
        to_x[half:] = top
        rest[half : 2 * half] = bottom

    @pl.when(step == 2)
    def _():
        rest[:half] = top
        to_y[half:] = bottom

    @pl.when(step == 3)
    def _():
        rest[2 * half : 3 * half] = top
        rest[3 * half :] = bottom


def arranged(rows, columns):
    sizes = (rows // 4, rows // 4, rows // 2)
    specs = [pl.BlockSpec((size, columns), lambda i, *_: (0, 0)) for size in sizes]
    return specs, [jax.ShapeDtypeStruct((size, columns), jnp.bfloat16) for size in sizes]


def products_kernel(width, order, active, left, own, other, *outs):
    here = active[order[pl.program_id(0)]] != 0

    @pl.when(here)
    def _():
        total = None
        for k in range(own.shape[0] // width):
            rows = slice(k * width, (k + 1) * width)
            for side, right in enumerate((own, other)):
                start = (2 * k + side) * width
                term = dot_nn(left[:, start : start + width], right[rows])
                total = term if total is None else total + term
        arrange(outs, total)

    @pl.when(jnp.logical_not(here))
    def _():
        arrange(outs, jnp.zeros((left.shape[0], own.shape[1]), jnp.float32))


def products(order, counts, left, own, other):
    blocks = counts.shape[0]
    rows, depth = left.shape
    columns = own.shape[1]
    specs, shapes = arranged(rows, columns)
    return pl.pallas_call(
        functools.partial(products_kernel, 256),
        grid_spec=pltpu.PrefetchScalarGridSpec(
            num_scalar_prefetch=2,
            grid=(blocks,),
            in_specs=[
                pl.BlockSpec((rows // blocks, depth), lambda i, order, *_: (order[i], 0)),
                pl.BlockSpec(own.shape, lambda i, *_: (0, 0)),
                pl.BlockSpec(own.shape, lambda i, *_: (0, 0)),
            ],
            out_specs=specs,
        ),
        out_shape=shapes,
        compiler_params=pltpu.CompilerParams(vmem_limit_bytes=VMEM_BYTES),
        cost_estimate=cost(1, 1),
    )(order, counts, left, own, other)


def attend_out_kernel(left, weight, bias, hidden, active, out_ref):
    out_ref[...] = hidden[...].astype(jnp.float32) + active[...] * (
        dot_nn(left[...], weight[...]) + bias[...]
    )


def attend_out(left, weight, bias, hidden, active):
    rows, depth = left.shape
    columns = weight.shape[1]
    width = 512
    column = pl.BlockSpec((rows, width), lambda j: (0, j))
    return pl.pallas_call(
        attend_out_kernel,
        grid=(columns // width,),
        in_specs=[
            pl.BlockSpec((rows, depth), lambda j: (0, 0)),
            pl.BlockSpec((depth, width), lambda j: (0, j)),
            pl.BlockSpec((1, width), lambda j: (0, j)),
            column,
            pl.BlockSpec((rows, 1), lambda j: (0, 0)),
        ],
        out_specs=column,
        out_shape=jax.ShapeDtypeStruct((rows, columns), jnp.float32),
        compiler_params=pltpu.CompilerParams(vmem_limit_bytes=VMEM_BYTES),
        cost_estimate=cost(2 * rows * depth * columns, 2 * depth * columns + 8 * rows * columns),
    )(left, weight, bias[None], hidden, active)


def attend_out_back_kernel(grad, weight, out_ref):
    out_ref[...] = dot_nt(grad[...], weight[...]).astype(out_ref.dtype)


def attend_out_back(grad, weight):
    rows, columns = grad.shape
    depth = weight.shape[0]
    width = 512
    return pl.pallas_call(
        attend_out_back_kernel,
        grid=(depth // width,),
        in_specs=[
            pl.BlockSpec((rows, columns), lambda j: (0, 0)),
            pl.BlockSpec((width, columns), lambda j: (j, 0)),
        ],
        out_specs=pl.BlockSpec((rows, width), lambda j: (0, j)),
        out_shape=jax.ShapeDtypeStruct((rows, depth), jnp.bfloat16),
        compiler_params=pltpu.CompilerParams(vmem_limit_bytes=VMEM_BYTES),
        cost_estimate=cost(1, 1),
    )(grad, weight)


def project_kernel(inputs, side, parts, *refs):
    xs = refs[:inputs]
    weights, shift, out_ref = refs[inputs:]
    slab = weights.shape[1]
    weight = weights[...].reshape(3 * slab, weights.shape[2])
    for k in range(inputs):

        @pl.when(pl.program_id(0) == k)
        def _(k=k):
            mixed = dot_nt(xs[k][...], weight)
            for t in range(3):
                columns = pl.ds(pl.multiple_of(parts[side, t] * slab, slab), slab)
                out_ref[:, columns] = (
                    mixed[:, t * slab : (t + 1) * slab] + shift[:, columns]
                ).astype(out_ref.dtype)


def project(parts, side, xs, weights, shift):
    size, model = xs[0].shape
    slab = weights.shape[1]
    return pl.pallas_call(
        functools.partial(project_kernel, len(xs), side),
        grid_spec=pltpu.PrefetchScalarGridSpec(
            num_scalar_prefetch=1,
            grid=(len(xs),),
            in_specs=[pl.BlockSpec((size, model), lambda i, *_: (0, 0))] * len(xs)
            + [
                pl.BlockSpec(weights.shape, lambda i, *_: (0, 0, 0)),
                pl.BlockSpec(shift.shape, lambda i, *_: (0, 0)),
            ],
            out_specs=pl.BlockSpec((size, 3 * slab), lambda i, *_: (i, 0)),
        ),
        out_shape=jax.ShapeDtypeStruct((len(xs) * size, 3 * slab), jnp.bfloat16),
        compiler_params=pltpu.CompilerParams(vmem_limit_bytes=VMEM_BYTES),
        cost_estimate=pl.CostEstimate(
            flops=6 * len(xs) * size * slab * model,
            bytes_accessed=6 * slab * model + 2 * len(xs) * size * (model + 3 * slab),
            transcendentals=0,
        ),
    )(parts, *xs, weights, shift)


def unproject_kernel(order, parts, active, mine, theirs, own, other, *outs):
    slab = own.shape[1]
    here = active[order[pl.program_id(0)]] != 0

    @pl.when(here)
    def _():
        total = None
        for side, (left, right) in enumerate(((mine, own), (theirs, other))):
            for t in range(3):
                columns = pl.ds(pl.multiple_of(parts[side, t] * slab, slab), slab)
                term = dot_nn(left[:, columns], right[t])
                total = term if total is None else total + term
        arrange(outs, total)

    @pl.when(jnp.logical_not(here))
    def _():
        arrange(outs, jnp.zeros((mine.shape[0], own.shape[2]), jnp.float32))


def unproject(order, parts, counts, mine, theirs, own, other):
    blocks = counts.shape[0]
    rows = mine.shape[0]
    slab, model = own.shape[1:]
    left = pl.BlockSpec((rows // blocks, 3 * slab), lambda i, order, *_: (order[i], 0))
    fixed = pl.BlockSpec(own.shape, lambda i, *_: (0, 0, 0))
    specs, shapes = arranged(rows, model)
    return pl.pallas_call(
        unproject_kernel,
        grid_spec=pltpu.PrefetchScalarGridSpec(
            num_scalar_prefetch=3,
            grid=(blocks,),
            in_specs=[left, left, fixed, fixed],
            out_specs=specs,
        ),
        out_shape=shapes,
        compiler_params=pltpu.CompilerParams(vmem_limit_bytes=VMEM_BYTES),
        cost_estimate=cost(1, 1),
    )(order, parts, counts, mine, theirs, own, other)


def weight_grad_kernel(inputs, added, columns, *refs):
    left, rights = refs[0], refs[1 : 1 + inputs]
    tokens, sems = refs[-2:]
    outs = refs[1 + inputs + added : -2]
    fetch(rights, tokens, sems)
    total = dot_tn(left[...], tokens[0])
    if added:
        total = total + refs[1 + inputs][...].astype(jnp.float32)
    size = outs[0].shape[0]
    if size == total.shape[0]:
        for k, out_ref in enumerate(outs):

            @pl.when((len(outs) == 1) | (pl.program_id(0) == k))
            def _(out_ref=out_ref):
                out_ref[...] = total.astype(out_ref.dtype)

    else:
        for k, out_ref in enumerate(outs):
            out_ref[...] = total[k * size : (k + 1) * size].astype(out_ref.dtype)


def weight_grad(left, columns, tile, rights, extra=None, outputs=1, apart=False):
    rows = left.shape[0]
    model = rights[0].shape[1]
    steps = columns.shape[0]
    output = pl.BlockSpec((tile // outputs, model), lambda i, *_: (i, 0))
    extras = [] if extra is None else [extra]
    shape = jax.ShapeDtypeStruct((steps * tile // outputs, model), jnp.bfloat16)
    added = [output] * len(extras)
    if apart:
        outputs = steps
        output = pl.BlockSpec((tile, model), lambda i, *_: (0, 0))
        shape = jax.ShapeDtypeStruct((tile, model), jnp.bfloat16)
    results = pl.pallas_call(
        functools.partial(weight_grad_kernel, len(rights), len(extras)),
        grid_spec=pltpu.PrefetchScalarGridSpec(
            num_scalar_prefetch=1,
            grid=(steps,),
            in_specs=[pl.BlockSpec((rows, tile), lambda i, columns: (0, columns[i]))]
            + [pl.BlockSpec(memory_space=pl.ANY)] * len(rights)
            + added,
            out_specs=[output] * outputs,
            scratch_shapes=[
                pltpu.VMEM((1, rows, model), jnp.bfloat16),
                pltpu.SemaphoreType.DMA((len(rights),)),
            ],
        ),
        out_shape=[shape] * outputs,
        compiler_params=pltpu.CompilerParams(vmem_limit_bytes=VMEM_BYTES),
        cost_estimate=cost(1, 1),
    )(columns, left, *rights, *extras)
    return results[0] if outputs == 1 else results


def chain_sum(values, axis):
    size = lax.axis_size(axis)
    if size != 4:
        return lax.psum(values.astype(jnp.bfloat16), axis).astype(jnp.float32)
    place = lax.axis_index(axis)
    outer = lax.ppermute(values.astype(jnp.bfloat16), axis, [(0, 1), (3, 2)])
    half = (values + outer.astype(jnp.float32)).astype(jnp.bfloat16)
    other = lax.ppermute(half, axis, [(1, 2), (2, 1)])
    whole = (half.astype(jnp.float32) + other.astype(jnp.float32)).astype(jnp.bfloat16)
    ends = lax.ppermute(whole, axis, [(1, 0), (2, 3)])
    inner = (place == 1) | (place == 2)
    return jnp.where(inner, whole, ends).astype(jnp.float32)


def normalize(values):
    center = values - jnp.mean(values, axis=-1, keepdims=True)
    inverse = lax.rsqrt(jnp.mean(center * center, axis=-1, keepdims=True) + epsilon)
    return center * inverse, inverse


def normalize_back(grad, gain, normal, inverse):
    scaled = grad * gain
    grad_values = inverse * (
        scaled
        - jnp.mean(scaled, axis=-1, keepdims=True)
        - normal * jnp.mean(scaled * normal, axis=-1, keepdims=True)
    )
    return grad_values, jnp.sum(grad * normal, axis=0), jnp.sum(grad, axis=0)


def local_general(
    hidden,
    cotangent,
    exit_layer,
    ln1_gain,
    ln1_bias,
    qkv_weight,
    query_bias,
    value_bias,
    out_weight,
    out_bias,
    ln2_gain,
    ln2_bias,
    up_weight,
    up_bias,
    down_weight,
    down_bias,
):
    width = lax.axis_size("wide")
    rank = lax.axis_index("wide")
    rows, model = hidden.shape
    group = rows * width
    slab = model // width
    head_size = model // HEADS
    units_own = up_weight.shape[0]
    keep = exit_layer >= LAYER
    counts = jnp.sum(keep.astype(jnp.int32), axis=1)
    active = lax.dynamic_slice_in_dim(keep.reshape(group), rank * rows, rows, 0)
    active = active.astype(jnp.float32)[:, None]
    grad_out = cotangent.astype(jnp.float32)

    routes = [[(w, (3 * w + t) % width) for w in range(width)] for t in range(3)]
    part_at = np.zeros((width, 3), np.int32)
    for t in range(3):
        for w, d in routes[t]:
            part_at[d, t] = (3 * w + t) // width
    place_of = jnp.asarray(np.argsort(part_at, axis=1).astype(np.int32))[rank]
    part_of = jnp.asarray(part_at)[rank]

    hidden_wide = hidden.astype(jnp.float32)
    normal1, inverse1 = normalize(hidden_wide)
    normed1 = lax.all_gather(
        (normal1 * ln1_gain + ln1_bias).astype(jnp.bfloat16), "wide", axis=0, tiled=True
    )
    slabs = qkv_weight.reshape(3, slab, model)
    received = jnp.stack([lax.ppermute(slabs[t], "wide", routes[t]) for t in range(3)])
    qkv_own = jnp.concatenate(
        [lax.dynamic_index_in_dim(received, place_of[p], 0, keepdims=False) for p in range(3)]
    )
    own = lambda vector: lax.dynamic_slice_in_dim(vector, rank * slab, slab, 0)
    qkv_shift = jnp.concatenate(
        [own(query_bias), jnp.zeros((slab,), jnp.float32), own(value_bias)]
    )

    grad_ffn = (active * grad_out).astype(jnp.bfloat16)
    down_bias_grad = jnp.sum(grad_ffn.astype(jnp.float32), axis=0)
    piece = rows // CHUNKS
    part = lambda values, c: values[c * piece : (c + 1) * piece]
    gather = lambda values: lax.all_gather(values, "wide", axis=0, tiled=True)
    scatter = lambda values: lax.psum_scatter(
        values.astype(jnp.bfloat16), "wide", scatter_dimension=0, tiled=True
    )
    grad_ffns = [gather(part(grad_ffn, c)) for c in range(CHUNKS)]
    out_whole = gather(out_weight)

    mixed = (dot_nt(normed1, qkv_own) + qkv_shift).astype(jnp.bfloat16)
    mixed = jnp.split(mixed, group // TILE)
    slots = jnp.arange(group // TILE, dtype=jnp.int32).reshape(counts.shape[0], -1)
    attended, logs = attend(mixed, slots, counts, head_size)
    attended_rows = lax.all_to_all(attended, "wide", split_axis=0, concat_axis=1, tiled=True)
    middle = hidden_wide + active * (dot_nn(attended_rows, out_whole) + out_bias)
    normal2, inverse2 = normalize(middle)
    normed2 = (normal2 * ln2_gain + ln2_bias).astype(jnp.bfloat16)
    up_shift = lax.dynamic_slice_in_dim(up_bias, rank * units_own, units_own, 0)

    normed2s = [gather(part(normed2, c)) for c in range(CHUNKS)]
    units, grad_pres, grad_normed2, ffn_out = [], [], [], []
    for c in range(CHUNKS):
        grad_units = dot_nt(grad_ffns[c], down_weight)
        pre = dot_nt(normed2s[c], up_weight) + up_shift
        below = 0.5 + 0.5 * lax.erf(pre * 0.7071067811865476)
        bell = jnp.exp(-0.5 * pre * pre) * 0.3989422804014327
        units.append((pre * below).astype(jnp.bfloat16))
        grad_pres.append((grad_units * (below + pre * bell)).astype(jnp.bfloat16))
        grad_normed2.append(scatter(dot_nn(grad_pres[c], up_weight)))
    for c in range(CHUNKS):
        ffn_out.append(scatter(dot_nn(units[c], down_weight)))
    grad_normed2 = jnp.concatenate(grad_normed2).astype(jnp.float32)
    ffn_out = jnp.concatenate(ffn_out).astype(jnp.float32)
    output = (middle + active * (ffn_out + down_bias)).astype(jnp.bfloat16)

    up_bias_own = sum(jnp.sum(g.astype(jnp.float32), axis=0) for g in grad_pres)
    down_grad = sum(dot_tn(units[c], grad_ffns[c]) for c in range(CHUNKS))
    up_grad = sum(dot_tn(grad_pres[c], normed2s[c]) for c in range(CHUNKS))
    halves = lambda values: jnp.concatenate(
        [chain_sum(half, "batch") for half in jnp.split(values, 2)]
    )
    down_grad = halves(down_grad)
    up_grad = halves(up_grad)

    grad_middle, ln2_gain_grad, ln2_bias_grad = normalize_back(
        grad_normed2, ln2_gain, normal2, inverse2
    )
    grad_middle = grad_out + grad_middle
    grad_branch = (active * grad_middle).astype(jnp.bfloat16)
    out_bias_grad = jnp.sum(grad_branch.astype(jnp.float32), axis=0)
    grad_attended = dot_nt(grad_branch, out_whole).astype(jnp.bfloat16)
    grad_heads = lax.all_to_all(grad_attended, "wide", split_axis=1, concat_axis=0, tiled=True)
    out_grad = chain_sum(scatter(dot_tn(attended_rows, grad_branch)).astype(jnp.float32), "batch")

    placed = lambda vector, size: lax.dynamic_update_slice_in_dim(
        jnp.zeros((size,), jnp.float32), vector, rank * vector.shape[0], 0
    )
    early = lax.psum(
        (
            out_bias_grad,
            ln2_gain_grad,
            ln2_bias_grad,
            placed(up_bias_own, up_bias.shape[0]),
            down_bias_grad,
        ),
        ("batch", "wide"),
    )

    grad_mixed = jnp.concatenate(
        attend_back(mixed, slots, grad_heads, attended, logs, counts, head_size)
    )
    grad_normed1 = scatter(dot_nn(grad_mixed, qkv_own)).astype(jnp.float32)
    sums = jnp.sum(grad_mixed.astype(jnp.float32), axis=0)
    qkv_parts = []
    for t in range(3):
        columns = lax.dynamic_slice_in_dim(grad_mixed, part_of[t] * slab, slab, 1)
        total = chain_sum(dot_tn(columns, normed1), "batch").astype(jnp.bfloat16)
        back = [(d, w) for w, d in routes[t]]
        qkv_parts.append(lax.ppermute(total, "wide", back).astype(jnp.float32))
    qkv_grad = jnp.concatenate(qkv_parts)

    grad_hidden, ln1_gain_grad, ln1_bias_grad = normalize_back(
        grad_normed1, ln1_gain, normal1, inverse1
    )
    input_grad = grad_middle + grad_hidden
    late = lax.psum(
        (
            ln1_gain_grad,
            ln1_bias_grad,
            placed(sums[:slab], model),
            placed(sums[2 * slab :], model),
        ),
        ("batch", "wide"),
    )
    return (
        output,
        input_grad,
        late[0],
        late[1],
        qkv_grad,
        late[2],
        late[3],
        out_grad,
        early[0],
        early[1],
        early[2],
        up_grad,
        early[3],
        down_grad,
        early[4],
    )


def swap(values, bits):
    width = lax.axis_size("wide")
    return lax.ppermute(values, "wide", [(w, w ^ bits) for w in range(width)])


def after(values, *done):
    return lax.optimization_barrier((values, done))[0]


def relay(along_x, along_y):
    half = along_x.shape[0] // 2
    return [swap(along_y[:half], 2), swap(along_x[half:], 4)]


class Scatter:
    def __init__(self, to_x, to_y, rest):
        self.half = half = to_x.shape[0] // 2
        self.sent = (to_x, to_y)
        self.rest = rest
        self.from_x, self.from_y = swap(to_x, 2), swap(to_y, 4)

    def second(self, *done):
        half = self.half
        from_x, from_y = after((self.from_x, self.from_y), *done)
        self.near = (from_x[half:], from_y[half:])
        self.own = self.rest[2 * half :]
        return self.forward(self.rest[:half], self.rest[half : 2 * half], from_x[:half], from_y[:half])

    def forward(self, along_y, along_x, top, bottom):
        wide = lambda values: values.astype(jnp.float32)
        y_top = (wide(along_y) + wide(top)).astype(jnp.bfloat16)
        x_bottom = (wide(along_x) + wide(bottom)).astype(jnp.bfloat16)
        self.last = (swap(y_top, 4), swap(x_bottom, 2))
        return y_top, x_bottom

    def finish(self, *done):
        wide = lambda values: values.astype(jnp.float32)
        y_top, x_bottom = after(self.last, *done)
        x_top, y_bottom = self.near
        return jnp.concatenate(
            [
                wide(self.own[: self.half]) + wide(x_top) + wide(y_top),
                wide(self.own[self.half :]) + wide(x_bottom) + wide(y_bottom),
            ]
        )


def split_for_scatter(own, along_x, along_y, diagonal):
    half = own.shape[0] // 2
    return (
        jnp.concatenate([diagonal[:half], along_x[:half]]),
        jnp.concatenate([diagonal[half:], along_y[half:]]),
        jnp.concatenate([along_y[:half], along_x[half:], own]),
    )


class EarlyScatter(Scatter):
    def __init__(self, own, along_x, along_y):
        self.half = half = own.shape[0] // 2
        self.own, self.along_x, self.along_y = own, along_x, along_y
        self.near = (swap(along_x[:half], 2), swap(along_y[half:], 4))

    def first(self, diagonal):
        self.from_far = (swap(diagonal[: self.half], 2), swap(diagonal[self.half :], 4))
        self.near = after(self.near, diagonal)
        return self.near

    def second(self, *done):
        half = self.half
        far = after(self.from_far, *done)
        return self.forward(self.along_y[:half], self.along_x[half:], *far)


def tree_sum(values):
    total = values + swap(values, 1)
    total = (total + swap(total, 2)) + (swap(total, 4) + swap(total, 6))
    size = lax.axis_size("batch")
    terms = [total] + [
        lax.ppermute(total, "batch", [(z, z ^ bits) for z in range(size)])
        for bits in range(1, size)
    ]
    while len(terms) > 1:
        terms = [terms[k] + terms[k + 1] for k in range(0, len(terms), 2)]
    return terms[0]


def local_chips(
    hidden,
    cotangent,
    exit_layer,
    ln1_gain,
    ln1_bias,
    qkv_weight,
    query_bias,
    value_bias,
    out_weight,
    out_bias,
    ln2_gain,
    ln2_bias,
    up_weight,
    up_bias,
    down_weight,
    down_bias,
):
    width = lax.axis_size("wide")
    rank = lax.axis_index("wide")
    rows, model = hidden.shape
    group = rows * width
    slab = model // width
    head_size = model // HEADS
    units_own = up_weight.shape[0]
    keep = exit_layer >= LAYER
    counts = jnp.sum(keep.astype(jnp.int32), axis=1)
    active = lax.dynamic_slice_in_dim(keep.reshape(group), rank * rows, rows, 0)
    active = active.astype(jnp.float32)[:, None]
    grad_out = cotangent.astype(jnp.float32)

    tiles = jnp.arange(group // rows, dtype=jnp.int32)
    slots = ((tiles ^ rank) & 1) * 4 + ((tiles >> 1) ^ (rank >> 1))
    slots = slots.reshape(counts.shape[0], -1)

    routes = [[(w, (3 * w + t) % width) for w in range(width)] for t in range(3)]
    part_at = np.zeros((width, 3), np.int32)
    for t in range(3):
        for w, d in routes[t]:
            part_at[d, t] = (3 * w + t) // width
    part_at = jnp.asarray(part_at)
    other = rank ^ 1
    parts = jnp.stack([part_at[rank], part_at[other]])

    hidden_wide = hidden.astype(jnp.float32)
    normal1, inverse1 = normalize(hidden_wide)
    slabs = qkv_weight.reshape(3, slab, model)
    slabs = [lax.ppermute(slabs[t], "wide", routes[t]) for t in range(3)]
    normed1 = (normal1 * ln1_gain + ln1_bias).astype(jnp.bfloat16)
    normed1 = [normed1, swap(normed1, 2), swap(normed1, 4)]
    diagonal1 = relay(normed1[1], normed1[2])
    qkv_own = jnp.stack(after(slabs, normed1[1:]))
    qkv_other = swap(qkv_own, 1)

    def shift_of(device):
        own = lambda vector: lax.dynamic_slice_in_dim(vector, device * slab, slab, 0)
        shift = [own(query_bias), jnp.zeros((slab,), jnp.float32), own(value_bias)]
        return jnp.concatenate(shift)[None]

    bias_of = lambda device: lax.dynamic_slice_in_dim(up_bias, device * units_own, units_own, 0)
    up_shifts = [bias_of(rank)[None], bias_of(other)[None]]

    mixed_near = project(parts, 0, normed1, qkv_own, shift_of(rank))
    qkv_other = after(qkv_other, mixed_near, diagonal1)
    lent_near = project(parts, 1, normed1, qkv_other, shift_of(other))
    diagonal1 = after(diagonal1, lent_near)
    lent_far = project(parts, 1, diagonal1, qkv_other, shift_of(other))
    mixed_far = project(parts, 0, after(diagonal1, lent_far), qkv_own, shift_of(rank))
    mixed = [mixed_near, mixed_far, swap(lent_near, 1), swap(lent_far, 1)]

    out_whole = lax.all_gather(after(out_weight, diagonal1), "wide", axis=0, tiled=True)
    grad_ffn = (after(active, diagonal1) * grad_out).astype(jnp.bfloat16)
    down_bias_grad = jnp.sum(grad_ffn.astype(jnp.float32), axis=0)

    attended, logs = attend(mixed, slots, counts, head_size)
    attended_rows = lax.all_to_all(attended, "wide", split_axis=0, concat_axis=1, tiled=True)
    grad_ffn = after(grad_ffn, attended_rows)
    grad_ffn = [grad_ffn, swap(grad_ffn, 2), swap(grad_ffn, 4)]
    up_other, down_other = swap(after((up_weight, down_weight), attended), 1)
    middle = attend_out(attended_rows, out_whole, out_bias, hidden, active)
    normal2, inverse2 = normalize(middle)
    normed2 = (normal2 * ln2_gain + ln2_bias).astype(jnp.bfloat16)
    normed2 = [normed2, swap(normed2, 2), swap(normed2, 4)]

    per_tile = jnp.sum(keep.reshape(group // rows, rows).astype(jnp.int32), axis=1)
    block_chip = (rank >> 1) ^ jnp.arange(4, dtype=jnp.int32)
    block_counts = per_tile[2 * block_chip + (rank & 1)]
    ups, downs = [up_weight, up_other], [down_weight, down_other]

    def ffn(place, block, xs, gs, kept):
        *kept, partial = ffn_blocks(
            place, block, block_counts, xs, gs, ups, downs, up_shifts, tuple(kept)
        )
        return kept, partial

    kept, partial_own = ffn(2, 0, [after(normed2[0], grad_ffn[1:])], grad_ffn[:1], ())
    normed2[1:] = after(normed2[1:], partial_own)
    diagonal2 = relay(normed2[1], normed2[2])
    diagonal_ffn = relay(*after(grad_ffn[1:], attended_rows))
    kept, partial_near = ffn(0, 1, normed2[1:], grad_ffn[1:], kept)
    scatter2 = EarlyScatter(partial_own, partial_near[:rows], partial_near[rows:])
    diagonal2 = after(diagonal2, partial_near)
    (units, grad_pres), partial_far = ffn(3, 3, diagonal2, diagonal_ffn, kept)
    wait = scatter2.first(partial_far)
    tokens2 = [*normed2[1:], normed2[0], *diagonal2]
    tokens_ffn = [*grad_ffn[1:], grad_ffn[0], *diagonal_ffn]

    wide = lambda values: values.astype(jnp.float32)
    lowered = lambda values: values.astype(jnp.bfloat16)
    tile = 512
    tiles = jnp.arange(2 * units_own // tile, dtype=jnp.int32)

    down_own, down_lent = weight_grad(after(units, wait), tiles, tile, tokens_ffn, outputs=2)
    wait = scatter2.second(down_lent)
    down_lent = swap(down_lent, 1)
    up_own, up_lent = weight_grad(after(grad_pres, wait), tiles, tile, tokens2, outputs=2)

    up_lent = swap(up_lent, 1)
    down_sum = lowered(wide(down_own) + wide(after(down_lent, up_own)))
    up_sum = lowered(wide(up_own) + wide(up_lent))
    down_grad, up_grad = lax.psum((down_sum, up_sum), "batch")
    grad_middle, ln2_gain_grad, ln2_bias_grad = normalize_back(
        scatter2.finish(up_own), ln2_gain, normal2, inverse2
    )
    grad_middle = grad_out + grad_middle
    grad_branch = (active * grad_middle).astype(jnp.bfloat16)
    out_bias_grad = jnp.sum(grad_branch.astype(jnp.float32), axis=0)
    grad_branch = after(grad_branch, down_sum, up_sum)
    grad_attended = attend_out_back(grad_branch, out_whole)
    grad_heads = lax.all_to_all(grad_attended, "wide", split_axis=1, concat_axis=0, tiled=True)
    owners = 2 * block_chip + (rank & 1)
    grad_branch = after(grad_branch, grad_attended)
    out_lent = weight_grad(attended_rows, owners ^ 1, slab, [grad_branch])
    out_lent = swap(out_lent, 1)
    out_own = weight_grad(after(attended_rows, out_lent), owners, slab, [grad_branch], out_lent)

    back_own, back_other = attend_back(
        mixed, slots, after(grad_heads, out_own), attended, logs, counts, head_size
    )

    theirs = swap(back_other, 1)
    out_own = after(out_own, back_own)
    scatter_out = Scatter(*split_for_scatter(*jnp.split(out_own, 4)))
    order = jnp.array([3, 0, 1, 2], jnp.int32)
    ffn_counts = block_counts[jnp.array([1, 2, 0, 3])]
    ffn_parts = products(order, ffn_counts, after(units, scatter_out.sent), *downs)
    tokens1 = [*normed1, *diagonal1]
    theirs = after(theirs, ffn_parts[0])
    qkv_lent = weight_grad(theirs, parts[1], slab, tokens1)
    wait = scatter_out.second(qkv_lent)
    grad_parts = unproject(
        jnp.array([3, 1, 2, 0], jnp.int32),
        parts,
        block_counts,
        after(back_own, wait),
        theirs,
        qkv_own,
        qkv_other,
    )
    qkv_lent = swap(qkv_lent, 1)
    scatter1 = Scatter(*grad_parts)
    qkv_total = weight_grad(
        after(back_own, grad_parts[0]),
        parts[0],
        slab,
        tokens1,
        after(qkv_lent, grad_parts[0]),
        apart=True,
    )

    returned = [
        lax.ppermute(total, "wide", [(d, w) for w, d in route])
        for total, route in zip(qkv_total, routes)
    ]
    down_grad, up_grad = after((down_grad, up_grad), returned)
    out_total = lowered(scatter_out.finish(up_grad))
    *qkv_grad, out_grad = lax.psum(after((*returned, out_total), up_grad), "batch")
    wait = scatter1.second(out_total, up_grad)
    scatter_ffn = Scatter(*after(ffn_parts, wait))
    grad_normed1 = scatter1.finish(wait, scatter_ffn.sent)
    grad_hidden, ln1_gain_grad, ln1_bias_grad = normalize_back(
        grad_normed1, ln1_gain, normal1, inverse1
    )
    input_grad = grad_middle + grad_hidden
    grad_pres, back_own, back_other = after((grad_pres, back_own, back_other), wait)
    up_bias_own = jnp.sum(wide(grad_pres), axis=0).reshape(-1, 2, 256)
    up_bias_own = [up_bias_own[:, side].reshape(units_own) for side in range(2)]
    sums = jnp.sum(wide(back_own), axis=0) + jnp.sum(wide(back_other), axis=0)
    wait = scatter_ffn.second(input_grad)
    down_grad, up_grad = wide(after(down_grad, wait)), wide(after(up_grad, wait))
    ffn_out = scatter_ffn.finish(down_grad, up_grad)
    output = (middle + active * (ffn_out + down_bias)).astype(jnp.bfloat16)
    placed = lambda vector, size, device: lax.dynamic_update_slice_in_dim(
        jnp.zeros((size,), jnp.float32), vector, device * vector.shape[0], 0
    )
    smalls = tree_sum(
        jnp.concatenate(
            [
                placed(up_bias_own[0], up_bias.shape[0], rank)
                + placed(up_bias_own[1], up_bias.shape[0], other),
                down_bias_grad,
                out_bias_grad,
                ln2_gain_grad,
                ln2_bias_grad,
                placed(sums[:slab], model, rank),
                placed(sums[2 * slab :], model, rank),
                ln1_gain_grad,
                ln1_bias_grad,
            ]
        )
    )
    up_bias_grad = smalls[: up_bias.shape[0]]
    smalls = smalls[up_bias.shape[0] :].reshape(8, model)
    qkv_grad = wide(jnp.concatenate(qkv_grad))
    out_grad = wide(out_grad)
    return (
        output,
        input_grad,
        smalls[6],
        smalls[7],
        qkv_grad,
        smalls[4],
        smalls[5],
        out_grad,
        smalls[1],
        smalls[2],
        smalls[3],
        up_grad,
        up_bias_grad,
        down_grad,
        smalls[0],
    )


def solution(mesh):
    chips = mesh.shape["wide"] == 8 and mesh.shape["batch"] == 4
    local = local_chips if chips else local_general
    rows = P(("batch", "wide"), None)
    weight = P("wide", None)
    return jax.shard_map(
        local,
        mesh=mesh,
        in_specs=(
            rows,
            rows,
            P("batch", None),
            P(),
            P(),
            weight,
            P(),
            P(),
            weight,
            P(),
            P(),
            P(),
            weight,
            P(),
            weight,
            P(),
        ),
        out_specs=(
            rows,
            rows,
            P(),
            P(),
            weight,
            P(),
            P(),
            weight,
            P(),
            P(),
            P(),
            weight,
            P(),
            weight,
            P(),
        ),
        check_vma=False,
    )
```

```python
import functools

import jax
import jax.numpy as jnp
import numpy as np
from jax import lax
from jax.experimental import pallas as pl
from jax.experimental.pallas import tpu as pltpu
from jax.sharding import PartitionSpec as P

HEADS = 32
LAYER = 12
LANES = 128
TILE = 512
CHUNKS = 2
LOG2E = 1.4426950408889634

epsilon = 1e-05
VMEM_BYTES = 48 * 2**20


def cost(flops, size, exponentials=0):
    return pl.CostEstimate(flops=flops, bytes_accessed=size, transcendentals=exponentials)


def dot_nt(left, right):
    return lax.dot_general(
        left, right, (((1,), (1,)), ((), ())), preferred_element_type=jnp.float32
    )


def dot_nn(left, right):
    return lax.dot_general(
        left, right, (((1,), (0,)), ((), ())), preferred_element_type=jnp.float32
    )


def dot_tn(left, right):
    return lax.dot_general(
        left, right, (((0,), (0,)), ((), ())), preferred_element_type=jnp.float32
    )


def head_masks(head_size):
    lane = lax.broadcasted_iota(jnp.int32, (1, LANES), 1)
    return [
        (lane >= h * head_size) & (lane < (h + 1) * head_size)
        for h in range(LANES // head_size)
    ]


def fetch(sources, target, sems):
    size = target.shape[1]
    copies = []
    row = 0
    for source in sources:
        rows = source.shape[0]
        least = min(rows, size)
        for k in range(rows // least):
            place = target.at[row // size, pl.ds(row % size, least)]
            copies.append(
                pltpu.make_async_copy(source.at[pl.ds(k * least, least)], place, sems.at[len(copies)])
            )
            row += least

    @pl.when(pl.program_id(0) == 0)
    def _():
        for copy in copies:
            copy.start()
        for copy in copies:
            copy.wait()


def attend_kernel(head_size, blocks_in, counts, slots, *refs):
    sources = refs[:blocks_in]
    out_ref, log_ref, mixed_ref, key_own, value_own, sems = refs[blocks_in:]
    fetch(sources, mixed_ref, sems)
    length, lanes = out_ref.shape
    tile = mixed_ref.shape[1]
    pack = LANES // head_size
    scale = head_size ** (-0.5) * LOG2E
    sequence = pl.program_id(0)
    blocks = lax.div(counts[sequence] + (tile - 1), tile)
    masks = head_masks(head_size)
    out_ref[...] = jnp.zeros(out_ref.shape, out_ref.dtype)
    log_ref[...] = jnp.zeros(log_ref.shape, log_ref.dtype)
    row = lax.broadcasted_iota(jnp.int32, (tile, tile), 0)
    col = lax.broadcasted_iota(jnp.int32, (tile, tile), 1)
    for pair in range(lanes // LANES):
        base = pair * LANES
        for i in range(length // tile):
            slot = slots[sequence, i]
            keys = mixed_ref[slot, :, lanes + base : lanes + base + LANES]
            values = mixed_ref[slot, :, 2 * lanes + base : 2 * lanes + base + LANES]
            for h in range(pack):
                key_own[h, i * tile : (i + 1) * tile] = jnp.where(masks[h], keys, jnp.zeros_like(keys))
                value_own[h, i * tile : (i + 1) * tile] = jnp.where(
                    masks[h], values, jnp.zeros_like(values)
                )

        def query_block(i, _, pair=pair, base=base):
            start = pl.multiple_of(i * tile, tile)
            queries = mixed_ref[slots[sequence, i], :, base : base + LANES]

            def step(j, carry, diagonal=False):
                total, tops, sums = carry
                first = pl.multiple_of(j * tile, tile)
                new_tops, new_sums, shrinks, adds = [], [], [], []
                for h in range(pack):
                    scores = dot_nt(queries, key_own[h, pl.ds(first, tile)]) * scale
                    if diagonal:
                        scores = jnp.where(col <= row, scores, -1e30)
                    top = jnp.maximum(tops[h], jnp.max(scores, axis=1, keepdims=True))
                    terms = jnp.exp2(scores - top)
                    shrink = jnp.exp2(tops[h] - top)
                    new_tops.append(top)
                    new_sums.append(sums[h] * shrink + jnp.sum(terms, axis=1, keepdims=True))
                    shrinks.append(shrink)
                    adds.append(dot_nn(terms.astype(jnp.bfloat16), value_own[h, pl.ds(first, tile)]))
                shrink = shrinks[0]
                for h in range(1, pack):
                    shrink = jnp.where(masks[h], shrinks[h], shrink)
                total = total * shrink
                for add in adds:
                    total = total + add
                return total, tuple(new_tops), tuple(new_sums)

            carry = (
                jnp.zeros((tile, LANES), jnp.float32),
                tuple(jnp.full((tile, 1), -1e30, jnp.float32) for _ in range(pack)),
                tuple(jnp.zeros((tile, 1), jnp.float32) for _ in range(pack)),
            )
            carry = lax.fori_loop(0, i, step, carry)
            total, tops, sums = step(i, carry, diagonal=True)
            share = 1.0 / sums[0]
            for h in range(1, pack):
                share = jnp.where(masks[h], 1.0 / sums[h], share)
            out_ref[pl.ds(start, tile), base : base + LANES] = (total * share).astype(out_ref.dtype)
            for h in range(pack):
                logs = jnp.broadcast_to(tops[h] + jnp.log2(sums[h]), (tile, LANES))
                index = pair * pack + h
                log_ref[0, index : index + 1, pl.ds(start, tile)] = jnp.transpose(logs)[0:1]
            return 0

        lax.fori_loop(0, blocks, query_block, 0)


def attend(mixed, slots, counts, head_size):
    sequences = counts.shape[0]
    rows = sum(part.shape[0] for part in mixed)
    tile = rows // slots.size
    blocks = rows // tile
    lanes = mixed[0].shape[1] // 3
    length = rows // sequences
    heads = lanes // head_size
    pack = LANES // head_size
    return pl.pallas_call(
        functools.partial(attend_kernel, head_size, len(mixed)),
        grid_spec=pltpu.PrefetchScalarGridSpec(
            num_scalar_prefetch=2,
            grid=(sequences,),
            in_specs=[pl.BlockSpec(memory_space=pl.ANY)] * len(mixed),
            out_specs=[
                pl.BlockSpec((length, lanes), lambda s, *_: (s, 0)),
                pl.BlockSpec((1, heads, length), lambda s, *_: (s, 0, 0)),
            ],
            scratch_shapes=[
                pltpu.VMEM((blocks, tile, 3 * lanes), jnp.bfloat16),
                pltpu.VMEM((pack, length, LANES), jnp.bfloat16),
                pltpu.VMEM((pack, length, LANES), jnp.bfloat16),
                pltpu.SemaphoreType.DMA((blocks,)),
            ],
        ),
        out_shape=[
            jax.ShapeDtypeStruct((rows, lanes), jnp.bfloat16),
            jax.ShapeDtypeStruct((sequences, heads, length), jnp.float32),
        ],
        compiler_params=pltpu.CompilerParams(vmem_limit_bytes=VMEM_BYTES),
        cost_estimate=cost(1, 1),
    )(counts, slots, *mixed)


def attend_back_kernel(
    head_size,
    blocks_in,
    counts,
    slots,
    *refs,
):
    sources = refs[:blocks_in]
    grad_ref, out_ref, log_ref, own_ref, other_ref, mixed_ref = refs[blocks_in : blocks_in + 6]
    query_own, key_own, grad_own, delta, grad_query, grad_key, grad_value, back_ref, sems = refs[
        blocks_in + 6 :
    ]
    fetch(sources, mixed_ref, sems)
    length, lanes = out_ref.shape
    tile = mixed_ref.shape[1]
    pack = LANES // head_size
    scale = head_size ** (-0.5)
    sequence = pl.program_id(0)
    blocks = lax.div(counts[sequence] + (tile - 1), tile)
    masks = head_masks(head_size)
    for i in range(length // tile):
        back_ref[slots[sequence, i]] = jnp.zeros((tile, 3 * lanes), back_ref.dtype)
    key_row = lax.broadcasted_iota(jnp.int32, (tile, tile), 0)
    query_col = lax.broadcasted_iota(jnp.int32, (tile, tile), 1)
    for pair in range(lanes // LANES):
        base = pair * LANES
        for i in range(length // tile):
            span = slice(i * tile, (i + 1) * tile)
            slot = slots[sequence, i]
            queries = mixed_ref[slot, :, base : base + LANES]
            keys = mixed_ref[slot, :, lanes + base : lanes + base + LANES]
            grads = grad_ref[span, base : base + LANES]
            for h in range(pack):
                query_own[h, span] = jnp.where(masks[h], queries, jnp.zeros_like(queries))
                key_own[h, span] = jnp.where(masks[h], keys, jnp.zeros_like(keys))
                grad_own[h, span] = jnp.where(masks[h], grads, jnp.zeros_like(grads))
        grad_query[...] = jnp.zeros(grad_query.shape, jnp.float32)

        def deltas(i, _, base=base):
            start = pl.multiple_of(i * tile, tile)
            grads = grad_ref[pl.ds(start, tile), base : base + LANES].astype(jnp.float32)
            outs = out_ref[pl.ds(start, tile), base : base + LANES].astype(jnp.float32)
            products = jnp.transpose(grads * outs)
            for h in range(pack):
                delta[h : h + 1, pl.ds(start, tile)] = jnp.sum(
                    products[h * head_size : (h + 1) * head_size], axis=0, keepdims=True
                )
            return 0

        lax.fori_loop(0, blocks, deltas, 0)

        def key_block(j, _, pair=pair, base=base):
            first = pl.multiple_of(j * tile, tile)
            place = slots[sequence, j]
            keys = mixed_ref[place, :, lanes + base : lanes + base + LANES]
            values = mixed_ref[place, :, 2 * lanes + base : 2 * lanes + base + LANES]
            grad_key[...] = jnp.zeros(grad_key.shape, jnp.float32)
            grad_value[...] = jnp.zeros(grad_value.shape, jnp.float32)

            def step(i, diagonal=False):
                start = pl.multiple_of(i * tile, tile)
                add_query, add_key, add_value = [], [], []
                for h in range(pack):
                    index = pair * pack + h
                    query_head = query_own[h, pl.ds(start, tile)]
                    grad_head = grad_own[h, pl.ds(start, tile)]
                    scores = dot_nt(keys, query_head) * (scale * LOG2E)
                    probs = jnp.exp2(scores - log_ref[0, index : index + 1, pl.ds(start, tile)])
                    if diagonal:
                        probs = jnp.where(key_row <= query_col, probs, 0.0)
                    grad_probs = dot_nt(values, grad_head)
                    grad_scores = (
                        probs * (grad_probs - delta[h : h + 1, pl.ds(start, tile)])
                    ).astype(jnp.bfloat16)
                    add_value.append(dot_nn(probs.astype(jnp.bfloat16), grad_head))
                    add_key.append(dot_nn(grad_scores, query_head))
                    add_query.append(dot_tn(grad_scores, key_own[h, pl.ds(first, tile)]))
                grad_value[...] += functools.reduce(jnp.add, add_value)
                grad_key[...] += functools.reduce(jnp.add, add_key)
                grad_query[pl.ds(start, tile), :] += functools.reduce(jnp.add, add_query)

            def off_diagonal(i, _):
                step(i)
                return 0

            step(j, diagonal=True)
            lax.fori_loop(j + 1, blocks, off_diagonal, 0)
            back_ref[place, :, lanes + base : lanes + base + LANES] = (grad_key[...] * scale).astype(
                back_ref.dtype
            )
            back_ref[place, :, 2 * lanes + base : 2 * lanes + base + LANES] = grad_value[...].astype(
                back_ref.dtype
            )
            return 0

        lax.fori_loop(0, blocks, key_block, 0)
        for i in range(length // tile):
            back_ref[slots[sequence, i], :, base : base + LANES] = (
                grad_query[i * tile : (i + 1) * tile] * scale
            ).astype(back_ref.dtype)

    @pl.when(sequence == pl.num_programs(0) - 1)
    def _():
        half = back_ref.shape[0] // 2
        for k in range(half):
            own_ref[k * tile : (k + 1) * tile] = back_ref[k]
            other_ref[k * tile : (k + 1) * tile] = back_ref[half + k]


def attend_back(mixed, slots, grads, outs, logs, counts, head_size):
    sequences = counts.shape[0]
    rows, lanes = outs.shape
    length = rows // sequences
    heads = lanes // head_size
    pack = LANES // head_size
    tile = rows // slots.size
    blocks = rows // tile
    whole = pl.BlockSpec((rows // 2, 3 * lanes), lambda s, *_: (0, 0))
    return pl.pallas_call(
        functools.partial(attend_back_kernel, head_size, len(mixed)),
        grid_spec=pltpu.PrefetchScalarGridSpec(
            num_scalar_prefetch=2,
            grid=(sequences,),
            in_specs=[pl.BlockSpec(memory_space=pl.ANY)] * len(mixed)
            + [
                pl.BlockSpec((length, lanes), lambda s, *_: (s, 0)),
                pl.BlockSpec((length, lanes), lambda s, *_: (s, 0)),
                pl.BlockSpec((1, heads, length), lambda s, *_: (s, 0, 0)),
            ],
            out_specs=[whole, whole],
            scratch_shapes=[
                pltpu.VMEM((blocks, tile, 3 * lanes), jnp.bfloat16),
                pltpu.VMEM((pack, length, LANES), jnp.bfloat16),
                pltpu.VMEM((pack, length, LANES), jnp.bfloat16),
                pltpu.VMEM((pack, length, LANES), jnp.bfloat16),
                pltpu.VMEM((pack, length), jnp.float32),
                pltpu.VMEM((length, LANES), jnp.float32),
                pltpu.VMEM((tile, LANES), jnp.float32),
                pltpu.VMEM((tile, LANES), jnp.float32),
                pltpu.VMEM((blocks, tile, 3 * lanes), jnp.bfloat16),
                pltpu.SemaphoreType.DMA((blocks,)),
            ],
        ),
        out_shape=[jax.ShapeDtypeStruct((rows // 2, 3 * lanes), jnp.bfloat16)] * 2,
        compiler_params=pltpu.CompilerParams(vmem_limit_bytes=VMEM_BYTES),
        cost_estimate=cost(1, 1),
    )(counts, slots, *mixed, grads, outs, logs)


def ffn_kernel(block, x_parts, g_parts, counts, *refs):
    xs, refs = refs[:x_parts], refs[x_parts:]
    gs, refs = refs[:g_parts], refs[g_parts:]
    ups, downs, shifts = refs[0:2], refs[2:4], refs[4:6]
    units_ref, back_ref, out_ref, x, g, total, x_sems, g_sems = refs[-8:]
    fetch(xs, x, x_sems)
    fetch(gs, g, g_sems)
    blocks, size, model = x.shape
    width = ups[0].shape[0]
    step = pl.program_id(0)

    @pl.when(step == 0)
    def _():
        total[...] = jnp.zeros(total.shape, total.dtype)

    for k in range(blocks):
        rows = slice(k * size, (k + 1) * size)

        @pl.when(counts[block + k] != 0)
        def _(k=k, rows=rows):
            backs = []
            for side in range(2):
                span = slice(side * width, (side + 1) * width)
                pre = dot_nt(x[k], ups[side][...]) + shifts[side][...]
                grad_units = dot_nt(g[k], downs[side][...])
                size_of = jnp.abs(pre)
                bell = jnp.exp2(pre * pre * (-0.5 * LOG2E))
                denominator = 1.0 + (0.3275911 * 0.7071067811865476) * size_of
                t = pl.reciprocal(denominator, approx=True)
                t = t * (2.0 - denominator * t)
                tail = 0.5 * 1.061405429
                for factor in (-1.453152027, 1.421413741, -0.284496736, 0.254829592):
                    tail = tail * t + 0.5 * factor
                tail = tail * t
                units = jnp.maximum(pre, 0.0) - size_of * (tail * bell)
                units_ref[rows, span] = units.astype(units_ref.dtype)
                slope = (tail - size_of * 0.3989422804014327) * bell
                slope = jnp.where(pre < 0, slope, 1.0 - slope)
                backs.append((grad_units * slope).astype(back_ref.dtype))
                back_ref[rows, span] = backs[-1]
            total[rows] += dot_nn(backs[0], ups[0][...]) + dot_nn(backs[1], ups[1][...])

        @pl.when(counts[block + k] == 0)
        def _(rows=rows):
            units_ref[rows] = jnp.zeros((size, 2 * width), units_ref.dtype)
            back_ref[rows] = jnp.zeros((size, 2 * width), back_ref.dtype)

    @pl.when(step == pl.num_programs(0) - 1)
    def _():
        out_ref[...] = total[...].astype(out_ref.dtype)


def ffn_blocks(place, block, counts, xs, gs, ups, downs, shifts, kept):
    size, width = 512, 256
    model = xs[0].shape[1]
    rows = sum(x.shape[0] for x in xs)
    units = ups[0].shape[0]
    whole = pl.BlockSpec(memory_space=pl.ANY)
    weights = pl.BlockSpec((width, model), lambda u, *_: (u, 0))
    shift = pl.BlockSpec((1, width), lambda u, *_: (0, u))
    output = pl.BlockSpec((rows, 2 * width), lambda u, *_: (place, u))
    full = jax.ShapeDtypeStruct((4 * size, 2 * units), jnp.bfloat16)
    return pl.pallas_call(
        functools.partial(ffn_kernel, block, len(xs), len(gs)),
        grid_spec=pltpu.PrefetchScalarGridSpec(
            num_scalar_prefetch=1,
            grid=(units // width,),
            in_specs=[whole] * (len(xs) + len(gs))
            + [weights] * 4
            + [shift] * 2
            + [whole] * len(kept),
            out_specs=[output, output, pl.BlockSpec((rows, model), lambda u, *_: (0, 0))],
            scratch_shapes=[
                pltpu.VMEM((rows // size, size, model), jnp.bfloat16),
                pltpu.VMEM((rows // size, size, model), jnp.bfloat16),
                pltpu.VMEM((rows, model), jnp.float32),
                pltpu.SemaphoreType.DMA((len(xs),)),
                pltpu.SemaphoreType.DMA((len(gs),)),
            ],
        ),
        out_shape=[full, full, jax.ShapeDtypeStruct((rows, model), jnp.bfloat16)],
        input_output_aliases={len(xs) + len(gs) + 7 + k: k for k in range(len(kept))},
        compiler_params=pltpu.CompilerParams(vmem_limit_bytes=VMEM_BYTES),
        cost_estimate=cost(1, 1),
    )(counts, *xs, *gs, *ups, *downs, *shifts, *kept)


def arrange(outs, total):
    to_x, to_y, rest = outs
    half = total.shape[0] // 2
    top, bottom = total[:half].astype(to_x.dtype), total[half:].astype(to_x.dtype)
    step = pl.program_id(0)

    @pl.when(step == 0)
    def _():
        to_x[:half] = top
        to_y[:half] = bottom

    @pl.when(step == 1)
    def _():
        to_x[half:] = top
        rest[half : 2 * half] = bottom

    @pl.when(step == 2)
    def _():
        rest[:half] = top
        to_y[half:] = bottom

    @pl.when(step == 3)
    def _():
        rest[2 * half : 3 * half] = top
        rest[3 * half :] = bottom


def arranged(rows, columns):
    sizes = (rows // 4, rows // 4, rows // 2)
    specs = [pl.BlockSpec((size, columns), lambda i, *_: (0, 0)) for size in sizes]
    return specs, [jax.ShapeDtypeStruct((size, columns), jnp.bfloat16) for size in sizes]


def products_kernel(width, order, active, left, own, other, *outs):
    here = active[order[pl.program_id(0)]] != 0

    @pl.when(here)
    def _():
        total = None
        for k in range(own.shape[0] // width):
            rows = slice(k * width, (k + 1) * width)
            for side, right in enumerate((own, other)):
                start = (2 * k + side) * width
                term = dot_nn(left[:, start : start + width], right[rows])
                total = term if total is None else total + term
        arrange(outs, total)

    @pl.when(jnp.logical_not(here))
    def _():
        arrange(outs, jnp.zeros((left.shape[0], own.shape[1]), jnp.float32))


def products(order, counts, left, own, other):
    blocks = counts.shape[0]
    rows, depth = left.shape
    columns = own.shape[1]
    specs, shapes = arranged(rows, columns)
    return pl.pallas_call(
        functools.partial(products_kernel, 256),
        grid_spec=pltpu.PrefetchScalarGridSpec(
            num_scalar_prefetch=2,
            grid=(blocks,),
            in_specs=[
                pl.BlockSpec((rows // blocks, depth), lambda i, order, *_: (order[i], 0)),
                pl.BlockSpec(own.shape, lambda i, *_: (0, 0)),
                pl.BlockSpec(own.shape, lambda i, *_: (0, 0)),
            ],
            out_specs=specs,
        ),
        out_shape=shapes,
        compiler_params=pltpu.CompilerParams(vmem_limit_bytes=VMEM_BYTES),
        cost_estimate=cost(1, 1),
    )(order, counts, left, own, other)


def attend_out_kernel(left, weight, bias, hidden, active, out_ref):
    out_ref[...] = hidden[...].astype(jnp.float32) + active[...] * (
        dot_nn(left[...], weight[...]) + bias[...]
    )


def attend_out(left, weight, bias, hidden, active):
    rows, depth = left.shape
    columns = weight.shape[1]
    width = 512
    column = pl.BlockSpec((rows, width), lambda j: (0, j))
    return pl.pallas_call(
        attend_out_kernel,
        grid=(columns // width,),
        in_specs=[
            pl.BlockSpec((rows, depth), lambda j: (0, 0)),
            pl.BlockSpec((depth, width), lambda j: (0, j)),
            pl.BlockSpec((1, width), lambda j: (0, j)),
            column,
            pl.BlockSpec((rows, 1), lambda j: (0, 0)),
        ],
        out_specs=column,
        out_shape=jax.ShapeDtypeStruct((rows, columns), jnp.float32),
        compiler_params=pltpu.CompilerParams(vmem_limit_bytes=VMEM_BYTES),
        cost_estimate=cost(1, 1),
    )(left, weight, bias[None], hidden, active)


def attend_out_back_kernel(grad, weight, out_ref):
    out_ref[...] = dot_nt(grad[...], weight[...]).astype(out_ref.dtype)


def attend_out_back(grad, weight):
    rows, columns = grad.shape
    depth = weight.shape[0]
    width = 512
    return pl.pallas_call(
        attend_out_back_kernel,
        grid=(depth // width,),
        in_specs=[
            pl.BlockSpec((rows, columns), lambda j: (0, 0)),
            pl.BlockSpec((width, columns), lambda j: (j, 0)),
        ],
        out_specs=pl.BlockSpec((rows, width), lambda j: (0, j)),
        out_shape=jax.ShapeDtypeStruct((rows, depth), jnp.bfloat16),
        compiler_params=pltpu.CompilerParams(vmem_limit_bytes=VMEM_BYTES),
        cost_estimate=cost(1, 1),
    )(grad, weight)


def project_kernel(inputs, side, parts, *refs):
    xs = refs[:inputs]
    weights, shift, out_ref = refs[inputs:]
    slab = weights.shape[1]
    weight = weights[...].reshape(3 * slab, weights.shape[2])
    for k in range(inputs):

        @pl.when(pl.program_id(0) == k)
        def _(k=k):
            mixed = dot_nt(xs[k][...], weight)
            for t in range(3):
                columns = pl.ds(pl.multiple_of(parts[side, t] * slab, slab), slab)
                out_ref[:, columns] = (
                    mixed[:, t * slab : (t + 1) * slab] + shift[:, columns]
                ).astype(out_ref.dtype)


def project(parts, side, xs, weights, shift):
    size, model = xs[0].shape
    slab = weights.shape[1]
    return pl.pallas_call(
        functools.partial(project_kernel, len(xs), side),
        grid_spec=pltpu.PrefetchScalarGridSpec(
            num_scalar_prefetch=1,
            grid=(len(xs),),
            in_specs=[pl.BlockSpec((size, model), lambda i, *_: (0, 0))] * len(xs)
            + [
                pl.BlockSpec(weights.shape, lambda i, *_: (0, 0, 0)),
                pl.BlockSpec(shift.shape, lambda i, *_: (0, 0)),
            ],
            out_specs=pl.BlockSpec((size, 3 * slab), lambda i, *_: (i, 0)),
        ),
        out_shape=jax.ShapeDtypeStruct((len(xs) * size, 3 * slab), jnp.bfloat16),
        compiler_params=pltpu.CompilerParams(vmem_limit_bytes=VMEM_BYTES),
        cost_estimate=cost(1, 1),
    )(parts, *xs, weights, shift)


def unproject_kernel(order, parts, active, mine, theirs, own, other, *outs):
    slab = own.shape[1]
    here = active[order[pl.program_id(0)]] != 0

    @pl.when(here)
    def _():
        total = None
        for side, (left, right) in enumerate(((mine, own), (theirs, other))):
            for t in range(3):
                columns = pl.ds(pl.multiple_of(parts[side, t] * slab, slab), slab)
                term = dot_nn(left[:, columns], right[t])
                total = term if total is None else total + term
        arrange(outs, total)

    @pl.when(jnp.logical_not(here))
    def _():
        arrange(outs, jnp.zeros((mine.shape[0], own.shape[2]), jnp.float32))


def unproject(order, parts, counts, mine, theirs, own, other):
    blocks = counts.shape[0]
    rows = mine.shape[0]
    slab, model = own.shape[1:]
    left = pl.BlockSpec((rows // blocks, 3 * slab), lambda i, order, *_: (order[i], 0))
    fixed = pl.BlockSpec(own.shape, lambda i, *_: (0, 0, 0))
    specs, shapes = arranged(rows, model)
    return pl.pallas_call(
        unproject_kernel,
        grid_spec=pltpu.PrefetchScalarGridSpec(
            num_scalar_prefetch=3,
            grid=(blocks,),
            in_specs=[left, left, fixed, fixed],
            out_specs=specs,
        ),
        out_shape=shapes,
        compiler_params=pltpu.CompilerParams(vmem_limit_bytes=VMEM_BYTES),
        cost_estimate=cost(1, 1),
    )(order, parts, counts, mine, theirs, own, other)


def weight_grad_kernel(inputs, added, columns, *refs):
    left, rights = refs[0], refs[1 : 1 + inputs]
    tokens, sems = refs[-2:]
    outs = refs[1 + inputs + added : -2]
    fetch(rights, tokens, sems)
    total = dot_tn(left[...], tokens[0])
    if added:
        total = total + refs[1 + inputs][...].astype(jnp.float32)
    size = outs[0].shape[0]
    if size == total.shape[0]:
        for k, out_ref in enumerate(outs):

            @pl.when((len(outs) == 1) | (pl.program_id(0) == k))
            def _(out_ref=out_ref):
                out_ref[...] = total.astype(out_ref.dtype)

    else:
        for k, out_ref in enumerate(outs):
            out_ref[...] = total[k * size : (k + 1) * size].astype(out_ref.dtype)


def weight_grad(left, columns, tile, rights, extra=None, outputs=1, apart=False, counted=False):
    rows = left.shape[0]
    model = rights[0].shape[1]
    steps = columns.shape[0]
    output = pl.BlockSpec((tile // outputs, model), lambda i, *_: (i, 0))
    extras = [] if extra is None else [extra]
    shape = jax.ShapeDtypeStruct((steps * tile // outputs, model), jnp.bfloat16)
    added = [output] * len(extras)
    if apart:
        outputs = steps
        output = pl.BlockSpec((tile, model), lambda i, *_: (0, 0))
        shape = jax.ShapeDtypeStruct((tile, model), jnp.bfloat16)
    results = pl.pallas_call(
        functools.partial(weight_grad_kernel, len(rights), len(extras)),
        grid_spec=pltpu.PrefetchScalarGridSpec(
            num_scalar_prefetch=1,
            grid=(steps,),
            in_specs=[pl.BlockSpec((rows, tile), lambda i, columns: (0, columns[i]))]
            + [pl.BlockSpec(memory_space=pl.ANY)] * len(rights)
            + added,
            out_specs=[output] * outputs,
            scratch_shapes=[
                pltpu.VMEM((1, rows, model), jnp.bfloat16),
                pltpu.SemaphoreType.DMA((len(rights),)),
            ],
        ),
        out_shape=[shape] * outputs,
        compiler_params=pltpu.CompilerParams(vmem_limit_bytes=VMEM_BYTES),
        cost_estimate=cost(2 * steps * tile * rows * model, 4 * rows * model) if counted else cost(1, 1),
    )(columns, left, *rights, *extras)
    return results[0] if outputs == 1 else results


def chain_sum(values, axis):
    size = lax.axis_size(axis)
    if size != 4:
        return lax.psum(values.astype(jnp.bfloat16), axis).astype(jnp.float32)
    place = lax.axis_index(axis)
    outer = lax.ppermute(values.astype(jnp.bfloat16), axis, [(0, 1), (3, 2)])
    half = (values + outer.astype(jnp.float32)).astype(jnp.bfloat16)
    other = lax.ppermute(half, axis, [(1, 2), (2, 1)])
    whole = (half.astype(jnp.float32) + other.astype(jnp.float32)).astype(jnp.bfloat16)
    ends = lax.ppermute(whole, axis, [(1, 0), (2, 3)])
    inner = (place == 1) | (place == 2)
    return jnp.where(inner, whole, ends).astype(jnp.float32)


def normalize(values):
    center = values - jnp.mean(values, axis=-1, keepdims=True)
    inverse = lax.rsqrt(jnp.mean(center * center, axis=-1, keepdims=True) + epsilon)
    return center * inverse, inverse


def normalize_back(grad, gain, normal, inverse):
    scaled = grad * gain
    grad_values = inverse * (
        scaled
        - jnp.mean(scaled, axis=-1, keepdims=True)
        - normal * jnp.mean(scaled * normal, axis=-1, keepdims=True)
    )
    return grad_values, jnp.sum(grad * normal, axis=0), jnp.sum(grad, axis=0)


def local_general(
    hidden,
    cotangent,
    exit_layer,
    ln1_gain,
    ln1_bias,
    qkv_weight,
    query_bias,
    value_bias,
    out_weight,
    out_bias,
    ln2_gain,
    ln2_bias,
    up_weight,
    up_bias,
    down_weight,
    down_bias,
):
    width = lax.axis_size("wide")
    rank = lax.axis_index("wide")
    rows, model = hidden.shape
    group = rows * width
    slab = model // width
    head_size = model // HEADS
    units_own = up_weight.shape[0]
    keep = exit_layer >= LAYER
    counts = jnp.sum(keep.astype(jnp.int32), axis=1)
    active = lax.dynamic_slice_in_dim(keep.reshape(group), rank * rows, rows, 0)
    active = active.astype(jnp.float32)[:, None]
    grad_out = cotangent.astype(jnp.float32)

    routes = [[(w, (3 * w + t) % width) for w in range(width)] for t in range(3)]
    part_at = np.zeros((width, 3), np.int32)
    for t in range(3):
        for w, d in routes[t]:
            part_at[d, t] = (3 * w + t) // width
    place_of = jnp.asarray(np.argsort(part_at, axis=1).astype(np.int32))[rank]
    part_of = jnp.asarray(part_at)[rank]

    hidden_wide = hidden.astype(jnp.float32)
    normal1, inverse1 = normalize(hidden_wide)
    normed1 = lax.all_gather(
        (normal1 * ln1_gain + ln1_bias).astype(jnp.bfloat16), "wide", axis=0, tiled=True
    )
    slabs = qkv_weight.reshape(3, slab, model)
    received = jnp.stack([lax.ppermute(slabs[t], "wide", routes[t]) for t in range(3)])
    qkv_own = jnp.concatenate(
        [lax.dynamic_index_in_dim(received, place_of[p], 0, keepdims=False) for p in range(3)]
    )
    own = lambda vector: lax.dynamic_slice_in_dim(vector, rank * slab, slab, 0)
    qkv_shift = jnp.concatenate(
        [own(query_bias), jnp.zeros((slab,), jnp.float32), own(value_bias)]
    )

    grad_ffn = (active * grad_out).astype(jnp.bfloat16)
    down_bias_grad = jnp.sum(grad_ffn.astype(jnp.float32), axis=0)
    piece = rows // CHUNKS
    part = lambda values, c: values[c * piece : (c + 1) * piece]
    gather = lambda values: lax.all_gather(values, "wide", axis=0, tiled=True)
    scatter = lambda values: lax.psum_scatter(
        values.astype(jnp.bfloat16), "wide", scatter_dimension=0, tiled=True
    )
    grad_ffns = [gather(part(grad_ffn, c)) for c in range(CHUNKS)]
    out_whole = gather(out_weight)

    mixed = (dot_nt(normed1, qkv_own) + qkv_shift).astype(jnp.bfloat16)
    mixed = jnp.split(mixed, group // TILE)
    slots = jnp.arange(group // TILE, dtype=jnp.int32).reshape(counts.shape[0], -1)
    attended, logs = attend(mixed, slots, counts, head_size)
    attended_rows = lax.all_to_all(attended, "wide", split_axis=0, concat_axis=1, tiled=True)
    middle = hidden_wide + active * (dot_nn(attended_rows, out_whole) + out_bias)
    normal2, inverse2 = normalize(middle)
    normed2 = (normal2 * ln2_gain + ln2_bias).astype(jnp.bfloat16)
    up_shift = lax.dynamic_slice_in_dim(up_bias, rank * units_own, units_own, 0)

    normed2s = [gather(part(normed2, c)) for c in range(CHUNKS)]
    units, grad_pres, grad_normed2, ffn_out = [], [], [], []
    for c in range(CHUNKS):
        grad_units = dot_nt(grad_ffns[c], down_weight)
        pre = dot_nt(normed2s[c], up_weight) + up_shift
        below = 0.5 + 0.5 * lax.erf(pre * 0.7071067811865476)
        bell = jnp.exp(-0.5 * pre * pre) * 0.3989422804014327
        units.append((pre * below).astype(jnp.bfloat16))
        grad_pres.append((grad_units * (below + pre * bell)).astype(jnp.bfloat16))
        grad_normed2.append(scatter(dot_nn(grad_pres[c], up_weight)))
    for c in range(CHUNKS):
        ffn_out.append(scatter(dot_nn(units[c], down_weight)))
    grad_normed2 = jnp.concatenate(grad_normed2).astype(jnp.float32)
    ffn_out = jnp.concatenate(ffn_out).astype(jnp.float32)
    output = (middle + active * (ffn_out + down_bias)).astype(jnp.bfloat16)

    up_bias_own = sum(jnp.sum(g.astype(jnp.float32), axis=0) for g in grad_pres)
    down_grad = sum(dot_tn(units[c], grad_ffns[c]) for c in range(CHUNKS))
    up_grad = sum(dot_tn(grad_pres[c], normed2s[c]) for c in range(CHUNKS))
    halves = lambda values: jnp.concatenate(
        [chain_sum(half, "batch") for half in jnp.split(values, 2)]
    )
    down_grad = halves(down_grad)
    up_grad = halves(up_grad)

    grad_middle, ln2_gain_grad, ln2_bias_grad = normalize_back(
        grad_normed2, ln2_gain, normal2, inverse2
    )
    grad_middle = grad_out + grad_middle
    grad_branch = (active * grad_middle).astype(jnp.bfloat16)
    out_bias_grad = jnp.sum(grad_branch.astype(jnp.float32), axis=0)
    grad_attended = dot_nt(grad_branch, out_whole).astype(jnp.bfloat16)
    grad_heads = lax.all_to_all(grad_attended, "wide", split_axis=1, concat_axis=0, tiled=True)
    out_grad = chain_sum(scatter(dot_tn(attended_rows, grad_branch)).astype(jnp.float32), "batch")

    placed = lambda vector, size: lax.dynamic_update_slice_in_dim(
        jnp.zeros((size,), jnp.float32), vector, rank * vector.shape[0], 0
    )
    early = lax.psum(
        (
            out_bias_grad,
            ln2_gain_grad,
            ln2_bias_grad,
            placed(up_bias_own, up_bias.shape[0]),
            down_bias_grad,
        ),
        ("batch", "wide"),
    )

    grad_mixed = jnp.concatenate(
        attend_back(mixed, slots, grad_heads, attended, logs, counts, head_size)
    )
    grad_normed1 = scatter(dot_nn(grad_mixed, qkv_own)).astype(jnp.float32)
    sums = jnp.sum(grad_mixed.astype(jnp.float32), axis=0)
    qkv_parts = []
    for t in range(3):
        columns = lax.dynamic_slice_in_dim(grad_mixed, part_of[t] * slab, slab, 1)
        total = chain_sum(dot_tn(columns, normed1), "batch").astype(jnp.bfloat16)
        back = [(d, w) for w, d in routes[t]]
        qkv_parts.append(lax.ppermute(total, "wide", back).astype(jnp.float32))
    qkv_grad = jnp.concatenate(qkv_parts)

    grad_hidden, ln1_gain_grad, ln1_bias_grad = normalize_back(
        grad_normed1, ln1_gain, normal1, inverse1
    )
    input_grad = grad_middle + grad_hidden
    late = lax.psum(
        (
            ln1_gain_grad,
            ln1_bias_grad,
            placed(sums[:slab], model),
            placed(sums[2 * slab :], model),
        ),
        ("batch", "wide"),
    )
    return (
        output,
        input_grad,
        late[0],
        late[1],
        qkv_grad,
        late[2],
        late[3],
        out_grad,
        early[0],
        early[1],
        early[2],
        up_grad,
        early[3],
        down_grad,
        early[4],
    )


def swap(values, bits):
    width = lax.axis_size("wide")
    return lax.ppermute(values, "wide", [(w, w ^ bits) for w in range(width)])


def after(values, *done):
    return lax.optimization_barrier((values, done))[0]


def relay(along_x, along_y):
    half = along_x.shape[0] // 2
    return [swap(along_y[:half], 2), swap(along_x[half:], 4)]


class Scatter:
    def __init__(self, to_x, to_y, rest):
        self.half = half = to_x.shape[0] // 2
        self.sent = (to_x, to_y)
        self.rest = rest
        self.from_x, self.from_y = swap(to_x, 2), swap(to_y, 4)

    def second(self, *done):
        half = self.half
        from_x, from_y = after((self.from_x, self.from_y), *done)
        self.near = (from_x[half:], from_y[half:])
        self.own = self.rest[2 * half :]
        return self.forward(self.rest[:half], self.rest[half : 2 * half], from_x[:half], from_y[:half])

    def forward(self, along_y, along_x, top, bottom):
        wide = lambda values: values.astype(jnp.float32)
        y_top = (wide(along_y) + wide(top)).astype(jnp.bfloat16)
        x_bottom = (wide(along_x) + wide(bottom)).astype(jnp.bfloat16)
        self.last = (swap(y_top, 4), swap(x_bottom, 2))
        return y_top, x_bottom

    def finish(self, *done):
        wide = lambda values: values.astype(jnp.float32)
        y_top, x_bottom = after(self.last, *done)
        x_top, y_bottom = self.near
        return jnp.concatenate(
            [
                wide(self.own[: self.half]) + wide(x_top) + wide(y_top),
                wide(self.own[self.half :]) + wide(x_bottom) + wide(y_bottom),
            ]
        )


def split_for_scatter(own, along_x, along_y, diagonal):
    half = own.shape[0] // 2
    return (
        jnp.concatenate([diagonal[:half], along_x[:half]]),
        jnp.concatenate([diagonal[half:], along_y[half:]]),
        jnp.concatenate([along_y[:half], along_x[half:], own]),
    )


class EarlyScatter(Scatter):
    def __init__(self, own, along_x, along_y):
        self.half = half = own.shape[0] // 2
        self.own, self.along_x, self.along_y = own, along_x, along_y
        self.near = (swap(along_x[:half], 2), swap(along_y[half:], 4))

    def first(self, diagonal):
        self.from_far = (swap(diagonal[: self.half], 2), swap(diagonal[self.half :], 4))
        self.near = after(self.near, diagonal)
        return self.near

    def second(self, *done):
        half = self.half
        far = after(self.from_far, *done)
        return self.forward(self.along_y[:half], self.along_x[half:], *far)


def tree_sum(values):
    total = values + swap(values, 1)
    total = (total + swap(total, 2)) + (swap(total, 4) + swap(total, 6))
    size = lax.axis_size("batch")
    terms = [total] + [
        lax.ppermute(total, "batch", [(z, z ^ bits) for z in range(size)])
        for bits in range(1, size)
    ]
    while len(terms) > 1:
        terms = [terms[k] + terms[k + 1] for k in range(0, len(terms), 2)]
    return terms[0]


def local_chips(
    hidden,
    cotangent,
    exit_layer,
    ln1_gain,
    ln1_bias,
    qkv_weight,
    query_bias,
    value_bias,
    out_weight,
    out_bias,
    ln2_gain,
    ln2_bias,
    up_weight,
    up_bias,
    down_weight,
    down_bias,
):
    width = lax.axis_size("wide")
    rank = lax.axis_index("wide")
    rows, model = hidden.shape
    group = rows * width
    slab = model // width
    head_size = model // HEADS
    units_own = up_weight.shape[0]
    keep = exit_layer >= LAYER
    counts = jnp.sum(keep.astype(jnp.int32), axis=1)
    active = lax.dynamic_slice_in_dim(keep.reshape(group), rank * rows, rows, 0)
    active = active.astype(jnp.float32)[:, None]
    grad_out = cotangent.astype(jnp.float32)

    tiles = jnp.arange(group // rows, dtype=jnp.int32)
    slots = ((tiles ^ rank) & 1) * 4 + ((tiles >> 1) ^ (rank >> 1))
    slots = slots.reshape(counts.shape[0], -1)

    routes = [[(w, (3 * w + t) % width) for w in range(width)] for t in range(3)]
    part_at = np.zeros((width, 3), np.int32)
    for t in range(3):
        for w, d in routes[t]:
            part_at[d, t] = (3 * w + t) // width
    part_at = jnp.asarray(part_at)
    other = rank ^ 1
    parts = jnp.stack([part_at[rank], part_at[other]])

    hidden_wide = hidden.astype(jnp.float32)
    normal1, inverse1 = normalize(hidden_wide)
    slabs = qkv_weight.reshape(3, slab, model)
    slabs = [lax.ppermute(slabs[t], "wide", routes[t]) for t in range(3)]
    normed1 = (normal1 * ln1_gain + ln1_bias).astype(jnp.bfloat16)
    normed1 = [normed1, swap(normed1, 2), swap(normed1, 4)]
    diagonal1 = relay(normed1[1], normed1[2])
    qkv_own = jnp.stack(after(slabs, normed1[1:]))
    qkv_other = swap(qkv_own, 1)

    def shift_of(device):
        own = lambda vector: lax.dynamic_slice_in_dim(vector, device * slab, slab, 0)
        shift = [own(query_bias), jnp.zeros((slab,), jnp.float32), own(value_bias)]
        return jnp.concatenate(shift)[None]

    bias_of = lambda device: lax.dynamic_slice_in_dim(up_bias, device * units_own, units_own, 0)
    up_shifts = [bias_of(rank)[None], bias_of(other)[None]]

    mixed_near = project(parts, 0, normed1, qkv_own, shift_of(rank))
    qkv_other = after(qkv_other, mixed_near)
    lent_near = project(parts, 1, normed1, qkv_other, shift_of(other))
    diagonal1 = after(diagonal1, lent_near)
    lent_far = project(parts, 1, diagonal1, qkv_other, shift_of(other))
    mixed_far = project(parts, 0, after(diagonal1, lent_far), qkv_own, shift_of(rank))
    mixed = [mixed_near, mixed_far, swap(lent_near, 1), swap(lent_far, 1)]

    out_whole = lax.all_gather(after(out_weight, diagonal1), "wide", axis=0, tiled=True)
    grad_ffn = (after(active, diagonal1) * grad_out).astype(jnp.bfloat16)
    down_bias_grad = jnp.sum(grad_ffn.astype(jnp.float32), axis=0)
    grad_ffn = [grad_ffn, swap(grad_ffn, 2), swap(grad_ffn, 4)]

    attended, logs = attend(mixed, slots, counts, head_size)
    attended_rows = lax.all_to_all(attended, "wide", split_axis=0, concat_axis=1, tiled=True)
    attended_rows = after(attended_rows, grad_ffn[1:])
    up_other, down_other = swap(after((up_weight, down_weight), attended), 1)
    middle = attend_out(attended_rows, out_whole, out_bias, hidden, active)
    normal2, inverse2 = normalize(middle)
    normed2 = (normal2 * ln2_gain + ln2_bias).astype(jnp.bfloat16)
    normed2 = [normed2, swap(normed2, 2), swap(normed2, 4)]

    per_tile = jnp.sum(keep.reshape(group // rows, rows).astype(jnp.int32), axis=1)
    block_chip = (rank >> 1) ^ jnp.arange(4, dtype=jnp.int32)
    block_counts = per_tile[2 * block_chip + (rank & 1)]
    ups, downs = [up_weight, up_other], [down_weight, down_other]

    def ffn(place, block, xs, gs, kept):
        *kept, partial = ffn_blocks(
            place, block, block_counts, xs, gs, ups, downs, up_shifts, tuple(kept)
        )
        return kept, partial

    kept, partial_own = ffn(2, 0, normed2[:1], grad_ffn[:1], ())
    normed2[1:] = after(normed2[1:], partial_own)
    diagonal2 = relay(normed2[1], normed2[2])
    diagonal_ffn = relay(*after(grad_ffn[1:], attended_rows))
    kept, partial_near = ffn(0, 1, normed2[1:], grad_ffn[1:], kept)
    scatter2 = EarlyScatter(partial_own, partial_near[:rows], partial_near[rows:])
    diagonal2 = after(diagonal2, partial_near)
    (units, grad_pres), partial_far = ffn(3, 3, diagonal2, diagonal_ffn, kept)
    wait = scatter2.first(partial_far)
    tokens2 = [*normed2[1:], normed2[0], *diagonal2]
    tokens_ffn = [*grad_ffn[1:], grad_ffn[0], *diagonal_ffn]

    wide = lambda values: values.astype(jnp.float32)
    lowered = lambda values: values.astype(jnp.bfloat16)
    tile = 512
    tiles = jnp.arange(2 * units_own // tile, dtype=jnp.int32)

    down_own, down_lent = weight_grad(after(units, wait), tiles, tile, tokens_ffn, outputs=2)
    wait = scatter2.second(down_lent)
    down_lent = swap(down_lent, 1)
    up_own, up_lent = weight_grad(
        after(grad_pres, wait), tiles, tile, tokens2, outputs=2, counted=True
    )

    up_lent = swap(up_lent, 1)
    down_sum = lowered(wide(down_own) + wide(after(down_lent, up_own)))
    up_sum = lowered(wide(up_own) + wide(up_lent))
    down_grad, up_grad = lax.psum((down_sum, up_sum), "batch")
    grad_middle, ln2_gain_grad, ln2_bias_grad = normalize_back(
        scatter2.finish(up_own), ln2_gain, normal2, inverse2
    )
    grad_middle = grad_out + grad_middle
    grad_branch = (active * grad_middle).astype(jnp.bfloat16)
    out_bias_grad = jnp.sum(grad_branch.astype(jnp.float32), axis=0)
    grad_branch = after(grad_branch, down_sum, up_sum)
    grad_attended = attend_out_back(grad_branch, out_whole)
    grad_heads = lax.all_to_all(grad_attended, "wide", split_axis=1, concat_axis=0, tiled=True)
    owners = 2 * block_chip + (rank & 1)
    grad_branch = after(grad_branch, grad_attended)
    out_lent = weight_grad(attended_rows, owners ^ 1, slab, [grad_branch])
    out_lent = swap(out_lent, 1)
    out_own = weight_grad(after(attended_rows, out_lent), owners, slab, [grad_branch], out_lent)

    back_own, back_other = attend_back(
        mixed, slots, after(grad_heads, out_own), attended, logs, counts, head_size
    )

    theirs = swap(back_other, 1)
    out_own = after(out_own, back_own)
    scatter_out = Scatter(*split_for_scatter(*jnp.split(out_own, 4)))
    order = jnp.array([3, 0, 1, 2], jnp.int32)
    ffn_counts = block_counts[jnp.array([1, 2, 0, 3])]
    ffn_parts = products(order, ffn_counts, after(units, scatter_out.sent), *downs)
    tokens1 = [*normed1, *diagonal1]
    theirs = after(theirs, ffn_parts[0])
    qkv_lent = weight_grad(theirs, parts[1], slab, tokens1)
    wait = scatter_out.second(qkv_lent)
    grad_parts = unproject(
        jnp.array([3, 1, 2, 0], jnp.int32),
        parts,
        block_counts,
        after(back_own, wait),
        theirs,
        qkv_own,
        qkv_other,
    )
    qkv_lent = swap(qkv_lent, 1)
    scatter1 = Scatter(*grad_parts)
    qkv_total = weight_grad(
        after(back_own, grad_parts[0]),
        parts[0],
        slab,
        tokens1,
        after(qkv_lent, grad_parts[0]),
        apart=True,
    )

    returned = [
        lax.ppermute(total, "wide", [(d, w) for w, d in route])
        for total, route in zip(qkv_total, routes)
    ]
    down_grad, up_grad = after((down_grad, up_grad), returned)
    out_total = lowered(scatter_out.finish(up_grad))
    *qkv_grad, out_grad = lax.psum(after((*returned, out_total), up_grad), "batch")
    wait = scatter1.second(out_total, up_grad)
    scatter_ffn = Scatter(*after(ffn_parts, wait))
    grad_normed1 = scatter1.finish(wait, scatter_ffn.sent)
    grad_hidden, ln1_gain_grad, ln1_bias_grad = normalize_back(
        grad_normed1, ln1_gain, normal1, inverse1
    )
    input_grad = grad_middle + grad_hidden
    grad_pres, back_own, back_other = after((grad_pres, back_own, back_other), wait)
    up_bias_own = jnp.sum(wide(grad_pres), axis=0).reshape(-1, 2, 256)
    up_bias_own = [up_bias_own[:, side].reshape(units_own) for side in range(2)]
    sums = jnp.sum(wide(back_own), axis=0) + jnp.sum(wide(back_other), axis=0)
    wait = scatter_ffn.second(input_grad)
    down_grad, up_grad = wide(after(down_grad, wait)), wide(after(up_grad, wait))
    ffn_out = scatter_ffn.finish(down_grad, up_grad)
    output = (middle + active * (ffn_out + down_bias)).astype(jnp.bfloat16)
    placed = lambda vector, size, device: lax.dynamic_update_slice_in_dim(
        jnp.zeros((size,), jnp.float32), vector, device * vector.shape[0], 0
    )
    smalls = tree_sum(
        jnp.concatenate(
            [
                placed(up_bias_own[0], up_bias.shape[0], rank)
                + placed(up_bias_own[1], up_bias.shape[0], other),
                down_bias_grad,
                out_bias_grad,
                ln2_gain_grad,
                ln2_bias_grad,
                placed(sums[:slab], model, rank),
                placed(sums[2 * slab :], model, rank),
                ln1_gain_grad,
                ln1_bias_grad,
            ]
        )
    )
    up_bias_grad = smalls[: up_bias.shape[0]]
    smalls = smalls[up_bias.shape[0] :].reshape(8, model)
    qkv_grad = wide(jnp.concatenate(qkv_grad))
    out_grad = wide(out_grad)
    return (
        output,
        input_grad,
        smalls[6],
        smalls[7],
        qkv_grad,
        smalls[4],
        smalls[5],
        out_grad,
        smalls[1],
        smalls[2],
        smalls[3],
        up_grad,
        up_bias_grad,
        down_grad,
        smalls[0],
    )


def solution(mesh):
    chips = mesh.shape["wide"] == 8 and mesh.shape["batch"] == 4
    local = local_chips if chips else local_general
    rows = P(("batch", "wide"), None)
    weight = P("wide", None)
    return jax.shard_map(
        local,
        mesh=mesh,
        in_specs=(
            rows,
            rows,
            P("batch", None),
            P(),
            P(),
            weight,
            P(),
            P(),
            weight,
            P(),
            P(),
            P(),
            weight,
            P(),
            weight,
            P(),
        ),
        out_specs=(
            rows,
            rows,
            P(),
            P(),
            weight,
            P(),
            P(),
            weight,
            P(),
            P(),
            P(),
            weight,
            P(),
            weight,
            P(),
        ),
        check_vma=False,
    )
```

```python
import functools

import jax
import jax.numpy as jnp
import numpy as np
from jax import lax
from jax.experimental import pallas as pl
from jax.experimental.pallas import tpu as pltpu
from jax.sharding import PartitionSpec as P

HEADS = 32
LAYER = 12
LANES = 128
TILE = 512
CHUNKS = 2
LOG2E = 1.4426950408889634

epsilon = 1e-05
VMEM_BYTES = 48 * 2**20


def cost(flops, size, exponentials=0):
    return pl.CostEstimate(flops=flops, bytes_accessed=size, transcendentals=exponentials)


def dot_nt(left, right):
    return lax.dot_general(
        left, right, (((1,), (1,)), ((), ())), preferred_element_type=jnp.float32
    )


def dot_nn(left, right):
    return lax.dot_general(
        left, right, (((1,), (0,)), ((), ())), preferred_element_type=jnp.float32
    )


def dot_tn(left, right):
    return lax.dot_general(
        left, right, (((0,), (0,)), ((), ())), preferred_element_type=jnp.float32
    )


def head_masks(head_size):
    lane = lax.broadcasted_iota(jnp.int32, (1, LANES), 1)
    return [
        (lane >= h * head_size) & (lane < (h + 1) * head_size)
        for h in range(LANES // head_size)
    ]


def fetch(sources, target, sems):
    size = target.shape[1]
    copies = []
    row = 0
    for source in sources:
        rows = source.shape[0]
        least = min(rows, size)
        for k in range(rows // least):
            place = target.at[row // size, pl.ds(row % size, least)]
            copies.append(
                pltpu.make_async_copy(source.at[pl.ds(k * least, least)], place, sems.at[len(copies)])
            )
            row += least

    @pl.when(pl.program_id(0) == 0)
    def _():
        for copy in copies:
            copy.start()
        for copy in copies:
            copy.wait()


def attend_kernel(head_size, blocks_in, counts, slots, *refs):
    sources = refs[:blocks_in]
    out_ref, log_ref, mixed_ref, key_own, value_own, sems = refs[blocks_in:]
    fetch(sources, mixed_ref, sems)
    length, lanes = out_ref.shape
    tile = mixed_ref.shape[1]
    pack = LANES // head_size
    scale = head_size ** (-0.5) * LOG2E
    sequence = pl.program_id(0)
    blocks = lax.div(counts[sequence] + (tile - 1), tile)
    masks = head_masks(head_size)
    out_ref[...] = jnp.zeros(out_ref.shape, out_ref.dtype)
    log_ref[...] = jnp.zeros(log_ref.shape, log_ref.dtype)
    row = lax.broadcasted_iota(jnp.int32, (tile, tile), 0)
    col = lax.broadcasted_iota(jnp.int32, (tile, tile), 1)
    for pair in range(lanes // LANES):
        base = pair * LANES
        for i in range(length // tile):
            slot = slots[sequence, i]
            keys = mixed_ref[slot, :, lanes + base : lanes + base + LANES]
            values = mixed_ref[slot, :, 2 * lanes + base : 2 * lanes + base + LANES]
            for h in range(pack):
                key_own[h, i * tile : (i + 1) * tile] = jnp.where(masks[h], keys, jnp.zeros_like(keys))
                value_own[h, i * tile : (i + 1) * tile] = jnp.where(
                    masks[h], values, jnp.zeros_like(values)
                )

        def query_block(i, _, pair=pair, base=base):
            start = pl.multiple_of(i * tile, tile)
            queries = mixed_ref[slots[sequence, i], :, base : base + LANES]

            def step(j, carry, diagonal=False):
                total, tops, sums = carry
                first = pl.multiple_of(j * tile, tile)
                new_tops, new_sums, shrinks, adds = [], [], [], []
                for h in range(pack):
                    scores = dot_nt(queries, key_own[h, pl.ds(first, tile)]) * scale
                    if diagonal:
                        scores = jnp.where(col <= row, scores, -1e30)
                    top = jnp.maximum(tops[h], jnp.max(scores, axis=1, keepdims=True))
                    terms = jnp.exp2(scores - top)
                    shrink = jnp.exp2(tops[h] - top)
                    new_tops.append(top)
                    new_sums.append(sums[h] * shrink + jnp.sum(terms, axis=1, keepdims=True))
                    shrinks.append(shrink)
                    adds.append(dot_nn(terms.astype(jnp.bfloat16), value_own[h, pl.ds(first, tile)]))
                shrink = shrinks[0]
                for h in range(1, pack):
                    shrink = jnp.where(masks[h], shrinks[h], shrink)
                total = total * shrink
                for add in adds:
                    total = total + add
                return total, tuple(new_tops), tuple(new_sums)

            carry = (
                jnp.zeros((tile, LANES), jnp.float32),
                tuple(jnp.full((tile, 1), -1e30, jnp.float32) for _ in range(pack)),
                tuple(jnp.zeros((tile, 1), jnp.float32) for _ in range(pack)),
            )
            carry = lax.fori_loop(0, i, step, carry)
            total, tops, sums = step(i, carry, diagonal=True)
            share = 1.0 / sums[0]
            for h in range(1, pack):
                share = jnp.where(masks[h], 1.0 / sums[h], share)
            out_ref[pl.ds(start, tile), base : base + LANES] = (total * share).astype(out_ref.dtype)
            for h in range(pack):
                logs = jnp.broadcast_to(tops[h] + jnp.log2(sums[h]), (tile, LANES))
                index = pair * pack + h
                log_ref[0, index : index + 1, pl.ds(start, tile)] = jnp.transpose(logs)[0:1]
            return 0

        lax.fori_loop(0, blocks, query_block, 0)


def attend(mixed, slots, counts, head_size):
    sequences = counts.shape[0]
    rows = sum(part.shape[0] for part in mixed)
    tile = rows // slots.size
    blocks = rows // tile
    lanes = mixed[0].shape[1] // 3
    length = rows // sequences
    heads = lanes // head_size
    pack = LANES // head_size
    return pl.pallas_call(
        functools.partial(attend_kernel, head_size, len(mixed)),
        grid_spec=pltpu.PrefetchScalarGridSpec(
            num_scalar_prefetch=2,
            grid=(sequences,),
            in_specs=[pl.BlockSpec(memory_space=pl.ANY)] * len(mixed),
            out_specs=[
                pl.BlockSpec((length, lanes), lambda s, *_: (s, 0)),
                pl.BlockSpec((1, heads, length), lambda s, *_: (s, 0, 0)),
            ],
            scratch_shapes=[
                pltpu.VMEM((blocks, tile, 3 * lanes), jnp.bfloat16),
                pltpu.VMEM((pack, length, LANES), jnp.bfloat16),
                pltpu.VMEM((pack, length, LANES), jnp.bfloat16),
                pltpu.SemaphoreType.DMA((blocks,)),
            ],
        ),
        out_shape=[
            jax.ShapeDtypeStruct((rows, lanes), jnp.bfloat16),
            jax.ShapeDtypeStruct((sequences, heads, length), jnp.float32),
        ],
        compiler_params=pltpu.CompilerParams(vmem_limit_bytes=VMEM_BYTES),
        cost_estimate=cost(1, 1),
    )(counts, slots, *mixed)


def attend_back_kernel(
    head_size,
    blocks_in,
    counts,
    slots,
    *refs,
):
    sources = refs[:blocks_in]
    grad_ref, out_ref, log_ref, own_ref, other_ref, mixed_ref = refs[blocks_in : blocks_in + 6]
    query_own, key_own, grad_own, delta, grad_query, grad_key, grad_value, back_ref, sems = refs[
        blocks_in + 6 :
    ]
    fetch(sources, mixed_ref, sems)
    length, lanes = out_ref.shape
    tile = mixed_ref.shape[1]
    pack = LANES // head_size
    scale = head_size ** (-0.5)
    sequence = pl.program_id(0)
    blocks = lax.div(counts[sequence] + (tile - 1), tile)
    masks = head_masks(head_size)
    for i in range(length // tile):
        back_ref[slots[sequence, i]] = jnp.zeros((tile, 3 * lanes), back_ref.dtype)
    key_row = lax.broadcasted_iota(jnp.int32, (tile, tile), 0)
    query_col = lax.broadcasted_iota(jnp.int32, (tile, tile), 1)
    for pair in range(lanes // LANES):
        base = pair * LANES
        for i in range(length // tile):
            span = slice(i * tile, (i + 1) * tile)
            slot = slots[sequence, i]
            queries = mixed_ref[slot, :, base : base + LANES]
            keys = mixed_ref[slot, :, lanes + base : lanes + base + LANES]
            grads = grad_ref[span, base : base + LANES]
            for h in range(pack):
                query_own[h, span] = jnp.where(masks[h], queries, jnp.zeros_like(queries))
                key_own[h, span] = jnp.where(masks[h], keys, jnp.zeros_like(keys))
                grad_own[h, span] = jnp.where(masks[h], grads, jnp.zeros_like(grads))
        grad_query[...] = jnp.zeros(grad_query.shape, jnp.float32)

        def deltas(i, _, base=base):
            start = pl.multiple_of(i * tile, tile)
            grads = grad_ref[pl.ds(start, tile), base : base + LANES].astype(jnp.float32)
            outs = out_ref[pl.ds(start, tile), base : base + LANES].astype(jnp.float32)
            products = jnp.transpose(grads * outs)
            for h in range(pack):
                delta[h : h + 1, pl.ds(start, tile)] = jnp.sum(
                    products[h * head_size : (h + 1) * head_size], axis=0, keepdims=True
                )
            return 0

        lax.fori_loop(0, blocks, deltas, 0)

        def key_block(j, _, pair=pair, base=base):
            first = pl.multiple_of(j * tile, tile)
            place = slots[sequence, j]
            keys = mixed_ref[place, :, lanes + base : lanes + base + LANES]
            values = mixed_ref[place, :, 2 * lanes + base : 2 * lanes + base + LANES]
            grad_key[...] = jnp.zeros(grad_key.shape, jnp.float32)
            grad_value[...] = jnp.zeros(grad_value.shape, jnp.float32)

            def step(i, diagonal=False):
                start = pl.multiple_of(i * tile, tile)
                add_query, add_key, add_value = [], [], []
                for h in range(pack):
                    index = pair * pack + h
                    query_head = query_own[h, pl.ds(start, tile)]
                    grad_head = grad_own[h, pl.ds(start, tile)]
                    scores = dot_nt(keys, query_head) * (scale * LOG2E)
                    probs = jnp.exp2(scores - log_ref[0, index : index + 1, pl.ds(start, tile)])
                    if diagonal:
                        probs = jnp.where(key_row <= query_col, probs, 0.0)
                    grad_probs = dot_nt(values, grad_head)
                    grad_scores = (
                        probs * (grad_probs - delta[h : h + 1, pl.ds(start, tile)])
                    ).astype(jnp.bfloat16)
                    add_value.append(dot_nn(probs.astype(jnp.bfloat16), grad_head))
                    add_key.append(dot_nn(grad_scores, query_head))
                    add_query.append(dot_tn(grad_scores, key_own[h, pl.ds(first, tile)]))
                grad_value[...] += functools.reduce(jnp.add, add_value)
                grad_key[...] += functools.reduce(jnp.add, add_key)
                grad_query[pl.ds(start, tile), :] += functools.reduce(jnp.add, add_query)

            def off_diagonal(i, _):
                step(i)
                return 0

            step(j, diagonal=True)
            lax.fori_loop(j + 1, blocks, off_diagonal, 0)
            back_ref[place, :, lanes + base : lanes + base + LANES] = (grad_key[...] * scale).astype(
                back_ref.dtype
            )
            back_ref[place, :, 2 * lanes + base : 2 * lanes + base + LANES] = grad_value[...].astype(
                back_ref.dtype
            )
            return 0

        lax.fori_loop(0, blocks, key_block, 0)
        for i in range(length // tile):
            back_ref[slots[sequence, i], :, base : base + LANES] = (
                grad_query[i * tile : (i + 1) * tile] * scale
            ).astype(back_ref.dtype)

    @pl.when(sequence == pl.num_programs(0) - 1)
    def _():
        half = back_ref.shape[0] // 2
        for k in range(half):
            own_ref[k * tile : (k + 1) * tile] = back_ref[k]
            other_ref[k * tile : (k + 1) * tile] = back_ref[half + k]


def attend_back(mixed, slots, grads, outs, logs, counts, head_size):
    sequences = counts.shape[0]
    rows, lanes = outs.shape
    length = rows // sequences
    heads = lanes // head_size
    pack = LANES // head_size
    tile = rows // slots.size
    blocks = rows // tile
    whole = pl.BlockSpec((rows // 2, 3 * lanes), lambda s, *_: (0, 0))
    return pl.pallas_call(
        functools.partial(attend_back_kernel, head_size, len(mixed)),
        grid_spec=pltpu.PrefetchScalarGridSpec(
            num_scalar_prefetch=2,
            grid=(sequences,),
            in_specs=[pl.BlockSpec(memory_space=pl.ANY)] * len(mixed)
            + [
                pl.BlockSpec((length, lanes), lambda s, *_: (s, 0)),
                pl.BlockSpec((length, lanes), lambda s, *_: (s, 0)),
                pl.BlockSpec((1, heads, length), lambda s, *_: (s, 0, 0)),
            ],
            out_specs=[whole, whole],
            scratch_shapes=[
                pltpu.VMEM((blocks, tile, 3 * lanes), jnp.bfloat16),
                pltpu.VMEM((pack, length, LANES), jnp.bfloat16),
                pltpu.VMEM((pack, length, LANES), jnp.bfloat16),
                pltpu.VMEM((pack, length, LANES), jnp.bfloat16),
                pltpu.VMEM((pack, length), jnp.float32),
                pltpu.VMEM((length, LANES), jnp.float32),
                pltpu.VMEM((tile, LANES), jnp.float32),
                pltpu.VMEM((tile, LANES), jnp.float32),
                pltpu.VMEM((blocks, tile, 3 * lanes), jnp.bfloat16),
                pltpu.SemaphoreType.DMA((blocks,)),
            ],
        ),
        out_shape=[jax.ShapeDtypeStruct((rows // 2, 3 * lanes), jnp.bfloat16)] * 2,
        compiler_params=pltpu.CompilerParams(vmem_limit_bytes=VMEM_BYTES),
        cost_estimate=cost(1, 1),
    )(counts, slots, *mixed, grads, outs, logs)


def ffn_kernel(block, x_parts, g_parts, counts, *refs):
    xs, refs = refs[:x_parts], refs[x_parts:]
    gs, refs = refs[:g_parts], refs[g_parts:]
    ups, downs, shifts = refs[0:2], refs[2:4], refs[4:6]
    units_ref, back_ref, out_ref, x, g, total, x_sems, g_sems = refs[-8:]
    fetch(xs, x, x_sems)
    fetch(gs, g, g_sems)
    blocks, size, model = x.shape
    width = ups[0].shape[0]
    step = pl.program_id(0)

    @pl.when(step == 0)
    def _():
        total[...] = jnp.zeros(total.shape, total.dtype)

    for k in range(blocks):
        rows = slice(k * size, (k + 1) * size)

        @pl.when(counts[block + k] != 0)
        def _(k=k, rows=rows):
            backs = []
            for side in range(2):
                span = slice(side * width, (side + 1) * width)
                pre = dot_nt(x[k], ups[side][...]) + shifts[side][...]
                grad_units = dot_nt(g[k], downs[side][...])
                size_of = jnp.abs(pre)
                bell = jnp.exp2(pre * pre * (-0.5 * LOG2E))
                denominator = 1.0 + (0.3275911 * 0.7071067811865476) * size_of
                t = pl.reciprocal(denominator, approx=True)
                t = t * (2.0 - denominator * t)
                tail = 0.5 * 1.061405429
                for factor in (-1.453152027, 1.421413741, -0.284496736, 0.254829592):
                    tail = tail * t + 0.5 * factor
                tail = tail * t
                units = jnp.maximum(pre, 0.0) - size_of * (tail * bell)
                units_ref[rows, span] = units.astype(units_ref.dtype)
                slope = (tail - size_of * 0.3989422804014327) * bell
                slope = jnp.where(pre < 0, slope, 1.0 - slope)
                backs.append((grad_units * slope).astype(back_ref.dtype))
                back_ref[rows, span] = backs[-1]
            total[rows] += dot_nn(backs[0], ups[0][...]) + dot_nn(backs[1], ups[1][...])

        @pl.when(counts[block + k] == 0)
        def _(rows=rows):
            units_ref[rows] = jnp.zeros((size, 2 * width), units_ref.dtype)
            back_ref[rows] = jnp.zeros((size, 2 * width), back_ref.dtype)

    @pl.when(step == pl.num_programs(0) - 1)
    def _():
        out_ref[...] = total[...].astype(out_ref.dtype)


def ffn_blocks(place, block, counts, xs, gs, ups, downs, shifts, kept):
    size, width = 512, 256
    model = xs[0].shape[1]
    rows = sum(x.shape[0] for x in xs)
    units = ups[0].shape[0]
    whole = pl.BlockSpec(memory_space=pl.ANY)
    weights = pl.BlockSpec((width, model), lambda u, *_: (u, 0))
    shift = pl.BlockSpec((1, width), lambda u, *_: (0, u))
    output = pl.BlockSpec((rows, 2 * width), lambda u, *_: (place, u))
    full = jax.ShapeDtypeStruct((4 * size, 2 * units), jnp.bfloat16)
    return pl.pallas_call(
        functools.partial(ffn_kernel, block, len(xs), len(gs)),
        grid_spec=pltpu.PrefetchScalarGridSpec(
            num_scalar_prefetch=1,
            grid=(units // width,),
            in_specs=[whole] * (len(xs) + len(gs))
            + [weights] * 4
            + [shift] * 2
            + [whole] * len(kept),
            out_specs=[output, output, pl.BlockSpec((rows, model), lambda u, *_: (0, 0))],
            scratch_shapes=[
                pltpu.VMEM((rows // size, size, model), jnp.bfloat16),
                pltpu.VMEM((rows // size, size, model), jnp.bfloat16),
                pltpu.VMEM((rows, model), jnp.float32),
                pltpu.SemaphoreType.DMA((len(xs),)),
                pltpu.SemaphoreType.DMA((len(gs),)),
            ],
        ),
        out_shape=[full, full, jax.ShapeDtypeStruct((rows, model), jnp.bfloat16)],
        input_output_aliases={len(xs) + len(gs) + 7 + k: k for k in range(len(kept))},
        compiler_params=pltpu.CompilerParams(vmem_limit_bytes=VMEM_BYTES),
        cost_estimate=cost(1, 1),
    )(counts, *xs, *gs, *ups, *downs, *shifts, *kept)


def arrange(outs, total):
    to_x, to_y, rest = outs
    half = total.shape[0] // 2
    top, bottom = total[:half].astype(to_x.dtype), total[half:].astype(to_x.dtype)
    step = pl.program_id(0)

    @pl.when(step == 0)
    def _():
        to_x[:half] = top
        to_y[:half] = bottom

    @pl.when(step == 1)
    def _():
        to_x[half:] = top
        rest[half : 2 * half] = bottom

    @pl.when(step == 2)
    def _():
        rest[:half] = top
        to_y[half:] = bottom

    @pl.when(step == 3)
    def _():
        rest[2 * half : 3 * half] = top
        rest[3 * half :] = bottom


def arranged(rows, columns):
    sizes = (rows // 4, rows // 4, rows // 2)
    specs = [pl.BlockSpec((size, columns), lambda i, *_: (0, 0)) for size in sizes]
    return specs, [jax.ShapeDtypeStruct((size, columns), jnp.bfloat16) for size in sizes]


def products_kernel(width, order, active, left, own, other, *outs):
    here = active[order[pl.program_id(0)]] != 0

    @pl.when(here)
    def _():
        total = None
        for k in range(own.shape[0] // width):
            rows = slice(k * width, (k + 1) * width)
            for side, right in enumerate((own, other)):
                start = (2 * k + side) * width
                term = dot_nn(left[:, start : start + width], right[rows])
                total = term if total is None else total + term
        arrange(outs, total)

    @pl.when(jnp.logical_not(here))
    def _():
        arrange(outs, jnp.zeros((left.shape[0], own.shape[1]), jnp.float32))


def products(order, counts, left, own, other):
    blocks = counts.shape[0]
    rows, depth = left.shape
    columns = own.shape[1]
    specs, shapes = arranged(rows, columns)
    return pl.pallas_call(
        functools.partial(products_kernel, 256),
        grid_spec=pltpu.PrefetchScalarGridSpec(
            num_scalar_prefetch=2,
            grid=(blocks,),
            in_specs=[
                pl.BlockSpec((rows // blocks, depth), lambda i, order, *_: (order[i], 0)),
                pl.BlockSpec(own.shape, lambda i, *_: (0, 0)),
                pl.BlockSpec(own.shape, lambda i, *_: (0, 0)),
            ],
            out_specs=specs,
        ),
        out_shape=shapes,
        compiler_params=pltpu.CompilerParams(vmem_limit_bytes=VMEM_BYTES),
        cost_estimate=cost(1, 1),
    )(order, counts, left, own, other)


def attend_out_kernel(left, weight, bias, hidden, active, out_ref):
    out_ref[...] = hidden[...].astype(jnp.float32) + active[...] * (
        dot_nn(left[...], weight[...]) + bias[...]
    )


def attend_out(left, weight, bias, hidden, active):
    rows, depth = left.shape
    columns = weight.shape[1]
    width = 512
    column = pl.BlockSpec((rows, width), lambda j: (0, j))
    return pl.pallas_call(
        attend_out_kernel,
        grid=(columns // width,),
        in_specs=[
            pl.BlockSpec((rows, depth), lambda j: (0, 0)),
            pl.BlockSpec((depth, width), lambda j: (0, j)),
            pl.BlockSpec((1, width), lambda j: (0, j)),
            column,
            pl.BlockSpec((rows, 1), lambda j: (0, 0)),
        ],
        out_specs=column,
        out_shape=jax.ShapeDtypeStruct((rows, columns), jnp.float32),
        compiler_params=pltpu.CompilerParams(vmem_limit_bytes=VMEM_BYTES),
        cost_estimate=cost(1, 1),
    )(left, weight, bias[None], hidden, active)


def attend_out_back_kernel(grad, weight, out_ref):
    out_ref[...] = dot_nt(grad[...], weight[...]).astype(out_ref.dtype)


def attend_out_back(grad, weight):
    rows, columns = grad.shape
    depth = weight.shape[0]
    width = 512
    return pl.pallas_call(
        attend_out_back_kernel,
        grid=(depth // width,),
        in_specs=[
            pl.BlockSpec((rows, columns), lambda j: (0, 0)),
            pl.BlockSpec((width, columns), lambda j: (j, 0)),
        ],
        out_specs=pl.BlockSpec((rows, width), lambda j: (0, j)),
        out_shape=jax.ShapeDtypeStruct((rows, depth), jnp.bfloat16),
        compiler_params=pltpu.CompilerParams(vmem_limit_bytes=VMEM_BYTES),
        cost_estimate=cost(1, 1),
    )(grad, weight)


def project_kernel(inputs, side, parts, *refs):
    xs = refs[:inputs]
    weights, shift, out_ref = refs[inputs:]
    slab = weights.shape[1]
    weight = weights[...].reshape(3 * slab, weights.shape[2])
    for k in range(inputs):

        @pl.when(pl.program_id(0) == k)
        def _(k=k):
            mixed = dot_nt(xs[k][...], weight)
            for t in range(3):
                columns = pl.ds(pl.multiple_of(parts[side, t] * slab, slab), slab)
                out_ref[:, columns] = (
                    mixed[:, t * slab : (t + 1) * slab] + shift[:, columns]
                ).astype(out_ref.dtype)


def project(parts, side, xs, weights, shift):
    size, model = xs[0].shape
    slab = weights.shape[1]
    return pl.pallas_call(
        functools.partial(project_kernel, len(xs), side),
        grid_spec=pltpu.PrefetchScalarGridSpec(
            num_scalar_prefetch=1,
            grid=(len(xs),),
            in_specs=[pl.BlockSpec((size, model), lambda i, *_: (0, 0))] * len(xs)
            + [
                pl.BlockSpec(weights.shape, lambda i, *_: (0, 0, 0)),
                pl.BlockSpec(shift.shape, lambda i, *_: (0, 0)),
            ],
            out_specs=pl.BlockSpec((size, 3 * slab), lambda i, *_: (i, 0)),
        ),
        out_shape=jax.ShapeDtypeStruct((len(xs) * size, 3 * slab), jnp.bfloat16),
        compiler_params=pltpu.CompilerParams(vmem_limit_bytes=VMEM_BYTES),
        cost_estimate=cost(1, 1),
    )(parts, *xs, weights, shift)


def unproject_kernel(order, parts, active, mine, theirs, own, other, *outs):
    slab = own.shape[1]
    here = active[order[pl.program_id(0)]] != 0

    @pl.when(here)
    def _():
        total = None
        for side, (left, right) in enumerate(((mine, own), (theirs, other))):
            for t in range(3):
                columns = pl.ds(pl.multiple_of(parts[side, t] * slab, slab), slab)
                term = dot_nn(left[:, columns], right[t])
                total = term if total is None else total + term
        arrange(outs, total)

    @pl.when(jnp.logical_not(here))
    def _():
        arrange(outs, jnp.zeros((mine.shape[0], own.shape[2]), jnp.float32))


def unproject(order, parts, counts, mine, theirs, own, other):
    blocks = counts.shape[0]
    rows = mine.shape[0]
    slab, model = own.shape[1:]
    left = pl.BlockSpec((rows // blocks, 3 * slab), lambda i, order, *_: (order[i], 0))
    fixed = pl.BlockSpec(own.shape, lambda i, *_: (0, 0, 0))
    specs, shapes = arranged(rows, model)
    return pl.pallas_call(
        unproject_kernel,
        grid_spec=pltpu.PrefetchScalarGridSpec(
            num_scalar_prefetch=3,
            grid=(blocks,),
            in_specs=[left, left, fixed, fixed],
            out_specs=specs,
        ),
        out_shape=shapes,
        compiler_params=pltpu.CompilerParams(vmem_limit_bytes=VMEM_BYTES),
        cost_estimate=cost(1, 1),
    )(order, parts, counts, mine, theirs, own, other)


def weight_grad_kernel(inputs, added, columns, *refs):
    left, rights = refs[0], refs[1 : 1 + inputs]
    tokens, sems = refs[-2:]
    outs = refs[1 + inputs + added : -2]
    fetch(rights, tokens, sems)
    total = dot_tn(left[...], tokens[0])
    if added:
        total = total + refs[1 + inputs][...].astype(jnp.float32)
    size = outs[0].shape[0]
    if size == total.shape[0]:
        for k, out_ref in enumerate(outs):

            @pl.when((len(outs) == 1) | (pl.program_id(0) == k))
            def _(out_ref=out_ref):
                out_ref[...] = total.astype(out_ref.dtype)

    else:
        for k, out_ref in enumerate(outs):
            out_ref[...] = total[k * size : (k + 1) * size].astype(out_ref.dtype)


def weight_grad(left, columns, tile, rights, extra=None, outputs=1, apart=False, counted=False):
    rows = left.shape[0]
    model = rights[0].shape[1]
    steps = columns.shape[0]
    output = pl.BlockSpec((tile // outputs, model), lambda i, *_: (i, 0))
    extras = [] if extra is None else [extra]
    shape = jax.ShapeDtypeStruct((steps * tile // outputs, model), jnp.bfloat16)
    added = [output] * len(extras)
    if apart:
        outputs = steps
        output = pl.BlockSpec((tile, model), lambda i, *_: (0, 0))
        shape = jax.ShapeDtypeStruct((tile, model), jnp.bfloat16)
    results = pl.pallas_call(
        functools.partial(weight_grad_kernel, len(rights), len(extras)),
        grid_spec=pltpu.PrefetchScalarGridSpec(
            num_scalar_prefetch=1,
            grid=(steps,),
            in_specs=[pl.BlockSpec((rows, tile), lambda i, columns: (0, columns[i]))]
            + [pl.BlockSpec(memory_space=pl.ANY)] * len(rights)
            + added,
            out_specs=[output] * outputs,
            scratch_shapes=[
                pltpu.VMEM((1, rows, model), jnp.bfloat16),
                pltpu.SemaphoreType.DMA((len(rights),)),
            ],
        ),
        out_shape=[shape] * outputs,
        compiler_params=pltpu.CompilerParams(vmem_limit_bytes=VMEM_BYTES),
        cost_estimate=cost(2 * steps * tile * rows * model, 4 * rows * model) if counted else cost(1, 1),
    )(columns, left, *rights, *extras)
    return results[0] if outputs == 1 else results


def chain_sum(values, axis):
    size = lax.axis_size(axis)
    if size != 4:
        return lax.psum(values.astype(jnp.bfloat16), axis).astype(jnp.float32)
    place = lax.axis_index(axis)
    outer = lax.ppermute(values.astype(jnp.bfloat16), axis, [(0, 1), (3, 2)])
    half = (values + outer.astype(jnp.float32)).astype(jnp.bfloat16)
    other = lax.ppermute(half, axis, [(1, 2), (2, 1)])
    whole = (half.astype(jnp.float32) + other.astype(jnp.float32)).astype(jnp.bfloat16)
    ends = lax.ppermute(whole, axis, [(1, 0), (2, 3)])
    inner = (place == 1) | (place == 2)
    return jnp.where(inner, whole, ends).astype(jnp.float32)


def normalize(values):
    center = values - jnp.mean(values, axis=-1, keepdims=True)
    inverse = lax.rsqrt(jnp.mean(center * center, axis=-1, keepdims=True) + epsilon)
    return center * inverse, inverse


def normalize_back(grad, gain, normal, inverse):
    scaled = grad * gain
    grad_values = inverse * (
        scaled
        - jnp.mean(scaled, axis=-1, keepdims=True)
        - normal * jnp.mean(scaled * normal, axis=-1, keepdims=True)
    )
    return grad_values, jnp.sum(grad * normal, axis=0), jnp.sum(grad, axis=0)


def local_general(
    hidden,
    cotangent,
    exit_layer,
    ln1_gain,
    ln1_bias,
    qkv_weight,
    query_bias,
    value_bias,
    out_weight,
    out_bias,
    ln2_gain,
    ln2_bias,
    up_weight,
    up_bias,
    down_weight,
    down_bias,
):
    width = lax.axis_size("wide")
    rank = lax.axis_index("wide")
    rows, model = hidden.shape
    group = rows * width
    slab = model // width
    head_size = model // HEADS
    units_own = up_weight.shape[0]
    keep = exit_layer >= LAYER
    counts = jnp.sum(keep.astype(jnp.int32), axis=1)
    active = lax.dynamic_slice_in_dim(keep.reshape(group), rank * rows, rows, 0)
    active = active.astype(jnp.float32)[:, None]
    grad_out = cotangent.astype(jnp.float32)

    routes = [[(w, (3 * w + t) % width) for w in range(width)] for t in range(3)]
    part_at = np.zeros((width, 3), np.int32)
    for t in range(3):
        for w, d in routes[t]:
            part_at[d, t] = (3 * w + t) // width
    place_of = jnp.asarray(np.argsort(part_at, axis=1).astype(np.int32))[rank]
    part_of = jnp.asarray(part_at)[rank]

    hidden_wide = hidden.astype(jnp.float32)
    normal1, inverse1 = normalize(hidden_wide)
    normed1 = lax.all_gather(
        (normal1 * ln1_gain + ln1_bias).astype(jnp.bfloat16), "wide", axis=0, tiled=True
    )
    slabs = qkv_weight.reshape(3, slab, model)
    received = jnp.stack([lax.ppermute(slabs[t], "wide", routes[t]) for t in range(3)])
    qkv_own = jnp.concatenate(
        [lax.dynamic_index_in_dim(received, place_of[p], 0, keepdims=False) for p in range(3)]
    )
    own = lambda vector: lax.dynamic_slice_in_dim(vector, rank * slab, slab, 0)
    qkv_shift = jnp.concatenate(
        [own(query_bias), jnp.zeros((slab,), jnp.float32), own(value_bias)]
    )

    grad_ffn = (active * grad_out).astype(jnp.bfloat16)
    down_bias_grad = jnp.sum(grad_ffn.astype(jnp.float32), axis=0)
    piece = rows // CHUNKS
    part = lambda values, c: values[c * piece : (c + 1) * piece]
    gather = lambda values: lax.all_gather(values, "wide", axis=0, tiled=True)
    scatter = lambda values: lax.psum_scatter(
        values.astype(jnp.bfloat16), "wide", scatter_dimension=0, tiled=True
    )
    grad_ffns = [gather(part(grad_ffn, c)) for c in range(CHUNKS)]
    out_whole = gather(out_weight)

    mixed = (dot_nt(normed1, qkv_own) + qkv_shift).astype(jnp.bfloat16)
    mixed = jnp.split(mixed, group // TILE)
    slots = jnp.arange(group // TILE, dtype=jnp.int32).reshape(counts.shape[0], -1)
    attended, logs = attend(mixed, slots, counts, head_size)
    attended_rows = lax.all_to_all(attended, "wide", split_axis=0, concat_axis=1, tiled=True)
    middle = hidden_wide + active * (dot_nn(attended_rows, out_whole) + out_bias)
    normal2, inverse2 = normalize(middle)
    normed2 = (normal2 * ln2_gain + ln2_bias).astype(jnp.bfloat16)
    up_shift = lax.dynamic_slice_in_dim(up_bias, rank * units_own, units_own, 0)

    normed2s = [gather(part(normed2, c)) for c in range(CHUNKS)]
    units, grad_pres, grad_normed2, ffn_out = [], [], [], []
    for c in range(CHUNKS):
        grad_units = dot_nt(grad_ffns[c], down_weight)
        pre = dot_nt(normed2s[c], up_weight) + up_shift
        below = 0.5 + 0.5 * lax.erf(pre * 0.7071067811865476)
        bell = jnp.exp(-0.5 * pre * pre) * 0.3989422804014327
        units.append((pre * below).astype(jnp.bfloat16))
        grad_pres.append((grad_units * (below + pre * bell)).astype(jnp.bfloat16))
        grad_normed2.append(scatter(dot_nn(grad_pres[c], up_weight)))
    for c in range(CHUNKS):
        ffn_out.append(scatter(dot_nn(units[c], down_weight)))
    grad_normed2 = jnp.concatenate(grad_normed2).astype(jnp.float32)
    ffn_out = jnp.concatenate(ffn_out).astype(jnp.float32)
    output = (middle + active * (ffn_out + down_bias)).astype(jnp.bfloat16)

    up_bias_own = sum(jnp.sum(g.astype(jnp.float32), axis=0) for g in grad_pres)
    down_grad = sum(dot_tn(units[c], grad_ffns[c]) for c in range(CHUNKS))
    up_grad = sum(dot_tn(grad_pres[c], normed2s[c]) for c in range(CHUNKS))
    halves = lambda values: jnp.concatenate(
        [chain_sum(half, "batch") for half in jnp.split(values, 2)]
    )
    down_grad = halves(down_grad)
    up_grad = halves(up_grad)

    grad_middle, ln2_gain_grad, ln2_bias_grad = normalize_back(
        grad_normed2, ln2_gain, normal2, inverse2
    )
    grad_middle = grad_out + grad_middle
    grad_branch = (active * grad_middle).astype(jnp.bfloat16)
    out_bias_grad = jnp.sum(grad_branch.astype(jnp.float32), axis=0)
    grad_attended = dot_nt(grad_branch, out_whole).astype(jnp.bfloat16)
    grad_heads = lax.all_to_all(grad_attended, "wide", split_axis=1, concat_axis=0, tiled=True)
    out_grad = chain_sum(scatter(dot_tn(attended_rows, grad_branch)).astype(jnp.float32), "batch")

    placed = lambda vector, size: lax.dynamic_update_slice_in_dim(
        jnp.zeros((size,), jnp.float32), vector, rank * vector.shape[0], 0
    )
    early = lax.psum(
        (
            out_bias_grad,
            ln2_gain_grad,
            ln2_bias_grad,
            placed(up_bias_own, up_bias.shape[0]),
            down_bias_grad,
        ),
        ("batch", "wide"),
    )

    grad_mixed = jnp.concatenate(
        attend_back(mixed, slots, grad_heads, attended, logs, counts, head_size)
    )
    grad_normed1 = scatter(dot_nn(grad_mixed, qkv_own)).astype(jnp.float32)
    sums = jnp.sum(grad_mixed.astype(jnp.float32), axis=0)
    qkv_parts = []
    for t in range(3):
        columns = lax.dynamic_slice_in_dim(grad_mixed, part_of[t] * slab, slab, 1)
        total = chain_sum(dot_tn(columns, normed1), "batch").astype(jnp.bfloat16)
        back = [(d, w) for w, d in routes[t]]
        qkv_parts.append(lax.ppermute(total, "wide", back).astype(jnp.float32))
    qkv_grad = jnp.concatenate(qkv_parts)

    grad_hidden, ln1_gain_grad, ln1_bias_grad = normalize_back(
        grad_normed1, ln1_gain, normal1, inverse1
    )
    input_grad = grad_middle + grad_hidden
    late = lax.psum(
        (
            ln1_gain_grad,
            ln1_bias_grad,
            placed(sums[:slab], model),
            placed(sums[2 * slab :], model),
        ),
        ("batch", "wide"),
    )
    return (
        output,
        input_grad,
        late[0],
        late[1],
        qkv_grad,
        late[2],
        late[3],
        out_grad,
        early[0],
        early[1],
        early[2],
        up_grad,
        early[3],
        down_grad,
        early[4],
    )


def swap(values, bits):
    width = lax.axis_size("wide")
    return lax.ppermute(values, "wide", [(w, w ^ bits) for w in range(width)])


def after(values, *done):
    return lax.optimization_barrier((values, done))[0]


def relay(along_x, along_y):
    half = along_x.shape[0] // 2
    return [swap(along_y[:half], 2), swap(along_x[half:], 4)]


class Scatter:
    def __init__(self, to_x, to_y, rest):
        self.half = half = to_x.shape[0] // 2
        self.sent = (to_x, to_y)
        self.rest = rest
        self.from_x, self.from_y = swap(to_x, 2), swap(to_y, 4)

    def second(self, *done):
        half = self.half
        from_x, from_y = after((self.from_x, self.from_y), *done)
        self.near = (from_x[half:], from_y[half:])
        self.own = self.rest[2 * half :]
        return self.forward(self.rest[:half], self.rest[half : 2 * half], from_x[:half], from_y[:half])

    def forward(self, along_y, along_x, top, bottom):
        wide = lambda values: values.astype(jnp.float32)
        y_top = (wide(along_y) + wide(top)).astype(jnp.bfloat16)
        x_bottom = (wide(along_x) + wide(bottom)).astype(jnp.bfloat16)
        self.last = (swap(y_top, 4), swap(x_bottom, 2))
        return y_top, x_bottom

    def finish(self, *done):
        wide = lambda values: values.astype(jnp.float32)
        y_top, x_bottom = after(self.last, *done)
        x_top, y_bottom = self.near
        return jnp.concatenate(
            [
                wide(self.own[: self.half]) + wide(x_top) + wide(y_top),
                wide(self.own[self.half :]) + wide(x_bottom) + wide(y_bottom),
            ]
        )


def split_for_scatter(own, along_x, along_y, diagonal):
    half = own.shape[0] // 2
    return (
        jnp.concatenate([diagonal[:half], along_x[:half]]),
        jnp.concatenate([diagonal[half:], along_y[half:]]),
        jnp.concatenate([along_y[:half], along_x[half:], own]),
    )


class EarlyScatter(Scatter):
    def __init__(self, own, along_x, along_y):
        self.half = half = own.shape[0] // 2
        self.own, self.along_x, self.along_y = own, along_x, along_y
        self.near = (swap(along_x[:half], 2), swap(along_y[half:], 4))

    def first(self, diagonal):
        self.from_far = (swap(diagonal[: self.half], 2), swap(diagonal[self.half :], 4))
        self.near = after(self.near, diagonal)
        return self.near

    def second(self, *done):
        half = self.half
        far = after(self.from_far, *done)
        return self.forward(self.along_y[:half], self.along_x[half:], *far)


def tree_sum(values):
    total = values + swap(values, 1)
    total = (total + swap(total, 2)) + (swap(total, 4) + swap(total, 6))
    size = lax.axis_size("batch")
    terms = [total] + [
        lax.ppermute(total, "batch", [(z, z ^ bits) for z in range(size)])
        for bits in range(1, size)
    ]
    while len(terms) > 1:
        terms = [terms[k] + terms[k + 1] for k in range(0, len(terms), 2)]
    return terms[0]


def local_chips(
    hidden,
    cotangent,
    exit_layer,
    ln1_gain,
    ln1_bias,
    qkv_weight,
    query_bias,
    value_bias,
    out_weight,
    out_bias,
    ln2_gain,
    ln2_bias,
    up_weight,
    up_bias,
    down_weight,
    down_bias,
):
    width = lax.axis_size("wide")
    rank = lax.axis_index("wide")
    rows, model = hidden.shape
    group = rows * width
    slab = model // width
    head_size = model // HEADS
    units_own = up_weight.shape[0]
    keep = exit_layer >= LAYER
    counts = jnp.sum(keep.astype(jnp.int32), axis=1)
    active = lax.dynamic_slice_in_dim(keep.reshape(group), rank * rows, rows, 0)
    active = active.astype(jnp.float32)[:, None]
    grad_out = cotangent.astype(jnp.float32)

    tiles = jnp.arange(group // rows, dtype=jnp.int32)
    slots = ((tiles ^ rank) & 1) * 4 + ((tiles >> 1) ^ (rank >> 1))
    slots = slots.reshape(counts.shape[0], -1)

    routes = [[(w, (3 * w + t) % width) for w in range(width)] for t in range(3)]
    part_at = np.zeros((width, 3), np.int32)
    for t in range(3):
        for w, d in routes[t]:
            part_at[d, t] = (3 * w + t) // width
    part_at = jnp.asarray(part_at)
    other = rank ^ 1
    parts = jnp.stack([part_at[rank], part_at[other]])

    hidden_wide = hidden.astype(jnp.float32)
    normal1, inverse1 = normalize(hidden_wide)
    slabs = qkv_weight.reshape(3, slab, model)
    slabs = [lax.ppermute(slabs[t], "wide", routes[t]) for t in range(3)]
    normed1 = (normal1 * ln1_gain + ln1_bias).astype(jnp.bfloat16)
    normed1 = [normed1, swap(normed1, 2), swap(normed1, 4)]
    diagonal1 = relay(normed1[1], normed1[2])
    qkv_own = jnp.stack(after(slabs, normed1[1:]))
    qkv_other = swap(qkv_own, 1)

    def shift_of(device):
        own = lambda vector: lax.dynamic_slice_in_dim(vector, device * slab, slab, 0)
        shift = [own(query_bias), jnp.zeros((slab,), jnp.float32), own(value_bias)]
        return jnp.concatenate(shift)[None]

    bias_of = lambda device: lax.dynamic_slice_in_dim(up_bias, device * units_own, units_own, 0)
    up_shifts = [bias_of(rank)[None], bias_of(other)[None]]

    mixed_near = project(parts, 0, normed1, qkv_own, shift_of(rank))
    qkv_other = after(qkv_other, mixed_near)
    lent_near = project(parts, 1, normed1, qkv_other, shift_of(other))
    diagonal1 = after(diagonal1, lent_near)
    lent_far = project(parts, 1, diagonal1, qkv_other, shift_of(other))
    mixed_far = project(parts, 0, after(diagonal1, lent_far), qkv_own, shift_of(rank))
    mixed = [mixed_near, mixed_far, swap(lent_near, 1), swap(lent_far, 1)]

    out_whole = lax.all_gather(after(out_weight, diagonal1), "wide", axis=0, tiled=True)
    grad_ffn = (after(active, diagonal1) * grad_out).astype(jnp.bfloat16)
    down_bias_grad = jnp.sum(grad_ffn.astype(jnp.float32), axis=0)
    grad_ffn = [grad_ffn, swap(grad_ffn, 2), swap(grad_ffn, 4)]

    attended, logs = attend(mixed, slots, counts, head_size)
    attended_rows = lax.all_to_all(attended, "wide", split_axis=0, concat_axis=1, tiled=True)
    attended_rows = after(attended_rows, grad_ffn[1:])
    up_other, down_other = swap(after((up_weight, down_weight), attended), 1)
    middle = attend_out(attended_rows, out_whole, out_bias, hidden, active)
    normal2, inverse2 = normalize(middle)
    normed2 = (normal2 * ln2_gain + ln2_bias).astype(jnp.bfloat16)
    normed2 = [normed2, swap(normed2, 2), swap(normed2, 4)]

    per_tile = jnp.sum(keep.reshape(group // rows, rows).astype(jnp.int32), axis=1)
    block_chip = (rank >> 1) ^ jnp.arange(4, dtype=jnp.int32)
    block_counts = per_tile[2 * block_chip + (rank & 1)]
    ups, downs = [up_weight, up_other], [down_weight, down_other]

    def ffn(place, block, xs, gs, kept):
        *kept, partial = ffn_blocks(
            place, block, block_counts, xs, gs, ups, downs, up_shifts, tuple(kept)
        )
        return kept, partial

    kept, partial_own = ffn(2, 0, normed2[:1], grad_ffn[:1], ())
    normed2[1:] = after(normed2[1:], partial_own)
    diagonal2 = relay(normed2[1], normed2[2])
    diagonal_ffn = relay(*after(grad_ffn[1:], attended_rows))
    kept, partial_near = ffn(0, 1, normed2[1:], grad_ffn[1:], kept)
    scatter2 = EarlyScatter(partial_own, partial_near[:rows], partial_near[rows:])
    diagonal2 = after(diagonal2, partial_near)
    (units, grad_pres), partial_far = ffn(3, 3, diagonal2, diagonal_ffn, kept)
    wait = scatter2.first(partial_far)
    tokens2 = [*normed2[1:], normed2[0], *diagonal2]
    tokens_ffn = [*grad_ffn[1:], grad_ffn[0], *diagonal_ffn]

    wide = lambda values: values.astype(jnp.float32)
    lowered = lambda values: values.astype(jnp.bfloat16)
    tile = 512
    tiles = jnp.arange(2 * units_own // tile, dtype=jnp.int32)

    down_own, down_lent = weight_grad(after(units, wait), tiles, tile, tokens_ffn, outputs=2)
    wait = scatter2.second(down_lent)
    down_lent = swap(down_lent, 1)
    up_own, up_lent = weight_grad(
        after(grad_pres, wait), tiles, tile, tokens2, outputs=2, counted=True
    )

    up_lent = swap(up_lent, 1)
    down_sum = lowered(wide(down_own) + wide(after(down_lent, up_own)))
    grad_middle, ln2_gain_grad, ln2_bias_grad = normalize_back(
        scatter2.finish(up_own), ln2_gain, normal2, inverse2
    )
    grad_middle = grad_out + grad_middle
    grad_branch = (active * grad_middle).astype(jnp.bfloat16)
    out_bias_grad = jnp.sum(grad_branch.astype(jnp.float32), axis=0)
    grad_branch = after(grad_branch, down_sum)
    grad_attended = attend_out_back(grad_branch, out_whole)
    grad_heads = lax.all_to_all(grad_attended, "wide", split_axis=1, concat_axis=0, tiled=True)
    owners = 2 * block_chip + (rank & 1)
    grad_branch = after(grad_branch, grad_attended)
    out_lent = weight_grad(attended_rows, owners ^ 1, slab, [grad_branch])
    up_sum = lowered(wide(up_own) + wide(after(up_lent, out_lent)))
    down_grad, up_grad = lax.psum((down_sum, up_sum), "batch")
    out_lent = swap(out_lent, 1)
    out_own = weight_grad(after(attended_rows, up_sum), owners, slab, [grad_branch], out_lent)

    back_own, back_other = attend_back(
        mixed, slots, after(grad_heads, out_own), attended, logs, counts, head_size
    )

    theirs = swap(back_other, 1)
    out_own = after(out_own, back_own)
    scatter_out = Scatter(*split_for_scatter(*jnp.split(out_own, 4)))
    order = jnp.array([3, 0, 1, 2], jnp.int32)
    ffn_counts = block_counts[jnp.array([1, 2, 0, 3])]
    ffn_parts = products(order, ffn_counts, after(units, scatter_out.sent), *downs)
    tokens1 = [*normed1, *diagonal1]
    theirs = after(theirs, ffn_parts[0])
    qkv_lent = weight_grad(theirs, parts[1], slab, tokens1)
    wait = scatter_out.second(qkv_lent)
    grad_parts = unproject(
        jnp.array([3, 1, 2, 0], jnp.int32),
        parts,
        block_counts,
        after(back_own, wait),
        theirs,
        qkv_own,
        qkv_other,
    )
    qkv_lent = swap(qkv_lent, 1)
    scatter1 = Scatter(*grad_parts)
    qkv_total = weight_grad(
        after(back_own, grad_parts[0]),
        parts[0],
        slab,
        tokens1,
        after(qkv_lent, grad_parts[0]),
        apart=True,
    )

    returned = [
        lax.ppermute(total, "wide", [(d, w) for w, d in route])
        for total, route in zip(qkv_total, routes)
    ]
    down_grad, up_grad = after((down_grad, up_grad), returned)
    out_total = lowered(scatter_out.finish(up_grad))
    *qkv_grad, out_grad = lax.psum(after((*returned, out_total), up_grad), "batch")
    wait = scatter1.second(out_total, up_grad)
    scatter_ffn = Scatter(*after(ffn_parts, wait))
    grad_normed1 = scatter1.finish(wait, scatter_ffn.sent)
    grad_hidden, ln1_gain_grad, ln1_bias_grad = normalize_back(
        grad_normed1, ln1_gain, normal1, inverse1
    )
    input_grad = grad_middle + grad_hidden
    grad_pres, back_own, back_other = after((grad_pres, back_own, back_other), wait)
    up_bias_own = jnp.sum(wide(grad_pres), axis=0).reshape(-1, 2, 256)
    up_bias_own = [up_bias_own[:, side].reshape(units_own) for side in range(2)]
    sums = jnp.sum(wide(back_own), axis=0) + jnp.sum(wide(back_other), axis=0)
    wait = scatter_ffn.second(input_grad)
    down_grad, up_grad = wide(after(down_grad, wait)), wide(after(up_grad, wait))
    ffn_out = scatter_ffn.finish(down_grad, up_grad)
    output = (middle + active * (ffn_out + down_bias)).astype(jnp.bfloat16)
    placed = lambda vector, size, device: lax.dynamic_update_slice_in_dim(
        jnp.zeros((size,), jnp.float32), vector, device * vector.shape[0], 0
    )
    smalls = tree_sum(
        jnp.concatenate(
            [
                placed(up_bias_own[0], up_bias.shape[0], rank)
                + placed(up_bias_own[1], up_bias.shape[0], other),
                down_bias_grad,
                out_bias_grad,
                ln2_gain_grad,
                ln2_bias_grad,
                placed(sums[:slab], model, rank),
                placed(sums[2 * slab :], model, rank),
                ln1_gain_grad,
                ln1_bias_grad,
            ]
        )
    )
    up_bias_grad = smalls[: up_bias.shape[0]]
    smalls = smalls[up_bias.shape[0] :].reshape(8, model)
    qkv_grad = wide(jnp.concatenate(qkv_grad))
    out_grad = wide(out_grad)
    return (
        output,
        input_grad,
        smalls[6],
        smalls[7],
        qkv_grad,
        smalls[4],
        smalls[5],
        out_grad,
        smalls[1],
        smalls[2],
        smalls[3],
        up_grad,
        up_bias_grad,
        down_grad,
        smalls[0],
    )


def solution(mesh):
    chips = mesh.shape["wide"] == 8 and mesh.shape["batch"] == 4
    local = local_chips if chips else local_general
    rows = P(("batch", "wide"), None)
    weight = P("wide", None)
    return jax.shard_map(
        local,
        mesh=mesh,
        in_specs=(
            rows,
            rows,
            P("batch", None),
            P(),
            P(),
            weight,
            P(),
            P(),
            weight,
            P(),
            P(),
            P(),
            weight,
            P(),
            weight,
            P(),
        ),
        out_specs=(
            rows,
            rows,
            P(),
            P(),
            weight,
            P(),
            P(),
            weight,
            P(),
            P(),
            P(),
            weight,
            P(),
            weight,
            P(),
        ),
        check_vma=False,
    )
```
